32 devices in a mesh: dp: 4 (over y, core), expert: 8 (over z, x).
Axes of the slice: x: 2, y: 2, z: 4, core: 2. Of those that a mesh axis runs over, the one named last changes fastest.
Arguments:
- tokens: bfloat16 [4096, 2048], P(('dp', 'expert')), may hold values from -6 to 6
- cotangent: bfloat16 [4096, 2048], P(('dp', 'expert')), may hold values from -1.1953125 to 1.1953125
- routes: int32 [4096, 1], P(('dp', 'expert')), may hold values from 0 to 7; in each aligned block of 128 rows (0 to 127, 128 to 255, ...) at most 18 rows name the same one
- expert_gates: float32 [4096, 1], P(('dp', 'expert')), may hold values from 0.1 to 1
- gate_proj: bfloat16 [2048, 6144], P(None, 'expert'), may hold values from -0.125 to 0.125
- up_proj: bfloat16 [2048, 6144], P(None, 'expert'), may hold values from -0.125 to 0.125
- down_proj: bfloat16 [6144, 2048], P('expert'), may hold values from -0.21875 to 0.21875
Outputs:
- grad_input: bfloat16 [4096, 2048], P(('dp', 'expert'))
- grad_gate: float32 [2048, 6144], P('dp', 'expert')
- grad_up: float32 [2048, 6144], P('dp', 'expert')
- grad_down: float32 [6144, 2048], P('expert', 'dp')
The draws below stay inside these ranges and needn't reach their ends.
Inputs may be any that keep to these rules, and one draw needn't show every extreme that they name: `routes`: each row names exactly one expert. Among the rows of one device no expert is named more than 18 times.
All inputs are finite; a program needn't handle non-finite values.
Results may differ from the reference program's by a relative error of at most 0.022.
Values may be sent and summed in bfloat16 or wider, within the bound.
No kernel may reach another device: no remote copies, remote signals or barrier semaphores. Data moves between devices by JAX's collectives and lax.ppermute only.
A program may use at most 64 MiB of HBM per device.

```python
import math
import jax
import jax.numpy as jnp
import numpy as np
from jax import lax

D = 2048
HID = 768
EXPERTS = 8
TOP = 1
TOK_DEV = 128
MOST = 18
TOKENS = 4096
N_DP = 4
N_EXPERT = 8


def strengthened(result, key, source, target, blocks, factor):
    owner, partner = [(jnp.arange(result.shape[position]) // (result.shape[position] // blocks)).reshape([-1 if axis == position else 1 for axis in range(result.ndim)]) for position in (source, target)]
    chosen = jax.random.permutation(key, blocks)[partner]
    strong = (owner == chosen) | (owner == (partner + blocks // 2) % blocks)
    return jnp.where(strong, factor * result, result)


def steps_of(rng, extent, split, smallest, largest):
    loudness, own = 1.0, jax.random.fold_in(rng, 6)
    for axis_at, shards_of in split:
        draws = jnp.exp(jax.random.uniform(jax.random.fold_in(own, axis_at), (shards_of,), jnp.float32, smallest / len(split), largest / len(split)))
        loudness = loudness * jnp.repeat(draws, extent[axis_at] // shards_of).reshape([-1 if axis == axis_at else 1 for axis in range(len(extent))])
    return loudness


def deal_out(stream_key, own, number, rows, number_of, top, most, lean):
    order = jax.random.permutation(stream_key, number_of)
    crowded, usual = shares(number_of, rows * top, most, lean, True), shares(number_of, rows * top, most, lean, False)
    places = jnp.arange(number_of)

    def named(lengths, offset_by):
        used = int((lengths > 0).sum())
        fixed = max(1, used // 4)
        moved = fixed + (places - fixed + offset_by * (used - fixed)) % max(1, number_of - fixed)
        return jnp.zeros((number_of,), jnp.int32).at[order[jnp.where(places < fixed, places, moved)]].set(jnp.asarray(lengths, jnp.int32))

    lengths = jnp.where(number % 4 == 0, named(crowded, number // 4), named(usual, number - number // 4 - 1))
    mixed = jax.random.permutation(jax.random.fold_in(own, 3), number_of)
    giver, taker = mixed[0:number_of // 2 * 2:2], mixed[1:number_of // 2 * 2:2]
    slack = jnp.minimum(lengths[giver] - 1, most - lengths[taker]) // 2
    slack = jnp.where((giver == order[0]) | (taker == order[0]) | (lengths[taker] == 0), 0, jnp.maximum(slack, 0))
    moved = jax.random.randint(jax.random.fold_in(own, 4), (number_of // 2,), 0, 1 << 20) % (slack + 1)
    lengths = lengths.at[giver].add(-moved).at[taker].add(moved)
    labels = jnp.searchsorted(jnp.cumsum(lengths), jnp.arange(rows * top), side="right").astype(jnp.int32)
    grid = labels.reshape(top, rows).T
    grid = grid[jax.random.permutation(jax.random.fold_in(own, 1), rows)]
    offset_by = jax.random.randint(jax.random.fold_in(own, 2), (rows, 1), 0, top)
    return jnp.take_along_axis(grid, (jnp.arange(top)[None, :] + offset_by) % top, axis=1)


def shares(number_of, total, reach, lean, full):
    weights = [(1 << 20) // math.isqrt(standing ** lean) + 1 for standing in range(1, number_of + 1)]
    largest = reach if full else min(reach, max(-(-total // number_of), total * weights[0] // sum(weights)))
    least = 1 if total - largest >= number_of - 1 else 0
    counts, rest = [largest] + [least] * (number_of - 1), total - largest - least * (number_of - 1)
    while rest > 0:
        movable = [i for i in range(1, number_of) if counts[i] < largest] or [i for i in range(1, number_of) if counts[i] < reach]
        pool, budget = sum([weights[i] for i in movable]), rest
        for i in movable:
            extra = min(reach - counts[i], max(1, budget * weights[i] // pool), rest)
            counts[i] = counts[i] + extra
            rest = rest - extra
    return np.array(counts)


def noise(stream_key, dims, deviation, bound, shards=(), held_as=jnp.bfloat16):
    drawn = jax.random.normal(stream_key, dims, jnp.float32) * deviation
    if len(shards) > 0:
        drawn = steps_of(stream_key, dims, shards, -0.22, 0.18) * drawn
    return jnp.clip(drawn, min=-bound, max=bound).astype(held_as)


def bell_draw_with(stream_key, shape, deviation, most, pieces, heavy, kind=jnp.bfloat16):
    result = deviation * jax.random.normal(stream_key, shape, jnp.float32)
    if pieces:
        result = result * steps_of(stream_key, shape, pieces, -0.22, 0.18)
    return jnp.clip(strengthened(result, jax.random.fold_in(stream_key, 3), *heavy), -most, most).astype(kind)


def setup_inputs(seed: int = 0) -> dict:
    keys = jax.random.split(jax.random.key(seed), 8)
    tokens = noise(keys[0], (TOKENS, D), 1.0, 6.0, ((0, 32),))
    cotangent = bell_draw_with(keys[1], (TOKENS, D), 0.2, 1.1953125, ((0, 32),), (0, 1, 32, 2.75))
    routes_keys = jax.random.split(jax.random.fold_in(keys[2], 1), TOKENS // TOK_DEV)
    routes_turns = jax.random.permutation(jax.random.fold_in(keys[2], 3), TOKENS // TOK_DEV)
    routes = jax.vmap(lambda own, number: deal_out(jax.random.fold_in(keys[2], 2), own, number, TOK_DEV, EXPERTS, TOP, MOST, 0))(routes_keys, routes_turns).reshape((TOKENS, TOP))
    expert_gates = jnp.clip(0.1 + 0.9 * jax.random.uniform(keys[3], (TOKENS, TOP), jnp.float32) ** steps_of(keys[3], (TOKENS, TOP), ((0, 32),), -0.2, 0.2), 0.1, 1.0)
    gate_proj = noise(keys[4], (D, EXPERTS * HID), D ** -0.5, 0.125, ((1, 8),))
    up_proj = noise(keys[5], (D, EXPERTS * HID), D ** -0.5, 0.125, ((1, 8),))
    down_proj = noise(keys[6], (EXPERTS * HID, D), HID ** -0.5, 0.21875, ((0, 8),))
    return {"tokens": tokens, "cotangent": cotangent, "routes": routes, "expert_gates": expert_gates, "gate_proj": gate_proj, "up_proj": up_proj, "down_proj": down_proj}


def slice_terms(group_x, scaled, gate_cols, up_cols, down_rows):
    pre_gate = jnp.dot(group_x, gate_cols, preferred_element_type=jnp.float32)
    pre_up = jnp.dot(group_x, up_cols, preferred_element_type=jnp.float32)
    gate_sig = jax.nn.sigmoid(pre_gate)
    hidden = (pre_gate * gate_sig * pre_up).astype(jnp.bfloat16)
    d_hidden = jnp.dot(scaled, down_rows.T, preferred_element_type=jnp.float32)
    d_gate = (d_hidden * pre_up * gate_sig * (1.0 + pre_gate * (1.0 - gate_sig))).astype(jnp.bfloat16)
    d_up = (d_hidden * pre_gate * gate_sig).astype(jnp.bfloat16)
    slice_input = (jnp.dot(d_gate, gate_cols.T, preferred_element_type=jnp.float32)
                   + jnp.dot(d_up, up_cols.T, preferred_element_type=jnp.float32)).astype(jnp.bfloat16)
    part_down = jnp.dot(hidden.T, scaled, preferred_element_type=jnp.float32)
    part_gate = jnp.dot(group_x.T, d_gate, preferred_element_type=jnp.float32)
    part_up = jnp.dot(group_x.T, d_up, preferred_element_type=jnp.float32)
    return slice_input, part_gate, part_up, part_down


def rounded(value):
    return lax.optimization_barrier(value.astype(jnp.bfloat16)).astype(jnp.float32)


def reference(tokens, cotangent, routes, expert_gates, gate_proj, up_proj, down_proj):
    group_size = N_EXPERT // EXPERTS
    hid_dev = HID // group_size
    group_rows = TOK_DEV * N_EXPERT
    capacity = N_EXPERT * MOST
    assigned = group_rows * TOP

    def one_group(totals, group_id):
        start = group_id * group_rows
        group_tok = lax.dynamic_slice_in_dim(tokens, start, group_rows, 0)
        group_dy = lax.dynamic_slice_in_dim(cotangent, start, group_rows, 0)
        flat_routes = lax.dynamic_slice_in_dim(routes, start, group_rows, 0).reshape(-1)
        weights = lax.dynamic_slice_in_dim(expert_gates, start, group_rows, 0).reshape(-1)
        grad_rows = jnp.zeros((group_rows, D), jnp.float32)
        list_gate, list_up, list_down = [], [], []
        for expert_id in range(EXPERTS):
            picked = jnp.nonzero(flat_routes == expert_id, size=capacity, fill_value=assigned)[0].astype(jnp.int32)
            owners = (picked // TOP).astype(jnp.int32)
            group_x = jnp.take(group_tok, owners, axis=0, mode="fill", fill_value=0)
            gate_vals = jnp.take(weights, picked, mode="fill", fill_value=0)
            scaled = (jnp.take(group_dy, owners, axis=0, mode="fill", fill_value=0).astype(jnp.float32)
                      * gate_vals[:, None]).astype(jnp.bfloat16)
            for piece_id in range(group_size):
                first = expert_id * HID + piece_id * hid_dev
                slice_input, part_gate, part_up, part_down = slice_terms(
                    group_x, scaled, gate_proj[:, first:first + hid_dev],
                    up_proj[:, first:first + hid_dev], down_proj[first:first + hid_dev, :])
                grad_rows = grad_rows.at[owners].add(slice_input.astype(jnp.float32), mode="drop")
                list_gate.append(part_gate)
                list_up.append(part_up)
                list_down.append(part_down)
        total_gate = totals[0] + rounded(jnp.concatenate(list_gate, 1))
        total_up = totals[1] + rounded(jnp.concatenate(list_up, 1))
        total_down = totals[2] + rounded(jnp.concatenate(list_down, 0))
        return (total_gate, total_up, total_down), grad_rows.astype(jnp.bfloat16)

    initial = (jnp.zeros((D, EXPERTS * HID), jnp.float32), jnp.zeros((D, EXPERTS * HID), jnp.float32),
               jnp.zeros((EXPERTS * HID, D), jnp.float32))
    sums, grad_input = lax.scan(one_group, initial, jnp.arange(N_DP, dtype=jnp.int32))
    return grad_input.reshape(TOKENS, D), sums[0], sums[1], sums[2]
```

```python
import jax
import jax.numpy as jnp
from jax import lax
from jax.experimental import pallas as pl
from jax.experimental.pallas import tpu as pltpu
from jax.sharding import PartitionSpec as P

EXPERTS = 8
MOST = 18
ROWS = 16
VMEM_LIMIT = 48 * 1024 * 1024


def build_slots(routes, capacity):
    flat_routes = routes.reshape(-1)
    one_hot = (flat_routes[:, None] == jnp.arange(EXPERTS, dtype=jnp.int32)[None, :]).astype(
        jnp.int32
    )
    before = jnp.cumsum(one_hot, axis=0) - one_hot
    position = jnp.sum(before * one_hot, axis=1)
    return flat_routes * capacity + position


def scatter_body(tokens, cotangent, routes, expert_gates, gate_proj, up_proj, down_proj):
    tok_dev, model_dim = tokens.shape
    top_k = routes.shape[1]
    expert_devs = lax.axis_size("expert")
    group_size = expert_devs // EXPERTS
    capacity = MOST
    slot_total = EXPERTS * capacity
    slot_of = build_slots(routes, capacity)
    owners = jnp.arange(tok_dev * top_k, dtype=jnp.int32) // top_k
    slot_table = jnp.full((slot_total,), tok_dev, jnp.int32).at[slot_of].set(owners)
    slot_gate = jnp.zeros((slot_total,), jnp.float32).at[slot_of].set(expert_gates.reshape(-1))
    x_slots = jnp.take(tokens, slot_table, axis=0, mode="fill", fill_value=0)
    dy_slots = (
        jnp.take(cotangent, slot_table, axis=0, mode="fill", fill_value=0).astype(jnp.float32)
        * slot_gate[:, None]
    ).astype(jnp.bfloat16)

    def copies(values):
        spread = values.reshape(EXPERTS, 1, capacity, model_dim)
        return jnp.broadcast_to(spread, (EXPERTS, group_size, capacity, model_dim)).reshape(
            expert_devs, capacity, model_dim
        )

    x_recv, dy_recv = (
        lax.all_to_all(copies(x_slots), "expert", split_axis=0, concat_axis=0, tiled=True),
        lax.all_to_all(copies(dy_slots), "expert", split_axis=0, concat_axis=0, tiled=True),
    )
    in_rows = x_recv.reshape(expert_devs * capacity, model_dim)
    scaled = dy_recv.reshape(expert_devs * capacity, model_dim)
    pre_gate = jnp.dot(in_rows, gate_proj, preferred_element_type=jnp.float32)
    pre_up = jnp.dot(in_rows, up_proj, preferred_element_type=jnp.float32)
    gate_sig = jax.nn.sigmoid(pre_gate)
    hidden = (pre_gate * gate_sig * pre_up).astype(jnp.bfloat16)
    by_width = (((1,), (1,)), ((), ()))
    by_rows = (((0,), (0,)), ((), ()))
    d_hidden = lax.dot_general(scaled, down_proj, by_width, preferred_element_type=jnp.float32)
    d_gate = (d_hidden * pre_up * gate_sig * (1.0 + pre_gate * (1.0 - gate_sig))).astype(
        jnp.bfloat16
    )
    d_up = (d_hidden * pre_gate * gate_sig).astype(jnp.bfloat16)
    grad_down = lax.dot_general(hidden, scaled, by_rows, preferred_element_type=jnp.float32)
    grad_gate = lax.dot_general(in_rows, d_gate, by_rows, preferred_element_type=jnp.float32)
    grad_up = lax.dot_general(in_rows, d_up, by_rows, preferred_element_type=jnp.float32)
    grad_gate, grad_up, grad_down = (
        lax.psum_scatter(
            grad_gate.astype(jnp.bfloat16), "dp", scatter_dimension=0, tiled=True
        ).astype(jnp.float32),
        lax.psum_scatter(
            grad_up.astype(jnp.bfloat16), "dp", scatter_dimension=0, tiled=True
        ).astype(jnp.float32),
        lax.psum_scatter(
            grad_down.astype(jnp.bfloat16), "dp", scatter_dimension=1, tiled=True
        ).astype(jnp.float32),
    )
    joined_grads = jnp.concatenate([d_gate, d_up], 1)
    joined_proj = jnp.concatenate([gate_proj, up_proj], 1)
    partial_value = lax.dot_general(
        joined_grads, joined_proj, by_width, preferred_element_type=jnp.float32
    ).astype(jnp.bfloat16)
    returned = lax.all_to_all(
        partial_value.reshape(expert_devs, capacity, model_dim),
        "expert",
        split_axis=0,
        concat_axis=0,
        tiled=True,
    )
    summed = jnp.sum(
        returned.reshape(EXPERTS, group_size, capacity, model_dim).astype(jnp.float32), axis=1
    )
    summed = summed.reshape(slot_total, model_dim)
    grad_input = jnp.take(summed, slot_of, axis=0).reshape(tok_dev, top_k, model_dim).sum(axis=1)
    return (grad_input.astype(jnp.bfloat16), grad_gate, grad_up, grad_down)


def cut(width):
    pieces = ROWS // (MOST - ROWS)
    return pieces, width // pieces


def params(limit=VMEM_LIMIT):
    return pltpu.CompilerParams(vmem_limit_bytes=limit)


def cost(flops, moved):
    return pl.CostEstimate(flops=flops, bytes_accessed=moved, transcendentals=0)


def whole(count):
    return [pl.BlockSpec(memory_space=pltpu.VMEM)] * count


def slot_masks(me, routes, blocks, width):
    tokens = routes.shape[1]
    pieces, _ = cut(width)
    experts = lax.broadcasted_iota(jnp.int32, (EXPERTS, tokens), 0)
    named = jnp.where(experts == routes, 1.0, 0.0)
    earlier = lax.broadcasted_iota(jnp.int32, (tokens, tokens), 0) < lax.broadcasted_iota(
        jnp.int32, (tokens, tokens), 1
    )
    before = jnp.dot(
        named.astype(jnp.bfloat16),
        jnp.where(earlier, 1.0, 0.0).astype(jnp.bfloat16),
        preferred_element_type=jnp.float32,
    )
    position = jnp.sum(before * named, axis=0, keepdims=True).astype(jnp.int32)
    slot = lax.broadcasted_iota(jnp.int32, (blocks * ROWS, tokens), 0)
    row = slot % ROWS
    mine = (slot // ROWS) ^ me == routes
    main = mine & (position == row)
    spill = mine & (position == ROWS + row // pieces)
    return main, spill, row % pieces


def ones(mask):
    return jnp.where(mask, 1.0, 0.0).astype(jnp.bfloat16)


def send_kernel(scaled, blocks, me_ref, routes_ref, gates_ref, values_ref, *outs):
    tokens, width = values_ref.shape
    pieces, step = cut(width)
    main, spill, piece = slot_masks(me_ref[0], routes_ref[...], blocks, width)
    rows = jnp.dot(ones(main), values_ref[...], preferred_element_type=jnp.float32)
    extra = jnp.zeros((blocks * ROWS, step), jnp.float32)
    for at in range(pieces):
        extra += jnp.dot(
            ones(spill & (piece == at)),
            values_ref[:, at * step : (at + 1) * step],
            preferred_element_type=jnp.float32,
        )
    if scaled:
        gates = gates_ref[...]
        rows = rows * jnp.sum(jnp.where(main, gates, 0.0), axis=1, keepdims=True)
        extra = extra * jnp.sum(jnp.where(spill, gates, 0.0), axis=1, keepdims=True)
    rows = rows.astype(jnp.bfloat16)
    extra = extra.astype(jnp.bfloat16)
    for block in range(blocks):
        part = slice(block * ROWS, (block + 1) * ROWS)
        outs[block][:, :width] = rows[part]
        outs[block][:, width:] = extra[part]


def pack(scaled, blocks, me, routes, gates, values):
    tokens, width = values.shape
    _, step = cut(width)
    shape = jax.ShapeDtypeStruct((ROWS, width + step), jnp.bfloat16)

    def kernel(*refs):
        send_kernel(scaled, blocks, *refs)

    return pl.pallas_call(
        kernel,
        out_shape=[shape] * blocks,
        in_specs=[pl.BlockSpec(memory_space=pltpu.SMEM)] + whole(3),
        out_specs=whole(blocks),
        compiler_params=params(),
        cost_estimate=cost(4 * blocks * ROWS * tokens * width, 4 * tokens * width),
        name="pack",
    )(me, routes, gates, values)


def spill_picks(blocks, pieces, at):
    slot = lax.broadcasted_iota(jnp.int32, (blocks * (MOST - ROWS), blocks * ROWS), 0)
    row = lax.broadcasted_iota(jnp.int32, (blocks * (MOST - ROWS), blocks * ROWS), 1)
    return ones(row == slot * pieces + at)


def unpack(blocks, width):
    tail = []
    extra = jnp.concatenate([block[:, width:] for block in blocks], 0)
    pieces, _ = cut(width)
    for at in range(pieces):
        tail.append(
            jnp.dot(
                spill_picks(len(blocks), pieces, at), extra, preferred_element_type=jnp.float32
            ).astype(jnp.bfloat16)
        )
    return jnp.concatenate([block[:, :width] for block in blocks], 0), jnp.concatenate(tail, 1)


def join(blocks):
    count = len(blocks)
    width = blocks[0].shape[1] * (ROWS // (MOST - ROWS)) // (ROWS // (MOST - ROWS) + 1)
    slots = count * MOST

    def kernel(*refs):
        rows, extra = unpack(refs[:count], width)
        refs[count][: count * ROWS, :] = rows
        refs[count][count * ROWS :, :] = extra

    return pl.pallas_call(
        kernel,
        out_shape=jax.ShapeDtypeStruct((slots, width), jnp.bfloat16),
        in_specs=whole(count),
        out_specs=pl.BlockSpec(memory_space=pltpu.VMEM),
        compiler_params=params(),
        cost_estimate=cost(0, 4 * slots * width),
        name="join",
    )(*blocks)


BY_WIDTH = (((1,), (1,)), ((), ()))
BY_ROWS = (((0,), (0,)), ((), ()))


def dot(left, right, dims=(((1,), (0,)), ((), ()))):
    return lax.dot_general(left, right, dims, preferred_element_type=jnp.float32)


def slice_grads(rows, scaled, gate_cols, up_cols, down_rows):
    pre_gate = dot(rows, gate_cols)
    pre_up = dot(rows, up_cols)
    d_hidden = dot(scaled, down_rows, BY_WIDTH)
    sig = jax.nn.sigmoid(pre_gate)
    silu = pre_gate * sig
    hidden = (silu * pre_up).astype(jnp.bfloat16)
    d_gate = (d_hidden * pre_up * sig * (1.0 + pre_gate * (1.0 - sig))).astype(jnp.bfloat16)
    d_up = (d_hidden * silu).astype(jnp.bfloat16)
    return hidden, d_gate, d_up


def weight_specs(width, tile):
    return [
        pl.BlockSpec((width, tile), lambda i: (0, i)),
        pl.BlockSpec((width, tile), lambda i: (0, i)),
        pl.BlockSpec((tile, width), lambda i: (i, 0)),
    ]


def back(blocks, tile, rows, scaled, gate_proj, up_proj, down_proj):
    slots, width = rows.shape
    hid = gate_proj.shape[1]
    pieces, step = cut(width)
    extras = blocks * (MOST - ROWS)

    def kernel(x_ref, dy_ref, gate_ref, up_ref, down_ref, *rest):
        outs, total = rest[:blocks], rest[blocks]
        gate, up = gate_ref[...], up_ref[...]
        _, d_gate, d_up = slice_grads(x_ref[...], dy_ref[...], gate, up, down_ref[...])
        part = dot(d_gate, gate, BY_WIDTH) + dot(d_up, up, BY_WIDTH)

        @pl.when(pl.program_id(0) == 0)
        def _():
            total[...] = part

        @pl.when(pl.program_id(0) > 0)
        def _():
            total[...] += part

        @pl.when(pl.program_id(0) == hid // tile - 1)
        def _():
            done = total[...].astype(jnp.bfloat16)
            extra = jnp.zeros((blocks * ROWS, step), jnp.float32)
            for at in range(pieces):
                extra += dot(
                    spill_picks(blocks, pieces, at),
                    done[blocks * ROWS :, at * step : (at + 1) * step],
                    BY_ROWS,
                )
            extra = extra.astype(jnp.bfloat16)
            for block in range(blocks):
                part_of = slice(block * ROWS, (block + 1) * ROWS)
                outs[block][:, :width] = done[part_of]
                outs[block][:, width:] = extra[part_of]

    shape = jax.ShapeDtypeStruct((ROWS, width + step), jnp.bfloat16)
    same = pl.BlockSpec((slots, width), lambda i: (0, 0))
    return pl.pallas_call(
        kernel,
        grid=(hid // tile,),
        out_shape=[shape] * blocks,
        in_specs=[same, same] + weight_specs(width, tile),
        out_specs=[pl.BlockSpec((ROWS, width + step), lambda i: (0, 0))] * blocks,
        scratch_shapes=[pltpu.VMEM((slots, width), jnp.float32)],
        compiler_params=params(),
        cost_estimate=cost(10 * slots * width * hid, 6 * width * hid),
        name="back",
    )(rows, scaled, gate_proj, up_proj, down_proj)


def weight_grads(tile, part, rows, scaled, gate_proj, up_proj, down_proj):
    groups = len(rows)
    slots, width = rows[0].shape
    hid = gate_proj.shape[1]
    own = width // groups
    total = groups * slots

    def kernel(part_ref, *refs):
        sources = refs[: 2 * groups]
        gate_ref, up_ref, down_ref, d_gate_ref, d_up_ref, d_down_ref = refs[
            2 * groups : 2 * groups + 6
        ]
        x_all, dy_all, arrived = refs[2 * groups + 6 :]

        @pl.when(pl.program_id(0) == 0)
        def _():
            copies = []
            for at in range(2 * groups):
                target = x_all if at < groups else dy_all
                begin = (at % groups) * slots
                copies.append(
                    pltpu.make_async_copy(
                        sources[at], target.at[begin : begin + slots, :], arrived.at[at]
                    )
                )
            for copy in copies:
                copy.start()
            for copy in copies:
                copy.wait()

        hidden, d_gate, d_up = slice_grads(
            x_all[...], dy_all[...], gate_ref[...], up_ref[...], down_ref[...]
        )
        columns = pl.ds(pl.multiple_of(part_ref[0] * own, own), own)
        both = dot(x_all[:, columns], jnp.concatenate([d_gate, d_up], 1), BY_ROWS)
        d_gate_ref[...] = both[:, :tile]
        d_up_ref[...] = both[:, tile:]
        d_down_ref[...] = dot(hidden, dy_all[:, columns], BY_ROWS)

    return pl.pallas_call(
        kernel,
        grid=(hid // tile,),
        out_shape=[
            jax.ShapeDtypeStruct((own, hid), jnp.float32),
            jax.ShapeDtypeStruct((own, hid), jnp.float32),
            jax.ShapeDtypeStruct((hid, own), jnp.float32),
        ],
        in_specs=[pl.BlockSpec(memory_space=pltpu.SMEM)]
        + [pl.BlockSpec(memory_space=pl.ANY)] * (2 * groups)
        + weight_specs(width, tile),
        out_specs=[
            pl.BlockSpec((own, tile), lambda i: (0, i)),
            pl.BlockSpec((own, tile), lambda i: (0, i)),
            pl.BlockSpec((tile, own), lambda i: (i, 0)),
        ],
        scratch_shapes=[
            pltpu.VMEM((total, width), jnp.bfloat16),
            pltpu.VMEM((total, width), jnp.bfloat16),
            pltpu.SemaphoreType.DMA((2 * groups,)),
        ],
        compiler_params=params(),
        cost_estimate=cost(
            6 * total * width * hid + 6 * total * own * hid, 6 * width * hid + 4 * total * width
        ),
        name="weight_grads",
    )(part, *rows, *scaled, gate_proj, up_proj, down_proj)


def merge(me, routes, returned):
    blocks = len(returned)
    tokens = routes.shape[1]
    width = returned[0].shape[1] * (ROWS // (MOST - ROWS)) // (ROWS // (MOST - ROWS) + 1)
    pieces, step = cut(width)

    def kernel(me_ref, routes_ref, *refs):
        out = refs[blocks]
        main, spill, piece = slot_masks(me_ref[0], routes_ref[...], blocks, width)
        rows = jnp.concatenate([ref[:, :width] for ref in refs[:blocks]], 0)
        extra = jnp.concatenate([ref[:, width:] for ref in refs[:blocks]], 0)
        picked = dot(ones(main), rows, BY_ROWS)
        for at in range(pieces):
            columns = slice(at * step, (at + 1) * step)
            out[:, columns] = (
                picked[:, columns] + dot(ones(spill & (piece == at)), extra, BY_ROWS)
            ).astype(jnp.bfloat16)

    return pl.pallas_call(
        kernel,
        out_shape=jax.ShapeDtypeStruct((tokens, width), jnp.bfloat16),
        in_specs=[pl.BlockSpec(memory_space=pltpu.SMEM)] + whole(1 + blocks),
        out_specs=pl.BlockSpec(memory_space=pltpu.VMEM),
        compiler_params=params(),
        cost_estimate=cost(4 * blocks * ROWS * tokens * width, 4 * tokens * width),
        name="merge",
    )(me, routes, *returned)


def swap(value, axis, distance):
    size = lax.axis_size(axis)
    return lax.ppermute(value, axis, [(at, at ^ distance) for at in range(size)])


def exchange(blocks, axis):
    out = list(blocks)
    for distance in reversed(range(1, len(blocks))):
        out[distance] = swap(blocks[distance], axis, distance)
    return out


def collect(value, axis):
    values = [value]
    distance = lax.axis_size(axis) // 2
    while distance > 0:
        values = values + [swap(one, axis, distance) for one in values]
        distance //= 2
    return values


def gather_body(tokens, cotangent, routes, expert_gates, gate_proj, up_proj, down_proj):
    blocks = lax.axis_size("expert")
    tile = 256
    me = lax.axis_index("expert").astype(jnp.int32).reshape(1)
    part = lax.axis_index("dp").astype(jnp.int32).reshape(1)
    routes = routes.reshape(1, -1)
    gates = expert_gates.reshape(1, -1)
    rows = join(exchange(pack(False, blocks, me, routes, gates, tokens), "expert"))
    all_rows = collect(rows, "dp")
    scaled = join(exchange(pack(True, blocks, me, routes, gates, cotangent), "expert"))
    all_scaled = collect(scaled, "dp")
    sent = back(blocks, tile, rows, scaled, gate_proj, up_proj, down_proj)
    grad_input = merge(me, routes, exchange(sent, "expert"))
    grads = weight_grads(tile, part, all_rows, all_scaled, gate_proj, up_proj, down_proj)
    return (grad_input, *grads)


def body(tokens, cotangent, routes, expert_gates, gate_proj, up_proj, down_proj):
    groups, blocks = lax.axis_size("dp"), lax.axis_size("expert")
    width, hid = gate_proj.shape
    rows_sent = (groups - 1) * 2 * blocks * MOST * width
    grads_sent = 3 * width * hid * (groups - 1) // groups
    fits = blocks == EXPERTS and groups & (groups - 1) == 0 and hid % 256 == 0
    fits = fits and tokens.shape[0] == 128 and routes.shape[1] == 1 and width // groups % 128 == 0
    chosen = gather_body if fits and rows_sent < grads_sent else scatter_body
    return chosen(tokens, cotangent, routes, expert_gates, gate_proj, up_proj, down_proj)


def solution(mesh):
    in_specs = (
        P(("dp", "expert"), None),
        P(("dp", "expert"), None),
        P(("dp", "expert"), None),
        P(("dp", "expert"), None),
        P(None, "expert"),
        P(None, "expert"),
        P("expert", None),
    )
    out_specs = (P(("dp", "expert"), None), P("dp", "expert"), P("dp", "expert"), P("expert", "dp"))
    return jax.shard_map(body, mesh=mesh, in_specs=in_specs, out_specs=out_specs, check_vma=False)
```

```python
import jax
import jax.numpy as jnp
from jax import lax
from jax.experimental import pallas as pl
from jax.experimental.pallas import tpu as pltpu
from jax.sharding import PartitionSpec as P

EXPERTS = 8
MOST = 18
ROWS = 16


def build_slots(routes, capacity):
    flat_routes = routes.reshape(-1)
    one_hot = (flat_routes[:, None] == jnp.arange(EXPERTS, dtype=jnp.int32)[None, :]).astype(
        jnp.int32
    )
    before = jnp.cumsum(one_hot, axis=0) - one_hot
    position = jnp.sum(before * one_hot, axis=1)
    return flat_routes * capacity + position


def scatter_body(tokens, cotangent, routes, expert_gates, gate_proj, up_proj, down_proj):
    tok_dev, model_dim = tokens.shape
    top_k = routes.shape[1]
    expert_devs = lax.axis_size("expert")
    group_size = expert_devs // EXPERTS
    capacity = MOST
    slot_total = EXPERTS * capacity
    slot_of = build_slots(routes, capacity)
    owners = jnp.arange(tok_dev * top_k, dtype=jnp.int32) // top_k
    slot_table = jnp.full((slot_total,), tok_dev, jnp.int32).at[slot_of].set(owners)
    slot_gate = jnp.zeros((slot_total,), jnp.float32).at[slot_of].set(expert_gates.reshape(-1))
    x_slots = jnp.take(tokens, slot_table, axis=0, mode="fill", fill_value=0)
    dy_slots = (
        jnp.take(cotangent, slot_table, axis=0, mode="fill", fill_value=0).astype(jnp.float32)
        * slot_gate[:, None]
    ).astype(jnp.bfloat16)

    def copies(values):
        spread = values.reshape(EXPERTS, 1, capacity, model_dim)
        return jnp.broadcast_to(spread, (EXPERTS, group_size, capacity, model_dim)).reshape(
            expert_devs, capacity, model_dim
        )

    x_recv, dy_recv = (
        lax.all_to_all(copies(x_slots), "expert", split_axis=0, concat_axis=0, tiled=True),
        lax.all_to_all(copies(dy_slots), "expert", split_axis=0, concat_axis=0, tiled=True),
    )
    in_rows = x_recv.reshape(expert_devs * capacity, model_dim)
    scaled = dy_recv.reshape(expert_devs * capacity, model_dim)
    pre_gate = jnp.dot(in_rows, gate_proj, preferred_element_type=jnp.float32)
    pre_up = jnp.dot(in_rows, up_proj, preferred_element_type=jnp.float32)
    gate_sig = jax.nn.sigmoid(pre_gate)
    hidden = (pre_gate * gate_sig * pre_up).astype(jnp.bfloat16)
    by_width = (((1,), (1,)), ((), ()))
    by_rows = (((0,), (0,)), ((), ()))
    d_hidden = lax.dot_general(scaled, down_proj, by_width, preferred_element_type=jnp.float32)
    d_gate = (d_hidden * pre_up * gate_sig * (1.0 + pre_gate * (1.0 - gate_sig))).astype(
        jnp.bfloat16
    )
    d_up = (d_hidden * pre_gate * gate_sig).astype(jnp.bfloat16)
    grad_down = lax.dot_general(hidden, scaled, by_rows, preferred_element_type=jnp.float32)
    grad_gate = lax.dot_general(in_rows, d_gate, by_rows, preferred_element_type=jnp.float32)
    grad_up = lax.dot_general(in_rows, d_up, by_rows, preferred_element_type=jnp.float32)
    grad_gate, grad_up, grad_down = (
        lax.psum_scatter(
            grad_gate.astype(jnp.bfloat16), "dp", scatter_dimension=0, tiled=True
        ).astype(jnp.float32),
        lax.psum_scatter(
            grad_up.astype(jnp.bfloat16), "dp", scatter_dimension=0, tiled=True
        ).astype(jnp.float32),
        lax.psum_scatter(
            grad_down.astype(jnp.bfloat16), "dp", scatter_dimension=1, tiled=True
        ).astype(jnp.float32),
    )
    joined_grads = jnp.concatenate([d_gate, d_up], 1)
    joined_proj = jnp.concatenate([gate_proj, up_proj], 1)
    partial_value = lax.dot_general(
        joined_grads, joined_proj, by_width, preferred_element_type=jnp.float32
    ).astype(jnp.bfloat16)
    returned = lax.all_to_all(
        partial_value.reshape(expert_devs, capacity, model_dim),
        "expert",
        split_axis=0,
        concat_axis=0,
        tiled=True,
    )
    summed = jnp.sum(
        returned.reshape(EXPERTS, group_size, capacity, model_dim).astype(jnp.float32), axis=1
    )
    summed = summed.reshape(slot_total, model_dim)
    grad_input = jnp.take(summed, slot_of, axis=0).reshape(tok_dev, top_k, model_dim).sum(axis=1)
    return (grad_input.astype(jnp.bfloat16), grad_gate, grad_up, grad_down)


BY_WIDTH = (((1,), (1,)), ((), ()))
BY_ROWS = (((0,), (0,)), ((), ()))


def cut(width):
    pieces = ROWS // (MOST - ROWS)
    return pieces, width // pieces


def cost(flops, moved):
    return pl.CostEstimate(flops=flops, bytes_accessed=moved, transcendentals=0)


def params(mib):
    return pltpu.CompilerParams(vmem_limit_bytes=mib * 1024 * 1024)


def anywhere(count):
    return [pl.BlockSpec(memory_space=pltpu.HBM)] * count


def dot(left, right, dims=(((1,), (0,)), ((), ()))):
    return lax.dot_general(left, right, dims, preferred_element_type=jnp.float32)


def ones(mask):
    return jnp.where(mask, 1.0, 0.0).astype(jnp.bfloat16)


def load(sources, targets, arrived):
    copies = [
        pltpu.make_async_copy(source, target, arrived.at[at])
        for at, (source, target) in enumerate(zip(sources, targets))
    ]
    for copy in copies:
        copy.start()
    for copy in copies:
        copy.wait()


def slot_masks(routes, blocks, width):
    tokens = routes.shape[1]
    pieces, _ = cut(width)
    experts = lax.broadcasted_iota(jnp.int32, (EXPERTS, tokens), 0)
    named = jnp.where(experts == routes, 1.0, 0.0)
    earlier = lax.broadcasted_iota(jnp.int32, (tokens, tokens), 0) < lax.broadcasted_iota(
        jnp.int32, (tokens, tokens), 1
    )
    before = dot(named.astype(jnp.bfloat16), ones(earlier))
    position = jnp.sum(before * named, axis=0, keepdims=True).astype(jnp.int32)
    slot = lax.broadcasted_iota(jnp.int32, (blocks * ROWS, tokens), 0)
    row = slot % ROWS
    mine = slot // ROWS == routes
    main = mine & (position == row)
    spill = mine & (position == ROWS + row // pieces)
    return main, spill, row % pieces


def pack(blocks, routes, values, gates=None):
    tokens, width = values.shape
    pieces, step = cut(width)
    scaled = gates is not None
    sources = (routes, values) + ((gates,) if scaled else ())

    def kernel(*refs):
        count = len(sources)
        out, held, arrived = refs[count], refs[count + 1 : 2 * count + 1], refs[-1]
        load(refs[:count], held, arrived)
        main, spill, piece = slot_masks(held[0][...], blocks, width)
        rows = dot(ones(main), held[1][...])
        extra = jnp.zeros((blocks * ROWS, step), jnp.float32)
        for at in range(pieces):
            extra += dot(ones(spill & (piece == at)), held[1][:, at * step : (at + 1) * step])
        if scaled:
            weights = held[2][...]
            rows = rows * jnp.sum(jnp.where(main, weights, 0.0), axis=1, keepdims=True)
            extra = extra * jnp.sum(jnp.where(spill, weights, 0.0), axis=1, keepdims=True)
        rows = rows.astype(jnp.bfloat16)
        extra = extra.astype(jnp.bfloat16)
        for block in range(blocks):
            part = slice(block * ROWS, (block + 1) * ROWS)
            out[block, :, :width] = rows[part]
            out[block, :, width:] = extra[part]

    return pl.pallas_call(
        kernel,
        out_shape=jax.ShapeDtypeStruct((blocks, ROWS, width + step), jnp.bfloat16),
        in_specs=anywhere(len(sources)),
        out_specs=pl.BlockSpec(memory_space=pltpu.VMEM),
        scratch_shapes=[pltpu.VMEM(source.shape, source.dtype) for source in sources]
        + [pltpu.SemaphoreType.DMA((len(sources),))],
        compiler_params=params(16),
        cost_estimate=cost(4 * blocks * ROWS * tokens * width, 4 * tokens * width),
        name="pack",
    )(*sources)


def merge(routes, returned):
    blocks = returned.shape[0]
    tokens = routes.shape[1]
    width = width_of(returned)
    pieces, step = cut(width)

    def kernel(routes_ref, back_ref, out, named, held, arrived):
        load((routes_ref, back_ref), (named, held), arrived)
        main, spill, piece = slot_masks(named[...], blocks, width)
        rows = jnp.concatenate([held[at, :, :width] for at in range(blocks)], 0)
        extra = jnp.concatenate([held[at, :, width:] for at in range(blocks)], 0)
        picked = dot(ones(main), rows, BY_ROWS)
        for at in range(pieces):
            columns = slice(at * step, (at + 1) * step)
            out[:, columns] = (
                picked[:, columns] + dot(ones(spill & (piece == at)), extra, BY_ROWS)
            ).astype(jnp.bfloat16)

    return pl.pallas_call(
        kernel,
        out_shape=jax.ShapeDtypeStruct((tokens, width), jnp.bfloat16),
        in_specs=anywhere(2),
        out_specs=pl.BlockSpec(memory_space=pltpu.VMEM),
        scratch_shapes=[
            pltpu.VMEM(routes.shape, routes.dtype),
            pltpu.VMEM(returned.shape, returned.dtype),
            pltpu.SemaphoreType.DMA((2,)),
        ],
        compiler_params=params(16),
        cost_estimate=cost(4 * blocks * ROWS * tokens * width, 4 * tokens * width),
        name="merge",
    )(routes, returned)


def width_of(packed):
    pieces = ROWS // (MOST - ROWS)
    return packed.shape[2] * pieces // (pieces + 1)


def spill_picks(blocks, pieces, at):
    shape = (blocks * (MOST - ROWS), blocks * ROWS)
    slot = lax.broadcasted_iota(jnp.int32, shape, 0)
    row = lax.broadcasted_iota(jnp.int32, shape, 1)
    return ones(row == slot * pieces + at)


def unpack(packed, out, begin):
    blocks = packed.shape[0]
    width = width_of(packed)
    pieces, step = cut(width)
    for at in range(blocks):
        out[begin + at * ROWS : begin + (at + 1) * ROWS, :] = packed[at, :, :width]
    extra = jnp.concatenate([packed[at, :, width:] for at in range(blocks)], 0)
    first, last = begin + blocks * ROWS, begin + blocks * MOST
    for at in range(pieces):
        out[first:last, at * step : (at + 1) * step] = dot(
            spill_picks(blocks, pieces, at), extra
        ).astype(jnp.bfloat16)


def column_tile(width, tile):
    return pl.BlockSpec((width, tile), lambda i: (0, i))


def row_tile(tile, width):
    return pl.BlockSpec((tile, width), lambda i: (i, 0))


def forward(tile, packed, gate_proj, up_proj):
    groups = len(packed)
    blocks = packed[0].shape[0]
    width, hid = gate_proj.shape
    slots = blocks * MOST

    def kernel(*refs):
        gate_ref, up_ref, rows_ref, pre_gate_ref, pre_up_ref = refs[groups : groups + 5]
        held, arrived = refs[groups + 5 :]

        @pl.when(pl.program_id(0) == 0)
        def _():
            load(refs[:groups], [held.at[at] for at in range(groups)], arrived)
            for at in range(groups):
                unpack(held.at[at], rows_ref, at * slots)

        pre_gate_ref[...] = dot(rows_ref[...], gate_ref[...])
        pre_up_ref[...] = dot(rows_ref[...], up_ref[...])

    total = groups * slots
    return pl.pallas_call(
        kernel,
        grid=(hid // tile,),
        out_shape=[
            jax.ShapeDtypeStruct((total, width), jnp.bfloat16),
            jax.ShapeDtypeStruct((total, hid), jnp.float32),
            jax.ShapeDtypeStruct((total, hid), jnp.float32),
        ],
        in_specs=anywhere(groups) + [column_tile(width, tile)] * 2,
        out_specs=[
            pl.BlockSpec((total, width), lambda i: (0, 0)),
            column_tile(total, tile),
            column_tile(total, tile),
        ],
        scratch_shapes=[
            pltpu.VMEM((groups,) + packed[0].shape, jnp.bfloat16),
            pltpu.SemaphoreType.DMA((groups,)),
        ],
        compiler_params=params(24),
        cost_estimate=cost(4 * total * width * hid, 4 * width * hid + 4 * total * width),
        name="forward",
    )(*packed, gate_proj, up_proj)


def hidden_grads(pre_gate, pre_up, d_hidden):
    sig = jax.nn.sigmoid(pre_gate)
    silu = pre_gate * sig
    hidden = (silu * pre_up).astype(jnp.bfloat16)
    d_gate = (d_hidden * pre_up * sig * (1.0 + pre_gate * (1.0 - sig))).astype(jnp.bfloat16)
    d_up = (d_hidden * silu).astype(jnp.bfloat16)
    return hidden, d_gate, d_up


def back(tile, packed, pre_gate, pre_up, gate_proj, up_proj, down_proj):
    blocks = packed.shape[0]
    width, hid = gate_proj.shape
    slots = blocks * MOST
    pieces, step = cut(width)

    def kernel(packed_ref, pre_gate_ref, pre_up_ref, gate_ref, up_ref, down_ref, *rest):
        out, scaled, hidden_ref, d_gate_ref, d_up_ref, held, total, arrived = rest

        @pl.when(pl.program_id(0) == 0)
        def _():
            load([packed_ref], [held], arrived)
            unpack(held, scaled, 0)

        d_hidden = dot(scaled[...], down_ref[...], BY_WIDTH)
        hidden, d_gate, d_up = hidden_grads(pre_gate_ref[...], pre_up_ref[...], d_hidden)
        hidden_ref[...] = hidden
        d_gate_ref[...] = d_gate
        d_up_ref[...] = d_up
        part = dot(d_gate, gate_ref[...], BY_WIDTH) + dot(d_up, up_ref[...], BY_WIDTH)

        @pl.when(pl.program_id(0) == 0)
        def _():
            total[...] = part

        @pl.when(pl.program_id(0) > 0)
        def _():
            total[...] += part

        @pl.when(pl.program_id(0) == hid // tile - 1)
        def _():
            done = total[...].astype(jnp.bfloat16)
            extra = jnp.zeros((blocks * ROWS, step), jnp.float32)
            for at in range(pieces):
                extra += dot(
                    spill_picks(blocks, pieces, at),
                    done[blocks * ROWS :, at * step : (at + 1) * step],
                    BY_ROWS,
                )
            extra = extra.astype(jnp.bfloat16)
            for block in range(blocks):
                part_of = slice(block * ROWS, (block + 1) * ROWS)
                out[block, :, :width] = done[part_of]
                out[block, :, width:] = extra[part_of]

    factor = jax.ShapeDtypeStruct((slots, hid), jnp.bfloat16)
    return pl.pallas_call(
        kernel,
        grid=(hid // tile,),
        out_shape=[
            jax.ShapeDtypeStruct(packed.shape, jnp.bfloat16),
            jax.ShapeDtypeStruct((slots, width), jnp.bfloat16),
            factor,
            factor,
            factor,
        ],
        in_specs=anywhere(1)
        + [column_tile(slots, tile)] * 2
        + [column_tile(width, tile)] * 2
        + [row_tile(tile, width)],
        out_specs=[
            pl.BlockSpec(packed.shape, lambda i: (0, 0, 0)),
            pl.BlockSpec((slots, width), lambda i: (0, 0)),
        ]
        + [column_tile(slots, tile)] * 3,
        scratch_shapes=[
            pltpu.VMEM(packed.shape, jnp.bfloat16),
            pltpu.VMEM((slots, width), jnp.float32),
            pltpu.SemaphoreType.DMA((1,)),
        ],
        compiler_params=params(24),
        cost_estimate=cost(6 * slots * width * hid, 6 * width * hid),
        name="back",
    )(packed, pre_gate, pre_up, gate_proj, up_proj, down_proj)


def weight_grads(tile, groups, part, packed, rows, pre_gate, pre_up, down_proj, own=(), sums=()):
    others = len(packed)
    blocks = packed[0].shape[0]
    hid, width = down_proj.shape
    slots = blocks * MOST
    known = slots if own else 0
    some = others * slots
    share = width // groups
    loaded = others + 1 + len(own[:1])

    def kernel(part_ref, *refs):
        refs = list(refs)
        sources = [refs.pop(0) for _ in range(loaded)]
        pre_gate_ref, pre_up_ref, down_ref = [refs.pop(0) for _ in range(3)]
        factors = [refs.pop(0) for _ in own[1:]]
        added = [refs.pop(0) for _ in sums]
        d_gate_ref, d_up_ref, d_down_ref, held, scaled, x_mine, dy_mine, arrived = refs

        @pl.when(pl.program_id(0) == 0)
        def _():
            columns = pl.ds(pl.multiple_of(part_ref[0] * share, share), share)
            here = [source.at[:, columns] for source in sources[others:]]
            targets = [held.at[at] for at in range(others)] + [x_mine]
            targets += [dy_mine.at[:known, :]] if own else []
            load(sources[:others] + here, targets, arrived)
            for at in range(others):
                unpack(held.at[at], scaled, at * slots)
            dy_mine[known:, :] = scaled[:, columns]

        d_hidden = dot(scaled[...], down_ref[...], BY_WIDTH)
        hidden, d_gate, d_up = hidden_grads(pre_gate_ref[...], pre_up_ref[...], d_hidden)
        if own:
            hidden = jnp.concatenate([factors[0][...], hidden], 0)
            d_gate = jnp.concatenate([factors[1][...], d_gate], 0)
            d_up = jnp.concatenate([factors[2][...], d_up], 0)
        both = dot(x_mine[...], jnp.concatenate([d_gate, d_up], 1), BY_ROWS)
        d_gate, d_up = both[:, :tile], both[:, tile:]
        d_down = dot(hidden, dy_mine[...], BY_ROWS)
        if sums:
            d_gate += added[0][...]
            d_up += added[1][...]
            d_down += added[2][...]
        d_gate_ref[...] = d_gate
        d_up_ref[...] = d_up
        d_down_ref[...] = d_down

    at_row = known // some
    behind = pl.BlockSpec((some, tile), lambda i: (at_row, i))
    grads = [column_tile(share, tile), column_tile(share, tile), row_tile(tile, share)]
    return pl.pallas_call(
        kernel,
        grid=(hid // tile,),
        out_shape=[
            jax.ShapeDtypeStruct((share, hid), jnp.float32),
            jax.ShapeDtypeStruct((share, hid), jnp.float32),
            jax.ShapeDtypeStruct((hid, share), jnp.float32),
        ],
        in_specs=[pl.BlockSpec(memory_space=pltpu.SMEM)]
        + anywhere(loaded)
        + [behind] * 2
        + [row_tile(tile, width)]
        + [column_tile(slots, tile)] * len(own[1:])
        + grads[: len(sums)],
        out_specs=grads,
        scratch_shapes=[
            pltpu.VMEM((others,) + packed[0].shape, jnp.bfloat16),
            pltpu.VMEM((some, width), jnp.bfloat16),
            pltpu.VMEM((known + some, share), jnp.bfloat16),
            pltpu.VMEM((known + some, share), jnp.bfloat16),
            pltpu.SemaphoreType.DMA((loaded,)),
        ],
        compiler_params=params(24),
        cost_estimate=cost(
            2 * some * width * hid + 6 * (known + some) * share * hid,
            2 * width * hid + 4 * some * width,
        ),
        name="weight_grads",
    )(part, *packed, rows, *own[:1], pre_gate, pre_up, down_proj, *own[1:], *sums)


def swap(value, axis, distance):
    size = lax.axis_size(axis)
    return lax.ppermute(value, axis, [(at, at ^ distance) for at in range(size)])


def exchange(blocks):
    return lax.all_to_all(blocks, "expert", split_axis=0, concat_axis=0, tiled=True)


def after(value, *earlier):
    return lax.optimization_barrier((value, *earlier))[0]


def gather_body(tokens, cotangent, routes, expert_gates, gate_proj, up_proj, down_proj):
    blocks, groups = lax.axis_size("expert"), lax.axis_size("dp")
    tile = 256
    part = lax.axis_index("dp").astype(jnp.int32).reshape(1)
    routes = routes.reshape(1, -1)
    gates = expert_gates.reshape(1, -1)
    x_own = exchange(pack(blocks, routes, tokens))
    x_far = swap(x_own, "dp", 2)
    x_near = swap(x_own, "dp", 1)
    dy_own = exchange(after(pack(blocks, routes, cotangent, gates), x_own))
    rows, pre_gate, pre_up = forward(tile, [x_own, x_near], gate_proj, up_proj)
    x_last = swap(x_far, "dp", 1)
    dy_far = swap(dy_own, "dp", 2)
    dy_near = swap(dy_own, "dp", 1)
    sent, *own = back(tile, dy_own, pre_gate, pre_up, gate_proj, up_proj, down_proj)
    returned = exchange(sent)
    far_rows, far_gate, far_up = forward(
        tile, [after(x_far, sent), x_last], gate_proj, up_proj
    )
    sums = weight_grads(
        tile, groups, part, [dy_near], rows, pre_gate, pre_up, down_proj, own=own
    )
    dy_last = swap(after(dy_far, sent), "dp", 1)
    grads = weight_grads(
        tile, groups, part, [dy_far, dy_last], far_rows, far_gate, far_up, down_proj, sums=sums
    )
    return (merge(routes, returned), *grads)


def body(tokens, cotangent, routes, expert_gates, gate_proj, up_proj, down_proj):
    groups, blocks = lax.axis_size("dp"), lax.axis_size("expert")
    width, hid = gate_proj.shape
    rows_sent = (groups - 1) * 2 * blocks * MOST * width
    grads_sent = 3 * width * hid * (groups - 1) // groups
    fits = blocks == EXPERTS and groups == 4 and hid % 256 == 0
    fits = fits and tokens.shape[0] == 128 and routes.shape[1] == 1 and width // groups % 128 == 0
    chosen = gather_body if fits and rows_sent < grads_sent else scatter_body
    return chosen(tokens, cotangent, routes, expert_gates, gate_proj, up_proj, down_proj)


def solution(mesh):
    in_specs = (
        P(("dp", "expert"), None),
        P(("dp", "expert"), None),
        P(("dp", "expert"), None),
        P(("dp", "expert"), None),
        P(None, "expert"),
        P(None, "expert"),
        P("expert", None),
    )
    out_specs = (P(("dp", "expert"), None), P("dp", "expert"), P("dp", "expert"), P("expert", "dp"))
    return jax.shard_map(body, mesh=mesh, in_specs=in_specs, out_specs=out_specs, check_vma=False)
```

```python
import jax
import jax.numpy as jnp
from jax import lax
from jax.experimental import pallas as pl
from jax.experimental.pallas import tpu as pltpu
from jax.sharding import PartitionSpec as P

EXPERTS = 8
MOST = 18
ROWS = 16
VMEM_BYTES = (63 * 1024 + 768) * 1024


def build_slots(routes, capacity):
    flat_routes = routes.reshape(-1)
    one_hot = (flat_routes[:, None] == jnp.arange(EXPERTS, dtype=jnp.int32)[None, :]).astype(
        jnp.int32
    )
    before = jnp.cumsum(one_hot, axis=0) - one_hot
    position = jnp.sum(before * one_hot, axis=1)
    return flat_routes * capacity + position


def scatter_body(tokens, cotangent, routes, expert_gates, gate_proj, up_proj, down_proj):
    tok_dev, model_dim = tokens.shape
    top_k = routes.shape[1]
    expert_devs = lax.axis_size("expert")
    group_size = expert_devs // EXPERTS
    capacity = MOST
    slot_total = EXPERTS * capacity
    slot_of = build_slots(routes, capacity)
    owners = jnp.arange(tok_dev * top_k, dtype=jnp.int32) // top_k
    slot_table = jnp.full((slot_total,), tok_dev, jnp.int32).at[slot_of].set(owners)
    slot_gate = jnp.zeros((slot_total,), jnp.float32).at[slot_of].set(expert_gates.reshape(-1))
    x_slots = jnp.take(tokens, slot_table, axis=0, mode="fill", fill_value=0)
    dy_slots = (
        jnp.take(cotangent, slot_table, axis=0, mode="fill", fill_value=0).astype(jnp.float32)
        * slot_gate[:, None]
    ).astype(jnp.bfloat16)

    def copies(values):
        spread = values.reshape(EXPERTS, 1, capacity, model_dim)
        return jnp.broadcast_to(spread, (EXPERTS, group_size, capacity, model_dim)).reshape(
            expert_devs, capacity, model_dim
        )

    x_recv, dy_recv = (
        lax.all_to_all(copies(x_slots), "expert", split_axis=0, concat_axis=0, tiled=True),
        lax.all_to_all(copies(dy_slots), "expert", split_axis=0, concat_axis=0, tiled=True),
    )
    in_rows = x_recv.reshape(expert_devs * capacity, model_dim)
    scaled = dy_recv.reshape(expert_devs * capacity, model_dim)
    pre_gate = jnp.dot(in_rows, gate_proj, preferred_element_type=jnp.float32)
    pre_up = jnp.dot(in_rows, up_proj, preferred_element_type=jnp.float32)
    gate_sig = jax.nn.sigmoid(pre_gate)
    hidden = (pre_gate * gate_sig * pre_up).astype(jnp.bfloat16)
    by_width = (((1,), (1,)), ((), ()))
    by_rows = (((0,), (0,)), ((), ()))
    d_hidden = lax.dot_general(scaled, down_proj, by_width, preferred_element_type=jnp.float32)
    d_gate = (d_hidden * pre_up * gate_sig * (1.0 + pre_gate * (1.0 - gate_sig))).astype(
        jnp.bfloat16
    )
    d_up = (d_hidden * pre_gate * gate_sig).astype(jnp.bfloat16)
    grad_down = lax.dot_general(hidden, scaled, by_rows, preferred_element_type=jnp.float32)
    grad_gate = lax.dot_general(in_rows, d_gate, by_rows, preferred_element_type=jnp.float32)
    grad_up = lax.dot_general(in_rows, d_up, by_rows, preferred_element_type=jnp.float32)
    grad_gate, grad_up, grad_down = (
        lax.psum_scatter(
            grad_gate.astype(jnp.bfloat16), "dp", scatter_dimension=0, tiled=True
        ).astype(jnp.float32),
        lax.psum_scatter(
            grad_up.astype(jnp.bfloat16), "dp", scatter_dimension=0, tiled=True
        ).astype(jnp.float32),
        lax.psum_scatter(
            grad_down.astype(jnp.bfloat16), "dp", scatter_dimension=1, tiled=True
        ).astype(jnp.float32),
    )
    joined_grads = jnp.concatenate([d_gate, d_up], 1)
    joined_proj = jnp.concatenate([gate_proj, up_proj], 1)
    partial_value = lax.dot_general(
        joined_grads, joined_proj, by_width, preferred_element_type=jnp.float32
    ).astype(jnp.bfloat16)
    returned = lax.all_to_all(
        partial_value.reshape(expert_devs, capacity, model_dim),
        "expert",
        split_axis=0,
        concat_axis=0,
        tiled=True,
    )
    summed = jnp.sum(
        returned.reshape(EXPERTS, group_size, capacity, model_dim).astype(jnp.float32), axis=1
    )
    summed = summed.reshape(slot_total, model_dim)
    grad_input = jnp.take(summed, slot_of, axis=0).reshape(tok_dev, top_k, model_dim).sum(axis=1)
    return (grad_input.astype(jnp.bfloat16), grad_gate, grad_up, grad_down)


BY_WIDTH = (((1,), (1,)), ((), ()))
BY_ROWS = (((0,), (0,)), ((), ()))


def cut(width):
    pieces = ROWS // (MOST - ROWS)
    return pieces, width // pieces


def cost(flops, moved):
    return pl.CostEstimate(flops=flops, bytes_accessed=moved, transcendentals=0)


def params():
    return pltpu.CompilerParams(vmem_limit_bytes=VMEM_BYTES)


def anywhere(count):
    return [pl.BlockSpec(memory_space=pl.ANY)] * count


def dot(left, right, dims=(((1,), (0,)), ((), ()))):
    return lax.dot_general(left, right, dims, preferred_element_type=jnp.float32)


def ones(mask):
    return jnp.where(mask, 1.0, 0.0).astype(jnp.bfloat16)


def load(sources, targets, arrived):
    copies = [
        pltpu.make_async_copy(source, target, arrived.at[at])
        for at, (source, target) in enumerate(zip(sources, targets))
    ]
    for copy in copies:
        copy.start()
    for copy in copies:
        copy.wait()


def slot_masks(routes, blocks, width):
    tokens = routes.shape[1]
    pieces, _ = cut(width)
    experts = lax.broadcasted_iota(jnp.int32, (EXPERTS, tokens), 0)
    named = jnp.where(experts == routes, 1.0, 0.0)
    earlier = lax.broadcasted_iota(jnp.int32, (tokens, tokens), 0) < lax.broadcasted_iota(
        jnp.int32, (tokens, tokens), 1
    )
    before = dot(named.astype(jnp.bfloat16), ones(earlier))
    position = jnp.sum(before * named, axis=0, keepdims=True).astype(jnp.int32)
    slot = lax.broadcasted_iota(jnp.int32, (blocks * ROWS, tokens), 0)
    row = slot % ROWS
    mine = slot // ROWS == routes
    main = mine & (position == row)
    spill = mine & (position == ROWS + row // pieces)
    return main, spill, row % pieces


def pack(blocks, routes, values, gates=None):
    tokens, width = values.shape
    pieces, step = cut(width)
    scaled = gates is not None
    sources = (routes, values) + ((gates,) if scaled else ())

    def kernel(*refs):
        count = len(sources)
        out, held, arrived = refs[count], refs[count + 1 : 2 * count + 1], refs[-1]
        load(refs[:count], held, arrived)
        main, spill, piece = slot_masks(held[0][...], blocks, width)
        rows = dot(ones(main), held[1][...])
        extra = jnp.zeros((blocks * ROWS, step), jnp.float32)
        for at in range(pieces):
            extra += dot(ones(spill & (piece == at)), held[1][:, at * step : (at + 1) * step])
        if scaled:
            weights = held[2][...]
            rows = rows * jnp.sum(jnp.where(main, weights, 0.0), axis=1, keepdims=True)
            extra = extra * jnp.sum(jnp.where(spill, weights, 0.0), axis=1, keepdims=True)
        rows = rows.astype(jnp.bfloat16)
        extra = extra.astype(jnp.bfloat16)
        for block in range(blocks):
            part = slice(block * ROWS, (block + 1) * ROWS)
            out[block, :, :width] = rows[part]
            out[block, :, width:] = extra[part]

    return pl.pallas_call(
        kernel,
        out_shape=jax.ShapeDtypeStruct((blocks, ROWS, width + step), jnp.bfloat16),
        in_specs=anywhere(len(sources)),
        out_specs=pl.BlockSpec(memory_space=pltpu.VMEM),
        scratch_shapes=[pltpu.VMEM(source.shape, source.dtype) for source in sources]
        + [pltpu.SemaphoreType.DMA((len(sources),))],
        compiler_params=params(),
        cost_estimate=cost(4 * blocks * ROWS * tokens * width, 4 * tokens * width),
        name="pack",
    )(*sources)


def merge(routes, returned):
    blocks = returned.shape[0]
    tokens = routes.shape[1]
    width = width_of(returned)
    pieces, step = cut(width)

    def kernel(routes_ref, back_ref, out, named, held, arrived):
        load((routes_ref, back_ref), (named, held), arrived)
        main, spill, piece = slot_masks(named[...], blocks, width)
        rows = jnp.concatenate([held[at, :, :width] for at in range(blocks)], 0)
        extra = jnp.concatenate([held[at, :, width:] for at in range(blocks)], 0)
        picked = dot(ones(main), rows, BY_ROWS)
        for at in range(pieces):
            columns = slice(at * step, (at + 1) * step)
            out[:, columns] = (
                picked[:, columns] + dot(ones(spill & (piece == at)), extra, BY_ROWS)
            ).astype(jnp.bfloat16)

    return pl.pallas_call(
        kernel,
        out_shape=jax.ShapeDtypeStruct((tokens, width), jnp.bfloat16),
        in_specs=anywhere(2),
        out_specs=pl.BlockSpec(memory_space=pltpu.VMEM),
        scratch_shapes=[
            pltpu.VMEM(routes.shape, routes.dtype),
            pltpu.VMEM(returned.shape, returned.dtype),
            pltpu.SemaphoreType.DMA((2,)),
        ],
        compiler_params=params(),
        cost_estimate=cost(4 * blocks * ROWS * tokens * width, 4 * tokens * width),
        name="merge",
    )(routes, returned)


def width_of(packed):
    pieces = ROWS // (MOST - ROWS)
    return packed.shape[2] * pieces // (pieces + 1)


def spill_picks(blocks, pieces, at):
    shape = (blocks * (MOST - ROWS), blocks * ROWS)
    slot = lax.broadcasted_iota(jnp.int32, shape, 0)
    row = lax.broadcasted_iota(jnp.int32, shape, 1)
    return ones(row == slot * pieces + at)


def unpack(packed, out, begin):
    blocks = packed.shape[0]
    width = width_of(packed)
    pieces, step = cut(width)
    for at in range(blocks):
        out[begin + at * ROWS : begin + (at + 1) * ROWS, :] = packed[at, :, :width]
    extra = jnp.concatenate([packed[at, :, width:] for at in range(blocks)], 0)
    first, last = begin + blocks * ROWS, begin + blocks * MOST
    for at in range(pieces):
        out[first:last, at * step : (at + 1) * step] = dot(
            spill_picks(blocks, pieces, at), extra
        ).astype(jnp.bfloat16)


def column_tile(width, tile):
    return pl.BlockSpec((width, tile), lambda i: (0, i))


def row_tile(tile, width):
    return pl.BlockSpec((tile, width), lambda i: (i, 0))


def forward(tile, packed, gate_proj, up_proj):
    groups = len(packed)
    blocks = packed[0].shape[0]
    width, hid = gate_proj.shape
    slots = blocks * MOST

    def kernel(*refs):
        gate_ref, up_ref, rows_ref, pre_gate_ref, pre_up_ref = refs[groups : groups + 5]
        held, arrived = refs[groups + 5 :]

        @pl.when(pl.program_id(0) == 0)
        def _():
            load(refs[:groups], [held.at[at] for at in range(groups)], arrived)
            for at in range(groups):
                unpack(held.at[at], rows_ref, at * slots)

        pre_gate_ref[...] = dot(rows_ref[...], gate_ref[...])
        pre_up_ref[...] = dot(rows_ref[...], up_ref[...])

    total = groups * slots
    return pl.pallas_call(
        kernel,
        grid=(hid // tile,),
        out_shape=[
            jax.ShapeDtypeStruct((total, width), jnp.bfloat16),
            jax.ShapeDtypeStruct((total, hid), jnp.float32),
            jax.ShapeDtypeStruct((total, hid), jnp.float32),
        ],
        in_specs=anywhere(groups) + [column_tile(width, tile)] * 2,
        out_specs=[
            pl.BlockSpec((total, width), lambda i: (0, 0)),
            column_tile(total, tile),
            column_tile(total, tile),
        ],
        scratch_shapes=[
            pltpu.VMEM((groups,) + packed[0].shape, jnp.bfloat16),
            pltpu.SemaphoreType.DMA((groups,)),
        ],
        compiler_params=params(),
        cost_estimate=cost(4 * total * width * hid, 4 * width * hid + 4 * total * width),
        name="forward",
    )(*packed, gate_proj, up_proj)


def hidden_grads(pre_gate, pre_up, d_hidden):
    sig = jax.nn.sigmoid(pre_gate)
    silu = pre_gate * sig
    hidden = (silu * pre_up).astype(jnp.bfloat16)
    d_gate = (d_hidden * pre_up * sig * (1.0 + pre_gate * (1.0 - sig))).astype(jnp.bfloat16)
    d_up = (d_hidden * silu).astype(jnp.bfloat16)
    return hidden, d_gate, d_up


def back(tile, packed, pre_gate, pre_up, gate_proj, up_proj, down_proj):
    blocks = packed.shape[0]
    width, hid = gate_proj.shape
    slots = blocks * MOST
    pieces, step = cut(width)

    def kernel(packed_ref, pre_gate_ref, pre_up_ref, gate_ref, up_ref, down_ref, *rest):
        out, scaled, hidden_ref, d_gate_ref, d_up_ref, held, total, arrived = rest

        @pl.when(pl.program_id(0) == 0)
        def _():
            load([packed_ref], [held], arrived)
            unpack(held, scaled, 0)

        d_hidden = dot(scaled[...], down_ref[...], BY_WIDTH)
        hidden, d_gate, d_up = hidden_grads(pre_gate_ref[...], pre_up_ref[...], d_hidden)
        hidden_ref[...] = hidden
        d_gate_ref[...] = d_gate
        d_up_ref[...] = d_up
        part = dot(d_gate, gate_ref[...], BY_WIDTH) + dot(d_up, up_ref[...], BY_WIDTH)

        @pl.when(pl.program_id(0) == 0)
        def _():
            total[...] = part

        @pl.when(pl.program_id(0) > 0)
        def _():
            total[...] += part

        @pl.when(pl.program_id(0) == hid // tile - 1)
        def _():
            done = total[...].astype(jnp.bfloat16)
            extra = jnp.zeros((blocks * ROWS, step), jnp.float32)
            for at in range(pieces):
                extra += dot(
                    spill_picks(blocks, pieces, at),
                    done[blocks * ROWS :, at * step : (at + 1) * step],
                    BY_ROWS,
                )
            extra = extra.astype(jnp.bfloat16)
            for block in range(blocks):
                part_of = slice(block * ROWS, (block + 1) * ROWS)
                out[block, :, :width] = done[part_of]
                out[block, :, width:] = extra[part_of]

    factor = jax.ShapeDtypeStruct((slots, hid), jnp.bfloat16)
    return pl.pallas_call(
        kernel,
        grid=(hid // tile,),
        out_shape=[
            jax.ShapeDtypeStruct(packed.shape, jnp.bfloat16),
            jax.ShapeDtypeStruct((slots, width), jnp.bfloat16),
            factor,
            factor,
            factor,
        ],
        in_specs=anywhere(1)
        + [column_tile(slots, tile)] * 2
        + [column_tile(width, tile)] * 2
        + [row_tile(tile, width)],
        out_specs=[
            pl.BlockSpec(packed.shape, lambda i: (0, 0, 0)),
            pl.BlockSpec((slots, width), lambda i: (0, 0)),
        ]
        + [column_tile(slots, tile)] * 3,
        scratch_shapes=[
            pltpu.VMEM(packed.shape, jnp.bfloat16),
            pltpu.VMEM((slots, width), jnp.float32),
            pltpu.SemaphoreType.DMA((1,)),
        ],
        compiler_params=params(),
        cost_estimate=cost(6 * slots * width * hid, 6 * width * hid),
        name="back",
    )(packed, pre_gate, pre_up, gate_proj, up_proj, down_proj)


def weight_grads(tile, groups, part, packed, rows, pre_gate, pre_up, down_proj, own=(), sums=()):
    others = len(packed)
    blocks = packed[0].shape[0]
    hid, width = down_proj.shape
    slots = blocks * MOST
    known = slots if own else 0
    some = others * slots
    share = width // groups
    loaded = others + 1 + len(own[:1])

    def kernel(part_ref, *refs):
        refs = list(refs)
        sources = [refs.pop(0) for _ in range(loaded)]
        pre_gate_ref, pre_up_ref, down_ref = [refs.pop(0) for _ in range(3)]
        factors = [refs.pop(0) for _ in own[1:]]
        added = [refs.pop(0) for _ in sums]
        d_gate_ref, d_up_ref, d_down_ref, held, scaled, x_mine, dy_mine, arrived = refs

        @pl.when(pl.program_id(0) == 0)
        def _():
            columns = pl.ds(pl.multiple_of(part_ref[0] * share, share), share)
            here = [source.at[:, columns] for source in sources[others:]]
            targets = [held.at[at] for at in range(others)] + [x_mine]
            targets += [dy_mine.at[:known, :]] if own else []
            load(sources[:others] + here, targets, arrived)
            for at in range(others):
                unpack(held.at[at], scaled, at * slots)
            dy_mine[known:, :] = scaled[:, columns]

        d_hidden = dot(scaled[...], down_ref[...], BY_WIDTH)
        hidden, d_gate, d_up = hidden_grads(pre_gate_ref[...], pre_up_ref[...], d_hidden)
        if own:
            hidden = jnp.concatenate([factors[0][...], hidden], 0)
            d_gate = jnp.concatenate([factors[1][...], d_gate], 0)
            d_up = jnp.concatenate([factors[2][...], d_up], 0)
        both = dot(x_mine[...], jnp.concatenate([d_gate, d_up], 1), BY_ROWS)
        d_gate, d_up = both[:, :tile], both[:, tile:]
        d_down = dot(hidden, dy_mine[...], BY_ROWS)
        if sums:
            d_gate += added[0][...]
            d_up += added[1][...]
            d_down += added[2][...]
        d_gate_ref[...] = d_gate
        d_up_ref[...] = d_up
        d_down_ref[...] = d_down

    at_row = known // some
    behind = pl.BlockSpec((some, tile), lambda i: (at_row, i))
    grads = [column_tile(share, tile), column_tile(share, tile), row_tile(tile, share)]
    return pl.pallas_call(
        kernel,
        grid=(hid // tile,),
        out_shape=[
            jax.ShapeDtypeStruct((share, hid), jnp.float32),
            jax.ShapeDtypeStruct((share, hid), jnp.float32),
            jax.ShapeDtypeStruct((hid, share), jnp.float32),
        ],
        in_specs=[pl.BlockSpec(memory_space=pltpu.SMEM)]
        + anywhere(loaded)
        + [behind] * 2
        + [row_tile(tile, width)]
        + [column_tile(slots, tile)] * len(own[1:])
        + grads[: len(sums)],
        out_specs=grads,
        scratch_shapes=[
            pltpu.VMEM((others,) + packed[0].shape, jnp.bfloat16),
            pltpu.VMEM((some, width), jnp.bfloat16),
            pltpu.VMEM((known + some, share), jnp.bfloat16),
            pltpu.VMEM((known + some, share), jnp.bfloat16),
            pltpu.SemaphoreType.DMA((loaded,)),
        ],
        compiler_params=params(),
        cost_estimate=cost(
            2 * some * width * hid + 6 * (known + some) * share * hid,
            2 * width * hid + 4 * some * width,
        ),
        name="weight_grads",
    )(part, *packed, rows, *own[:1], pre_gate, pre_up, down_proj, *own[1:], *sums)


def swap(value, axis, distance):
    size = lax.axis_size(axis)
    return lax.ppermute(value, axis, [(at, at ^ distance) for at in range(size)])


def exchange(blocks):
    return lax.all_to_all(blocks, "expert", split_axis=0, concat_axis=0, tiled=True)


def after(value, *earlier):
    return lax.optimization_barrier((value, *earlier))[0]


def gather_body(tokens, cotangent, routes, expert_gates, gate_proj, up_proj, down_proj):
    blocks, groups = lax.axis_size("expert"), lax.axis_size("dp")
    tile = 256
    part = lax.axis_index("dp").astype(jnp.int32).reshape(1)
    routes = routes.reshape(1, -1)
    gates = expert_gates.reshape(1, -1)
    x_own = exchange(pack(blocks, routes, tokens))
    x_far = swap(x_own, "dp", 2)
    x_near = swap(x_own, "dp", 1)
    dy_own = exchange(after(pack(blocks, routes, cotangent, gates), x_own))
    rows, pre_gate, pre_up = forward(tile, [x_own, x_near], gate_proj, up_proj)
    x_last = swap(x_far, "dp", 1)
    dy_own = after(dy_own, pre_gate)
    dy_far = swap(dy_own, "dp", 2)
    dy_near = swap(dy_own, "dp", 1)
    sent, *own = back(tile, dy_own, pre_gate, pre_up, gate_proj, up_proj, down_proj)
    returned = exchange(sent)
    far_rows, far_gate, far_up = forward(
        tile, [after(x_far, sent), x_last], gate_proj, up_proj
    )
    sums = weight_grads(
        tile, groups, part, [dy_near], rows, pre_gate, pre_up, down_proj, own=own
    )
    dy_last = swap(after(dy_far, sent), "dp", 1)
    grads = weight_grads(
        tile, groups, part, [dy_far, dy_last], far_rows, far_gate, far_up, down_proj, sums=sums
    )
    return (merge(routes, returned), *grads)


def body(tokens, cotangent, routes, expert_gates, gate_proj, up_proj, down_proj):
    groups, blocks = lax.axis_size("dp"), lax.axis_size("expert")
    width, hid = gate_proj.shape
    rows_sent = (groups - 1) * 2 * blocks * MOST * width
    grads_sent = 3 * width * hid * (groups - 1) // groups
    fits = blocks == EXPERTS and groups == 4 and hid % 256 == 0
    fits = fits and tokens.shape[0] == 128 and routes.shape[1] == 1 and width // groups % 128 == 0
    chosen = gather_body if fits and rows_sent < grads_sent else scatter_body
    return chosen(tokens, cotangent, routes, expert_gates, gate_proj, up_proj, down_proj)


def solution(mesh):
    in_specs = (
        P(("dp", "expert"), None),
        P(("dp", "expert"), None),
        P(("dp", "expert"), None),
        P(("dp", "expert"), None),
        P(None, "expert"),
        P(None, "expert"),
        P("expert", None),
    )
    out_specs = (P(("dp", "expert"), None), P("dp", "expert"), P("dp", "expert"), P("expert", "dp"))
    return jax.shard_map(body, mesh=mesh, in_specs=in_specs, out_specs=out_specs, check_vma=False)
```

```python
import jax
import jax.numpy as jnp
from jax import lax
from jax.experimental import pallas as pl
from jax.experimental.pallas import tpu as pltpu
from jax.sharding import PartitionSpec as P

EXPERTS = 8
MOST = 18
ROWS = 16


def build_slots(routes, capacity):
    flat_routes = routes.reshape(-1)
    one_hot = (flat_routes[:, None] == jnp.arange(EXPERTS, dtype=jnp.int32)[None, :]).astype(
        jnp.int32
    )
    before = jnp.cumsum(one_hot, axis=0) - one_hot
    position = jnp.sum(before * one_hot, axis=1)
    return flat_routes * capacity + position


def scatter_body(tokens, cotangent, routes, expert_gates, gate_proj, up_proj, down_proj):
    tok_dev, model_dim = tokens.shape
    top_k = routes.shape[1]
    expert_devs = lax.axis_size("expert")
    group_size = expert_devs // EXPERTS
    capacity = MOST
    slot_total = EXPERTS * capacity
    slot_of = build_slots(routes, capacity)
    owners = jnp.arange(tok_dev * top_k, dtype=jnp.int32) // top_k
    slot_table = jnp.full((slot_total,), tok_dev, jnp.int32).at[slot_of].set(owners)
    slot_gate = jnp.zeros((slot_total,), jnp.float32).at[slot_of].set(expert_gates.reshape(-1))
    x_slots = jnp.take(tokens, slot_table, axis=0, mode="fill", fill_value=0)
    dy_slots = (
        jnp.take(cotangent, slot_table, axis=0, mode="fill", fill_value=0).astype(jnp.float32)
        * slot_gate[:, None]
    ).astype(jnp.bfloat16)

    def copies(values):
        spread = values.reshape(EXPERTS, 1, capacity, model_dim)
        return jnp.broadcast_to(spread, (EXPERTS, group_size, capacity, model_dim)).reshape(
            expert_devs, capacity, model_dim
        )

    x_recv, dy_recv = (
        lax.all_to_all(copies(x_slots), "expert", split_axis=0, concat_axis=0, tiled=True),
        lax.all_to_all(copies(dy_slots), "expert", split_axis=0, concat_axis=0, tiled=True),
    )
    in_rows = x_recv.reshape(expert_devs * capacity, model_dim)
    scaled = dy_recv.reshape(expert_devs * capacity, model_dim)
    pre_gate = jnp.dot(in_rows, gate_proj, preferred_element_type=jnp.float32)
    pre_up = jnp.dot(in_rows, up_proj, preferred_element_type=jnp.float32)
    gate_sig = jax.nn.sigmoid(pre_gate)
    hidden = (pre_gate * gate_sig * pre_up).astype(jnp.bfloat16)
    by_width = (((1,), (1,)), ((), ()))
    by_rows = (((0,), (0,)), ((), ()))
    d_hidden = lax.dot_general(scaled, down_proj, by_width, preferred_element_type=jnp.float32)
    d_gate = (d_hidden * pre_up * gate_sig * (1.0 + pre_gate * (1.0 - gate_sig))).astype(
        jnp.bfloat16
    )
    d_up = (d_hidden * pre_gate * gate_sig).astype(jnp.bfloat16)
    grad_down = lax.dot_general(hidden, scaled, by_rows, preferred_element_type=jnp.float32)
    grad_gate = lax.dot_general(in_rows, d_gate, by_rows, preferred_element_type=jnp.float32)
    grad_up = lax.dot_general(in_rows, d_up, by_rows, preferred_element_type=jnp.float32)
    grad_gate, grad_up, grad_down = (
        lax.psum_scatter(
            grad_gate.astype(jnp.bfloat16), "dp", scatter_dimension=0, tiled=True
        ).astype(jnp.float32),
        lax.psum_scatter(
            grad_up.astype(jnp.bfloat16), "dp", scatter_dimension=0, tiled=True
        ).astype(jnp.float32),
        lax.psum_scatter(
            grad_down.astype(jnp.bfloat16), "dp", scatter_dimension=1, tiled=True
        ).astype(jnp.float32),
    )
    joined_grads = jnp.concatenate([d_gate, d_up], 1)
    joined_proj = jnp.concatenate([gate_proj, up_proj], 1)
    partial_value = lax.dot_general(
        joined_grads, joined_proj, by_width, preferred_element_type=jnp.float32
    ).astype(jnp.bfloat16)
    returned = lax.all_to_all(
        partial_value.reshape(expert_devs, capacity, model_dim),
        "expert",
        split_axis=0,
        concat_axis=0,
        tiled=True,
    )
    summed = jnp.sum(
        returned.reshape(EXPERTS, group_size, capacity, model_dim).astype(jnp.float32), axis=1
    )
    summed = summed.reshape(slot_total, model_dim)
    grad_input = jnp.take(summed, slot_of, axis=0).reshape(tok_dev, top_k, model_dim).sum(axis=1)
    return (grad_input.astype(jnp.bfloat16), grad_gate, grad_up, grad_down)


BY_WIDTH = (((1,), (1,)), ((), ()))
BY_ROWS = (((0,), (0,)), ((), ()))


def cut(width):
    pieces = ROWS // (MOST - ROWS)
    return pieces, width // pieces


def width_of(block):
    pieces = ROWS // (MOST - ROWS)
    return block.shape[1] * pieces // (pieces + 1)


def cost(flops, moved):
    return pl.CostEstimate(flops=flops, bytes_accessed=moved, transcendentals=0)


def params(mib):
    return pltpu.CompilerParams(vmem_limit_bytes=mib * 1024 * 1024)


def inside(count):
    return [pl.BlockSpec(memory_space=pltpu.VMEM)] * count


def dot(left, right, dims=(((1,), (0,)), ((), ()))):
    return lax.dot_general(left, right, dims, preferred_element_type=jnp.float32)


def ones(mask):
    return jnp.where(mask, 1.0, 0.0).astype(jnp.bfloat16)


def slot_masks(me, routes, blocks, width):
    tokens = routes.shape[1]
    pieces, _ = cut(width)
    experts = lax.broadcasted_iota(jnp.int32, (EXPERTS, tokens), 0)
    named = jnp.where(experts == routes, 1.0, 0.0)
    earlier = lax.broadcasted_iota(jnp.int32, (tokens, tokens), 0) < lax.broadcasted_iota(
        jnp.int32, (tokens, tokens), 1
    )
    before = dot(named.astype(jnp.bfloat16), ones(earlier))
    position = jnp.sum(before * named, axis=0, keepdims=True).astype(jnp.int32)
    slot = lax.broadcasted_iota(jnp.int32, (blocks * ROWS, tokens), 0)
    row = slot % ROWS
    mine = (slot // ROWS) ^ me == routes
    main = mine & (position == row)
    spill = mine & (position == ROWS + row // pieces)
    return main, spill, row % pieces


def pack(blocks, me, routes, values, gates=None):
    tokens, width = values.shape
    pieces, step = cut(width)
    sources = (routes, values) + (() if gates is None else (gates,))

    def kernel(me_ref, routes_ref, values_ref, *rest):
        outs = rest[-blocks:]
        main, spill, piece = slot_masks(me_ref[0], routes_ref[...], blocks, width)
        rows = dot(ones(main), values_ref[...])
        extra = jnp.zeros((blocks * ROWS, step), jnp.float32)
        for at in range(pieces):
            extra += dot(ones(spill & (piece == at)), values_ref[:, at * step : (at + 1) * step])
        if gates is not None:
            weights = rest[0][...]
            rows = rows * jnp.sum(jnp.where(main, weights, 0.0), axis=1, keepdims=True)
            extra = extra * jnp.sum(jnp.where(spill, weights, 0.0), axis=1, keepdims=True)
        rows = rows.astype(jnp.bfloat16)
        extra = extra.astype(jnp.bfloat16)
        for block in range(blocks):
            part = slice(block * ROWS, (block + 1) * ROWS)
            outs[block][:, :width] = rows[part]
            outs[block][:, width:] = extra[part]

    return pl.pallas_call(
        kernel,
        out_shape=[jax.ShapeDtypeStruct((ROWS, width + step), jnp.bfloat16)] * blocks,
        in_specs=[pl.BlockSpec(memory_space=pltpu.SMEM)] + inside(len(sources)),
        out_specs=inside(blocks),
        compiler_params=params(16),
        cost_estimate=cost(4 * blocks * ROWS * tokens * width, 4 * tokens * width),
        name="pack",
    )(me, *sources)


def merge(me, routes, returned):
    blocks = len(returned)
    tokens = routes.shape[1]
    width = width_of(returned[0])
    pieces, step = cut(width)

    def kernel(me_ref, routes_ref, *refs):
        out = refs[blocks]
        main, spill, piece = slot_masks(me_ref[0], routes_ref[...], blocks, width)
        rows = jnp.concatenate([ref[:, :width] for ref in refs[:blocks]], 0)
        extra = jnp.concatenate([ref[:, width:] for ref in refs[:blocks]], 0)
        picked = dot(ones(main), rows, BY_ROWS)
        for at in range(pieces):
            columns = slice(at * step, (at + 1) * step)
            out[:, columns] = (
                picked[:, columns] + dot(ones(spill & (piece == at)), extra, BY_ROWS)
            ).astype(jnp.bfloat16)

    return pl.pallas_call(
        kernel,
        out_shape=jax.ShapeDtypeStruct((tokens, width), jnp.bfloat16),
        in_specs=[pl.BlockSpec(memory_space=pltpu.SMEM)] + inside(1 + blocks),
        out_specs=pl.BlockSpec(memory_space=pltpu.VMEM),
        compiler_params=params(16),
        cost_estimate=cost(4 * blocks * ROWS * tokens * width, 4 * tokens * width),
        name="merge",
    )(me, routes, *returned)


def spill_picks(blocks, pieces, at):
    shape = (blocks * (MOST - ROWS), blocks * ROWS)
    slot = lax.broadcasted_iota(jnp.int32, shape, 0)
    row = lax.broadcasted_iota(jnp.int32, shape, 1)
    return ones(row == slot * pieces + at)


def join(blocks):
    count = len(blocks)
    width = width_of(blocks[0])
    pieces, step = cut(width)
    first, last = count * ROWS, count * MOST

    def kernel(*refs):
        out = refs[count]
        for at in range(count):
            out[at * ROWS : (at + 1) * ROWS, :] = refs[at][:, :width]
        extra = jnp.concatenate([ref[:, width:] for ref in refs[:count]], 0)
        for at in range(pieces):
            out[first:last, at * step : (at + 1) * step] = dot(
                spill_picks(count, pieces, at), extra
            ).astype(jnp.bfloat16)

    return pl.pallas_call(
        kernel,
        out_shape=jax.ShapeDtypeStruct((last, width), jnp.bfloat16),
        in_specs=inside(count),
        out_specs=pl.BlockSpec(memory_space=pltpu.VMEM),
        compiler_params=params(16),
        cost_estimate=cost(0, 4 * last * width),
        name="join",
    )(*blocks)


def column_tile(width, tile):
    return pl.BlockSpec((width, tile), lambda i: (0, i))


def row_tile(tile, width):
    return pl.BlockSpec((tile, width), lambda i: (i, 0))


def tile_of(tile):
    return pl.ds(pl.multiple_of(pl.program_id(0) * tile, tile), tile)


def forward(tile, rows, gate_proj, up_proj):
    groups = len(rows)
    slots = rows[0].shape[0]
    width, hid = gate_proj.shape
    total = groups * slots

    def kernel(*refs):
        gate_ref, up_ref, pre_gate_ref, pre_up_ref, held = refs[groups:]

        @pl.when(pl.program_id(0) == 0)
        def _():
            for at in range(groups):
                held[at * slots : (at + 1) * slots, :] = refs[at][...]

        columns = tile_of(tile)
        pre_gate_ref[...] = dot(held[...], gate_ref[:, columns])
        pre_up_ref[...] = dot(held[...], up_ref[:, columns])

    return pl.pallas_call(
        kernel,
        grid=(hid // tile,),
        out_shape=[jax.ShapeDtypeStruct((total, hid), jnp.float32)] * 2,
        in_specs=inside(groups + 2),
        out_specs=[column_tile(total, tile)] * 2,
        scratch_shapes=[pltpu.VMEM((total, width), jnp.bfloat16)],
        compiler_params=params(20),
        cost_estimate=cost(4 * total * width * hid, 4 * width * hid + 4 * total * width),
        name="forward",
    )(*rows, gate_proj, up_proj)


def hidden_grads(pre_gate, pre_up, d_hidden):
    sig = jax.nn.sigmoid(pre_gate)
    silu = pre_gate * sig
    hidden = (silu * pre_up).astype(jnp.bfloat16)
    d_gate = (d_hidden * pre_up * sig * (1.0 + pre_gate * (1.0 - sig))).astype(jnp.bfloat16)
    d_up = (d_hidden * silu).astype(jnp.bfloat16)
    return hidden, d_gate, d_up


def back(blocks, tile, scaled, pre_gate, pre_up, gate_proj, up_proj, down_proj):
    slots, width = scaled.shape
    hid = gate_proj.shape[1]
    pieces, step = cut(width)

    def kernel(scaled_ref, gate_ref, up_ref, down_ref, pre_gate_ref, pre_up_ref, *rest):
        outs = rest[:blocks]
        hidden_ref, d_gate_ref, d_up_ref, total = rest[blocks:]
        columns = tile_of(tile)
        d_hidden = dot(scaled_ref[...], down_ref[columns, :], BY_WIDTH)
        hidden, d_gate, d_up = hidden_grads(pre_gate_ref[...], pre_up_ref[...], d_hidden)
        hidden_ref[...] = hidden
        d_gate_ref[...] = d_gate
        d_up_ref[...] = d_up
        part = dot(d_gate, gate_ref[:, columns], BY_WIDTH)
        part += dot(d_up, up_ref[:, columns], BY_WIDTH)

        @pl.when(pl.program_id(0) == 0)
        def _():
            total[...] = part

        @pl.when(pl.program_id(0) > 0)
        def _():
            total[...] += part

        @pl.when(pl.program_id(0) == hid // tile - 1)
        def _():
            done = total[...].astype(jnp.bfloat16)
            extra = jnp.zeros((blocks * ROWS, step), jnp.float32)
            for at in range(pieces):
                extra += dot(
                    spill_picks(blocks, pieces, at),
                    done[blocks * ROWS :, at * step : (at + 1) * step],
                    BY_ROWS,
                )
            extra = extra.astype(jnp.bfloat16)
            for block in range(blocks):
                part_of = slice(block * ROWS, (block + 1) * ROWS)
                outs[block][:, :width] = done[part_of]
                outs[block][:, width:] = extra[part_of]

    factor = jax.ShapeDtypeStruct((slots, hid), jnp.bfloat16)
    result = pl.pallas_call(
        kernel,
        grid=(hid // tile,),
        out_shape=[jax.ShapeDtypeStruct((ROWS, width + step), jnp.bfloat16)] * blocks
        + [factor] * 3,
        in_specs=inside(4) + [column_tile(slots, tile)] * 2,
        out_specs=inside(blocks) + [column_tile(slots, tile)] * 3,
        scratch_shapes=[pltpu.VMEM((slots, width), jnp.float32)],
        compiler_params=params(20),
        cost_estimate=cost(6 * slots * width * hid, 6 * width * hid),
        name="back",
    )(scaled, gate_proj, up_proj, down_proj, pre_gate, pre_up)
    return result[:blocks], result[blocks:]


def weight_grads(tile, part, rows, scaled, pre_gate, pre_up, down_proj, own):
    groups = len(rows)
    slots, width = rows[0].shape
    hid = down_proj.shape[0]
    some = (groups - 1) * slots
    share = width // groups

    def kernel(part_ref, *refs):
        x_refs, dy_refs = refs[:groups], refs[groups : 2 * groups]
        down_ref, pre_gate_ref, pre_up_ref, own_hidden, own_gate, own_up = refs[
            2 * groups : 2 * groups + 6
        ]
        d_gate_ref, d_up_ref, d_down_ref, others, x_mine, dy_mine = refs[2 * groups + 6 :]

        @pl.when(pl.program_id(0) == 0)
        def _():
            columns = pl.ds(pl.multiple_of(part_ref[0] * share, share), share)
            for at in range(groups):
                here = slice(at * slots, (at + 1) * slots)
                x_mine[here, :] = x_refs[at][:, columns]
                dy_mine[here, :] = dy_refs[at][:, columns]
                if at > 0:
                    others[(at - 1) * slots : at * slots, :] = dy_refs[at][...]

        d_hidden = dot(others[...], down_ref[tile_of(tile), :], BY_WIDTH)
        hidden, d_gate, d_up = hidden_grads(pre_gate_ref[...], pre_up_ref[...], d_hidden)
        hidden = jnp.concatenate([own_hidden[...], hidden], 0)
        d_gate = jnp.concatenate([own_gate[...], d_gate], 0)
        d_up = jnp.concatenate([own_up[...], d_up], 0)
        both = dot(x_mine[...], jnp.concatenate([d_gate, d_up], 1), BY_ROWS)
        d_gate_ref[...] = both[:, :tile]
        d_up_ref[...] = both[:, tile:]
        d_down_ref[...] = dot(hidden, dy_mine[...], BY_ROWS)

    return pl.pallas_call(
        kernel,
        grid=(hid // tile,),
        out_shape=[
            jax.ShapeDtypeStruct((share, hid), jnp.float32),
            jax.ShapeDtypeStruct((share, hid), jnp.float32),
            jax.ShapeDtypeStruct((hid, share), jnp.float32),
        ],
        in_specs=[pl.BlockSpec(memory_space=pltpu.SMEM)]
        + inside(2 * groups + 1)
        + [column_tile(some, tile)] * 2
        + [column_tile(slots, tile)] * 3,
        out_specs=[column_tile(share, tile), column_tile(share, tile), row_tile(tile, share)],
        scratch_shapes=[
            pltpu.VMEM((some, width), jnp.bfloat16),
            pltpu.VMEM((groups * slots, share), jnp.bfloat16),
            pltpu.VMEM((groups * slots, share), jnp.bfloat16),
        ],
        compiler_params=params(20),
        cost_estimate=cost(
            2 * some * width * hid + 6 * groups * slots * share * hid,
            2 * width * hid + 4 * groups * slots * width,
        ),
        name="weight_grads",
    )(part, *rows, *scaled, down_proj, pre_gate, pre_up, *own)


def swap(value, axis, distance):
    size = lax.axis_size(axis)
    return lax.ppermute(value, axis, [(at, at ^ distance) for at in range(size)])


def exchange(blocks):
    out = list(blocks)
    for distance in reversed(range(1, len(blocks))):
        out[distance] = swap(blocks[distance], "expert", distance)
    return out


def after(values, *earlier):
    return lax.optimization_barrier((list(values), *earlier))[0]


def gather_body(tokens, cotangent, routes, expert_gates, gate_proj, up_proj, down_proj):
    blocks = lax.axis_size("expert")
    tile = 256
    me = lax.axis_index("expert").astype(jnp.int32).reshape(1)
    part = lax.axis_index("dp").astype(jnp.int32).reshape(1)
    routes = routes.reshape(1, -1)
    gates = expert_gates.reshape(1, -1)
    weights = (gate_proj, up_proj, down_proj)
    received = exchange(pack(blocks, me, routes, tokens))
    packed, *received[-3:] = lax.optimization_barrier(
        (pack(blocks, me, routes, cotangent, gates), *received[-3:])
    )
    rows = join(received)
    far = swap(rows, "dp", 2)
    near = swap(rows, "dp", 1)
    pre = forward(tile, [rows], gate_proj, up_proj)
    received, far = lax.optimization_barrier((exchange(packed), far, pre))[:2]
    last = swap(far, "dp", 1)
    scaled = join(received)
    dy_far = swap(scaled, "dp", 2)
    dy_near = swap(scaled, "dp", 1)
    sent, own = back(blocks, tile, scaled, *pre, *weights)
    sent, last, dy_near = lax.optimization_barrier((sent, last, dy_near))
    returned = exchange(sent)
    others = forward(tile, [near, far, last], gate_proj, up_proj)
    dy_far = after([dy_far], sent)[0]
    dy_last = swap(dy_far, "dp", 1)
    grads = weight_grads(
        tile,
        part,
        [rows, near, far, last],
        [scaled, dy_near, dy_far, dy_last],
        *others,
        down_proj,
        own,
    )
    return (merge(me, routes, returned), *grads)


def body(tokens, cotangent, routes, expert_gates, gate_proj, up_proj, down_proj):
    groups, blocks = lax.axis_size("dp"), lax.axis_size("expert")
    width, hid = gate_proj.shape
    rows_sent = (groups - 1) * 2 * blocks * MOST * width
    grads_sent = 3 * width * hid * (groups - 1) // groups
    fits = blocks == EXPERTS and groups == 4 and hid % 256 == 0
    fits = fits and tokens.shape[0] == 128 and routes.shape[1] == 1 and width // groups % 128 == 0
    chosen = gather_body if fits and rows_sent < grads_sent else scatter_body
    return chosen(tokens, cotangent, routes, expert_gates, gate_proj, up_proj, down_proj)


def solution(mesh):
    in_specs = (
        P(("dp", "expert"), None),
        P(("dp", "expert"), None),
        P(("dp", "expert"), None),
        P(("dp", "expert"), None),
        P(None, "expert"),
        P(None, "expert"),
        P("expert", None),
    )
    out_specs = (P(("dp", "expert"), None), P("dp", "expert"), P("dp", "expert"), P("expert", "dp"))
    return jax.shard_map(body, mesh=mesh, in_specs=in_specs, out_specs=out_specs, check_vma=False)
```

```python
import jax
import jax.numpy as jnp
from jax import lax
from jax.experimental import pallas as pl
from jax.experimental.pallas import tpu as pltpu
from jax.sharding import PartitionSpec as P

EXPERTS = 8
MOST = 18
ROWS = 16
VMEM_BYTES = (63 * 1024 + 768) * 1024


def build_slots(routes, capacity):
    flat_routes = routes.reshape(-1)
    one_hot = (flat_routes[:, None] == jnp.arange(EXPERTS, dtype=jnp.int32)[None, :]).astype(
        jnp.int32
    )
    before = jnp.cumsum(one_hot, axis=0) - one_hot
    position = jnp.sum(before * one_hot, axis=1)
    return flat_routes * capacity + position


def scatter_body(tokens, cotangent, routes, expert_gates, gate_proj, up_proj, down_proj):
    tok_dev, model_dim = tokens.shape
    top_k = routes.shape[1]
    expert_devs = lax.axis_size("expert")
    group_size = expert_devs // EXPERTS
    capacity = MOST
    slot_total = EXPERTS * capacity
    slot_of = build_slots(routes, capacity)
    owners = jnp.arange(tok_dev * top_k, dtype=jnp.int32) // top_k
    slot_table = jnp.full((slot_total,), tok_dev, jnp.int32).at[slot_of].set(owners)
    slot_gate = jnp.zeros((slot_total,), jnp.float32).at[slot_of].set(expert_gates.reshape(-1))
    x_slots = jnp.take(tokens, slot_table, axis=0, mode="fill", fill_value=0)
    dy_slots = (
        jnp.take(cotangent, slot_table, axis=0, mode="fill", fill_value=0).astype(jnp.float32)
        * slot_gate[:, None]
    ).astype(jnp.bfloat16)

    def copies(values):
        spread = values.reshape(EXPERTS, 1, capacity, model_dim)
        return jnp.broadcast_to(spread, (EXPERTS, group_size, capacity, model_dim)).reshape(
            expert_devs, capacity, model_dim
        )

    x_recv, dy_recv = (
        lax.all_to_all(copies(x_slots), "expert", split_axis=0, concat_axis=0, tiled=True),
        lax.all_to_all(copies(dy_slots), "expert", split_axis=0, concat_axis=0, tiled=True),
    )
    in_rows = x_recv.reshape(expert_devs * capacity, model_dim)
    scaled = dy_recv.reshape(expert_devs * capacity, model_dim)
    pre_gate = jnp.dot(in_rows, gate_proj, preferred_element_type=jnp.float32)
    pre_up = jnp.dot(in_rows, up_proj, preferred_element_type=jnp.float32)
    gate_sig = jax.nn.sigmoid(pre_gate)
    hidden = (pre_gate * gate_sig * pre_up).astype(jnp.bfloat16)
    by_width = (((1,), (1,)), ((), ()))
    by_rows = (((0,), (0,)), ((), ()))
    d_hidden = lax.dot_general(scaled, down_proj, by_width, preferred_element_type=jnp.float32)
    d_gate = (d_hidden * pre_up * gate_sig * (1.0 + pre_gate * (1.0 - gate_sig))).astype(
        jnp.bfloat16
    )
    d_up = (d_hidden * pre_gate * gate_sig).astype(jnp.bfloat16)
    grad_down = lax.dot_general(hidden, scaled, by_rows, preferred_element_type=jnp.float32)
    grad_gate = lax.dot_general(in_rows, d_gate, by_rows, preferred_element_type=jnp.float32)
    grad_up = lax.dot_general(in_rows, d_up, by_rows, preferred_element_type=jnp.float32)
    grad_gate, grad_up, grad_down = (
        lax.psum_scatter(
            grad_gate.astype(jnp.bfloat16), "dp", scatter_dimension=0, tiled=True
        ).astype(jnp.float32),
        lax.psum_scatter(
            grad_up.astype(jnp.bfloat16), "dp", scatter_dimension=0, tiled=True
        ).astype(jnp.float32),
        lax.psum_scatter(
            grad_down.astype(jnp.bfloat16), "dp", scatter_dimension=1, tiled=True
        ).astype(jnp.float32),
    )
    joined_grads = jnp.concatenate([d_gate, d_up], 1)
    joined_proj = jnp.concatenate([gate_proj, up_proj], 1)
    partial_value = lax.dot_general(
        joined_grads, joined_proj, by_width, preferred_element_type=jnp.float32
    ).astype(jnp.bfloat16)
    returned = lax.all_to_all(
        partial_value.reshape(expert_devs, capacity, model_dim),
        "expert",
        split_axis=0,
        concat_axis=0,
        tiled=True,
    )
    summed = jnp.sum(
        returned.reshape(EXPERTS, group_size, capacity, model_dim).astype(jnp.float32), axis=1
    )
    summed = summed.reshape(slot_total, model_dim)
    grad_input = jnp.take(summed, slot_of, axis=0).reshape(tok_dev, top_k, model_dim).sum(axis=1)
    return (grad_input.astype(jnp.bfloat16), grad_gate, grad_up, grad_down)


BY_WIDTH = (((1,), (1,)), ((), ()))
BY_ROWS = (((0,), (0,)), ((), ()))


def cut(width):
    pieces = ROWS // (MOST - ROWS)
    return pieces, width // pieces


def width_of(packed):
    pieces = ROWS // (MOST - ROWS)
    return packed.shape[2] * pieces // (pieces + 1)


def cost(flops, moved):
    return pl.CostEstimate(flops=flops, bytes_accessed=moved, transcendentals=0)


def params():
    return pltpu.CompilerParams(vmem_limit_bytes=VMEM_BYTES)


def anywhere(count):
    return [pl.BlockSpec(memory_space=pl.ANY)] * count


def dot(left, right, dims=(((1,), (0,)), ((), ()))):
    return lax.dot_general(left, right, dims, preferred_element_type=jnp.float32)


def ones(mask):
    return jnp.where(mask, 1.0, 0.0).astype(jnp.bfloat16)


def start(pairs, arrived):
    for at, (source, target) in enumerate(pairs):
        pltpu.make_async_copy(source, target, arrived.at[at]).start()


def wait(pairs, arrived, first=0):
    for at, (source, target) in enumerate(pairs):
        if at >= first:
            pltpu.make_async_copy(source, target, arrived.at[at]).wait()


def slot_masks(routes, blocks, width):
    tokens = routes.shape[1]
    pieces, _ = cut(width)
    experts = lax.broadcasted_iota(jnp.int32, (EXPERTS, tokens), 0)
    named = jnp.where(experts == routes, 1.0, 0.0)
    earlier = lax.broadcasted_iota(jnp.int32, (tokens, tokens), 0) < lax.broadcasted_iota(
        jnp.int32, (tokens, tokens), 1
    )
    before = dot(named.astype(jnp.bfloat16), ones(earlier))
    position = jnp.sum(before * named, axis=0, keepdims=True).astype(jnp.int32)
    slot = lax.broadcasted_iota(jnp.int32, (blocks * ROWS, tokens), 0)
    row = slot % ROWS
    mine = slot // ROWS == routes
    main = mine & (position == row)
    spill = mine & (position == ROWS + row // pieces)
    return main, spill, row % pieces


def pack(blocks, routes, values, gates=None):
    tokens, width = values.shape
    pieces, step = cut(width)
    sources = (routes,) + (() if gates is None else (gates,)) + (values,)
    count = len(sources)

    def kernel(*refs):
        out, held, arrived = refs[count], refs[count + 1 : 2 * count + 1], refs[-1]
        pairs = list(zip(refs[:count], held))
        start(pairs, arrived)
        wait(pairs[:-1], arrived)
        main, spill, piece = slot_masks(held[0][...], blocks, width)
        picks = [ones(spill & (piece == at)) for at in range(pieces)]
        if gates is not None:
            weights = held[1][...]
            main_scale = jnp.sum(jnp.where(main, weights, 0.0), axis=1, keepdims=True)
            spill_scale = jnp.sum(jnp.where(spill, weights, 0.0), axis=1, keepdims=True)
        wait(pairs, arrived, count - 1)
        rows = dot(ones(main), held[-1][...])
        extra = jnp.zeros((blocks * ROWS, step), jnp.float32)
        for at in range(pieces):
            extra += dot(picks[at], held[-1][:, at * step : (at + 1) * step])
        if gates is not None:
            rows, extra = rows * main_scale, extra * spill_scale
        rows = rows.astype(jnp.bfloat16)
        extra = extra.astype(jnp.bfloat16)
        for block in range(blocks):
            part = slice(block * ROWS, (block + 1) * ROWS)
            out[block, :, :width] = rows[part]
            out[block, :, width:] = extra[part]

    return pl.pallas_call(
        kernel,
        out_shape=jax.ShapeDtypeStruct((blocks, ROWS, width + step), jnp.bfloat16),
        in_specs=anywhere(count),
        out_specs=pl.BlockSpec(memory_space=pltpu.VMEM),
        scratch_shapes=[pltpu.VMEM(source.shape, source.dtype) for source in sources]
        + [pltpu.SemaphoreType.DMA((count,))],
        compiler_params=params(),
        cost_estimate=cost(4 * blocks * ROWS * tokens * width, 4 * tokens * width),
        name="pack",
    )(*sources)


def merge(routes, returned):
    blocks = returned.shape[0]
    tokens = routes.shape[1]
    width = width_of(returned)
    pieces, step = cut(width)

    def kernel(routes_ref, back_ref, out, named, held, arrived):
        pairs = [(routes_ref, named), (back_ref, held)]
        start(pairs, arrived)
        wait(pairs[:1], arrived)
        main, spill, piece = slot_masks(named[...], blocks, width)
        mains = ones(main)
        picks = [ones(spill & (piece == at)) for at in range(pieces)]
        wait(pairs, arrived, 1)
        rows = jnp.concatenate([held[at, :, :width] for at in range(blocks)], 0)
        extra = jnp.concatenate([held[at, :, width:] for at in range(blocks)], 0)
        picked = dot(mains, rows, BY_ROWS)
        for at in range(pieces):
            columns = slice(at * step, (at + 1) * step)
            out[:, columns] = (picked[:, columns] + dot(picks[at], extra, BY_ROWS)).astype(
                jnp.bfloat16
            )

    return pl.pallas_call(
        kernel,
        out_shape=jax.ShapeDtypeStruct((tokens, width), jnp.bfloat16),
        in_specs=anywhere(2),
        out_specs=pl.BlockSpec(memory_space=pltpu.VMEM),
        scratch_shapes=[
            pltpu.VMEM(routes.shape, routes.dtype),
            pltpu.VMEM(returned.shape, returned.dtype),
            pltpu.SemaphoreType.DMA((2,)),
        ],
        compiler_params=params(),
        cost_estimate=cost(4 * blocks * ROWS * tokens * width, 4 * tokens * width),
        name="merge",
    )(routes, returned)


def spill_picks(blocks, pieces, at):
    shape = (blocks * (MOST - ROWS), blocks * ROWS)
    slot = lax.broadcasted_iota(jnp.int32, shape, 0)
    row = lax.broadcasted_iota(jnp.int32, shape, 1)
    return ones(row == slot * pieces + at)


def unpack(main, tail, pieces, begin, first, out):
    blocks = main.shape[0]
    step = tail.shape[2]
    for at in range(blocks):
        out[first + at * ROWS : first + (at + 1) * ROWS, :] = main[at]
    extra = jnp.concatenate([tail[at] for at in range(blocks)], 0)
    spill = slice(first + blocks * ROWS, first + blocks * MOST)
    for at in range(out.shape[1] // step):
        out[spill, at * step : (at + 1) * step] = dot(
            spill_picks(blocks, pieces, begin + at), extra
        ).astype(jnp.bfloat16)


def column_tile(width, tile):
    return pl.BlockSpec((width, tile), lambda i: (0, i))


def row_tile(tile, width):
    return pl.BlockSpec((tile, width), lambda i: (i, 0))


def tile_of(index, tile):
    return pl.ds(pl.multiple_of(index * tile, tile), tile)


def weight_copy(source, target, arrived, index, axis, tile):
    here = tile_of(index, tile)
    view = source.at[:, here] if axis else source.at[here, :]
    return pltpu.make_async_copy(view, target.at[index], arrived.at[index])


def forward(tile, packed, gate_proj, up_proj):
    groups = len(packed)
    blocks = packed[0].shape[0]
    width, hid = gate_proj.shape
    pieces, _ = cut(width)
    slots = blocks * MOST
    total = groups * slots
    tiles = hid // tile

    def kernel(*refs):
        gate_ref, up_ref, pre_gate_ref, pre_up_ref = refs[groups : groups + 4]
        held, rows, gate, up, arrived, gate_in, up_in = refs[groups + 4 :]
        now = pl.program_id(0)

        @pl.when(now == 0)
        def _():
            pairs = [(refs[at], held.at[at]) for at in range(groups)]
            start(pairs, arrived)
            for at in range(tiles):
                weight_copy(gate_ref, gate, gate_in, at, 1, tile).start()
                weight_copy(up_ref, up, up_in, at, 1, tile).start()
            wait(pairs, arrived)
            for at in range(groups):
                unpack(
                    held.at[at, :, :, :width], held.at[at, :, :, width:], pieces, 0, at * slots, rows
                )

        weight_copy(gate_ref, gate, gate_in, now, 1, tile).wait()
        pre_gate_ref[...] = dot(rows[...], gate[now])
        weight_copy(up_ref, up, up_in, now, 1, tile).wait()
        pre_up_ref[...] = dot(rows[...], up[now])

    return pl.pallas_call(
        kernel,
        grid=(tiles,),
        out_shape=[jax.ShapeDtypeStruct((total, hid), jnp.float32)] * 2,
        in_specs=anywhere(groups + 2),
        out_specs=[column_tile(total, tile)] * 2,
        scratch_shapes=[
            pltpu.VMEM((groups,) + packed[0].shape, jnp.bfloat16),
            pltpu.VMEM((total, width), jnp.bfloat16),
            pltpu.VMEM((tiles, width, tile), jnp.bfloat16),
            pltpu.VMEM((tiles, width, tile), jnp.bfloat16),
            pltpu.SemaphoreType.DMA((groups,)),
            pltpu.SemaphoreType.DMA((tiles,)),
            pltpu.SemaphoreType.DMA((tiles,)),
        ],
        compiler_params=params(),
        cost_estimate=cost(4 * total * width * hid, 4 * width * hid + 4 * total * width),
        name="forward",
    )(*packed, gate_proj, up_proj)


def hidden_grads(pre_gate, pre_up, d_hidden):
    sig = jax.nn.sigmoid(pre_gate)
    silu = pre_gate * sig
    hidden = (silu * pre_up).astype(jnp.bfloat16)
    d_gate = (d_hidden * pre_up * sig * (1.0 + pre_gate * (1.0 - sig))).astype(jnp.bfloat16)
    d_up = (d_hidden * silu).astype(jnp.bfloat16)
    return hidden, d_gate, d_up


def back(tile, packed, pre_gate, pre_up, gate_proj, up_proj, down_proj):
    blocks = packed.shape[0]
    width, hid = gate_proj.shape
    slots = blocks * MOST
    pieces, step = cut(width)
    tiles = hid // tile

    def kernel(packed_ref, gate_ref, up_ref, down_ref, pre_gate_ref, pre_up_ref, *rest):
        out, hidden_ref, d_gate_ref, d_up_ref, held, scaled, total, gate, up, down = rest[:10]
        arrived, gate_in, up_in, down_in = rest[10:]
        now = pl.program_id(0)

        @pl.when(now == 0)
        def _():
            start([(packed_ref, held)], arrived)
            for at in range(tiles):
                weight_copy(down_ref, down, down_in, at, 0, tile).start()
                weight_copy(gate_ref, gate, gate_in, at, 1, tile).start()
                weight_copy(up_ref, up, up_in, at, 1, tile).start()
            wait([(packed_ref, held)], arrived)
            unpack(held.at[:, :, :width], held.at[:, :, width:], pieces, 0, 0, scaled)

        weight_copy(down_ref, down, down_in, now, 0, tile).wait()
        d_hidden = dot(scaled[...], down[now], BY_WIDTH)
        hidden, d_gate, d_up = hidden_grads(pre_gate_ref[...], pre_up_ref[...], d_hidden)
        hidden_ref[...] = hidden
        d_gate_ref[...] = d_gate
        d_up_ref[...] = d_up
        weight_copy(gate_ref, gate, gate_in, now, 1, tile).wait()
        weight_copy(up_ref, up, up_in, now, 1, tile).wait()
        part = dot(d_gate, gate[now], BY_WIDTH) + dot(d_up, up[now], BY_WIDTH)

        @pl.when(now == 0)
        def _():
            total[...] = part

        @pl.when(now > 0)
        def _():
            total[...] += part

        @pl.when(now == tiles - 1)
        def _():
            done = total[...].astype(jnp.bfloat16)
            extra = jnp.zeros((blocks * ROWS, step), jnp.float32)
            for at in range(pieces):
                extra += dot(
                    spill_picks(blocks, pieces, at),
                    done[blocks * ROWS :, at * step : (at + 1) * step],
                    BY_ROWS,
                )
            extra = extra.astype(jnp.bfloat16)
            for block in range(blocks):
                part_of = slice(block * ROWS, (block + 1) * ROWS)
                out[block, :, :width] = done[part_of]
                out[block, :, width:] = extra[part_of]

    factor = jax.ShapeDtypeStruct((slots, hid), jnp.bfloat16)
    sent, *own = pl.pallas_call(
        kernel,
        grid=(tiles,),
        out_shape=[jax.ShapeDtypeStruct(packed.shape, jnp.bfloat16)] + [factor] * 3,
        in_specs=anywhere(4) + [column_tile(slots, tile)] * 2,
        out_specs=[pl.BlockSpec(packed.shape, lambda i: (0, 0, 0))]
        + [column_tile(slots, tile)] * 3,
        scratch_shapes=[
            pltpu.VMEM(packed.shape, jnp.bfloat16),
            pltpu.VMEM((slots, width), jnp.bfloat16),
            pltpu.VMEM((slots, width), jnp.float32),
            pltpu.VMEM((tiles, width, tile), jnp.bfloat16),
            pltpu.VMEM((tiles, width, tile), jnp.bfloat16),
            pltpu.VMEM((tiles, tile, width), jnp.bfloat16),
            pltpu.SemaphoreType.DMA((1,)),
            pltpu.SemaphoreType.DMA((tiles,)),
            pltpu.SemaphoreType.DMA((tiles,)),
            pltpu.SemaphoreType.DMA((tiles,)),
        ],
        compiler_params=params(),
        cost_estimate=cost(6 * slots * width * hid, 6 * width * hid),
        name="back",
    )(packed, gate_proj, up_proj, down_proj, pre_gate, pre_up)
    return sent, own


def weight_grads(tile, part, rows, scaled, pre_gate, pre_up, down_proj, own):
    groups = len(rows)
    blocks = rows[0].shape[0]
    hid, width = down_proj.shape
    pieces, step = cut(width)
    slots = blocks * MOST
    some = (groups - 1) * slots
    share = width // groups
    tiles = hid // tile

    def kernel(part_ref, *refs):
        x_refs, dy_refs = refs[:groups], refs[groups : 2 * groups]
        down_ref, pre_gate_ref, pre_up_ref, own_hidden, own_gate, own_up = refs[
            2 * groups : 2 * groups + 6
        ]
        d_gate_ref, d_up_ref, d_down_ref = refs[2 * groups + 6 : 2 * groups + 9]
        held, mains, tails, others, x_mine, dy_mine, down = refs[2 * groups + 9 : 2 * groups + 16]
        held_in, mains_in, tails_in, down_in = refs[2 * groups + 16 :]
        now = pl.program_id(0)

        @pl.when(now == 0)
        def _():
            columns = pl.ds(pl.multiple_of(part_ref[0] * share, share), share)
            begin = part_ref[0] * (share // step)
            whole = [(dy_refs[at], held.at[at - 1]) for at in range(1, groups)]
            sources = list(x_refs) + [dy_refs[0]]
            cuts = [(ref.at[:, :, columns], mains.at[at]) for at, ref in enumerate(sources)]
            ends = [(ref.at[:, :, width:], tails.at[at]) for at, ref in enumerate(sources)]
            start(whole, held_in)
            for at in range(tiles):
                weight_copy(down_ref, down, down_in, at, 0, tile).start()
            start(cuts, mains_in)
            start(ends, tails_in)
            wait(whole, held_in)
            for at in range(groups - 1):
                unpack(
                    held.at[at, :, :, :width],
                    held.at[at, :, :, width:],
                    pieces,
                    0,
                    at * slots,
                    others,
                )
            dy_mine[slots:, :] = others[:, columns]
            wait(cuts, mains_in)
            wait(ends, tails_in)
            for at in range(groups):
                unpack(mains.at[at], tails.at[at], pieces, begin, at * slots, x_mine)
            unpack(mains.at[groups], tails.at[groups], pieces, begin, 0, dy_mine)

        weight_copy(down_ref, down, down_in, now, 0, tile).wait()
        d_hidden = dot(others[...], down[now], BY_WIDTH)
        hidden, d_gate, d_up = hidden_grads(pre_gate_ref[...], pre_up_ref[...], d_hidden)
        hidden = jnp.concatenate([own_hidden[...], hidden], 0)
        d_gate = jnp.concatenate([own_gate[...], d_gate], 0)
        d_up = jnp.concatenate([own_up[...], d_up], 0)
        both = dot(x_mine[...], jnp.concatenate([d_gate, d_up], 1), BY_ROWS)
        d_gate_ref[...] = both[:, :tile]
        d_up_ref[...] = both[:, tile:]
        d_down_ref[...] = dot(hidden, dy_mine[...], BY_ROWS)

    return pl.pallas_call(
        kernel,
        grid=(tiles,),
        out_shape=[
            jax.ShapeDtypeStruct((share, hid), jnp.float32),
            jax.ShapeDtypeStruct((share, hid), jnp.float32),
            jax.ShapeDtypeStruct((hid, share), jnp.float32),
        ],
        in_specs=[pl.BlockSpec(memory_space=pltpu.SMEM)]
        + anywhere(2 * groups + 1)
        + [column_tile(some, tile)] * 2
        + [column_tile(slots, tile)] * 3,
        out_specs=[column_tile(share, tile), column_tile(share, tile), row_tile(tile, share)],
        scratch_shapes=[
            pltpu.VMEM((groups - 1,) + rows[0].shape, jnp.bfloat16),
            pltpu.VMEM((groups + 1, blocks, ROWS, share), jnp.bfloat16),
            pltpu.VMEM((groups + 1, blocks, ROWS, step), jnp.bfloat16),
            pltpu.VMEM((some, width), jnp.bfloat16),
            pltpu.VMEM((groups * slots, share), jnp.bfloat16),
            pltpu.VMEM((groups * slots, share), jnp.bfloat16),
            pltpu.VMEM((tiles, tile, width), jnp.bfloat16),
            pltpu.SemaphoreType.DMA((groups - 1,)),
            pltpu.SemaphoreType.DMA((groups + 1,)),
            pltpu.SemaphoreType.DMA((groups + 1,)),
            pltpu.SemaphoreType.DMA((tiles,)),
        ],
        compiler_params=params(),
        cost_estimate=cost(
            2 * some * width * hid + 6 * groups * slots * share * hid,
            2 * width * hid + 4 * groups * slots * width,
        ),
        name="weight_grads",
    )(part, *rows, *scaled, down_proj, pre_gate, pre_up, *own)


def swap(value, axis, distance):
    size = lax.axis_size(axis)
    return lax.ppermute(value, axis, [(at, at ^ distance) for at in range(size)])


def exchange(blocks):
    return lax.all_to_all(blocks, "expert", split_axis=0, concat_axis=0, tiled=True)


def after(value, *earlier):
    return lax.optimization_barrier((value, *earlier))[0]


def gather_body(tokens, cotangent, routes, expert_gates, gate_proj, up_proj, down_proj):
    blocks = lax.axis_size("expert")
    tile = 256
    part = lax.axis_index("dp").astype(jnp.int32).reshape(1)
    routes = routes.reshape(1, -1)
    gates = expert_gates.reshape(1, -1)
    packed = pack(blocks, routes, tokens)
    rows = exchange(packed)
    scaled = exchange(pack(blocks, routes, after(cotangent, packed), gates))
    far = swap(rows, "dp", 2)
    near = swap(rows, "dp", 1)
    pre = forward(tile, [rows], gate_proj, up_proj)
    scaled = after(scaled, *pre)
    dy_far = swap(scaled, "dp", 2)
    dy_near = swap(scaled, "dp", 1)
    sent, own = back(tile, scaled, *pre, gate_proj, up_proj, down_proj)
    returned = exchange(sent)
    last = swap(after(far, pre[0]), "dp", 1)
    others = forward(tile, [after(near, sent), far, last], gate_proj, up_proj)
    dy_last = swap(after(dy_far, sent), "dp", 1)
    grads = weight_grads(
        tile,
        part,
        [rows, near, far, last],
        [scaled, dy_near, dy_far, dy_last],
        *others,
        down_proj,
        own,
    )
    return (merge(routes, returned), *grads)


def body(tokens, cotangent, routes, expert_gates, gate_proj, up_proj, down_proj):
    groups, blocks = lax.axis_size("dp"), lax.axis_size("expert")
    width, hid = gate_proj.shape
    rows_sent = (groups - 1) * 2 * blocks * MOST * width
    grads_sent = 3 * width * hid * (groups - 1) // groups
    fits = blocks == EXPERTS and groups == 4 and hid % 256 == 0
    fits = fits and tokens.shape[0] == 128 and routes.shape[1] == 1 and width // groups % 128 == 0
    chosen = gather_body if fits and rows_sent < grads_sent else scatter_body
    return chosen(tokens, cotangent, routes, expert_gates, gate_proj, up_proj, down_proj)


def solution(mesh):
    in_specs = (
        P(("dp", "expert"), None),
        P(("dp", "expert"), None),
        P(("dp", "expert"), None),
        P(("dp", "expert"), None),
        P(None, "expert"),
        P(None, "expert"),
        P("expert", None),
    )
    out_specs = (P(("dp", "expert"), None), P("dp", "expert"), P("dp", "expert"), P("expert", "dp"))
    return jax.shard_map(body, mesh=mesh, in_specs=in_specs, out_specs=out_specs, check_vma=False)
```

```python
import jax
import jax.numpy as jnp
from jax import lax
from jax.experimental import pallas as pl
from jax.experimental.pallas import tpu as pltpu
from jax.sharding import PartitionSpec as P

EXPERTS = 8
MOST = 18
ROWS = 16
VMEM_BYTES = (63 * 1024 + 768) * 1024


def build_slots(routes, capacity):
    flat_routes = routes.reshape(-1)
    one_hot = (flat_routes[:, None] == jnp.arange(EXPERTS, dtype=jnp.int32)[None, :]).astype(
        jnp.int32
    )
    before = jnp.cumsum(one_hot, axis=0) - one_hot
    position = jnp.sum(before * one_hot, axis=1)
    return flat_routes * capacity + position


def scatter_body(tokens, cotangent, routes, expert_gates, gate_proj, up_proj, down_proj):
    tok_dev, model_dim = tokens.shape
    top_k = routes.shape[1]
    expert_devs = lax.axis_size("expert")
    group_size = expert_devs // EXPERTS
    capacity = MOST
    slot_total = EXPERTS * capacity
    slot_of = build_slots(routes, capacity)
    owners = jnp.arange(tok_dev * top_k, dtype=jnp.int32) // top_k
    slot_table = jnp.full((slot_total,), tok_dev, jnp.int32).at[slot_of].set(owners)
    slot_gate = jnp.zeros((slot_total,), jnp.float32).at[slot_of].set(expert_gates.reshape(-1))
    x_slots = jnp.take(tokens, slot_table, axis=0, mode="fill", fill_value=0)
    dy_slots = (
        jnp.take(cotangent, slot_table, axis=0, mode="fill", fill_value=0).astype(jnp.float32)
        * slot_gate[:, None]
    ).astype(jnp.bfloat16)

    def copies(values):
        spread = values.reshape(EXPERTS, 1, capacity, model_dim)
        return jnp.broadcast_to(spread, (EXPERTS, group_size, capacity, model_dim)).reshape(
            expert_devs, capacity, model_dim
        )

    x_recv, dy_recv = (
        lax.all_to_all(copies(x_slots), "expert", split_axis=0, concat_axis=0, tiled=True),
        lax.all_to_all(copies(dy_slots), "expert", split_axis=0, concat_axis=0, tiled=True),
    )
    in_rows = x_recv.reshape(expert_devs * capacity, model_dim)
    scaled = dy_recv.reshape(expert_devs * capacity, model_dim)
    pre_gate = jnp.dot(in_rows, gate_proj, preferred_element_type=jnp.float32)
    pre_up = jnp.dot(in_rows, up_proj, preferred_element_type=jnp.float32)
    gate_sig = jax.nn.sigmoid(pre_gate)
    hidden = (pre_gate * gate_sig * pre_up).astype(jnp.bfloat16)
    by_width = (((1,), (1,)), ((), ()))
    by_rows = (((0,), (0,)), ((), ()))
    d_hidden = lax.dot_general(scaled, down_proj, by_width, preferred_element_type=jnp.float32)
    d_gate = (d_hidden * pre_up * gate_sig * (1.0 + pre_gate * (1.0 - gate_sig))).astype(
        jnp.bfloat16
    )
    d_up = (d_hidden * pre_gate * gate_sig).astype(jnp.bfloat16)
    grad_down = lax.dot_general(hidden, scaled, by_rows, preferred_element_type=jnp.float32)
    grad_gate = lax.dot_general(in_rows, d_gate, by_rows, preferred_element_type=jnp.float32)
    grad_up = lax.dot_general(in_rows, d_up, by_rows, preferred_element_type=jnp.float32)
    grad_gate, grad_up, grad_down = (
        lax.psum_scatter(
            grad_gate.astype(jnp.bfloat16), "dp", scatter_dimension=0, tiled=True
        ).astype(jnp.float32),
        lax.psum_scatter(
            grad_up.astype(jnp.bfloat16), "dp", scatter_dimension=0, tiled=True
        ).astype(jnp.float32),
        lax.psum_scatter(
            grad_down.astype(jnp.bfloat16), "dp", scatter_dimension=1, tiled=True
        ).astype(jnp.float32),
    )
    joined_grads = jnp.concatenate([d_gate, d_up], 1)
    joined_proj = jnp.concatenate([gate_proj, up_proj], 1)
    partial_value = lax.dot_general(
        joined_grads, joined_proj, by_width, preferred_element_type=jnp.float32
    ).astype(jnp.bfloat16)
    returned = lax.all_to_all(
        partial_value.reshape(expert_devs, capacity, model_dim),
        "expert",
        split_axis=0,
        concat_axis=0,
        tiled=True,
    )
    summed = jnp.sum(
        returned.reshape(EXPERTS, group_size, capacity, model_dim).astype(jnp.float32), axis=1
    )
    summed = summed.reshape(slot_total, model_dim)
    grad_input = jnp.take(summed, slot_of, axis=0).reshape(tok_dev, top_k, model_dim).sum(axis=1)
    return (grad_input.astype(jnp.bfloat16), grad_gate, grad_up, grad_down)


BY_WIDTH = (((1,), (1,)), ((), ()))
BY_ROWS = (((0,), (0,)), ((), ()))


def cut(width):
    pieces = ROWS // (MOST - ROWS)
    return pieces, width // pieces


def width_of(packed):
    pieces = ROWS // (MOST - ROWS)
    return packed.shape[2] * pieces // (pieces + 1)


def cost(flops, moved):
    return pl.CostEstimate(flops=flops, bytes_accessed=moved, transcendentals=0)


def params():
    return pltpu.CompilerParams(vmem_limit_bytes=VMEM_BYTES)


def anywhere(count):
    return [pl.BlockSpec(memory_space=pl.ANY)] * count


def dot(left, right, dims=(((1,), (0,)), ((), ()))):
    return lax.dot_general(left, right, dims, preferred_element_type=jnp.float32)


def ones(mask):
    return jnp.where(mask, 1.0, 0.0).astype(jnp.bfloat16)


def start(pairs, arrived):
    for at, (source, target) in enumerate(pairs):
        pltpu.make_async_copy(source, target, arrived.at[at]).start()


def wait(pairs, arrived, first=0):
    for at, (source, target) in enumerate(pairs):
        if at >= first:
            pltpu.make_async_copy(source, target, arrived.at[at]).wait()


def slot_masks(routes, blocks, width):
    tokens = routes.shape[1]
    pieces, _ = cut(width)
    experts = lax.broadcasted_iota(jnp.int32, (EXPERTS, tokens), 0)
    named = jnp.where(experts == routes, 1.0, 0.0)
    earlier = lax.broadcasted_iota(jnp.int32, (tokens, tokens), 0) < lax.broadcasted_iota(
        jnp.int32, (tokens, tokens), 1
    )
    before = dot(named.astype(jnp.bfloat16), ones(earlier))
    position = jnp.sum(before * named, axis=0, keepdims=True).astype(jnp.int32)
    slot = lax.broadcasted_iota(jnp.int32, (blocks * ROWS, tokens), 0)
    row = slot % ROWS
    mine = slot // ROWS == routes
    main = mine & (position == row)
    spill = mine & (position == ROWS + row // pieces)
    return main, spill, row % pieces


def pack(blocks, routes, values, gates=None):
    tokens, width = values.shape
    pieces, step = cut(width)
    sources = (routes,) + (() if gates is None else (gates,)) + (values,)
    count = len(sources)

    def kernel(*refs):
        out, held, arrived = refs[count], refs[count + 1 : 2 * count + 1], refs[-1]
        pairs = list(zip(refs[:count], held))
        start(pairs, arrived)
        wait(pairs[:-1], arrived)
        main, spill, piece = slot_masks(held[0][...], blocks, width)
        picks = [ones(spill & (piece == at)) for at in range(pieces)]
        if gates is not None:
            weights = held[1][...]
            main_scale = jnp.sum(jnp.where(main, weights, 0.0), axis=1, keepdims=True)
            spill_scale = jnp.sum(jnp.where(spill, weights, 0.0), axis=1, keepdims=True)
        wait(pairs, arrived, count - 1)
        rows = dot(ones(main), held[-1][...])
        extra = jnp.zeros((blocks * ROWS, step), jnp.float32)
        for at in range(pieces):
            extra += dot(picks[at], held[-1][:, at * step : (at + 1) * step])
        if gates is not None:
            rows, extra = rows * main_scale, extra * spill_scale
        rows = rows.astype(jnp.bfloat16)
        extra = extra.astype(jnp.bfloat16)
        for block in range(blocks):
            part = slice(block * ROWS, (block + 1) * ROWS)
            out[block, :, :width] = rows[part]
            out[block, :, width:] = extra[part]

    return pl.pallas_call(
        kernel,
        out_shape=jax.ShapeDtypeStruct((blocks, ROWS, width + step), jnp.bfloat16),
        in_specs=anywhere(count),
        out_specs=pl.BlockSpec(memory_space=pltpu.VMEM),
        scratch_shapes=[pltpu.VMEM(source.shape, source.dtype) for source in sources]
        + [pltpu.SemaphoreType.DMA((count,))],
        compiler_params=params(),
        cost_estimate=cost(4 * blocks * ROWS * tokens * width, 4 * tokens * width),
        name="pack",
    )(*sources)


def merge(routes, returned):
    blocks = returned.shape[0]
    tokens = routes.shape[1]
    width = width_of(returned)
    pieces, step = cut(width)

    def kernel(routes_ref, back_ref, out, named, held, arrived):
        pairs = [(routes_ref, named), (back_ref, held)]
        start(pairs, arrived)
        wait(pairs[:1], arrived)
        main, spill, piece = slot_masks(named[...], blocks, width)
        mains = ones(main)
        picks = [ones(spill & (piece == at)) for at in range(pieces)]
        wait(pairs, arrived, 1)
        rows = jnp.concatenate([held[at, :, :width] for at in range(blocks)], 0)
        extra = jnp.concatenate([held[at, :, width:] for at in range(blocks)], 0)
        picked = dot(mains, rows, BY_ROWS)
        for at in range(pieces):
            columns = slice(at * step, (at + 1) * step)
            out[:, columns] = (picked[:, columns] + dot(picks[at], extra, BY_ROWS)).astype(
                jnp.bfloat16
            )

    return pl.pallas_call(
        kernel,
        out_shape=jax.ShapeDtypeStruct((tokens, width), jnp.bfloat16),
        in_specs=anywhere(2),
        out_specs=pl.BlockSpec(memory_space=pltpu.VMEM),
        scratch_shapes=[
            pltpu.VMEM(routes.shape, routes.dtype),
            pltpu.VMEM(returned.shape, returned.dtype),
            pltpu.SemaphoreType.DMA((2,)),
        ],
        compiler_params=params(),
        cost_estimate=cost(4 * blocks * ROWS * tokens * width, 4 * tokens * width),
        name="merge",
    )(routes, returned)


def spill_picks(blocks, pieces, at):
    shape = (blocks * (MOST - ROWS), blocks * ROWS)
    slot = lax.broadcasted_iota(jnp.int32, shape, 0)
    row = lax.broadcasted_iota(jnp.int32, shape, 1)
    return ones(row == slot * pieces + at)


def unpack(main, tail, pieces, begin, first, out):
    blocks = main.shape[0]
    step = tail.shape[2]
    for at in range(blocks):
        out[first + at * ROWS : first + (at + 1) * ROWS, :] = main[at]
    extra = jnp.concatenate([tail[at] for at in range(blocks)], 0)
    spill = slice(first + blocks * ROWS, first + blocks * MOST)
    for at in range(out.shape[1] // step):
        out[spill, at * step : (at + 1) * step] = dot(
            spill_picks(blocks, pieces, begin + at), extra
        ).astype(jnp.bfloat16)


def column_tile(width, tile):
    return pl.BlockSpec((width, tile), lambda i: (0, i))


def row_tile(tile, width):
    return pl.BlockSpec((tile, width), lambda i: (i, 0))


def tile_of(index, tile):
    return pl.ds(pl.multiple_of(index * tile, tile), tile)


def weight_copy(source, target, arrived, index, axis, tile):
    here = tile_of(index, tile)
    view = source.at[:, here] if axis else source.at[here, :]
    return pltpu.make_async_copy(view, target.at[index], arrived.at[index])


def forward(tile, packed, gate_proj, up_proj):
    groups = len(packed)
    blocks = packed[0].shape[0]
    width, hid = gate_proj.shape
    pieces, _ = cut(width)
    slots = blocks * MOST
    total = groups * slots
    tiles = hid // tile

    def kernel(*refs):
        gate_ref, up_ref, pre_gate_ref, pre_up_ref = refs[groups : groups + 4]
        held, rows, gate, up, arrived, gate_in, up_in = refs[groups + 4 :]
        now = pl.program_id(0)

        def fetch(index):
            weight_copy(gate_ref, gate, gate_in, index, 1, tile).start()
            weight_copy(up_ref, up, up_in, index, 1, tile).start()

        @pl.when(now == 0)
        def _():
            pairs = [(refs[at], held.at[at]) for at in range(groups)]
            start(pairs, arrived)
            fetch(0)
            wait(pairs, arrived)
            for at in range(groups):
                unpack(
                    held.at[at, :, :, :width], held.at[at, :, :, width:], pieces, 0, at * slots, rows
                )

        @pl.when(now < tiles - 1)
        def _():
            fetch(now + 1)

        weight_copy(gate_ref, gate, gate_in, now, 1, tile).wait()
        pre_gate_ref[...] = dot(rows[...], gate[now])
        weight_copy(up_ref, up, up_in, now, 1, tile).wait()
        pre_up_ref[...] = dot(rows[...], up[now])

    return pl.pallas_call(
        kernel,
        grid=(tiles,),
        out_shape=[jax.ShapeDtypeStruct((total, hid), jnp.float32)] * 2,
        in_specs=anywhere(groups + 2),
        out_specs=[column_tile(total, tile)] * 2,
        scratch_shapes=[
            pltpu.VMEM((groups,) + packed[0].shape, jnp.bfloat16),
            pltpu.VMEM((total, width), jnp.bfloat16),
            pltpu.VMEM((tiles, width, tile), jnp.bfloat16),
            pltpu.VMEM((tiles, width, tile), jnp.bfloat16),
            pltpu.SemaphoreType.DMA((groups,)),
            pltpu.SemaphoreType.DMA((tiles,)),
            pltpu.SemaphoreType.DMA((tiles,)),
        ],
        compiler_params=params(),
        cost_estimate=cost(0, 4 * total * width),
        name="forward",
    )(*packed, gate_proj, up_proj)


def hidden_grads(pre_gate, pre_up, d_hidden):
    sig = jax.nn.sigmoid(pre_gate)
    silu = pre_gate * sig
    hidden = (silu * pre_up).astype(jnp.bfloat16)
    d_gate = (d_hidden * pre_up * sig * (1.0 + pre_gate * (1.0 - sig))).astype(jnp.bfloat16)
    d_up = (d_hidden * silu).astype(jnp.bfloat16)
    return hidden, d_gate, d_up


def back(tile, packed, pre_gate, pre_up, gate_proj, up_proj, down_proj):
    blocks = packed.shape[0]
    width, hid = gate_proj.shape
    slots = blocks * MOST
    pieces, step = cut(width)
    tiles = hid // tile
    chunk = 2 * step
    chunks = width // chunk

    def kernel(packed_ref, gate_ref, up_ref, down_ref, pre_gate_ref, pre_up_ref, *rest):
        out, hidden_ref, d_gate_ref, d_up_ref = rest[:4]
        held, scaled, both, tail, staged, gate, up, down = rest[4:12]
        arrived, gate_in, up_in, down_in, gone = rest[12:]
        now = pl.program_id(0)

        def fetch(index):
            @pl.when(index < tiles)
            def _():
                weight_copy(down_ref, down, down_in, index, 0, tile).start()

            @pl.when((index >= tiles) & (index < tiles + chunks))
            def _():
                weight_copy(gate_ref, gate, gate_in, index - tiles, 0, chunk).start()
                weight_copy(up_ref, up, up_in, index - tiles, 0, chunk).start()

        def leave(index):
            columns = tile_of(index, chunk)
            return pltpu.make_async_copy(
                staged.at[:, :, columns], out.at[:, :, columns], gone.at[index]
            )

        @pl.when(now == 0)
        def _():
            start([(packed_ref, held)], arrived)
            fetch(0)
            fetch(1)
            wait([(packed_ref, held)], arrived)
            unpack(held.at[:, :, :width], held.at[:, :, width:], pieces, 0, 0, scaled)
            tail[...] = jnp.zeros_like(tail)

        fetch(now + 2)

        @pl.when(now < tiles)
        def _():
            weight_copy(down_ref, down, down_in, now, 0, tile).wait()
            d_hidden = dot(scaled[...], down[now], BY_WIDTH)
            hidden, d_gate, d_up = hidden_grads(pre_gate_ref[...], pre_up_ref[...], d_hidden)
            hidden_ref[...] = hidden
            d_gate_ref[...] = d_gate
            d_up_ref[...] = d_up
            both[:, tile_of(now, tile)] = d_gate
            both[:, tile_of(tiles + now, tile)] = d_up

        @pl.when(now >= tiles)
        def _():
            at = now - tiles
            weight_copy(gate_ref, gate, gate_in, at, 0, chunk).wait()
            weight_copy(up_ref, up, up_in, at, 0, chunk).wait()
            done = dot(both[:, :hid], gate[at], BY_WIDTH) + dot(both[:, hid:], up[at], BY_WIDTH)
            done = done.astype(jnp.bfloat16)
            for block in range(blocks):
                staged[block, :, tile_of(at, chunk)] = done[block * ROWS : (block + 1) * ROWS]
            for piece in range(chunk // step):
                tail[...] += dot(
                    spill_picks(blocks, pieces, at * (chunk // step) + piece),
                    done[blocks * ROWS :, piece * step : (piece + 1) * step],
                    BY_ROWS,
                )
            leave(at).start()

        @pl.when(now == tiles + chunks - 1)
        def _():
            for block in range(blocks):
                part = tail[block * ROWS : (block + 1) * ROWS, :]
                staged[block, :, width:] = part.astype(jnp.bfloat16)
            last = pltpu.make_async_copy(
                staged.at[:, :, width:], out.at[:, :, width:], gone.at[chunks]
            )
            last.start()
            for at in range(chunks):
                leave(at).wait()
            last.wait()

    factor = jax.ShapeDtypeStruct((slots, hid), jnp.bfloat16)
    held_tile = pl.BlockSpec((slots, tile), lambda i: (0, jnp.minimum(i, tiles - 1)))
    sent, *own = pl.pallas_call(
        kernel,
        grid=(tiles + chunks,),
        out_shape=[jax.ShapeDtypeStruct(packed.shape, jnp.bfloat16)] + [factor] * 3,
        in_specs=anywhere(4) + [held_tile] * 2,
        out_specs=anywhere(1) + [held_tile] * 3,
        scratch_shapes=[
            pltpu.VMEM(packed.shape, jnp.bfloat16),
            pltpu.VMEM((slots, width), jnp.bfloat16),
            pltpu.VMEM((slots, 2 * hid), jnp.bfloat16),
            pltpu.VMEM((blocks * ROWS, step), jnp.float32),
            pltpu.VMEM(packed.shape, jnp.bfloat16),
            pltpu.VMEM((chunks, chunk, hid), jnp.bfloat16),
            pltpu.VMEM((chunks, chunk, hid), jnp.bfloat16),
            pltpu.VMEM((tiles, tile, width), jnp.bfloat16),
            pltpu.SemaphoreType.DMA((1,)),
            pltpu.SemaphoreType.DMA((chunks,)),
            pltpu.SemaphoreType.DMA((chunks,)),
            pltpu.SemaphoreType.DMA((tiles,)),
            pltpu.SemaphoreType.DMA((chunks + 1,)),
        ],
        compiler_params=params(),
        cost_estimate=cost(0, 4 * slots * width),
        name="back",
    )(packed, gate_proj, up_proj, down_proj, pre_gate, pre_up)
    return sent, own


def weight_grads(tile, part, rows, scaled, pre_near, pre_far, down_proj, own):
    groups = len(rows)
    blocks = rows[0].shape[0]
    hid, width = down_proj.shape
    pieces, step = cut(width)
    slots = blocks * MOST
    some = (groups - 1) * slots
    share = width // groups
    tiles = hid // tile

    def kernel(part_ref, *refs):
        refs = list(refs)
        x_refs = [refs.pop(0) for _ in range(groups)]
        dy_refs = [refs.pop(0) for _ in range(groups)]
        down_ref, near_gate, near_up, far_gate, far_up = [refs.pop(0) for _ in range(5)]
        own_hidden, own_gate, own_up = [refs.pop(0) for _ in range(3)]
        d_gate_ref, d_up_ref, d_down_ref = [refs.pop(0) for _ in range(3)]
        held, mains, tails, others, x_mine, dy_mine, down = [refs.pop(0) for _ in range(7)]
        held_in, mains_in, tails_in, down_in = refs
        now = pl.program_id(0)
        columns = pl.ds(pl.multiple_of(part_ref[0] * share, share), share)
        begin = part_ref[0] * (share // step)
        sources = x_refs + [dy_refs[0]]
        cuts = [(ref.at[:, :, columns], mains.at[at]) for at, ref in enumerate(sources)]
        ends = [(ref.at[:, :, width:], tails.at[at]) for at, ref in enumerate(sources)]

        def fetch(index):
            weight_copy(down_ref, down, down_in, index, 0, tile).start()

        @pl.when(now == 0)
        def _():
            whole = [(dy_refs[at], held.at[at - 1]) for at in range(1, groups)]
            start(whole, held_in)
            fetch(0)
            wait(whole, held_in)
            start(cuts, mains_in)
            start(ends, tails_in)
            for at in range(groups - 1):
                unpack(
                    held.at[at, :, :, :width],
                    held.at[at, :, :, width:],
                    pieces,
                    0,
                    at * slots,
                    others,
                )
            dy_mine[slots:, :] = others[:, columns]

        @pl.when(now < tiles - 1)
        def _():
            fetch(now + 1)

        weight_copy(down_ref, down, down_in, now, 0, tile).wait()
        d_hidden = dot(others[...], down[now], BY_WIDTH)
        pre_gate = jnp.concatenate([near_gate[...], far_gate[...]], 0)
        pre_up = jnp.concatenate([near_up[...], far_up[...]], 0)
        hidden, d_gate, d_up = hidden_grads(pre_gate, pre_up, d_hidden)
        hidden = jnp.concatenate([own_hidden[...], hidden], 0)
        d_gate = jnp.concatenate([own_gate[...], d_gate], 0)
        d_up = jnp.concatenate([own_up[...], d_up], 0)

        @pl.when(now == 0)
        def _():
            wait(cuts, mains_in)
            wait(ends, tails_in)
            for at in range(groups):
                unpack(mains.at[at], tails.at[at], pieces, begin, at * slots, x_mine)
            unpack(mains.at[groups], tails.at[groups], pieces, begin, 0, dy_mine)

        both = dot(x_mine[...], jnp.concatenate([d_gate, d_up], 1), BY_ROWS)
        d_gate_ref[...] = both[:, :tile]
        d_up_ref[...] = both[:, tile:]
        d_down_ref[...] = dot(hidden, dy_mine[...], BY_ROWS)

    behind = pl.BlockSpec((slots, tile), lambda i: (1, i))
    return pl.pallas_call(
        kernel,
        grid=(tiles,),
        out_shape=[
            jax.ShapeDtypeStruct((share, hid), jnp.float32),
            jax.ShapeDtypeStruct((share, hid), jnp.float32),
            jax.ShapeDtypeStruct((hid, share), jnp.float32),
        ],
        in_specs=[pl.BlockSpec(memory_space=pltpu.SMEM)]
        + anywhere(2 * groups + 1)
        + [behind] * 2
        + [column_tile(some - slots, tile)] * 2
        + [column_tile(slots, tile)] * 3,
        out_specs=[column_tile(share, tile), column_tile(share, tile), row_tile(tile, share)],
        scratch_shapes=[
            pltpu.VMEM((groups - 1,) + rows[0].shape, jnp.bfloat16),
            pltpu.VMEM((groups + 1, blocks, ROWS, share), jnp.bfloat16),
            pltpu.VMEM((groups + 1, blocks, ROWS, step), jnp.bfloat16),
            pltpu.VMEM((some, width), jnp.bfloat16),
            pltpu.VMEM((groups * slots, share), jnp.bfloat16),
            pltpu.VMEM((groups * slots, share), jnp.bfloat16),
            pltpu.VMEM((tiles, tile, width), jnp.bfloat16),
            pltpu.SemaphoreType.DMA((groups - 1,)),
            pltpu.SemaphoreType.DMA((groups + 1,)),
            pltpu.SemaphoreType.DMA((groups + 1,)),
            pltpu.SemaphoreType.DMA((tiles,)),
        ],
        compiler_params=params(),
        cost_estimate=cost(0, 4 * slots * width),
        name="weight_grads",
    )(part, *rows, *scaled, down_proj, *pre_near, *pre_far, *own)


def swap(value, axis, distance):
    size = lax.axis_size(axis)
    return lax.ppermute(value, axis, [(at, at ^ distance) for at in range(size)])


def exchange(blocks):
    return lax.all_to_all(blocks, "expert", split_axis=0, concat_axis=0, tiled=True)


def after(value, *earlier):
    return lax.optimization_barrier((value, *earlier))[0]


def gather_body(tokens, cotangent, routes, expert_gates, gate_proj, up_proj, down_proj):
    blocks = lax.axis_size("expert")
    tile = 256
    part = lax.axis_index("dp").astype(jnp.int32).reshape(1)
    routes = routes.reshape(1, -1)
    gates = expert_gates.reshape(1, -1)
    rows = exchange(pack(blocks, routes, tokens))
    far = swap(rows, "dp", 2)
    near = swap(rows, "dp", 1)
    scaled = exchange(after(pack(blocks, routes, cotangent, gates), rows))
    pre_near = forward(tile, [rows, near], gate_proj, up_proj)
    scaled, *pre_near = lax.optimization_barrier((scaled, *pre_near))
    dy_far = swap(scaled, "dp", 2)
    dy_near = swap(scaled, "dp", 1)
    sent, own = back(tile, scaled, *pre_near, gate_proj, up_proj, down_proj)
    returned = exchange(sent)
    last = swap(after(far, pre_near[0]), "dp", 1)
    pre_far = forward(tile, [after(far, sent), last], gate_proj, up_proj)
    dy_last = swap(after(dy_far, sent), "dp", 1)
    grads = weight_grads(
        tile,
        part,
        [rows, near, far, last],
        [scaled, dy_near, dy_far, dy_last],
        pre_near,
        pre_far,
        down_proj,
        own,
    )
    return (merge(routes, returned), *grads)


def body(tokens, cotangent, routes, expert_gates, gate_proj, up_proj, down_proj):
    groups, blocks = lax.axis_size("dp"), lax.axis_size("expert")
    width, hid = gate_proj.shape
    rows_sent = (groups - 1) * 2 * blocks * MOST * width
    grads_sent = 3 * width * hid * (groups - 1) // groups
    fits = blocks == EXPERTS and groups == 4 and hid % 256 == 0
    fits = fits and tokens.shape[0] == 128 and routes.shape[1] == 1 and width // groups % 128 == 0
    chosen = gather_body if fits and rows_sent < grads_sent else scatter_body
    return chosen(tokens, cotangent, routes, expert_gates, gate_proj, up_proj, down_proj)


def solution(mesh):
    in_specs = (
        P(("dp", "expert"), None),
        P(("dp", "expert"), None),
        P(("dp", "expert"), None),
        P(("dp", "expert"), None),
        P(None, "expert"),
        P(None, "expert"),
        P("expert", None),
    )
    out_specs = (P(("dp", "expert"), None), P("dp", "expert"), P("dp", "expert"), P("expert", "dp"))
    return jax.shard_map(body, mesh=mesh, in_specs=in_specs, out_specs=out_specs, check_vma=False)
```

```python
import jax
import jax.numpy as jnp
from jax import lax
from jax.experimental import pallas as pl
from jax.experimental.pallas import tpu as pltpu
from jax.sharding import PartitionSpec as P

EXPERTS = 8
MOST = 18
ROWS = 16
VMEM_BYTES = (63 * 1024 + 768) * 1024


def build_slots(routes, capacity):
    flat_routes = routes.reshape(-1)
    one_hot = (flat_routes[:, None] == jnp.arange(EXPERTS, dtype=jnp.int32)[None, :]).astype(
        jnp.int32
    )
    before = jnp.cumsum(one_hot, axis=0) - one_hot
    position = jnp.sum(before * one_hot, axis=1)
    return flat_routes * capacity + position


def scatter_body(tokens, cotangent, routes, expert_gates, gate_proj, up_proj, down_proj):
    tok_dev, model_dim = tokens.shape
    top_k = routes.shape[1]
    expert_devs = lax.axis_size("expert")
    group_size = expert_devs // EXPERTS
    capacity = MOST
    slot_total = EXPERTS * capacity
    slot_of = build_slots(routes, capacity)
    owners = jnp.arange(tok_dev * top_k, dtype=jnp.int32) // top_k
    slot_table = jnp.full((slot_total,), tok_dev, jnp.int32).at[slot_of].set(owners)
    slot_gate = jnp.zeros((slot_total,), jnp.float32).at[slot_of].set(expert_gates.reshape(-1))
    x_slots = jnp.take(tokens, slot_table, axis=0, mode="fill", fill_value=0)
    dy_slots = (
        jnp.take(cotangent, slot_table, axis=0, mode="fill", fill_value=0).astype(jnp.float32)
        * slot_gate[:, None]
    ).astype(jnp.bfloat16)

    def copies(values):
        spread = values.reshape(EXPERTS, 1, capacity, model_dim)
        return jnp.broadcast_to(spread, (EXPERTS, group_size, capacity, model_dim)).reshape(
            expert_devs, capacity, model_dim
        )

    x_recv, dy_recv = (
        lax.all_to_all(copies(x_slots), "expert", split_axis=0, concat_axis=0, tiled=True),
        lax.all_to_all(copies(dy_slots), "expert", split_axis=0, concat_axis=0, tiled=True),
    )
    in_rows = x_recv.reshape(expert_devs * capacity, model_dim)
    scaled = dy_recv.reshape(expert_devs * capacity, model_dim)
    pre_gate = jnp.dot(in_rows, gate_proj, preferred_element_type=jnp.float32)
    pre_up = jnp.dot(in_rows, up_proj, preferred_element_type=jnp.float32)
    gate_sig = jax.nn.sigmoid(pre_gate)
    hidden = (pre_gate * gate_sig * pre_up).astype(jnp.bfloat16)
    by_width = (((1,), (1,)), ((), ()))
    by_rows = (((0,), (0,)), ((), ()))
    d_hidden = lax.dot_general(scaled, down_proj, by_width, preferred_element_type=jnp.float32)
    d_gate = (d_hidden * pre_up * gate_sig * (1.0 + pre_gate * (1.0 - gate_sig))).astype(
        jnp.bfloat16
    )
    d_up = (d_hidden * pre_gate * gate_sig).astype(jnp.bfloat16)
    grad_down = lax.dot_general(hidden, scaled, by_rows, preferred_element_type=jnp.float32)
    grad_gate = lax.dot_general(in_rows, d_gate, by_rows, preferred_element_type=jnp.float32)
    grad_up = lax.dot_general(in_rows, d_up, by_rows, preferred_element_type=jnp.float32)
    grad_gate, grad_up, grad_down = (
        lax.psum_scatter(
            grad_gate.astype(jnp.bfloat16), "dp", scatter_dimension=0, tiled=True
        ).astype(jnp.float32),
        lax.psum_scatter(
            grad_up.astype(jnp.bfloat16), "dp", scatter_dimension=0, tiled=True
        ).astype(jnp.float32),
        lax.psum_scatter(
            grad_down.astype(jnp.bfloat16), "dp", scatter_dimension=1, tiled=True
        ).astype(jnp.float32),
    )
    joined_grads = jnp.concatenate([d_gate, d_up], 1)
    joined_proj = jnp.concatenate([gate_proj, up_proj], 1)
    partial_value = lax.dot_general(
        joined_grads, joined_proj, by_width, preferred_element_type=jnp.float32
    ).astype(jnp.bfloat16)
    returned = lax.all_to_all(
        partial_value.reshape(expert_devs, capacity, model_dim),
        "expert",
        split_axis=0,
        concat_axis=0,
        tiled=True,
    )
    summed = jnp.sum(
        returned.reshape(EXPERTS, group_size, capacity, model_dim).astype(jnp.float32), axis=1
    )
    summed = summed.reshape(slot_total, model_dim)
    grad_input = jnp.take(summed, slot_of, axis=0).reshape(tok_dev, top_k, model_dim).sum(axis=1)
    return (grad_input.astype(jnp.bfloat16), grad_gate, grad_up, grad_down)


BY_WIDTH = (((1,), (1,)), ((), ()))
BY_ROWS = (((0,), (0,)), ((), ()))


def cut(width):
    pieces = ROWS // (MOST - ROWS)
    return pieces, width // pieces


def width_of(packed):
    pieces = ROWS // (MOST - ROWS)
    return packed.shape[2] * pieces // (pieces + 1)


def cost(flops, moved):
    return pl.CostEstimate(flops=flops, bytes_accessed=moved, transcendentals=0)


def params():
    return pltpu.CompilerParams(vmem_limit_bytes=VMEM_BYTES)


def anywhere(count):
    return [pl.BlockSpec(memory_space=pl.ANY)] * count


def dot(left, right, dims=(((1,), (0,)), ((), ()))):
    return lax.dot_general(left, right, dims, preferred_element_type=jnp.float32)


def ones(mask):
    return jnp.where(mask, 1.0, 0.0).astype(jnp.bfloat16)


def start(pairs, arrived, first=0):
    for at, (source, target) in enumerate(pairs):
        if at >= first:
            pltpu.make_async_copy(source, target, arrived.at[at]).start()


def wait(pairs, arrived, first=0):
    for at, (source, target) in enumerate(pairs):
        if at >= first:
            pltpu.make_async_copy(source, target, arrived.at[at]).wait()


def slot_masks(routes, blocks, width):
    tokens = routes.shape[1]
    pieces, _ = cut(width)
    experts = lax.broadcasted_iota(jnp.int32, (EXPERTS, tokens), 0)
    named = jnp.where(experts == routes, 1.0, 0.0)
    earlier = lax.broadcasted_iota(jnp.int32, (tokens, tokens), 0) < lax.broadcasted_iota(
        jnp.int32, (tokens, tokens), 1
    )
    before = dot(named.astype(jnp.bfloat16), ones(earlier))
    position = jnp.sum(before * named, axis=0, keepdims=True).astype(jnp.int32)
    slot = lax.broadcasted_iota(jnp.int32, (blocks * ROWS, tokens), 0)
    row = slot % ROWS
    mine = slot // ROWS == routes
    main = mine & (position == row)
    spill = mine & (position == ROWS + row // pieces)
    return main, spill, row % pieces


def pack(blocks, routes, values, gates=None):
    tokens, width = values.shape
    pieces, step = cut(width)
    sources = (routes,) + (() if gates is None else (gates,)) + (values,)
    count = len(sources)

    def kernel(*refs):
        out, held, arrived = refs[count], refs[count + 1 : 2 * count + 1], refs[-1]
        pairs = list(zip(refs[:count], held))
        start(pairs, arrived)
        wait(pairs[:-1], arrived)
        main, spill, piece = slot_masks(held[0][...], blocks, width)
        picks = [ones(spill & (piece == at)) for at in range(pieces)]
        if gates is not None:
            weights = held[1][...]
            main_scale = jnp.sum(jnp.where(main, weights, 0.0), axis=1, keepdims=True)
            spill_scale = jnp.sum(jnp.where(spill, weights, 0.0), axis=1, keepdims=True)
        wait(pairs, arrived, count - 1)
        rows = dot(ones(main), held[-1][...])
        extra = jnp.zeros((blocks * ROWS, step), jnp.float32)
        for at in range(pieces):
            extra += dot(picks[at], held[-1][:, at * step : (at + 1) * step])
        if gates is not None:
            rows, extra = rows * main_scale, extra * spill_scale
        rows = rows.astype(jnp.bfloat16)
        extra = extra.astype(jnp.bfloat16)
        for block in range(blocks):
            part = slice(block * ROWS, (block + 1) * ROWS)
            out[block, :, :width] = rows[part]
            out[block, :, width:] = extra[part]

    return pl.pallas_call(
        kernel,
        out_shape=jax.ShapeDtypeStruct((blocks, ROWS, width + step), jnp.bfloat16),
        in_specs=anywhere(count),
        out_specs=pl.BlockSpec(memory_space=pltpu.VMEM),
        scratch_shapes=[pltpu.VMEM(source.shape, source.dtype) for source in sources]
        + [pltpu.SemaphoreType.DMA((count,))],
        compiler_params=params(),
        cost_estimate=cost(4 * blocks * ROWS * tokens * width, 4 * tokens * width),
        name="pack",
    )(*sources)


def merge(routes, returned):
    blocks = returned.shape[0]
    tokens = routes.shape[1]
    width = width_of(returned)
    pieces, step = cut(width)

    def kernel(routes_ref, back_ref, out, named, held, arrived):
        pairs = [(routes_ref, named), (back_ref, held)]
        start(pairs, arrived)
        wait(pairs[:1], arrived)
        main, spill, piece = slot_masks(named[...], blocks, width)
        mains = ones(main)
        picks = [ones(spill & (piece == at)) for at in range(pieces)]
        wait(pairs, arrived, 1)
        rows = jnp.concatenate([held[at, :, :width] for at in range(blocks)], 0)
        extra = jnp.concatenate([held[at, :, width:] for at in range(blocks)], 0)
        picked = dot(mains, rows, BY_ROWS)
        for at in range(pieces):
            columns = slice(at * step, (at + 1) * step)
            out[:, columns] = (picked[:, columns] + dot(picks[at], extra, BY_ROWS)).astype(
                jnp.bfloat16
            )

    return pl.pallas_call(
        kernel,
        out_shape=jax.ShapeDtypeStruct((tokens, width), jnp.bfloat16),
        in_specs=anywhere(2),
        out_specs=pl.BlockSpec(memory_space=pltpu.VMEM),
        scratch_shapes=[
            pltpu.VMEM(routes.shape, routes.dtype),
            pltpu.VMEM(returned.shape, returned.dtype),
            pltpu.SemaphoreType.DMA((2,)),
        ],
        compiler_params=params(),
        cost_estimate=cost(4 * blocks * ROWS * tokens * width, 4 * tokens * width),
        name="merge",
    )(routes, returned)


def spill_picks(blocks, pieces, at):
    shape = (blocks * (MOST - ROWS), blocks * ROWS)
    slot = lax.broadcasted_iota(jnp.int32, shape, 0)
    row = lax.broadcasted_iota(jnp.int32, shape, 1)
    return ones(row == slot * pieces + at)


def unpack(main, tail, pieces, begin, first, out):
    blocks = main.shape[0]
    step = tail.shape[2]
    for at in range(blocks):
        out[first + at * ROWS : first + (at + 1) * ROWS, :] = main[at]
    extra = jnp.concatenate([tail[at] for at in range(blocks)], 0)
    spill = slice(first + blocks * ROWS, first + blocks * MOST)
    for at in range(out.shape[1] // step):
        out[spill, at * step : (at + 1) * step] = dot(
            spill_picks(blocks, pieces, begin + at), extra
        ).astype(jnp.bfloat16)


def column_tile(width, tile):
    return pl.BlockSpec((width, tile), lambda i: (0, i))


def row_tile(tile, width):
    return pl.BlockSpec((tile, width), lambda i: (i, 0))


def tile_of(index, tile):
    return pl.ds(pl.multiple_of(index * tile, tile), tile)


def weight_copy(source, target, arrived, index, axis, tile):
    here = tile_of(index, tile)
    view = source.at[:, here] if axis else source.at[here, :]
    return pltpu.make_async_copy(view, target.at[index], arrived.at[index])


def forward(tile, packed, gate_proj, up_proj):
    groups = len(packed)
    blocks = packed[0].shape[0]
    width, hid = gate_proj.shape
    pieces, _ = cut(width)
    slots = blocks * MOST
    total = groups * slots
    tiles = hid // tile

    def kernel(*refs):
        gate_ref, up_ref, pre_gate_ref, pre_up_ref = refs[groups : groups + 4]
        held, rows, gate, up, arrived, gate_in, up_in = refs[groups + 4 :]
        now = pl.program_id(0)

        def fetch(index):
            weight_copy(gate_ref, gate, gate_in, index, 1, tile).start()
            weight_copy(up_ref, up, up_in, index, 1, tile).start()

        @pl.when(now == 0)
        def _():
            pairs = [(refs[at], held.at[at]) for at in range(groups)]
            start(pairs, arrived)
            fetch(0)
            wait(pairs, arrived)
            for at in range(groups):
                unpack(
                    held.at[at, :, :, :width], held.at[at, :, :, width:], pieces, 0, at * slots, rows
                )

        @pl.when(now < tiles - 1)
        def _():
            fetch(now + 1)

        weight_copy(gate_ref, gate, gate_in, now, 1, tile).wait()
        pre_gate_ref[...] = dot(rows[...], gate[now])
        weight_copy(up_ref, up, up_in, now, 1, tile).wait()
        pre_up_ref[...] = dot(rows[...], up[now])

    return pl.pallas_call(
        kernel,
        grid=(tiles,),
        out_shape=[jax.ShapeDtypeStruct((total, hid), jnp.float32)] * 2,
        in_specs=anywhere(groups + 2),
        out_specs=[column_tile(total, tile)] * 2,
        scratch_shapes=[
            pltpu.VMEM((groups,) + packed[0].shape, jnp.bfloat16),
            pltpu.VMEM((total, width), jnp.bfloat16),
            pltpu.VMEM((tiles, width, tile), jnp.bfloat16),
            pltpu.VMEM((tiles, width, tile), jnp.bfloat16),
            pltpu.SemaphoreType.DMA((groups,)),
            pltpu.SemaphoreType.DMA((tiles,)),
            pltpu.SemaphoreType.DMA((tiles,)),
        ],
        compiler_params=params(),
        cost_estimate=cost(0, 4 * total * width),
        name="forward",
    )(*packed, gate_proj, up_proj)


def hidden_grads(pre_gate, pre_up, d_hidden):
    sig = jax.nn.sigmoid(pre_gate)
    silu = pre_gate * sig
    hidden = (silu * pre_up).astype(jnp.bfloat16)
    d_gate = (d_hidden * pre_up * sig * (1.0 + pre_gate * (1.0 - sig))).astype(jnp.bfloat16)
    d_up = (d_hidden * silu).astype(jnp.bfloat16)
    return hidden, d_gate, d_up


def back(tile, packed, pre_gate, pre_up, gate_proj, up_proj, down_proj):
    blocks = packed.shape[0]
    width, hid = gate_proj.shape
    slots = blocks * MOST
    pieces, step = cut(width)
    tiles = hid // tile
    chunk = 2 * step
    chunks = width // chunk

    def kernel(packed_ref, gate_ref, up_ref, down_ref, pre_gate_ref, pre_up_ref, *rest):
        out, hidden_ref, both_ref, held, scaled, pre_gate, pre_up, hidden, both = rest[:9]
        tail, staged, gate, up, down, arrived, gate_in, up_in, down_in, gone = rest[9:]
        now = pl.program_id(0)
        first = [(packed_ref, held), (pre_gate_ref, pre_gate), (pre_up_ref, pre_up)]

        def fetch(index):
            @pl.when(index < tiles)
            def _():
                weight_copy(down_ref, down, down_in, index, 0, tile).start()

            @pl.when((index >= tiles) & (index < tiles + chunks))
            def _():
                weight_copy(gate_ref, gate, gate_in, index - tiles, 0, chunk).start()
                weight_copy(up_ref, up, up_in, index - tiles, 0, chunk).start()

        def leave(index):
            columns = tile_of(index, chunk)
            return pltpu.make_async_copy(
                staged.at[:, :, columns], out.at[:, :, columns], gone.at[index]
            )

        def leave_factors():
            return [
                pltpu.make_async_copy(hidden, hidden_ref, gone.at[chunks + 1]),
                pltpu.make_async_copy(both, both_ref, gone.at[chunks + 2]),
            ]

        @pl.when(now == 0)
        def _():
            start(first[:1], arrived)
            fetch(0)
            start(first, arrived, 1)
            wait(first[:1], arrived)
            fetch(1)
            unpack(held.at[:, :, :width], held.at[:, :, width:], pieces, 0, 0, scaled)
            tail[...] = jnp.zeros_like(tail)

        fetch(now + 2)

        @pl.when(now < tiles)
        def _():
            columns = tile_of(now, tile)
            weight_copy(down_ref, down, down_in, now, 0, tile).wait()
            d_hidden = dot(scaled[...], down[now], BY_WIDTH)

            @pl.when(now == 0)
            def _():
                wait(first, arrived, 1)

            made, d_gate, d_up = hidden_grads(pre_gate[:, columns], pre_up[:, columns], d_hidden)
            hidden[:, columns] = made
            both[:, columns] = d_gate
            both[:, tile_of(tiles + now, tile)] = d_up

        @pl.when(now == tiles)
        def _():
            for copy in leave_factors():
                copy.start()

        @pl.when(now >= tiles)
        def _():
            at = now - tiles
            weight_copy(gate_ref, gate, gate_in, at, 0, chunk).wait()
            done = dot(both[:, :hid], gate[at], BY_WIDTH)
            weight_copy(up_ref, up, up_in, at, 0, chunk).wait()
            done = (done + dot(both[:, hid:], up[at], BY_WIDTH)).astype(jnp.bfloat16)
            for block in range(blocks):
                staged[block, :, tile_of(at, chunk)] = done[block * ROWS : (block + 1) * ROWS]
            leave(at).start()
            for piece in range(chunk // step):
                tail[...] += dot(
                    spill_picks(blocks, pieces, at * (chunk // step) + piece),
                    done[blocks * ROWS :, piece * step : (piece + 1) * step],
                    BY_ROWS,
                )

        @pl.when(now == tiles + chunks - 1)
        def _():
            for block in range(blocks):
                part = tail[block * ROWS : (block + 1) * ROWS, :]
                staged[block, :, width:] = part.astype(jnp.bfloat16)
            last = pltpu.make_async_copy(
                staged.at[:, :, width:], out.at[:, :, width:], gone.at[chunks]
            )
            last.start()
            for at in range(chunks):
                leave(at).wait()
            for copy in leave_factors():
                copy.wait()
            last.wait()

    return pl.pallas_call(
        kernel,
        grid=(tiles + chunks,),
        out_shape=[
            jax.ShapeDtypeStruct(packed.shape, jnp.bfloat16),
            jax.ShapeDtypeStruct((slots, hid), jnp.bfloat16),
            jax.ShapeDtypeStruct((slots, 2 * hid), jnp.bfloat16),
        ],
        in_specs=anywhere(6),
        out_specs=anywhere(3),
        scratch_shapes=[
            pltpu.VMEM(packed.shape, jnp.bfloat16),
            pltpu.VMEM((slots, width), jnp.bfloat16),
            pltpu.VMEM((slots, hid), jnp.float32),
            pltpu.VMEM((slots, hid), jnp.float32),
            pltpu.VMEM((slots, hid), jnp.bfloat16),
            pltpu.VMEM((slots, 2 * hid), jnp.bfloat16),
            pltpu.VMEM((blocks * ROWS, step), jnp.float32),
            pltpu.VMEM(packed.shape, jnp.bfloat16),
            pltpu.VMEM((chunks, chunk, hid), jnp.bfloat16),
            pltpu.VMEM((chunks, chunk, hid), jnp.bfloat16),
            pltpu.VMEM((tiles, tile, width), jnp.bfloat16),
            pltpu.SemaphoreType.DMA((3,)),
            pltpu.SemaphoreType.DMA((chunks,)),
            pltpu.SemaphoreType.DMA((chunks,)),
            pltpu.SemaphoreType.DMA((tiles,)),
            pltpu.SemaphoreType.DMA((chunks + 3,)),
        ],
        compiler_params=params(),
        cost_estimate=cost(0, 4 * slots * width),
        name="back",
    )(packed, gate_proj, up_proj, down_proj, pre_gate, pre_up)


def weight_grads(tile, part, rows, scaled, hidden, both, gate_proj, up_proj, down_proj):
    groups = len(rows)
    blocks = rows[0].shape[0]
    hid, width = down_proj.shape
    pieces, step = cut(width)
    slots = blocks * MOST
    some = (groups - 1) * slots
    share = width // groups
    tiles = hid // tile

    def kernel(part_ref, *refs):
        refs = list(refs)
        x_refs = [refs.pop(0) for _ in range(groups)]
        dy_refs = [refs.pop(0) for _ in range(groups)]
        hidden_ref, both_ref, gate_ref, up_ref, down_ref = [refs.pop(0) for _ in range(5)]
        d_gate_ref, d_up_ref, d_down_ref = [refs.pop(0) for _ in range(3)]
        x_held, dy_held, mains, tails, x_all, dy_all = [refs.pop(0) for _ in range(6)]
        x_mine, dy_mine, own_hidden, own_both = [refs.pop(0) for _ in range(4)]
        gate, up, down, x_in, dy_in, own_in, gate_in, up_in, down_in = refs
        now = pl.program_id(0)
        columns = pl.ds(pl.multiple_of(part_ref[0] * share, share), share)
        begin = part_ref[0] * (share // step)
        x_pairs = [(x_refs[at], x_held.at[at - 1]) for at in range(1, groups)]
        dy_pairs = [(dy_refs[at], dy_held.at[at - 1]) for at in range(1, groups)]
        own_pairs = [(hidden_ref, own_hidden), (both_ref, own_both)]
        for at, ref in enumerate([x_refs[0], dy_refs[0]]):
            own_pairs.append((ref.at[:, :, columns], mains.at[at]))
            own_pairs.append((ref.at[:, :, width:], tails.at[at]))

        def arrange(held, rows_out, target):
            for at in range(groups - 1):
                unpack(
                    held.at[at, :, :, :width],
                    held.at[at, :, :, width:],
                    pieces,
                    0,
                    at * slots,
                    rows_out,
                )
            target[slots:, :] = rows_out[:, columns]

        def fetch_x(index):
            weight_copy(gate_ref, gate, gate_in, index, 1, tile).start()
            weight_copy(up_ref, up, up_in, index, 1, tile).start()

        def fetch_dy(index):
            weight_copy(down_ref, down, down_in, index, 0, tile).start()

        @pl.when(now == 0)
        def _():
            start(x_pairs, x_in)
            fetch_x(0)
            wait(x_pairs, x_in)
            start(dy_pairs, dy_in)
            fetch_dy(0)
            arrange(x_held, x_all, x_mine)

        weight_copy(gate_ref, gate, gate_in, now, 1, tile).wait()
        pre_gate = dot(x_all[...], gate[now])
        weight_copy(up_ref, up, up_in, now, 1, tile).wait()
        pre_up = dot(x_all[...], up[now])

        @pl.when(now == 0)
        def _():
            wait(dy_pairs, dy_in)
            start(own_pairs, own_in)
            arrange(dy_held, dy_all, dy_mine)

        @pl.when(now < tiles - 1)
        def _():
            fetch_x(now + 1)
            fetch_dy(now + 1)

        weight_copy(down_ref, down, down_in, now, 0, tile).wait()
        d_hidden = dot(dy_all[...], down[now], BY_WIDTH)
        made, d_gate, d_up = hidden_grads(pre_gate, pre_up, d_hidden)

        @pl.when(now == 0)
        def _():
            wait(own_pairs, own_in)
            unpack(mains.at[0], tails.at[0], pieces, begin, 0, x_mine)
            unpack(mains.at[1], tails.at[1], pieces, begin, 0, dy_mine)

        made = jnp.concatenate([own_hidden[:, tile_of(now, tile)], made], 0)
        d_gate = jnp.concatenate([own_both[:, tile_of(now, tile)], d_gate], 0)
        d_up = jnp.concatenate([own_both[:, tile_of(tiles + now, tile)], d_up], 0)
        sums = dot(x_mine[...], jnp.concatenate([d_gate, d_up], 1), BY_ROWS)
        d_gate_ref[...] = sums[:, :tile]
        d_up_ref[...] = sums[:, tile:]
        d_down_ref[...] = dot(made, dy_mine[...], BY_ROWS)

    return pl.pallas_call(
        kernel,
        grid=(tiles,),
        out_shape=[
            jax.ShapeDtypeStruct((share, hid), jnp.float32),
            jax.ShapeDtypeStruct((share, hid), jnp.float32),
            jax.ShapeDtypeStruct((hid, share), jnp.float32),
        ],
        in_specs=[pl.BlockSpec(memory_space=pltpu.SMEM)] + anywhere(2 * groups + 5),
        out_specs=[column_tile(share, tile), column_tile(share, tile), row_tile(tile, share)],
        scratch_shapes=[
            pltpu.VMEM((groups - 1,) + rows[0].shape, jnp.bfloat16),
            pltpu.VMEM((groups - 1,) + rows[0].shape, jnp.bfloat16),
            pltpu.VMEM((2, blocks, ROWS, share), jnp.bfloat16),
            pltpu.VMEM((2, blocks, ROWS, step), jnp.bfloat16),
            pltpu.VMEM((some, width), jnp.bfloat16),
            pltpu.VMEM((some, width), jnp.bfloat16),
            pltpu.VMEM((groups * slots, share), jnp.bfloat16),
            pltpu.VMEM((groups * slots, share), jnp.bfloat16),
            pltpu.VMEM((slots, hid), jnp.bfloat16),
            pltpu.VMEM((slots, 2 * hid), jnp.bfloat16),
            pltpu.VMEM((tiles, width, tile), jnp.bfloat16),
            pltpu.VMEM((tiles, width, tile), jnp.bfloat16),
            pltpu.VMEM((tiles, tile, width), jnp.bfloat16),
            pltpu.SemaphoreType.DMA((groups - 1,)),
            pltpu.SemaphoreType.DMA((groups - 1,)),
            pltpu.SemaphoreType.DMA((6,)),
            pltpu.SemaphoreType.DMA((tiles,)),
            pltpu.SemaphoreType.DMA((tiles,)),
            pltpu.SemaphoreType.DMA((tiles,)),
        ],
        compiler_params=params(),
        cost_estimate=cost(0, 4 * slots * width),
        name="weight_grads",
    )(part, *rows, *scaled, hidden, both, gate_proj, up_proj, down_proj)


def swap(value, axis, distance):
    size = lax.axis_size(axis)
    return lax.ppermute(value, axis, [(at, at ^ distance) for at in range(size)])


def exchange(blocks):
    return lax.all_to_all(blocks, "expert", split_axis=0, concat_axis=0, tiled=True)


def after(value, *earlier):
    return lax.optimization_barrier((value, *earlier))[0]


def gather_body(tokens, cotangent, routes, expert_gates, gate_proj, up_proj, down_proj):
    blocks = lax.axis_size("expert")
    tile = 256
    part = lax.axis_index("dp").astype(jnp.int32).reshape(1)
    routes = routes.reshape(1, -1)
    gates = expert_gates.reshape(1, -1)
    weights = (gate_proj, up_proj, down_proj)
    rows = exchange(pack(blocks, routes, tokens))
    far = swap(rows, "dp", 2)
    near = swap(rows, "dp", 1)
    scaled = exchange(after(pack(blocks, routes, cotangent, gates), rows))
    pre = forward(tile, [rows], gate_proj, up_proj)
    scaled, *pre = lax.optimization_barrier((scaled, *pre))
    dy_far = swap(scaled, "dp", 2)
    dy_near = swap(scaled, "dp", 1)
    sent, hidden, both = back(tile, scaled, *pre, *weights)
    returned = exchange(sent)
    last = swap(after(far, pre[0]), "dp", 1)
    dy_last = swap(after(dy_far, sent), "dp", 1)
    grads = weight_grads(
        tile,
        part,
        [rows, near, far, last],
        [scaled, dy_near, dy_far, dy_last],
        hidden,
        both,
        *weights,
    )
    return (merge(routes, after(returned, *grads)), *grads)


def body(tokens, cotangent, routes, expert_gates, gate_proj, up_proj, down_proj):
    groups, blocks = lax.axis_size("dp"), lax.axis_size("expert")
    width, hid = gate_proj.shape
    rows_sent = (groups - 1) * 2 * blocks * MOST * width
    grads_sent = 3 * width * hid * (groups - 1) // groups
    fits = blocks == EXPERTS and groups == 4 and hid % 256 == 0
    fits = fits and tokens.shape[0] == 128 and routes.shape[1] == 1 and width // groups % 128 == 0
    chosen = gather_body if fits and rows_sent < grads_sent else scatter_body
    return chosen(tokens, cotangent, routes, expert_gates, gate_proj, up_proj, down_proj)


def solution(mesh):
    in_specs = (
        P(("dp", "expert"), None),
        P(("dp", "expert"), None),
        P(("dp", "expert"), None),
        P(("dp", "expert"), None),
        P(None, "expert"),
        P(None, "expert"),
        P("expert", None),
    )
    out_specs = (P(("dp", "expert"), None), P("dp", "expert"), P("dp", "expert"), P("expert", "dp"))
    return jax.shard_map(body, mesh=mesh, in_specs=in_specs, out_specs=out_specs, check_vma=False)
```

```python
import jax
import jax.numpy as jnp
from jax import lax
from jax.experimental import pallas as pl
from jax.experimental.pallas import tpu as pltpu
from jax.sharding import PartitionSpec as P

EXPERTS = 8
MOST = 18
ROWS = 16
VMEM_BYTES = (63 * 1024 + 768) * 1024


def build_slots(routes, capacity):
    flat_routes = routes.reshape(-1)
    one_hot = (flat_routes[:, None] == jnp.arange(EXPERTS, dtype=jnp.int32)[None, :]).astype(
        jnp.int32
    )
    before = jnp.cumsum(one_hot, axis=0) - one_hot
    position = jnp.sum(before * one_hot, axis=1)
    return flat_routes * capacity + position


def scatter_body(tokens, cotangent, routes, expert_gates, gate_proj, up_proj, down_proj):
    tok_dev, model_dim = tokens.shape
    top_k = routes.shape[1]
    expert_devs = lax.axis_size("expert")
    group_size = expert_devs // EXPERTS
    capacity = MOST
    slot_total = EXPERTS * capacity
    slot_of = build_slots(routes, capacity)
    owners = jnp.arange(tok_dev * top_k, dtype=jnp.int32) // top_k
    slot_table = jnp.full((slot_total,), tok_dev, jnp.int32).at[slot_of].set(owners)
    slot_gate = jnp.zeros((slot_total,), jnp.float32).at[slot_of].set(expert_gates.reshape(-1))
    x_slots = jnp.take(tokens, slot_table, axis=0, mode="fill", fill_value=0)
    dy_slots = (
        jnp.take(cotangent, slot_table, axis=0, mode="fill", fill_value=0).astype(jnp.float32)
        * slot_gate[:, None]
    ).astype(jnp.bfloat16)

    def copies(values):
        spread = values.reshape(EXPERTS, 1, capacity, model_dim)
        return jnp.broadcast_to(spread, (EXPERTS, group_size, capacity, model_dim)).reshape(
            expert_devs, capacity, model_dim
        )

    x_recv, dy_recv = (
        lax.all_to_all(copies(x_slots), "expert", split_axis=0, concat_axis=0, tiled=True),
        lax.all_to_all(copies(dy_slots), "expert", split_axis=0, concat_axis=0, tiled=True),
    )
    in_rows = x_recv.reshape(expert_devs * capacity, model_dim)
    scaled = dy_recv.reshape(expert_devs * capacity, model_dim)
    pre_gate = jnp.dot(in_rows, gate_proj, preferred_element_type=jnp.float32)
    pre_up = jnp.dot(in_rows, up_proj, preferred_element_type=jnp.float32)
    gate_sig = jax.nn.sigmoid(pre_gate)
    hidden = (pre_gate * gate_sig * pre_up).astype(jnp.bfloat16)
    by_width = (((1,), (1,)), ((), ()))
    by_rows = (((0,), (0,)), ((), ()))
    d_hidden = lax.dot_general(scaled, down_proj, by_width, preferred_element_type=jnp.float32)
    d_gate = (d_hidden * pre_up * gate_sig * (1.0 + pre_gate * (1.0 - gate_sig))).astype(
        jnp.bfloat16
    )
    d_up = (d_hidden * pre_gate * gate_sig).astype(jnp.bfloat16)
    grad_down = lax.dot_general(hidden, scaled, by_rows, preferred_element_type=jnp.float32)
    grad_gate = lax.dot_general(in_rows, d_gate, by_rows, preferred_element_type=jnp.float32)
    grad_up = lax.dot_general(in_rows, d_up, by_rows, preferred_element_type=jnp.float32)
    grad_gate, grad_up, grad_down = (
        lax.psum_scatter(
            grad_gate.astype(jnp.bfloat16), "dp", scatter_dimension=0, tiled=True
        ).astype(jnp.float32),
        lax.psum_scatter(
            grad_up.astype(jnp.bfloat16), "dp", scatter_dimension=0, tiled=True
        ).astype(jnp.float32),
        lax.psum_scatter(
            grad_down.astype(jnp.bfloat16), "dp", scatter_dimension=1, tiled=True
        ).astype(jnp.float32),
    )
    joined_grads = jnp.concatenate([d_gate, d_up], 1)
    joined_proj = jnp.concatenate([gate_proj, up_proj], 1)
    partial_value = lax.dot_general(
        joined_grads, joined_proj, by_width, preferred_element_type=jnp.float32
    ).astype(jnp.bfloat16)
    returned = lax.all_to_all(
        partial_value.reshape(expert_devs, capacity, model_dim),
        "expert",
        split_axis=0,
        concat_axis=0,
        tiled=True,
    )
    summed = jnp.sum(
        returned.reshape(EXPERTS, group_size, capacity, model_dim).astype(jnp.float32), axis=1
    )
    summed = summed.reshape(slot_total, model_dim)
    grad_input = jnp.take(summed, slot_of, axis=0).reshape(tok_dev, top_k, model_dim).sum(axis=1)
    return (grad_input.astype(jnp.bfloat16), grad_gate, grad_up, grad_down)


BY_WIDTH = (((1,), (1,)), ((), ()))
BY_ROWS = (((0,), (0,)), ((), ()))


def cut(width):
    pieces = ROWS // (MOST - ROWS)
    return pieces, width // pieces


def width_of(packed):
    pieces = ROWS // (MOST - ROWS)
    return packed.shape[2] * pieces // (pieces + 1)


def cost(flops, moved):
    return pl.CostEstimate(flops=flops, bytes_accessed=moved, transcendentals=0)


def params():
    return pltpu.CompilerParams(vmem_limit_bytes=VMEM_BYTES)


def anywhere(count):
    return [pl.BlockSpec(memory_space=pl.ANY)] * count


def dot(left, right, dims=(((1,), (0,)), ((), ()))):
    return lax.dot_general(left, right, dims, preferred_element_type=jnp.float32)


def ones(mask):
    return jnp.where(mask, 1.0, 0.0).astype(jnp.bfloat16)


def start(pairs, arrived, first=0):
    for at, (source, target) in enumerate(pairs):
        if at >= first:
            pltpu.make_async_copy(source, target, arrived.at[at]).start()


def wait(pairs, arrived, first=0):
    for at, (source, target) in enumerate(pairs):
        if at >= first:
            pltpu.make_async_copy(source, target, arrived.at[at]).wait()


def slot_masks(routes, blocks, width):
    tokens = routes.shape[1]
    pieces, _ = cut(width)
    experts = lax.broadcasted_iota(jnp.int32, (EXPERTS, tokens), 0)
    named = jnp.where(experts == routes, 1.0, 0.0)
    earlier = lax.broadcasted_iota(jnp.int32, (tokens, tokens), 0) < lax.broadcasted_iota(
        jnp.int32, (tokens, tokens), 1
    )
    before = dot(named.astype(jnp.bfloat16), ones(earlier))
    position = jnp.sum(before * named, axis=0, keepdims=True).astype(jnp.int32)
    slot = lax.broadcasted_iota(jnp.int32, (blocks * ROWS, tokens), 0)
    row = slot % ROWS
    mine = slot // ROWS == routes
    main = mine & (position == row)
    spill = mine & (position == ROWS + row // pieces)
    return main, spill, row % pieces


def pack(blocks, routes, values, gates=None):
    tokens, width = values.shape
    pieces, step = cut(width)
    sources = (routes,) + (() if gates is None else (gates,)) + (values,)
    count = len(sources)

    def kernel(*refs):
        out, held, arrived = refs[count], refs[count + 1 : 2 * count + 1], refs[-1]
        pairs = list(zip(refs[:count], held))
        start(pairs, arrived)
        wait(pairs[:-1], arrived)
        main, spill, piece = slot_masks(held[0][...], blocks, width)
        picks = [ones(spill & (piece == at)) for at in range(pieces)]
        if gates is not None:
            weights = held[1][...]
            main_scale = jnp.sum(jnp.where(main, weights, 0.0), axis=1, keepdims=True)
            spill_scale = jnp.sum(jnp.where(spill, weights, 0.0), axis=1, keepdims=True)
        wait(pairs, arrived, count - 1)
        rows = dot(ones(main), held[-1][...])
        extra = jnp.zeros((blocks * ROWS, step), jnp.float32)
        for at in range(pieces):
            extra += dot(picks[at], held[-1][:, at * step : (at + 1) * step])
        if gates is not None:
            rows, extra = rows * main_scale, extra * spill_scale
        rows = rows.astype(jnp.bfloat16)
        extra = extra.astype(jnp.bfloat16)
        for block in range(blocks):
            part = slice(block * ROWS, (block + 1) * ROWS)
            out[block, :, :width] = rows[part]
            out[block, :, width:] = extra[part]

    return pl.pallas_call(
        kernel,
        out_shape=jax.ShapeDtypeStruct((blocks, ROWS, width + step), jnp.bfloat16),
        in_specs=anywhere(count),
        out_specs=pl.BlockSpec(memory_space=pltpu.VMEM),
        scratch_shapes=[pltpu.VMEM(source.shape, source.dtype) for source in sources]
        + [pltpu.SemaphoreType.DMA((count,))],
        compiler_params=params(),
        cost_estimate=cost(4 * blocks * ROWS * tokens * width, 4 * tokens * width),
        name="pack",
    )(*sources)


def merge(routes, returned):
    blocks = returned.shape[0]
    tokens = routes.shape[1]
    width = width_of(returned)
    pieces, step = cut(width)

    def kernel(routes_ref, back_ref, out, named, held, arrived):
        pairs = [(routes_ref, named), (back_ref, held)]
        start(pairs, arrived)
        wait(pairs[:1], arrived)
        main, spill, piece = slot_masks(named[...], blocks, width)
        mains = ones(main)
        picks = [ones(spill & (piece == at)) for at in range(pieces)]
        wait(pairs, arrived, 1)
        rows = jnp.concatenate([held[at, :, :width] for at in range(blocks)], 0)
        extra = jnp.concatenate([held[at, :, width:] for at in range(blocks)], 0)
        picked = dot(mains, rows, BY_ROWS)
        for at in range(pieces):
            columns = slice(at * step, (at + 1) * step)
            out[:, columns] = (picked[:, columns] + dot(picks[at], extra, BY_ROWS)).astype(
                jnp.bfloat16
            )

    return pl.pallas_call(
        kernel,
        out_shape=jax.ShapeDtypeStruct((tokens, width), jnp.bfloat16),
        in_specs=anywhere(2),
        out_specs=pl.BlockSpec(memory_space=pltpu.VMEM),
        scratch_shapes=[
            pltpu.VMEM(routes.shape, routes.dtype),
            pltpu.VMEM(returned.shape, returned.dtype),
            pltpu.SemaphoreType.DMA((2,)),
        ],
        compiler_params=params(),
        cost_estimate=cost(4 * blocks * ROWS * tokens * width, 4 * tokens * width),
        name="merge",
    )(routes, returned)


def spill_picks(blocks, pieces, at):
    shape = (blocks * (MOST - ROWS), blocks * ROWS)
    slot = lax.broadcasted_iota(jnp.int32, shape, 0)
    row = lax.broadcasted_iota(jnp.int32, shape, 1)
    return ones(row == slot * pieces + at)


def unpack(main, tail, pieces, begin, first, out):
    blocks = main.shape[0]
    step = tail.shape[2]
    for at in range(blocks):
        out[first + at * ROWS : first + (at + 1) * ROWS, :] = main[at]
    extra = jnp.concatenate([tail[at] for at in range(blocks)], 0)
    spill = slice(first + blocks * ROWS, first + blocks * MOST)
    for at in range(out.shape[1] // step):
        out[spill, at * step : (at + 1) * step] = dot(
            spill_picks(blocks, pieces, begin + at), extra
        ).astype(jnp.bfloat16)


def column_tile(width, tile):
    return pl.BlockSpec((width, tile), lambda i: (0, i))


def row_tile(tile, width):
    return pl.BlockSpec((tile, width), lambda i: (i, 0))


def tile_of(index, tile):
    return pl.ds(pl.multiple_of(index * tile, tile), tile)


def weight_copy(source, target, arrived, index, axis, tile):
    here = tile_of(index, tile)
    view = source.at[:, here] if axis else source.at[here, :]
    return pltpu.make_async_copy(view, target.at[index], arrived.at[index])


def forward(tile, packed, gate_proj, up_proj):
    groups = len(packed)
    blocks = packed[0].shape[0]
    width, hid = gate_proj.shape
    pieces, _ = cut(width)
    slots = blocks * MOST
    total = groups * slots
    tiles = hid // tile

    def kernel(*refs):
        gate_ref, up_ref, pre_gate_ref, pre_up_ref = refs[groups : groups + 4]
        held, rows, gate, up, arrived, gate_in, up_in = refs[groups + 4 :]
        now = pl.program_id(0)

        def fetch(index):
            weight_copy(gate_ref, gate, gate_in, index, 1, tile).start()
            weight_copy(up_ref, up, up_in, index, 1, tile).start()

        @pl.when(now == 0)
        def _():
            pairs = [(refs[at], held.at[at]) for at in range(groups)]
            start(pairs, arrived)
            fetch(0)
            wait(pairs, arrived)
            for at in range(groups):
                unpack(
                    held.at[at, :, :, :width], held.at[at, :, :, width:], pieces, 0, at * slots, rows
                )

        @pl.when(now < tiles - 1)
        def _():
            fetch(now + 1)

        weight_copy(gate_ref, gate, gate_in, now, 1, tile).wait()
        pre_gate_ref[...] = dot(rows[...], gate[now])
        weight_copy(up_ref, up, up_in, now, 1, tile).wait()
        pre_up_ref[...] = dot(rows[...], up[now])

    return pl.pallas_call(
        kernel,
        grid=(tiles,),
        out_shape=[jax.ShapeDtypeStruct((total, hid), jnp.float32)] * 2,
        in_specs=anywhere(groups + 2),
        out_specs=[column_tile(total, tile)] * 2,
        scratch_shapes=[
            pltpu.VMEM((groups,) + packed[0].shape, jnp.bfloat16),
            pltpu.VMEM((total, width), jnp.bfloat16),
            pltpu.VMEM((tiles, width, tile), jnp.bfloat16),
            pltpu.VMEM((tiles, width, tile), jnp.bfloat16),
            pltpu.SemaphoreType.DMA((groups,)),
            pltpu.SemaphoreType.DMA((tiles,)),
            pltpu.SemaphoreType.DMA((tiles,)),
        ],
        compiler_params=params(),
        cost_estimate=cost(0, 4 * total * width),
        name="forward",
    )(*packed, gate_proj, up_proj)


def hidden_grads(pre_gate, pre_up, d_hidden):
    sig = jax.nn.sigmoid(pre_gate)
    silu = pre_gate * sig
    hidden = (silu * pre_up).astype(jnp.bfloat16)
    d_gate = (d_hidden * pre_up * sig * (1.0 + pre_gate * (1.0 - sig))).astype(jnp.bfloat16)
    d_up = (d_hidden * silu).astype(jnp.bfloat16)
    return hidden, d_gate, d_up


def back(tile, packed, pre_gate, pre_up, gate_proj, up_proj, down_proj):
    blocks = packed.shape[0]
    width, hid = gate_proj.shape
    slots = blocks * MOST
    pieces, step = cut(width)
    tiles = hid // tile
    chunk = 2 * step
    chunks = width // chunk

    def kernel(packed_ref, gate_ref, up_ref, down_ref, pre_gate_ref, pre_up_ref, *rest):
        out, factors_ref, held, scaled, pre_gate, pre_up, factors = rest[:7]
        tail, staged, gate, up, down, arrived, gate_in, up_in, down_in, gone = rest[7:]
        now = pl.program_id(0)
        first = [(packed_ref, held), (pre_gate_ref, pre_gate), (pre_up_ref, pre_up)]

        def fetch(index):
            @pl.when(index < tiles)
            def _():
                weight_copy(down_ref, down, down_in, index, 0, tile).start()

            @pl.when((index >= tiles) & (index < tiles + chunks))
            def _():
                weight_copy(gate_ref, gate, gate_in, index - tiles, 0, chunk).start()
                weight_copy(up_ref, up, up_in, index - tiles, 0, chunk).start()

        def leave(index):
            columns = tile_of(index, chunk)
            return pltpu.make_async_copy(
                staged.at[:, :, columns], out.at[:, :, columns], gone.at[index]
            )

        def leave_factors():
            return pltpu.make_async_copy(factors, factors_ref, gone.at[chunks + 1])

        @pl.when(now == 0)
        def _():
            start(first[:1], arrived)
            fetch(0)
            start(first, arrived, 1)
            wait(first[:1], arrived)
            fetch(1)
            unpack(held.at[:, :, :width], held.at[:, :, width:], pieces, 0, 0, scaled)
            tail[...] = jnp.zeros_like(tail)

        fetch(now + 2)

        @pl.when(now < tiles)
        def _():
            columns = tile_of(now, tile)
            weight_copy(down_ref, down, down_in, now, 0, tile).wait()
            d_hidden = dot(scaled[...], down[now], BY_WIDTH)

            @pl.when(now == 0)
            def _():
                wait(first, arrived, 1)

            made, d_gate, d_up = hidden_grads(pre_gate[:, columns], pre_up[:, columns], d_hidden)
            factors[:, columns] = made
            factors[:, tile_of(tiles + now, tile)] = d_gate
            factors[:, tile_of(2 * tiles + now, tile)] = d_up

        @pl.when(now == tiles)
        def _():
            leave_factors().start()

        @pl.when(now >= tiles)
        def _():
            at = now - tiles
            weight_copy(gate_ref, gate, gate_in, at, 0, chunk).wait()
            done = dot(factors[:, hid : 2 * hid], gate[at], BY_WIDTH)
            weight_copy(up_ref, up, up_in, at, 0, chunk).wait()
            done = (done + dot(factors[:, 2 * hid :], up[at], BY_WIDTH)).astype(jnp.bfloat16)
            for block in range(blocks):
                staged[block, :, tile_of(at, chunk)] = done[block * ROWS : (block + 1) * ROWS]
            leave(at).start()
            for piece in range(chunk // step):
                tail[...] += dot(
                    spill_picks(blocks, pieces, at * (chunk // step) + piece),
                    done[blocks * ROWS :, piece * step : (piece + 1) * step],
                    BY_ROWS,
                )

        @pl.when(now == tiles + chunks - 1)
        def _():
            for block in range(blocks):
                part = tail[block * ROWS : (block + 1) * ROWS, :]
                staged[block, :, width:] = part.astype(jnp.bfloat16)
            last = pltpu.make_async_copy(
                staged.at[:, :, width:], out.at[:, :, width:], gone.at[chunks]
            )
            last.start()
            for at in range(chunks):
                leave(at).wait()
            leave_factors().wait()
            last.wait()

    return pl.pallas_call(
        kernel,
        grid=(tiles + chunks,),
        out_shape=[
            jax.ShapeDtypeStruct(packed.shape, jnp.bfloat16),
            jax.ShapeDtypeStruct((slots, 3 * hid), jnp.bfloat16),
        ],
        in_specs=anywhere(6),
        out_specs=anywhere(2),
        scratch_shapes=[
            pltpu.VMEM(packed.shape, jnp.bfloat16),
            pltpu.VMEM((slots, width), jnp.bfloat16),
            pltpu.VMEM((slots, hid), jnp.float32),
            pltpu.VMEM((slots, hid), jnp.float32),
            pltpu.VMEM((slots, 3 * hid), jnp.bfloat16),
            pltpu.VMEM((blocks * ROWS, step), jnp.float32),
            pltpu.VMEM(packed.shape, jnp.bfloat16),
            pltpu.VMEM((chunks, chunk, hid), jnp.bfloat16),
            pltpu.VMEM((chunks, chunk, hid), jnp.bfloat16),
            pltpu.VMEM((tiles, tile, width), jnp.bfloat16),
            pltpu.SemaphoreType.DMA((3,)),
            pltpu.SemaphoreType.DMA((chunks,)),
            pltpu.SemaphoreType.DMA((chunks,)),
            pltpu.SemaphoreType.DMA((tiles,)),
            pltpu.SemaphoreType.DMA((chunks + 2,)),
        ],
        compiler_params=params(),
        cost_estimate=cost(0, 4 * slots * width),
        name="back",
    )(packed, gate_proj, up_proj, down_proj, pre_gate, pre_up)


def weight_grads(tile, part, rows, scaled, factors, gate_proj, up_proj, down_proj):
    groups = len(rows)
    blocks = rows[0].shape[0]
    hid, width = down_proj.shape
    pieces, step = cut(width)
    slots = blocks * MOST
    given = len(factors)
    some = (groups - given) * slots
    share = width // groups
    tiles = hid // tile

    def kernel(part_ref, *refs):
        refs = list(refs)
        x_refs = [refs.pop(0) for _ in range(groups)]
        dy_refs = [refs.pop(0) for _ in range(groups)]
        factor_refs = [refs.pop(0) for _ in range(given)]
        gate_ref, up_ref, down_ref = [refs.pop(0) for _ in range(3)]
        d_gate_ref, d_up_ref, d_down_ref = [refs.pop(0) for _ in range(3)]
        x_held, dy_held, mains, tails, x_all, dy_all = [refs.pop(0) for _ in range(6)]
        x_mine, dy_mine, known = [refs.pop(0) for _ in range(3)]
        gate, up, down, x_in, dy_in, known_in, gate_in, up_in, down_in = refs
        now = pl.program_id(0)
        columns = pl.ds(pl.multiple_of(part_ref[0] * share, share), share)
        begin = part_ref[0] * (share // step)
        x_pairs = [(x_refs[at], x_held.at[at - given]) for at in range(given, groups)]
        dy_pairs = [(dy_refs[at], dy_held.at[at - given]) for at in range(given, groups)]
        known_pairs = []
        for at in range(given):
            known_pairs.append((factor_refs[at], known.at[at * slots : (at + 1) * slots, :]))
        for at, ref in enumerate(x_refs[:given] + dy_refs[:given]):
            known_pairs.append((ref.at[:, :, columns], mains.at[at]))
            known_pairs.append((ref.at[:, :, width:], tails.at[at]))

        def arrange(held, rows_out, target):
            for at in range(groups - given):
                unpack(
                    held.at[at, :, :, :width],
                    held.at[at, :, :, width:],
                    pieces,
                    0,
                    at * slots,
                    rows_out,
                )
            target[given * slots :, :] = rows_out[:, columns]

        def fetch_x(index):
            weight_copy(gate_ref, gate, gate_in, index, 1, tile).start()
            weight_copy(up_ref, up, up_in, index, 1, tile).start()

        def fetch_dy(index):
            weight_copy(down_ref, down, down_in, index, 0, tile).start()

        @pl.when(now == 0)
        def _():
            start(x_pairs, x_in)
            fetch_x(0)
            wait(x_pairs, x_in)
            start(dy_pairs, dy_in)
            fetch_dy(0)
            arrange(x_held, x_all, x_mine)

        weight_copy(gate_ref, gate, gate_in, now, 1, tile).wait()
        pre_gate = dot(x_all[...], gate[now])
        weight_copy(up_ref, up, up_in, now, 1, tile).wait()
        pre_up = dot(x_all[...], up[now])

        @pl.when(now == 0)
        def _():
            wait(dy_pairs, dy_in)
            start(known_pairs, known_in)
            arrange(dy_held, dy_all, dy_mine)

        @pl.when(now < tiles - 1)
        def _():
            fetch_x(now + 1)
            fetch_dy(now + 1)

        weight_copy(down_ref, down, down_in, now, 0, tile).wait()
        d_hidden = dot(dy_all[...], down[now], BY_WIDTH)
        made, d_gate, d_up = hidden_grads(pre_gate, pre_up, d_hidden)

        @pl.when(now == 0)
        def _():
            wait(known_pairs, known_in)
            for at in range(given):
                unpack(mains.at[at], tails.at[at], pieces, begin, at * slots, x_mine)
                behind = given + at
                unpack(mains.at[behind], tails.at[behind], pieces, begin, at * slots, dy_mine)

        made = jnp.concatenate([known[:, tile_of(now, tile)], made], 0)
        d_gate = jnp.concatenate([known[:, tile_of(tiles + now, tile)], d_gate], 0)
        d_up = jnp.concatenate([known[:, tile_of(2 * tiles + now, tile)], d_up], 0)
        sums = dot(x_mine[...], jnp.concatenate([d_gate, d_up], 1), BY_ROWS)
        d_gate_ref[...] = sums[:, :tile]
        d_up_ref[...] = sums[:, tile:]
        d_down_ref[...] = dot(made, dy_mine[...], BY_ROWS)

    return pl.pallas_call(
        kernel,
        grid=(tiles,),
        out_shape=[
            jax.ShapeDtypeStruct((share, hid), jnp.float32),
            jax.ShapeDtypeStruct((share, hid), jnp.float32),
            jax.ShapeDtypeStruct((hid, share), jnp.float32),
        ],
        in_specs=[pl.BlockSpec(memory_space=pltpu.SMEM)] + anywhere(2 * groups + given + 3),
        out_specs=[column_tile(share, tile), column_tile(share, tile), row_tile(tile, share)],
        scratch_shapes=[
            pltpu.VMEM((groups - given,) + rows[0].shape, jnp.bfloat16),
            pltpu.VMEM((groups - given,) + rows[0].shape, jnp.bfloat16),
            pltpu.VMEM((2 * given, blocks, ROWS, share), jnp.bfloat16),
            pltpu.VMEM((2 * given, blocks, ROWS, step), jnp.bfloat16),
            pltpu.VMEM((some, width), jnp.bfloat16),
            pltpu.VMEM((some, width), jnp.bfloat16),
            pltpu.VMEM((groups * slots, share), jnp.bfloat16),
            pltpu.VMEM((groups * slots, share), jnp.bfloat16),
            pltpu.VMEM((given * slots, 3 * hid), jnp.bfloat16),
            pltpu.VMEM((tiles, width, tile), jnp.bfloat16),
            pltpu.VMEM((tiles, width, tile), jnp.bfloat16),
            pltpu.VMEM((tiles, tile, width), jnp.bfloat16),
            pltpu.SemaphoreType.DMA((groups - given,)),
            pltpu.SemaphoreType.DMA((groups - given,)),
            pltpu.SemaphoreType.DMA((5 * given,)),
            pltpu.SemaphoreType.DMA((tiles,)),
            pltpu.SemaphoreType.DMA((tiles,)),
            pltpu.SemaphoreType.DMA((tiles,)),
        ],
        compiler_params=params(),
        cost_estimate=cost(0, 4 * slots * width),
        name="weight_grads",
    )(part, *rows, *scaled, *factors, gate_proj, up_proj, down_proj)


def swap(value, axis, distance):
    size = lax.axis_size(axis)
    return lax.ppermute(value, axis, [(at, at ^ distance) for at in range(size)])


def exchange(blocks):
    return lax.all_to_all(blocks, "expert", split_axis=0, concat_axis=0, tiled=True)


def after(value, *earlier):
    return lax.optimization_barrier((value, *earlier))[0]


def gather_body(tokens, cotangent, routes, expert_gates, gate_proj, up_proj, down_proj):
    blocks = lax.axis_size("expert")
    tile = 256
    part = lax.axis_index("dp").astype(jnp.int32).reshape(1)
    routes = routes.reshape(1, -1)
    gates = expert_gates.reshape(1, -1)
    weights = (gate_proj, up_proj, down_proj)
    rows = exchange(pack(blocks, routes, tokens))
    far = swap(rows, "dp", 2)
    near = swap(rows, "dp", 1)
    scaled = exchange(after(pack(blocks, routes, cotangent, gates), rows))
    pre = forward(tile, [rows], gate_proj, up_proj)
    scaled, far, near, *pre = lax.optimization_barrier((scaled, far, near, *pre))
    last = swap(far, "dp", 1)
    dy_far = swap(scaled, "dp", 2)
    dy_near = swap(scaled, "dp", 1)
    sent, factors = back(tile, scaled, *pre, *weights)
    sent, factors, last, dy_near = lax.optimization_barrier((sent, factors, last, dy_near))
    returned = exchange(sent)
    dy_last = swap(after(dy_far, sent), "dp", 1)
    grads = weight_grads(
        tile,
        part,
        [rows, near, far, last],
        [scaled, dy_near, dy_far, dy_last],
        [factors, swap(factors, "dp", 1)],
        *weights,
    )
    return (merge(routes, after(returned, *grads)), *grads)


def body(tokens, cotangent, routes, expert_gates, gate_proj, up_proj, down_proj):
    groups, blocks = lax.axis_size("dp"), lax.axis_size("expert")
    width, hid = gate_proj.shape
    rows_sent = (groups - 1) * 2 * blocks * MOST * width
    grads_sent = 3 * width * hid * (groups - 1) // groups
    fits = blocks == EXPERTS and groups == 4 and hid % 256 == 0
    fits = fits and tokens.shape[0] == 128 and routes.shape[1] == 1 and width // groups % 128 == 0
    chosen = gather_body if fits and rows_sent < grads_sent else scatter_body
    return chosen(tokens, cotangent, routes, expert_gates, gate_proj, up_proj, down_proj)


def solution(mesh):
    in_specs = (
        P(("dp", "expert"), None),
        P(("dp", "expert"), None),
        P(("dp", "expert"), None),
        P(("dp", "expert"), None),
        P(None, "expert"),
        P(None, "expert"),
        P("expert", None),
    )
    out_specs = (P(("dp", "expert"), None), P("dp", "expert"), P("dp", "expert"), P("expert", "dp"))
    return jax.shard_map(body, mesh=mesh, in_specs=in_specs, out_specs=out_specs, check_vma=False)
```

```python
import jax
import jax.numpy as jnp
from jax import lax
from jax.experimental import pallas as pl
from jax.experimental.pallas import tpu as pltpu
from jax.sharding import PartitionSpec as P

EXPERTS = 8
MOST = 18
ROWS = 16
VMEM_BYTES = (63 * 1024 + 768) * 1024


def build_slots(routes, capacity):
    flat_routes = routes.reshape(-1)
    one_hot = (flat_routes[:, None] == jnp.arange(EXPERTS, dtype=jnp.int32)[None, :]).astype(
        jnp.int32
    )
    before = jnp.cumsum(one_hot, axis=0) - one_hot
    position = jnp.sum(before * one_hot, axis=1)
    return flat_routes * capacity + position


def scatter_body(tokens, cotangent, routes, expert_gates, gate_proj, up_proj, down_proj):
    tok_dev, model_dim = tokens.shape
    top_k = routes.shape[1]
    expert_devs = lax.axis_size("expert")
    group_size = expert_devs // EXPERTS
    capacity = MOST
    slot_total = EXPERTS * capacity
    slot_of = build_slots(routes, capacity)
    owners = jnp.arange(tok_dev * top_k, dtype=jnp.int32) // top_k
    slot_table = jnp.full((slot_total,), tok_dev, jnp.int32).at[slot_of].set(owners)
    slot_gate = jnp.zeros((slot_total,), jnp.float32).at[slot_of].set(expert_gates.reshape(-1))
    x_slots = jnp.take(tokens, slot_table, axis=0, mode="fill", fill_value=0)
    dy_slots = (
        jnp.take(cotangent, slot_table, axis=0, mode="fill", fill_value=0).astype(jnp.float32)
        * slot_gate[:, None]
    ).astype(jnp.bfloat16)

    def copies(values):
        spread = values.reshape(EXPERTS, 1, capacity, model_dim)
        return jnp.broadcast_to(spread, (EXPERTS, group_size, capacity, model_dim)).reshape(
            expert_devs, capacity, model_dim
        )

    x_recv, dy_recv = (
        lax.all_to_all(copies(x_slots), "expert", split_axis=0, concat_axis=0, tiled=True),
        lax.all_to_all(copies(dy_slots), "expert", split_axis=0, concat_axis=0, tiled=True),
    )
    in_rows = x_recv.reshape(expert_devs * capacity, model_dim)
    scaled = dy_recv.reshape(expert_devs * capacity, model_dim)
    pre_gate = jnp.dot(in_rows, gate_proj, preferred_element_type=jnp.float32)
    pre_up = jnp.dot(in_rows, up_proj, preferred_element_type=jnp.float32)
    gate_sig = jax.nn.sigmoid(pre_gate)
    hidden = (pre_gate * gate_sig * pre_up).astype(jnp.bfloat16)
    by_width = (((1,), (1,)), ((), ()))
    by_rows = (((0,), (0,)), ((), ()))
    d_hidden = lax.dot_general(scaled, down_proj, by_width, preferred_element_type=jnp.float32)
    d_gate = (d_hidden * pre_up * gate_sig * (1.0 + pre_gate * (1.0 - gate_sig))).astype(
        jnp.bfloat16
    )
    d_up = (d_hidden * pre_gate * gate_sig).astype(jnp.bfloat16)
    grad_down = lax.dot_general(hidden, scaled, by_rows, preferred_element_type=jnp.float32)
    grad_gate = lax.dot_general(in_rows, d_gate, by_rows, preferred_element_type=jnp.float32)
    grad_up = lax.dot_general(in_rows, d_up, by_rows, preferred_element_type=jnp.float32)
    grad_gate, grad_up, grad_down = (
        lax.psum_scatter(
            grad_gate.astype(jnp.bfloat16), "dp", scatter_dimension=0, tiled=True
        ).astype(jnp.float32),
        lax.psum_scatter(
            grad_up.astype(jnp.bfloat16), "dp", scatter_dimension=0, tiled=True
        ).astype(jnp.float32),
        lax.psum_scatter(
            grad_down.astype(jnp.bfloat16), "dp", scatter_dimension=1, tiled=True
        ).astype(jnp.float32),
    )
    joined_grads = jnp.concatenate([d_gate, d_up], 1)
    joined_proj = jnp.concatenate([gate_proj, up_proj], 1)
    partial_value = lax.dot_general(
        joined_grads, joined_proj, by_width, preferred_element_type=jnp.float32
    ).astype(jnp.bfloat16)
    returned = lax.all_to_all(
        partial_value.reshape(expert_devs, capacity, model_dim),
        "expert",
        split_axis=0,
        concat_axis=0,
        tiled=True,
    )
    summed = jnp.sum(
        returned.reshape(EXPERTS, group_size, capacity, model_dim).astype(jnp.float32), axis=1
    )
    summed = summed.reshape(slot_total, model_dim)
    grad_input = jnp.take(summed, slot_of, axis=0).reshape(tok_dev, top_k, model_dim).sum(axis=1)
    return (grad_input.astype(jnp.bfloat16), grad_gate, grad_up, grad_down)


BY_WIDTH = (((1,), (1,)), ((), ()))
BY_ROWS = (((0,), (0,)), ((), ()))


def cut(width):
    pieces = ROWS // (MOST - ROWS)
    return pieces, width // pieces


def width_of(packed):
    pieces = ROWS // (MOST - ROWS)
    return packed.shape[2] * pieces // (pieces + 1)


def cost(flops, moved):
    return pl.CostEstimate(flops=flops, bytes_accessed=moved, transcendentals=0)


def params():
    return pltpu.CompilerParams(vmem_limit_bytes=VMEM_BYTES)


def anywhere(count):
    return [pl.BlockSpec(memory_space=pl.ANY)] * count


def dot(left, right, dims=(((1,), (0,)), ((), ()))):
    return lax.dot_general(left, right, dims, preferred_element_type=jnp.float32)


def ones(mask):
    return jnp.where(mask, 1.0, 0.0).astype(jnp.bfloat16)


def start(pairs, arrived, first=0):
    for at, (source, target) in enumerate(pairs):
        if at >= first:
            pltpu.make_async_copy(source, target, arrived.at[at]).start()


def wait(pairs, arrived, first=0):
    for at, (source, target) in enumerate(pairs):
        if at >= first:
            pltpu.make_async_copy(source, target, arrived.at[at]).wait()


def slot_masks(routes, blocks, width, me=0):
    tokens = routes.shape[1]
    pieces, _ = cut(width)
    experts = lax.broadcasted_iota(jnp.int32, (EXPERTS, tokens), 0)
    named = jnp.where(experts == routes, 1.0, 0.0)
    earlier = lax.broadcasted_iota(jnp.int32, (tokens, tokens), 0) < lax.broadcasted_iota(
        jnp.int32, (tokens, tokens), 1
    )
    before = dot(named.astype(jnp.bfloat16), ones(earlier))
    position = jnp.sum(before * named, axis=0, keepdims=True).astype(jnp.int32)
    slot = lax.broadcasted_iota(jnp.int32, (blocks * ROWS, tokens), 0)
    row = slot % ROWS
    mine = (slot // ROWS) ^ me == routes
    main = mine & (position == row)
    spill = mine & (position == ROWS + row // pieces)
    return main, spill, row % pieces


def pack(blocks, routes, values, gates=None, me=None):
    tokens, width = values.shape
    pieces, step = cut(width)
    sources = (routes,) + (() if gates is None else (gates,)) + (values,)
    count = len(sources)
    apart = me is not None
    whole = jax.ShapeDtypeStruct((blocks, ROWS, width + step), jnp.bfloat16)
    alone = jax.ShapeDtypeStruct((ROWS, width + step), jnp.bfloat16)

    def kernel(*refs):
        refs = list(refs)
        index = refs.pop(0)[0] if apart else 0
        given = [refs.pop(0) for _ in range(count)]
        outs = [refs.pop(0) for _ in range(blocks if apart else 1)]
        held, arrived = refs[:-1], refs[-1]
        pairs = list(zip(given, held))
        start(pairs, arrived)
        wait(pairs[:-1], arrived)
        main, spill, piece = slot_masks(held[0][...], blocks, width, index)
        picks = [ones(spill & (piece == at)) for at in range(pieces)]
        if gates is not None:
            weights = held[1][...]
            main_scale = jnp.sum(jnp.where(main, weights, 0.0), axis=1, keepdims=True)
            spill_scale = jnp.sum(jnp.where(spill, weights, 0.0), axis=1, keepdims=True)
        wait(pairs, arrived, count - 1)
        rows = dot(ones(main), held[-1][...])
        extra = jnp.zeros((blocks * ROWS, step), jnp.float32)
        for at in range(pieces):
            extra += dot(picks[at], held[-1][:, at * step : (at + 1) * step])
        if gates is not None:
            rows, extra = rows * main_scale, extra * spill_scale
        rows = rows.astype(jnp.bfloat16)
        extra = extra.astype(jnp.bfloat16)
        for block in range(blocks):
            part = slice(block * ROWS, (block + 1) * ROWS)
            out = outs[block] if apart else outs[0].at[block]
            out[:, :width] = rows[part]
            out[:, width:] = extra[part]

    inside = pl.BlockSpec(memory_space=pltpu.VMEM)
    return pl.pallas_call(
        kernel,
        out_shape=[alone] * blocks if apart else whole,
        in_specs=[pl.BlockSpec(memory_space=pltpu.SMEM)] * apart + anywhere(count),
        out_specs=[inside] * blocks if apart else inside,
        scratch_shapes=[pltpu.VMEM(source.shape, source.dtype) for source in sources]
        + [pltpu.SemaphoreType.DMA((count,))],
        compiler_params=params(),
        cost_estimate=cost(4 * blocks * ROWS * tokens * width, 4 * tokens * width),
        name="pack",
    )(*((me,) if apart else ()), *sources)


def join(me, received):
    count = len(received)

    def kernel(me_ref, *refs):
        arrived = refs[-1]
        pairs = [(refs[at], refs[count].at[me_ref[0] ^ at]) for at in range(count)]
        start(pairs, arrived)
        wait(pairs, arrived)

    return pl.pallas_call(
        kernel,
        out_shape=jax.ShapeDtypeStruct((count,) + received[0].shape, jnp.bfloat16),
        in_specs=[pl.BlockSpec(memory_space=pltpu.SMEM)] + anywhere(count),
        out_specs=pl.BlockSpec(memory_space=pl.ANY),
        scratch_shapes=[pltpu.SemaphoreType.DMA((count,))],
        compiler_params=params(),
        cost_estimate=cost(0, 4 * received[0].size * count),
        name="join",
    )(me, *received)


def merge(routes, returned):
    blocks = returned.shape[0]
    tokens = routes.shape[1]
    width = width_of(returned)
    pieces, step = cut(width)

    def kernel(routes_ref, back_ref, out, named, held, arrived):
        pairs = [(routes_ref, named), (back_ref, held)]
        start(pairs, arrived)
        wait(pairs[:1], arrived)
        main, spill, piece = slot_masks(named[...], blocks, width)
        mains = ones(main)
        picks = [ones(spill & (piece == at)) for at in range(pieces)]
        wait(pairs, arrived, 1)
        rows = jnp.concatenate([held[at, :, :width] for at in range(blocks)], 0)
        extra = jnp.concatenate([held[at, :, width:] for at in range(blocks)], 0)
        picked = dot(mains, rows, BY_ROWS)
        for at in range(pieces):
            columns = slice(at * step, (at + 1) * step)
            out[:, columns] = (picked[:, columns] + dot(picks[at], extra, BY_ROWS)).astype(
                jnp.bfloat16
            )

    return pl.pallas_call(
        kernel,
        out_shape=jax.ShapeDtypeStruct((tokens, width), jnp.bfloat16),
        in_specs=anywhere(2),
        out_specs=pl.BlockSpec(memory_space=pltpu.VMEM),
        scratch_shapes=[
            pltpu.VMEM(routes.shape, routes.dtype),
            pltpu.VMEM(returned.shape, returned.dtype),
            pltpu.SemaphoreType.DMA((2,)),
        ],
        compiler_params=params(),
        cost_estimate=cost(4 * blocks * ROWS * tokens * width, 4 * tokens * width),
        name="merge",
    )(routes, returned)


def spill_picks(blocks, pieces, at):
    shape = (blocks * (MOST - ROWS), blocks * ROWS)
    slot = lax.broadcasted_iota(jnp.int32, shape, 0)
    row = lax.broadcasted_iota(jnp.int32, shape, 1)
    return ones(row == slot * pieces + at)


def unpack(main, tail, pieces, begin, first, out):
    blocks = main.shape[0]
    step = tail.shape[2]
    for at in range(blocks):
        out[first + at * ROWS : first + (at + 1) * ROWS, :] = main[at]
    extra = jnp.concatenate([tail[at] for at in range(blocks)], 0)
    spill = slice(first + blocks * ROWS, first + blocks * MOST)
    for at in range(out.shape[1] // step):
        out[spill, at * step : (at + 1) * step] = dot(
            spill_picks(blocks, pieces, begin + at), extra
        ).astype(jnp.bfloat16)


def column_tile(width, tile):
    return pl.BlockSpec((width, tile), lambda i: (0, i))


def row_tile(tile, width):
    return pl.BlockSpec((tile, width), lambda i: (i, 0))


def tile_of(index, tile):
    return pl.ds(pl.multiple_of(index * tile, tile), tile)


def weight_copy(source, target, arrived, index, axis, tile):
    here = tile_of(index, tile)
    view = source.at[:, here] if axis else source.at[here, :]
    return pltpu.make_async_copy(view, target.at[index], arrived.at[index])


def forward(tile, packed, gate_proj, up_proj):
    groups = len(packed)
    blocks = packed[0].shape[0]
    width, hid = gate_proj.shape
    pieces, _ = cut(width)
    slots = blocks * MOST
    total = groups * slots
    tiles = hid // tile

    def kernel(*refs):
        gate_ref, up_ref, pre_gate_ref, pre_up_ref = refs[groups : groups + 4]
        held, rows, gate, up, arrived, gate_in, up_in = refs[groups + 4 :]
        now = pl.program_id(0)

        def fetch(index):
            weight_copy(gate_ref, gate, gate_in, index, 1, tile).start()
            weight_copy(up_ref, up, up_in, index, 1, tile).start()

        @pl.when(now == 0)
        def _():
            pairs = [(refs[at], held.at[at]) for at in range(groups)]
            start(pairs, arrived)
            fetch(0)
            wait(pairs, arrived)
            for at in range(groups):
                unpack(
                    held.at[at, :, :, :width], held.at[at, :, :, width:], pieces, 0, at * slots, rows
                )

        @pl.when(now < tiles - 1)
        def _():
            fetch(now + 1)

        weight_copy(gate_ref, gate, gate_in, now, 1, tile).wait()
        pre_gate_ref[...] = dot(rows[...], gate[now])
        weight_copy(up_ref, up, up_in, now, 1, tile).wait()
        pre_up_ref[...] = dot(rows[...], up[now])

    return pl.pallas_call(
        kernel,
        grid=(tiles,),
        out_shape=[jax.ShapeDtypeStruct((total, hid), jnp.float32)] * 2,
        in_specs=anywhere(groups + 2),
        out_specs=[column_tile(total, tile)] * 2,
        scratch_shapes=[
            pltpu.VMEM((groups,) + packed[0].shape, jnp.bfloat16),
            pltpu.VMEM((total, width), jnp.bfloat16),
            pltpu.VMEM((tiles, width, tile), jnp.bfloat16),
            pltpu.VMEM((tiles, width, tile), jnp.bfloat16),
            pltpu.SemaphoreType.DMA((groups,)),
            pltpu.SemaphoreType.DMA((tiles,)),
            pltpu.SemaphoreType.DMA((tiles,)),
        ],
        compiler_params=params(),
        cost_estimate=cost(0, 4 * total * width),
        name="forward",
    )(*packed, gate_proj, up_proj)


def hidden_grads(pre_gate, pre_up, d_hidden):
    sig = jax.nn.sigmoid(pre_gate)
    silu = pre_gate * sig
    hidden = (silu * pre_up).astype(jnp.bfloat16)
    d_gate = (d_hidden * pre_up * sig * (1.0 + pre_gate * (1.0 - sig))).astype(jnp.bfloat16)
    d_up = (d_hidden * silu).astype(jnp.bfloat16)
    return hidden, d_gate, d_up


def back(tile, packed, pre_gate, pre_up, gate_proj, up_proj, down_proj):
    blocks = packed.shape[0]
    width, hid = gate_proj.shape
    slots = blocks * MOST
    pieces, step = cut(width)
    tiles = hid // tile
    chunk = 2 * step
    chunks = width // chunk

    def kernel(packed_ref, gate_ref, up_ref, down_ref, pre_gate_ref, pre_up_ref, *rest):
        out, factors_ref, held, scaled, pre_gate, pre_up, factors = rest[:7]
        tail, staged, gate, up, down, arrived, gate_in, up_in, down_in, gone = rest[7:]
        now = pl.program_id(0)
        first = [(packed_ref, held), (pre_gate_ref, pre_gate), (pre_up_ref, pre_up)]

        def fetch(index):
            @pl.when(index < tiles)
            def _():
                weight_copy(down_ref, down, down_in, index, 0, tile).start()

            @pl.when((index >= tiles) & (index < tiles + chunks))
            def _():
                weight_copy(gate_ref, gate, gate_in, index - tiles, 0, chunk).start()
                weight_copy(up_ref, up, up_in, index - tiles, 0, chunk).start()

        def leave(index):
            columns = tile_of(index, chunk)
            return pltpu.make_async_copy(
                staged.at[:, :, columns], out.at[:, :, columns], gone.at[index]
            )

        def leave_factors():
            return pltpu.make_async_copy(factors, factors_ref, gone.at[chunks + 1])

        @pl.when(now == 0)
        def _():
            start(first[:1], arrived)
            fetch(0)
            start(first, arrived, 1)
            wait(first[:1], arrived)
            fetch(1)
            unpack(held.at[:, :, :width], held.at[:, :, width:], pieces, 0, 0, scaled)
            tail[...] = jnp.zeros_like(tail)

        fetch(now + 2)

        @pl.when(now < tiles)
        def _():
            columns = tile_of(now, tile)
            weight_copy(down_ref, down, down_in, now, 0, tile).wait()
            d_hidden = dot(scaled[...], down[now], BY_WIDTH)

            @pl.when(now == 0)
            def _():
                wait(first, arrived, 1)

            made, d_gate, d_up = hidden_grads(pre_gate[:, columns], pre_up[:, columns], d_hidden)
            factors[:, columns] = made
            factors[:, tile_of(tiles + now, tile)] = d_gate
            factors[:, tile_of(2 * tiles + now, tile)] = d_up

        @pl.when(now == tiles)
        def _():
            leave_factors().start()

        @pl.when(now >= tiles)
        def _():
            at = now - tiles
            weight_copy(gate_ref, gate, gate_in, at, 0, chunk).wait()
            done = dot(factors[:, hid : 2 * hid], gate[at], BY_WIDTH)
            weight_copy(up_ref, up, up_in, at, 0, chunk).wait()
            done = (done + dot(factors[:, 2 * hid :], up[at], BY_WIDTH)).astype(jnp.bfloat16)
            for block in range(blocks):
                staged[block, :, tile_of(at, chunk)] = done[block * ROWS : (block + 1) * ROWS]
            leave(at).start()
            for piece in range(chunk // step):
                tail[...] += dot(
                    spill_picks(blocks, pieces, at * (chunk // step) + piece),
                    done[blocks * ROWS :, piece * step : (piece + 1) * step],
                    BY_ROWS,
                )

        @pl.when(now == tiles + chunks - 1)
        def _():
            for block in range(blocks):
                part = tail[block * ROWS : (block + 1) * ROWS, :]
                staged[block, :, width:] = part.astype(jnp.bfloat16)
            last = pltpu.make_async_copy(
                staged.at[:, :, width:], out.at[:, :, width:], gone.at[chunks]
            )
            last.start()
            for at in range(chunks):
                leave(at).wait()
            leave_factors().wait()
            last.wait()

    return pl.pallas_call(
        kernel,
        grid=(tiles + chunks,),
        out_shape=[
            jax.ShapeDtypeStruct(packed.shape, jnp.bfloat16),
            jax.ShapeDtypeStruct((slots, 3 * hid), jnp.bfloat16),
        ],
        in_specs=anywhere(6),
        out_specs=anywhere(2),
        scratch_shapes=[
            pltpu.VMEM(packed.shape, jnp.bfloat16),
            pltpu.VMEM((slots, width), jnp.bfloat16),
            pltpu.VMEM((slots, hid), jnp.float32),
            pltpu.VMEM((slots, hid), jnp.float32),
            pltpu.VMEM((slots, 3 * hid), jnp.bfloat16),
            pltpu.VMEM((blocks * ROWS, step), jnp.float32),
            pltpu.VMEM(packed.shape, jnp.bfloat16),
            pltpu.VMEM((chunks, chunk, hid), jnp.bfloat16),
            pltpu.VMEM((chunks, chunk, hid), jnp.bfloat16),
            pltpu.VMEM((tiles, tile, width), jnp.bfloat16),
            pltpu.SemaphoreType.DMA((3,)),
            pltpu.SemaphoreType.DMA((chunks,)),
            pltpu.SemaphoreType.DMA((chunks,)),
            pltpu.SemaphoreType.DMA((tiles,)),
            pltpu.SemaphoreType.DMA((chunks + 2,)),
        ],
        compiler_params=params(),
        cost_estimate=cost(0, 4 * slots * width),
        name="back",
    )(packed, gate_proj, up_proj, down_proj, pre_gate, pre_up)


def weight_grads(tile, part, rows, scaled, factors, gate_proj, up_proj, down_proj):
    groups = len(rows)
    blocks = rows[0].shape[0]
    hid, width = down_proj.shape
    pieces, step = cut(width)
    slots = blocks * MOST
    given = len(factors)
    some = (groups - given) * slots
    share = width // groups
    tiles = hid // tile

    def kernel(part_ref, *refs):
        refs = list(refs)
        x_refs = [refs.pop(0) for _ in range(groups)]
        dy_refs = [refs.pop(0) for _ in range(groups)]
        factor_refs = [refs.pop(0) for _ in range(given)]
        gate_ref, up_ref, down_ref = [refs.pop(0) for _ in range(3)]
        d_gate_ref, d_up_ref, d_down_ref = [refs.pop(0) for _ in range(3)]
        x_held, dy_held, mains, tails, x_all, dy_all = [refs.pop(0) for _ in range(6)]
        x_mine, dy_mine, known = [refs.pop(0) for _ in range(3)]
        gate, up, down, x_in, dy_in, known_in, gate_in, up_in, down_in = refs
        now = pl.program_id(0)
        columns = pl.ds(pl.multiple_of(part_ref[0] * share, share), share)
        begin = part_ref[0] * (share // step)
        x_pairs = [(x_refs[at], x_held.at[at - given]) for at in range(given, groups)]
        dy_pairs = [(dy_refs[at], dy_held.at[at - given]) for at in range(given, groups)]
        known_pairs = []
        for at in range(given):
            known_pairs.append((factor_refs[at], known.at[at * slots : (at + 1) * slots, :]))
        for at, ref in enumerate(x_refs[:given] + dy_refs[:given]):
            known_pairs.append((ref.at[:, :, columns], mains.at[at]))
            known_pairs.append((ref.at[:, :, width:], tails.at[at]))

        def arrange(held, rows_out, target):
            for at in range(groups - given):
                unpack(
                    held.at[at, :, :, :width],
                    held.at[at, :, :, width:],
                    pieces,
                    0,
                    at * slots,
                    rows_out,
                )
            target[given * slots :, :] = rows_out[:, columns]

        def fetch_x(index):
            weight_copy(gate_ref, gate, gate_in, index, 1, tile).start()
            weight_copy(up_ref, up, up_in, index, 1, tile).start()

        def fetch_dy(index):
            weight_copy(down_ref, down, down_in, index, 0, tile).start()

        @pl.when(now == 0)
        def _():
            start(x_pairs, x_in)
            fetch_x(0)
            wait(x_pairs, x_in)
            start(dy_pairs, dy_in)
            fetch_dy(0)
            arrange(x_held, x_all, x_mine)

        weight_copy(gate_ref, gate, gate_in, now, 1, tile).wait()
        pre_gate = dot(x_all[...], gate[now])
        weight_copy(up_ref, up, up_in, now, 1, tile).wait()
        pre_up = dot(x_all[...], up[now])

        @pl.when(now == 0)
        def _():
            wait(dy_pairs, dy_in)
            start(known_pairs, known_in)
            arrange(dy_held, dy_all, dy_mine)

        @pl.when(now < tiles - 1)
        def _():
            fetch_x(now + 1)
            fetch_dy(now + 1)

        weight_copy(down_ref, down, down_in, now, 0, tile).wait()
        d_hidden = dot(dy_all[...], down[now], BY_WIDTH)
        made, d_gate, d_up = hidden_grads(pre_gate, pre_up, d_hidden)

        @pl.when(now == 0)
        def _():
            wait(known_pairs, known_in)
            for at in range(given):
                unpack(mains.at[at], tails.at[at], pieces, begin, at * slots, x_mine)
                behind = given + at
                unpack(mains.at[behind], tails.at[behind], pieces, begin, at * slots, dy_mine)

        made = jnp.concatenate([known[:, tile_of(now, tile)], made], 0)
        d_gate = jnp.concatenate([known[:, tile_of(tiles + now, tile)], d_gate], 0)
        d_up = jnp.concatenate([known[:, tile_of(2 * tiles + now, tile)], d_up], 0)
        sums = dot(x_mine[...], jnp.concatenate([d_gate, d_up], 1), BY_ROWS)
        d_gate_ref[...] = sums[:, :tile]
        d_up_ref[...] = sums[:, tile:]
        d_down_ref[...] = dot(made, dy_mine[...], BY_ROWS)

    return pl.pallas_call(
        kernel,
        grid=(tiles,),
        out_shape=[
            jax.ShapeDtypeStruct((share, hid), jnp.float32),
            jax.ShapeDtypeStruct((share, hid), jnp.float32),
            jax.ShapeDtypeStruct((hid, share), jnp.float32),
        ],
        in_specs=[pl.BlockSpec(memory_space=pltpu.SMEM)] + anywhere(2 * groups + given + 3),
        out_specs=[column_tile(share, tile), column_tile(share, tile), row_tile(tile, share)],
        scratch_shapes=[
            pltpu.VMEM((groups - given,) + rows[0].shape, jnp.bfloat16),
            pltpu.VMEM((groups - given,) + rows[0].shape, jnp.bfloat16),
            pltpu.VMEM((2 * given, blocks, ROWS, share), jnp.bfloat16),
            pltpu.VMEM((2 * given, blocks, ROWS, step), jnp.bfloat16),
            pltpu.VMEM((some, width), jnp.bfloat16),
            pltpu.VMEM((some, width), jnp.bfloat16),
            pltpu.VMEM((groups * slots, share), jnp.bfloat16),
            pltpu.VMEM((groups * slots, share), jnp.bfloat16),
            pltpu.VMEM((given * slots, 3 * hid), jnp.bfloat16),
            pltpu.VMEM((tiles, width, tile), jnp.bfloat16),
            pltpu.VMEM((tiles, width, tile), jnp.bfloat16),
            pltpu.VMEM((tiles, tile, width), jnp.bfloat16),
            pltpu.SemaphoreType.DMA((groups - given,)),
            pltpu.SemaphoreType.DMA((groups - given,)),
            pltpu.SemaphoreType.DMA((5 * given,)),
            pltpu.SemaphoreType.DMA((tiles,)),
            pltpu.SemaphoreType.DMA((tiles,)),
            pltpu.SemaphoreType.DMA((tiles,)),
        ],
        compiler_params=params(),
        cost_estimate=cost(0, 4 * slots * width),
        name="weight_grads",
    )(part, *rows, *scaled, *factors, gate_proj, up_proj, down_proj)


def swap(value, axis, distance):
    size = lax.axis_size(axis)
    return lax.ppermute(value, axis, [(at, at ^ distance) for at in range(size)])


def exchange(blocks):
    return lax.all_to_all(blocks, "expert", split_axis=0, concat_axis=0, tiled=True)


def after(value, *earlier):
    return lax.optimization_barrier((value, *earlier))[0]


def gather_body(tokens, cotangent, routes, expert_gates, gate_proj, up_proj, down_proj):
    blocks = lax.axis_size("expert")
    tile = 256
    part = lax.axis_index("dp").astype(jnp.int32).reshape(1)
    routes = routes.reshape(1, -1)
    gates = expert_gates.reshape(1, -1)
    weights = (gate_proj, up_proj, down_proj)
    me = lax.axis_index("expert").astype(jnp.int32).reshape(1)
    received = list(pack(blocks, routes, tokens, me=me))
    for distance in reversed(range(1, blocks)):
        received[distance] = swap(received[distance], "expert", distance)
    packed = pack(blocks, routes, cotangent, gates)
    packed, received[-1] = lax.optimization_barrier((packed, received[-1]))
    scaled = exchange(packed)
    rows = join(me, received)
    far = swap(rows, "dp", 2)
    near = swap(rows, "dp", 1)
    pre = forward(tile, [rows], gate_proj, up_proj)
    scaled, far, near, *pre = lax.optimization_barrier((scaled, far, near, *pre))
    last = swap(far, "dp", 1)
    dy_far = swap(scaled, "dp", 2)
    dy_near = swap(scaled, "dp", 1)
    sent, factors = back(tile, scaled, *pre, *weights)
    sent, factors, last, dy_near = lax.optimization_barrier((sent, factors, last, dy_near))
    returned = exchange(sent)
    dy_last = swap(after(dy_far, sent), "dp", 1)
    grads = weight_grads(
        tile,
        part,
        [rows, near, far, last],
        [scaled, dy_near, dy_far, dy_last],
        [factors, swap(factors, "dp", 1)],
        *weights,
    )
    return (merge(routes, after(returned, *grads)), *grads)


def body(tokens, cotangent, routes, expert_gates, gate_proj, up_proj, down_proj):
    groups, blocks = lax.axis_size("dp"), lax.axis_size("expert")
    width, hid = gate_proj.shape
    rows_sent = (groups - 1) * 2 * blocks * MOST * width
    grads_sent = 3 * width * hid * (groups - 1) // groups
    fits = blocks == EXPERTS and groups == 4 and hid % 256 == 0
    fits = fits and tokens.shape[0] == 128 and routes.shape[1] == 1 and width // groups % 128 == 0
    chosen = gather_body if fits and rows_sent < grads_sent else scatter_body
    return chosen(tokens, cotangent, routes, expert_gates, gate_proj, up_proj, down_proj)


def solution(mesh):
    in_specs = (
        P(("dp", "expert"), None),
        P(("dp", "expert"), None),
        P(("dp", "expert"), None),
        P(("dp", "expert"), None),
        P(None, "expert"),
        P(None, "expert"),
        P("expert", None),
    )
    out_specs = (P(("dp", "expert"), None), P("dp", "expert"), P("dp", "expert"), P("expert", "dp"))
    return jax.shard_map(body, mesh=mesh, in_specs=in_specs, out_specs=out_specs, check_vma=False)
```

```python
import jax
import jax.numpy as jnp
from jax import lax
from jax.experimental import pallas as pl
from jax.experimental.pallas import tpu as pltpu
from jax.sharding import PartitionSpec as P

EXPERTS = 8
MOST = 18
ROWS = 16
VMEM_BYTES = (63 * 1024 + 768) * 1024


def build_slots(routes, capacity):
    flat_routes = routes.reshape(-1)
    one_hot = (flat_routes[:, None] == jnp.arange(EXPERTS, dtype=jnp.int32)[None, :]).astype(
        jnp.int32
    )
    before = jnp.cumsum(one_hot, axis=0) - one_hot
    position = jnp.sum(before * one_hot, axis=1)
    return flat_routes * capacity + position


def scatter_body(tokens, cotangent, routes, expert_gates, gate_proj, up_proj, down_proj):
    tok_dev, model_dim = tokens.shape
    top_k = routes.shape[1]
    expert_devs = lax.axis_size("expert")
    group_size = expert_devs // EXPERTS
    capacity = MOST
    slot_total = EXPERTS * capacity
    slot_of = build_slots(routes, capacity)
    owners = jnp.arange(tok_dev * top_k, dtype=jnp.int32) // top_k
    slot_table = jnp.full((slot_total,), tok_dev, jnp.int32).at[slot_of].set(owners)
    slot_gate = jnp.zeros((slot_total,), jnp.float32).at[slot_of].set(expert_gates.reshape(-1))
    x_slots = jnp.take(tokens, slot_table, axis=0, mode="fill", fill_value=0)
    dy_slots = (
        jnp.take(cotangent, slot_table, axis=0, mode="fill", fill_value=0).astype(jnp.float32)
        * slot_gate[:, None]
    ).astype(jnp.bfloat16)

    def copies(values):
        spread = values.reshape(EXPERTS, 1, capacity, model_dim)
        return jnp.broadcast_to(spread, (EXPERTS, group_size, capacity, model_dim)).reshape(
            expert_devs, capacity, model_dim
        )

    x_recv, dy_recv = (
        lax.all_to_all(copies(x_slots), "expert", split_axis=0, concat_axis=0, tiled=True),
        lax.all_to_all(copies(dy_slots), "expert", split_axis=0, concat_axis=0, tiled=True),
    )
    in_rows = x_recv.reshape(expert_devs * capacity, model_dim)
    scaled = dy_recv.reshape(expert_devs * capacity, model_dim)
    pre_gate = jnp.dot(in_rows, gate_proj, preferred_element_type=jnp.float32)
    pre_up = jnp.dot(in_rows, up_proj, preferred_element_type=jnp.float32)
    gate_sig = jax.nn.sigmoid(pre_gate)
    hidden = (pre_gate * gate_sig * pre_up).astype(jnp.bfloat16)
    by_width = (((1,), (1,)), ((), ()))
    by_rows = (((0,), (0,)), ((), ()))
    d_hidden = lax.dot_general(scaled, down_proj, by_width, preferred_element_type=jnp.float32)
    d_gate = (d_hidden * pre_up * gate_sig * (1.0 + pre_gate * (1.0 - gate_sig))).astype(
        jnp.bfloat16
    )
    d_up = (d_hidden * pre_gate * gate_sig).astype(jnp.bfloat16)
    grad_down = lax.dot_general(hidden, scaled, by_rows, preferred_element_type=jnp.float32)
    grad_gate = lax.dot_general(in_rows, d_gate, by_rows, preferred_element_type=jnp.float32)
    grad_up = lax.dot_general(in_rows, d_up, by_rows, preferred_element_type=jnp.float32)
    grad_gate, grad_up, grad_down = (
        lax.psum_scatter(
            grad_gate.astype(jnp.bfloat16), "dp", scatter_dimension=0, tiled=True
        ).astype(jnp.float32),
        lax.psum_scatter(
            grad_up.astype(jnp.bfloat16), "dp", scatter_dimension=0, tiled=True
        ).astype(jnp.float32),
        lax.psum_scatter(
            grad_down.astype(jnp.bfloat16), "dp", scatter_dimension=1, tiled=True
        ).astype(jnp.float32),
    )
    joined_grads = jnp.concatenate([d_gate, d_up], 1)
    joined_proj = jnp.concatenate([gate_proj, up_proj], 1)
    partial_value = lax.dot_general(
        joined_grads, joined_proj, by_width, preferred_element_type=jnp.float32
    ).astype(jnp.bfloat16)
    returned = lax.all_to_all(
        partial_value.reshape(expert_devs, capacity, model_dim),
        "expert",
        split_axis=0,
        concat_axis=0,
        tiled=True,
    )
    summed = jnp.sum(
        returned.reshape(EXPERTS, group_size, capacity, model_dim).astype(jnp.float32), axis=1
    )
    summed = summed.reshape(slot_total, model_dim)
    grad_input = jnp.take(summed, slot_of, axis=0).reshape(tok_dev, top_k, model_dim).sum(axis=1)
    return (grad_input.astype(jnp.bfloat16), grad_gate, grad_up, grad_down)


BY_WIDTH = (((1,), (1,)), ((), ()))
BY_ROWS = (((0,), (0,)), ((), ()))


def cut(width):
    pieces = ROWS // (MOST - ROWS)
    return pieces, width // pieces


def width_of(packed):
    pieces = ROWS // (MOST - ROWS)
    return packed.shape[2] * pieces // (pieces + 1)


def cost(flops, moved):
    return pl.CostEstimate(flops=flops, bytes_accessed=moved, transcendentals=0)


def params():
    return pltpu.CompilerParams(vmem_limit_bytes=VMEM_BYTES)


def anywhere(count):
    return [pl.BlockSpec(memory_space=pl.ANY)] * count


def dot(left, right, dims=(((1,), (0,)), ((), ()))):
    return lax.dot_general(left, right, dims, preferred_element_type=jnp.float32)


def ones(mask):
    return jnp.where(mask, 1.0, 0.0).astype(jnp.bfloat16)


def start(pairs, arrived, first=0):
    for at, (source, target) in enumerate(pairs):
        if at >= first:
            pltpu.make_async_copy(source, target, arrived.at[at]).start()


def wait(pairs, arrived, first=0):
    for at, (source, target) in enumerate(pairs):
        if at >= first:
            pltpu.make_async_copy(source, target, arrived.at[at]).wait()


def slot_masks(routes, blocks, width, me=0):
    tokens = routes.shape[1]
    pieces, _ = cut(width)
    experts = lax.broadcasted_iota(jnp.int32, (EXPERTS, tokens), 0)
    named = jnp.where(experts == routes, 1.0, 0.0)
    earlier = lax.broadcasted_iota(jnp.int32, (tokens, tokens), 0) < lax.broadcasted_iota(
        jnp.int32, (tokens, tokens), 1
    )
    before = dot(named.astype(jnp.bfloat16), ones(earlier))
    position = jnp.sum(before * named, axis=0, keepdims=True).astype(jnp.int32)
    slot = lax.broadcasted_iota(jnp.int32, (blocks * ROWS, tokens), 0)
    row = slot % ROWS
    mine = (slot // ROWS) ^ me == routes
    main = mine & (position == row)
    spill = mine & (position == ROWS + row // pieces)
    return main, spill, row % pieces


def pack(blocks, me, routes, gates, tokens, cotangent):
    count, width = tokens.shape
    pieces, step = cut(width)
    sources = (routes, gates, tokens, cotangent)

    def kernel(me_ref, *refs):
        outs, held, arrived = refs[4 : 4 + blocks], refs[4 + blocks : 8 + blocks], refs[-1]
        pairs = list(zip(refs[:4], held))
        start(pairs, arrived)
        wait(pairs[:2], arrived)
        main, spill, piece = slot_masks(held[0][...], blocks, width, me_ref[0])
        mains = ones(main)
        picks = [ones(spill & (piece == at)) for at in range(pieces)]
        main_scale = jnp.sum(jnp.where(main, held[1][...], 0.0), axis=1, keepdims=True)
        spill_scale = jnp.sum(jnp.where(spill, held[1][...], 0.0), axis=1, keepdims=True)
        for half in range(2):
            wait(pairs[: 3 + half], arrived, 2 + half)
            values = held[2 + half]
            rows = dot(mains, values[...])
            extra = jnp.zeros((blocks * ROWS, step), jnp.float32)
            for at in range(pieces):
                extra += dot(picks[at], values[:, at * step : (at + 1) * step])
            if half > 0:
                rows, extra = rows * main_scale, extra * spill_scale
            rows = rows.astype(jnp.bfloat16)
            extra = extra.astype(jnp.bfloat16)
            here = slice(half * ROWS, (half + 1) * ROWS)
            for block in range(blocks):
                part = slice(block * ROWS, (block + 1) * ROWS)
                outs[block][here, :width] = rows[part]
                outs[block][here, width:] = extra[part]

    inside = pl.BlockSpec(memory_space=pltpu.VMEM)
    return pl.pallas_call(
        kernel,
        out_shape=[jax.ShapeDtypeStruct((2 * ROWS, width + step), jnp.bfloat16)] * blocks,
        in_specs=[pl.BlockSpec(memory_space=pltpu.SMEM)] + anywhere(4),
        out_specs=[inside] * blocks,
        scratch_shapes=[pltpu.VMEM(source.shape, source.dtype) for source in sources]
        + [pltpu.SemaphoreType.DMA((4,))],
        compiler_params=params(),
        cost_estimate=cost(8 * blocks * ROWS * count * width, 8 * count * width),
        name="pack",
    )(me, *sources)


def join(received):
    count = len(received)

    def kernel(*refs):
        pairs = [(refs[at], refs[count].at[at]) for at in range(count)]
        start(pairs, refs[-1])
        wait(pairs, refs[-1])

    return pl.pallas_call(
        kernel,
        out_shape=jax.ShapeDtypeStruct((count,) + received[0].shape, jnp.bfloat16),
        in_specs=anywhere(count),
        out_specs=pl.BlockSpec(memory_space=pltpu.VMEM),
        scratch_shapes=[pltpu.SemaphoreType.DMA((count,))],
        compiler_params=params(),
        cost_estimate=cost(0, 4 * received[0].size * count),
        name="join",
    )(*received)


def merge(routes, returned):
    blocks = returned.shape[0]
    tokens = routes.shape[1]
    width = width_of(returned)
    pieces, step = cut(width)

    def kernel(routes_ref, back_ref, out, named, held, arrived):
        pairs = [(routes_ref, named), (back_ref, held)]
        start(pairs, arrived)
        wait(pairs[:1], arrived)
        main, spill, piece = slot_masks(named[...], blocks, width)
        mains = ones(main)
        picks = [ones(spill & (piece == at)) for at in range(pieces)]
        wait(pairs, arrived, 1)
        rows = jnp.concatenate([held[at, :, :width] for at in range(blocks)], 0)
        extra = jnp.concatenate([held[at, :, width:] for at in range(blocks)], 0)
        picked = dot(mains, rows, BY_ROWS)
        for at in range(pieces):
            columns = slice(at * step, (at + 1) * step)
            out[:, columns] = (picked[:, columns] + dot(picks[at], extra, BY_ROWS)).astype(
                jnp.bfloat16
            )

    return pl.pallas_call(
        kernel,
        out_shape=jax.ShapeDtypeStruct((tokens, width), jnp.bfloat16),
        in_specs=anywhere(2),
        out_specs=pl.BlockSpec(memory_space=pltpu.VMEM),
        scratch_shapes=[
            pltpu.VMEM(routes.shape, routes.dtype),
            pltpu.VMEM(returned.shape, returned.dtype),
            pltpu.SemaphoreType.DMA((2,)),
        ],
        compiler_params=params(),
        cost_estimate=cost(4 * blocks * ROWS * tokens * width, 4 * tokens * width),
        name="merge",
    )(routes, returned)


def spill_picks(blocks, pieces, at):
    shape = (blocks * (MOST - ROWS), blocks * ROWS)
    slot = lax.broadcasted_iota(jnp.int32, shape, 0)
    row = lax.broadcasted_iota(jnp.int32, shape, 1)
    return ones(row == slot * pieces + at)


def unpack(main, tail, pieces, begin, first, out):
    blocks = main.shape[0]
    step = tail.shape[2]
    for at in range(blocks):
        out[first + at * ROWS : first + (at + 1) * ROWS, :] = main[at]
    extra = jnp.concatenate([tail[at] for at in range(blocks)], 0)
    spill = slice(first + blocks * ROWS, first + blocks * MOST)
    for at in range(out.shape[1] // step):
        out[spill, at * step : (at + 1) * step] = dot(
            spill_picks(blocks, pieces, begin + at), extra
        ).astype(jnp.bfloat16)


def column_tile(width, tile):
    return pl.BlockSpec((width, tile), lambda i: (0, i))


def row_tile(tile, width):
    return pl.BlockSpec((tile, width), lambda i: (i, 0))


def tile_of(index, tile):
    return pl.ds(pl.multiple_of(index * tile, tile), tile)


def weight_copy(source, target, arrived, index, axis, tile):
    here = tile_of(index, tile)
    view = source.at[:, here] if axis else source.at[here, :]
    return pltpu.make_async_copy(view, target.at[index], arrived.at[index])


def halves(parts, half, out):
    here = slice(half * ROWS, (half + 1) * ROWS)
    count = parts[0].shape[0]
    return [
        (part.at[:, here, :], out.at[at * count : (at + 1) * count])
        for at, part in enumerate(parts)
    ]


def hidden_grads(pre_gate, pre_up, d_hidden):
    sig = jax.nn.sigmoid(pre_gate)
    silu = pre_gate * sig
    hidden = (silu * pre_up).astype(jnp.bfloat16)
    d_gate = (d_hidden * pre_up * sig * (1.0 + pre_gate * (1.0 - sig))).astype(jnp.bfloat16)
    d_up = (d_hidden * silu).astype(jnp.bfloat16)
    return hidden, d_gate, d_up


def back(tile, me, parts, gate_proj, up_proj, down_proj):
    count = len(parts)
    blocks = count * parts[0].shape[0]
    width, hid = gate_proj.shape
    slots = blocks * MOST
    pieces, step = cut(width)
    tiles = hid // tile
    chunk = 2 * step
    chunks = width // chunk
    shape = (blocks, ROWS, width + step)

    def kernel(me_ref, *refs):
        refs = list(refs)
        part_refs = [refs.pop(0) for _ in range(count)]
        gate_ref, up_ref, down_ref, out, factors_ref = [refs.pop(0) for _ in range(5)]
        x_held, dy_held, rows, scaled, factors = [refs.pop(0) for _ in range(5)]
        tail, staged, gate, up, down = [refs.pop(0) for _ in range(5)]
        x_in, dy_in, gate_in, up_in, down_in, gone = refs
        now = pl.program_id(0)
        x_pairs, dy_pairs = halves(part_refs, 0, x_held), halves(part_refs, 1, dy_held)

        def column_copy(source, target, arrived, index):
            here = tile_of(index, tile)
            return pltpu.make_async_copy(
                source.at[:, here], target.at[:, here], arrived.at[index]
            )

        def fetch_x(index):
            column_copy(gate_ref, gate, gate_in, index).start()
            column_copy(up_ref, up, up_in, index).start()

        def fetch_dy(index):
            weight_copy(down_ref, down, down_in, index, 0, tile).start()

        def leave(index):
            columns = tile_of(index, chunk)
            return pltpu.make_async_copy(
                staged.at[:, :, columns], out.at[:, :, columns], gone.at[index]
            )

        def leave_factors():
            return pltpu.make_async_copy(factors, factors_ref, gone.at[chunks + 1])

        @pl.when(now == 0)
        def _():
            start(x_pairs, x_in)
            fetch_x(0)
            wait(x_pairs, x_in)
            start(dy_pairs, dy_in)
            fetch_dy(0)
            unpack(x_held.at[:, :, :width], x_held.at[:, :, width:], pieces, 0, 0, rows)
            tail[...] = jnp.zeros_like(tail)

        @pl.when(now < tiles)
        def _():
            columns = tile_of(now, tile)
            column_copy(gate_ref, gate, gate_in, now).wait()
            pre_gate = dot(rows[...], gate[:, columns])

            @pl.when(now < tiles - 1)
            def _():
                fetch_x(now + 1)

            column_copy(up_ref, up, up_in, now).wait()
            pre_up = dot(rows[...], up[:, columns])

            @pl.when(now == 0)
            def _():
                wait(dy_pairs, dy_in)
                unpack(dy_held.at[:, :, :width], dy_held.at[:, :, width:], pieces, 0, 0, scaled)

            @pl.when(now < tiles - 1)
            def _():
                fetch_dy(now + 1)

            weight_copy(down_ref, down, down_in, now, 0, tile).wait()
            d_hidden = dot(scaled[...], down[now], BY_WIDTH)
            made, d_gate, d_up = hidden_grads(pre_gate, pre_up, d_hidden)
            factors[:, columns] = made
            factors[:, tile_of(tiles + now, tile)] = d_gate
            factors[:, tile_of(2 * tiles + now, tile)] = d_up

        @pl.when(now == tiles)
        def _():
            leave_factors().start()

        @pl.when(now >= tiles)
        def _():
            at = now - tiles
            here = tile_of(at, chunk)
            done = dot(factors[:, hid : 2 * hid], gate[here, :], BY_WIDTH)
            done += dot(factors[:, 2 * hid :], up[here, :], BY_WIDTH)
            done = done.astype(jnp.bfloat16)
            for block in range(blocks):
                staged[me_ref[0] ^ block, :, here] = done[block * ROWS : (block + 1) * ROWS]
            leave(at).start()
            for piece in range(chunk // step):
                tail[...] += dot(
                    spill_picks(blocks, pieces, at * (chunk // step) + piece),
                    done[blocks * ROWS :, piece * step : (piece + 1) * step],
                    BY_ROWS,
                )

        @pl.when(now == tiles + chunks - 1)
        def _():
            for block in range(blocks):
                part = tail[block * ROWS : (block + 1) * ROWS, :]
                staged[me_ref[0] ^ block, :, width:] = part.astype(jnp.bfloat16)
            last = pltpu.make_async_copy(
                staged.at[:, :, width:], out.at[:, :, width:], gone.at[chunks]
            )
            last.start()
            for at in range(chunks):
                leave(at).wait()
            leave_factors().wait()
            last.wait()

    return pl.pallas_call(
        kernel,
        grid=(tiles + chunks,),
        out_shape=[
            jax.ShapeDtypeStruct(shape, jnp.bfloat16),
            jax.ShapeDtypeStruct((slots, 3 * hid), jnp.bfloat16),
        ],
        in_specs=[pl.BlockSpec(memory_space=pltpu.SMEM)] + anywhere(count + 3),
        out_specs=anywhere(2),
        scratch_shapes=[
            pltpu.VMEM(shape, jnp.bfloat16),
            pltpu.VMEM(shape, jnp.bfloat16),
            pltpu.VMEM((slots, width), jnp.bfloat16),
            pltpu.VMEM((slots, width), jnp.bfloat16),
            pltpu.VMEM((slots, 3 * hid), jnp.bfloat16),
            pltpu.VMEM((blocks * ROWS, step), jnp.float32),
            pltpu.VMEM(shape, jnp.bfloat16),
            pltpu.VMEM((width, hid), jnp.bfloat16),
            pltpu.VMEM((width, hid), jnp.bfloat16),
            pltpu.VMEM((tiles, tile, width), jnp.bfloat16),
            pltpu.SemaphoreType.DMA((count,)),
            pltpu.SemaphoreType.DMA((count,)),
            pltpu.SemaphoreType.DMA((tiles,)),
            pltpu.SemaphoreType.DMA((tiles,)),
            pltpu.SemaphoreType.DMA((tiles,)),
            pltpu.SemaphoreType.DMA((chunks + 2,)),
        ],
        compiler_params=params(),
        cost_estimate=cost(0, 4 * slots * width),
        name="back",
    )(me, *parts, gate_proj, up_proj, down_proj)


def weight_grads(tile, part, parts, factors, gate_proj, up_proj, down_proj):
    groups, count = len(parts), len(parts[0])
    each = parts[0][0].shape[0]
    blocks = count * each
    hid, width = down_proj.shape
    pieces, step = cut(width)
    slots = blocks * MOST
    given = len(factors)
    some = (groups - given) * slots
    share = width // groups
    tiles = hid // tile

    def kernel(part_ref, *refs):
        refs = list(refs)
        part_refs = [[refs.pop(0) for _ in range(count)] for _ in range(groups)]
        factor_refs = [refs.pop(0) for _ in range(given)]
        gate_ref, up_ref, down_ref = [refs.pop(0) for _ in range(3)]
        d_gate_ref, d_up_ref, d_down_ref = [refs.pop(0) for _ in range(3)]
        x_held, dy_held, mains, tails, x_all, dy_all = [refs.pop(0) for _ in range(6)]
        x_mine, dy_mine, known = [refs.pop(0) for _ in range(3)]
        gate, up, down, x_in, dy_in, known_in, gate_in, up_in, down_in = refs
        now = pl.program_id(0)
        columns = pl.ds(pl.multiple_of(part_ref[0] * share, share), share)
        begin = part_ref[0] * (share // step)
        x_pairs, dy_pairs, known_pairs = [], [], []
        for at in range(given, groups):
            x_pairs += halves(part_refs[at], 0, x_held.at[at - given])
            dy_pairs += halves(part_refs[at], 1, dy_held.at[at - given])
        for at in range(given):
            known_pairs.append((factor_refs[at], known.at[at * slots : (at + 1) * slots, :]))
            for half in range(2):
                here = slice(half * ROWS, (half + 1) * ROWS)
                behind = half * given + at
                for number, ref in enumerate(part_refs[at]):
                    some_blocks = slice(number * each, (number + 1) * each)
                    known_pairs.append((ref.at[:, here, columns], mains.at[behind, some_blocks]))
                    known_pairs.append((ref.at[:, here, width:], tails.at[behind, some_blocks]))

        def arrange(held, rows_out, target):
            for at in range(groups - given):
                unpack(
                    held.at[at, :, :, :width],
                    held.at[at, :, :, width:],
                    pieces,
                    0,
                    at * slots,
                    rows_out,
                )
            target[given * slots :, :] = rows_out[:, columns]

        def fetch_x(index):
            weight_copy(gate_ref, gate, gate_in, index, 1, tile).start()
            weight_copy(up_ref, up, up_in, index, 1, tile).start()

        def fetch_dy(index):
            weight_copy(down_ref, down, down_in, index, 0, tile).start()

        @pl.when(now == 0)
        def _():
            start(x_pairs, x_in)
            fetch_x(0)
            wait(x_pairs, x_in)
            start(dy_pairs, dy_in)
            fetch_dy(0)
            arrange(x_held, x_all, x_mine)

        weight_copy(gate_ref, gate, gate_in, now, 1, tile).wait()
        pre_gate = dot(x_all[...], gate[now])
        weight_copy(up_ref, up, up_in, now, 1, tile).wait()
        pre_up = dot(x_all[...], up[now])

        @pl.when(now == 0)
        def _():
            wait(dy_pairs, dy_in)
            start(known_pairs, known_in)
            arrange(dy_held, dy_all, dy_mine)

        @pl.when(now < tiles - 1)
        def _():
            fetch_x(now + 1)
            fetch_dy(now + 1)

        weight_copy(down_ref, down, down_in, now, 0, tile).wait()
        d_hidden = dot(dy_all[...], down[now], BY_WIDTH)
        made, d_gate, d_up = hidden_grads(pre_gate, pre_up, d_hidden)

        @pl.when(now == 0)
        def _():
            wait(known_pairs, known_in)
            for at in range(given):
                unpack(mains.at[at], tails.at[at], pieces, begin, at * slots, x_mine)
                behind = given + at
                unpack(mains.at[behind], tails.at[behind], pieces, begin, at * slots, dy_mine)

        made = jnp.concatenate([known[:, tile_of(now, tile)], made], 0)
        d_gate = jnp.concatenate([known[:, tile_of(tiles + now, tile)], d_gate], 0)
        d_up = jnp.concatenate([known[:, tile_of(2 * tiles + now, tile)], d_up], 0)
        sums = dot(x_mine[...], jnp.concatenate([d_gate, d_up], 1), BY_ROWS)
        d_gate_ref[...] = sums[:, :tile]
        d_up_ref[...] = sums[:, tile:]
        d_down_ref[...] = dot(made, dy_mine[...], BY_ROWS)

    return pl.pallas_call(
        kernel,
        grid=(tiles,),
        out_shape=[
            jax.ShapeDtypeStruct((share, hid), jnp.float32),
            jax.ShapeDtypeStruct((share, hid), jnp.float32),
            jax.ShapeDtypeStruct((hid, share), jnp.float32),
        ],
        in_specs=[pl.BlockSpec(memory_space=pltpu.SMEM)] + anywhere(groups * count + given + 3),
        out_specs=[column_tile(share, tile), column_tile(share, tile), row_tile(tile, share)],
        scratch_shapes=[
            pltpu.VMEM((groups - given, blocks, ROWS, width + step), jnp.bfloat16),
            pltpu.VMEM((groups - given, blocks, ROWS, width + step), jnp.bfloat16),
            pltpu.VMEM((2 * given, blocks, ROWS, share), jnp.bfloat16),
            pltpu.VMEM((2 * given, blocks, ROWS, step), jnp.bfloat16),
            pltpu.VMEM((some, width), jnp.bfloat16),
            pltpu.VMEM((some, width), jnp.bfloat16),
            pltpu.VMEM((groups * slots, share), jnp.bfloat16),
            pltpu.VMEM((groups * slots, share), jnp.bfloat16),
            pltpu.VMEM((given * slots, 3 * hid), jnp.bfloat16),
            pltpu.VMEM((tiles, width, tile), jnp.bfloat16),
            pltpu.VMEM((tiles, width, tile), jnp.bfloat16),
            pltpu.VMEM((tiles, tile, width), jnp.bfloat16),
            pltpu.SemaphoreType.DMA(((groups - given) * count,)),
            pltpu.SemaphoreType.DMA(((groups - given) * count,)),
            pltpu.SemaphoreType.DMA(((1 + 4 * count) * given,)),
            pltpu.SemaphoreType.DMA((tiles,)),
            pltpu.SemaphoreType.DMA((tiles,)),
            pltpu.SemaphoreType.DMA((tiles,)),
        ],
        compiler_params=params(),
        cost_estimate=cost(0, 4 * slots * width),
        name="weight_grads",
    )(part, *[one for group in parts for one in group], *factors, gate_proj, up_proj, down_proj)


def swap(value, axis, distance):
    size = lax.axis_size(axis)
    return lax.ppermute(value, axis, [(at, at ^ distance) for at in range(size)])


def exchange(blocks):
    return lax.all_to_all(blocks, "expert", split_axis=0, concat_axis=0, tiled=True)


def after(value, *earlier):
    return lax.optimization_barrier((value, *earlier))[0]


def gather_body(tokens, cotangent, routes, expert_gates, gate_proj, up_proj, down_proj):
    blocks = lax.axis_size("expert")
    tile = 256
    me = lax.axis_index("expert").astype(jnp.int32).reshape(1)
    part = lax.axis_index("dp").astype(jnp.int32).reshape(1)
    routes = routes.reshape(1, -1)
    gates = expert_gates.reshape(1, -1)
    weights = (gate_proj, up_proj, down_proj)
    received = list(pack(blocks, me, routes, gates, tokens, cotangent))
    half = blocks // 2
    order = [7, 6, 3, 2, 1, 5, 4]
    for distance in order:
        received[distance] = swap(received[distance], "expert", distance)
    *received[1:half], received[6], received[7] = lax.optimization_barrier(
        (*received[1:half], received[6], received[7])
    )
    first = join(received[:half])
    far = swap(first, "dp", 2)
    near = swap(first, "dp", 1)
    *received[half:], far, near = lax.optimization_barrier((*received[half:], far, near))
    last = swap(far, "dp", 1)
    second = join(received[half:])
    second_far = swap(second, "dp", 2)
    second_near = swap(second, "dp", 1)
    sent, factors = back(tile, me, [first, second], *weights)
    sent, factors, last, second_near = lax.optimization_barrier(
        (sent, factors, last, second_near)
    )
    returned = exchange(sent)
    second_last = swap(after(second_far, sent), "dp", 1)
    grads = weight_grads(
        tile,
        part,
        [[first, second], [near, second_near], [far, second_far], [last, second_last]],
        [factors, swap(factors, "dp", 1)],
        *weights,
    )
    return (merge(routes, after(returned, *grads)), *grads)


def body(tokens, cotangent, routes, expert_gates, gate_proj, up_proj, down_proj):
    groups, blocks = lax.axis_size("dp"), lax.axis_size("expert")
    width, hid = gate_proj.shape
    rows_sent = (groups - 1) * 2 * blocks * MOST * width
    grads_sent = 3 * width * hid * (groups - 1) // groups
    fits = blocks == EXPERTS and groups == 4 and hid % 256 == 0
    fits = fits and tokens.shape[0] == 128 and routes.shape[1] == 1 and width // groups % 128 == 0
    chosen = gather_body if fits and rows_sent < grads_sent else scatter_body
    return chosen(tokens, cotangent, routes, expert_gates, gate_proj, up_proj, down_proj)


def solution(mesh):
    in_specs = (
        P(("dp", "expert"), None),
        P(("dp", "expert"), None),
        P(("dp", "expert"), None),
        P(("dp", "expert"), None),
        P(None, "expert"),
        P(None, "expert"),
        P("expert", None),
    )
    out_specs = (P(("dp", "expert"), None), P("dp", "expert"), P("dp", "expert"), P("expert", "dp"))
    return jax.shard_map(body, mesh=mesh, in_specs=in_specs, out_specs=out_specs, check_vma=False)
```

```python
import jax
import jax.numpy as jnp
from jax import lax
from jax.experimental import pallas as pl
from jax.experimental.pallas import tpu as pltpu
from jax.sharding import PartitionSpec as P

EXPERTS = 8
MOST = 18
ROWS = 16
VMEM_BYTES = (63 * 1024 + 768) * 1024


def build_slots(routes, capacity):
    flat_routes = routes.reshape(-1)
    one_hot = (flat_routes[:, None] == jnp.arange(EXPERTS, dtype=jnp.int32)[None, :]).astype(
        jnp.int32
    )
    before = jnp.cumsum(one_hot, axis=0) - one_hot
    position = jnp.sum(before * one_hot, axis=1)
    return flat_routes * capacity + position


def scatter_body(tokens, cotangent, routes, expert_gates, gate_proj, up_proj, down_proj):
    tok_dev, model_dim = tokens.shape
    top_k = routes.shape[1]
    expert_devs = lax.axis_size("expert")
    group_size = expert_devs // EXPERTS
    capacity = MOST
    slot_total = EXPERTS * capacity
    slot_of = build_slots(routes, capacity)
    owners = jnp.arange(tok_dev * top_k, dtype=jnp.int32) // top_k
    slot_table = jnp.full((slot_total,), tok_dev, jnp.int32).at[slot_of].set(owners)
    slot_gate = jnp.zeros((slot_total,), jnp.float32).at[slot_of].set(expert_gates.reshape(-1))
    x_slots = jnp.take(tokens, slot_table, axis=0, mode="fill", fill_value=0)
    dy_slots = (
        jnp.take(cotangent, slot_table, axis=0, mode="fill", fill_value=0).astype(jnp.float32)
        * slot_gate[:, None]
    ).astype(jnp.bfloat16)

    def copies(values):
        spread = values.reshape(EXPERTS, 1, capacity, model_dim)
        return jnp.broadcast_to(spread, (EXPERTS, group_size, capacity, model_dim)).reshape(
            expert_devs, capacity, model_dim
        )

    x_recv, dy_recv = (
        lax.all_to_all(copies(x_slots), "expert", split_axis=0, concat_axis=0, tiled=True),
        lax.all_to_all(copies(dy_slots), "expert", split_axis=0, concat_axis=0, tiled=True),
    )
    in_rows = x_recv.reshape(expert_devs * capacity, model_dim)
    scaled = dy_recv.reshape(expert_devs * capacity, model_dim)
    pre_gate = jnp.dot(in_rows, gate_proj, preferred_element_type=jnp.float32)
    pre_up = jnp.dot(in_rows, up_proj, preferred_element_type=jnp.float32)
    gate_sig = jax.nn.sigmoid(pre_gate)
    hidden = (pre_gate * gate_sig * pre_up).astype(jnp.bfloat16)
    by_width = (((1,), (1,)), ((), ()))
    by_rows = (((0,), (0,)), ((), ()))
    d_hidden = lax.dot_general(scaled, down_proj, by_width, preferred_element_type=jnp.float32)
    d_gate = (d_hidden * pre_up * gate_sig * (1.0 + pre_gate * (1.0 - gate_sig))).astype(
        jnp.bfloat16
    )
    d_up = (d_hidden * pre_gate * gate_sig).astype(jnp.bfloat16)
    grad_down = lax.dot_general(hidden, scaled, by_rows, preferred_element_type=jnp.float32)
    grad_gate = lax.dot_general(in_rows, d_gate, by_rows, preferred_element_type=jnp.float32)
    grad_up = lax.dot_general(in_rows, d_up, by_rows, preferred_element_type=jnp.float32)
    grad_gate, grad_up, grad_down = (
        lax.psum_scatter(
            grad_gate.astype(jnp.bfloat16), "dp", scatter_dimension=0, tiled=True
        ).astype(jnp.float32),
        lax.psum_scatter(
            grad_up.astype(jnp.bfloat16), "dp", scatter_dimension=0, tiled=True
        ).astype(jnp.float32),
        lax.psum_scatter(
            grad_down.astype(jnp.bfloat16), "dp", scatter_dimension=1, tiled=True
        ).astype(jnp.float32),
    )
    joined_grads = jnp.concatenate([d_gate, d_up], 1)
    joined_proj = jnp.concatenate([gate_proj, up_proj], 1)
    partial_value = lax.dot_general(
        joined_grads, joined_proj, by_width, preferred_element_type=jnp.float32
    ).astype(jnp.bfloat16)
    returned = lax.all_to_all(
        partial_value.reshape(expert_devs, capacity, model_dim),
        "expert",
        split_axis=0,
        concat_axis=0,
        tiled=True,
    )
    summed = jnp.sum(
        returned.reshape(EXPERTS, group_size, capacity, model_dim).astype(jnp.float32), axis=1
    )
    summed = summed.reshape(slot_total, model_dim)
    grad_input = jnp.take(summed, slot_of, axis=0).reshape(tok_dev, top_k, model_dim).sum(axis=1)
    return (grad_input.astype(jnp.bfloat16), grad_gate, grad_up, grad_down)


BY_WIDTH = (((1,), (1,)), ((), ()))
BY_ROWS = (((0,), (0,)), ((), ()))


def cut(width):
    pieces = ROWS // (MOST - ROWS)
    return pieces, width // pieces


def width_of(packed):
    pieces = ROWS // (MOST - ROWS)
    return packed.shape[2] * pieces // (pieces + 1)


def cost(flops, moved):
    return pl.CostEstimate(flops=flops, bytes_accessed=moved, transcendentals=0)


def params():
    return pltpu.CompilerParams(vmem_limit_bytes=VMEM_BYTES)


def anywhere(count):
    return [pl.BlockSpec(memory_space=pl.ANY)] * count


def dot(left, right, dims=(((1,), (0,)), ((), ()))):
    return lax.dot_general(left, right, dims, preferred_element_type=jnp.float32)


def ones(mask):
    return jnp.where(mask, 1.0, 0.0).astype(jnp.bfloat16)


def start(pairs, arrived, first=0):
    for at, (source, target) in enumerate(pairs):
        if at >= first:
            pltpu.make_async_copy(source, target, arrived.at[at]).start()


def wait(pairs, arrived, first=0):
    for at, (source, target) in enumerate(pairs):
        if at >= first:
            pltpu.make_async_copy(source, target, arrived.at[at]).wait()


def slot_masks(routes, blocks, width, me=0):
    tokens = routes.shape[1]
    pieces, _ = cut(width)
    experts = lax.broadcasted_iota(jnp.int32, (EXPERTS, tokens), 0)
    named = jnp.where(experts == routes, 1.0, 0.0)
    earlier = lax.broadcasted_iota(jnp.int32, (tokens, tokens), 0) < lax.broadcasted_iota(
        jnp.int32, (tokens, tokens), 1
    )
    before = dot(named.astype(jnp.bfloat16), ones(earlier))
    position = jnp.sum(before * named, axis=0, keepdims=True).astype(jnp.int32)
    slot = lax.broadcasted_iota(jnp.int32, (blocks * ROWS, tokens), 0)
    row = slot % ROWS
    mine = (slot // ROWS) ^ me == routes
    main = mine & (position == row)
    spill = mine & (position == ROWS + row // pieces)
    return main, spill, row % pieces


def pack(blocks, me, routes, gates, tokens, cotangent):
    count, width = tokens.shape
    pieces, step = cut(width)
    sources = (routes, gates, tokens, cotangent)

    def kernel(me_ref, *refs):
        outs, held, arrived = refs[4 : 4 + blocks], refs[4 + blocks : 8 + blocks], refs[-1]
        pairs = list(zip(refs[:4], held))
        start(pairs, arrived)
        wait(pairs[:2], arrived)
        main, spill, piece = slot_masks(held[0][...], blocks, width, me_ref[0])
        mains = ones(main)
        picks = [ones(spill & (piece == at)) for at in range(pieces)]
        main_scale = jnp.sum(jnp.where(main, held[1][...], 0.0), axis=1, keepdims=True)
        spill_scale = jnp.sum(jnp.where(spill, held[1][...], 0.0), axis=1, keepdims=True)
        for half in range(2):
            wait(pairs[: 3 + half], arrived, 2 + half)
            values = held[2 + half]
            rows = dot(mains, values[...])
            extra = jnp.zeros((blocks * ROWS, step), jnp.float32)
            for at in range(pieces):
                extra += dot(picks[at], values[:, at * step : (at + 1) * step])
            if half > 0:
                rows, extra = rows * main_scale, extra * spill_scale
            rows = rows.astype(jnp.bfloat16)
            extra = extra.astype(jnp.bfloat16)
            here = slice(half * ROWS, (half + 1) * ROWS)
            for block in range(blocks):
                part = slice(block * ROWS, (block + 1) * ROWS)
                outs[block][here, :width] = rows[part]
                outs[block][here, width:] = extra[part]

    inside = pl.BlockSpec(memory_space=pltpu.VMEM)
    return pl.pallas_call(
        kernel,
        out_shape=[jax.ShapeDtypeStruct((2 * ROWS, width + step), jnp.bfloat16)] * blocks,
        in_specs=[pl.BlockSpec(memory_space=pltpu.SMEM)] + anywhere(4),
        out_specs=[inside] * blocks,
        scratch_shapes=[pltpu.VMEM(source.shape, source.dtype) for source in sources]
        + [pltpu.SemaphoreType.DMA((4,))],
        compiler_params=params(),
        cost_estimate=cost(8 * blocks * ROWS * count * width, 8 * count * width),
        name="pack",
    )(me, *sources)


def merge(routes, returned):
    blocks = returned.shape[0]
    tokens = routes.shape[1]
    width = width_of(returned)
    pieces, step = cut(width)

    def kernel(routes_ref, back_ref, out, named, held, arrived):
        pairs = [(routes_ref, named), (back_ref, held)]
        start(pairs, arrived)
        wait(pairs[:1], arrived)
        main, spill, piece = slot_masks(named[...], blocks, width)
        mains = ones(main)
        picks = [ones(spill & (piece == at)) for at in range(pieces)]
        wait(pairs, arrived, 1)
        rows = jnp.concatenate([held[at, :, :width] for at in range(blocks)], 0)
        extra = jnp.concatenate([held[at, :, width:] for at in range(blocks)], 0)
        picked = dot(mains, rows, BY_ROWS)
        for at in range(pieces):
            columns = slice(at * step, (at + 1) * step)
            out[:, columns] = (picked[:, columns] + dot(picks[at], extra, BY_ROWS)).astype(
                jnp.bfloat16
            )

    return pl.pallas_call(
        kernel,
        out_shape=jax.ShapeDtypeStruct((tokens, width), jnp.bfloat16),
        in_specs=anywhere(2),
        out_specs=pl.BlockSpec(memory_space=pltpu.VMEM),
        scratch_shapes=[
            pltpu.VMEM(routes.shape, routes.dtype),
            pltpu.VMEM(returned.shape, returned.dtype),
            pltpu.SemaphoreType.DMA((2,)),
        ],
        compiler_params=params(),
        cost_estimate=cost(4 * blocks * ROWS * tokens * width, 4 * tokens * width),
        name="merge",
    )(routes, returned)


def spill_picks(blocks, pieces, at):
    shape = (blocks * (MOST - ROWS), blocks * ROWS)
    slot = lax.broadcasted_iota(jnp.int32, shape, 0)
    row = lax.broadcasted_iota(jnp.int32, shape, 1)
    return ones(row == slot * pieces + at)


def unpack(main, tail, pieces, begin, first, out):
    blocks = main.shape[0]
    step = tail.shape[2]
    for at in range(blocks):
        out[first + at * ROWS : first + (at + 1) * ROWS, :] = main[at]
    extra = jnp.concatenate([tail[at] for at in range(blocks)], 0)
    spill = slice(first + blocks * ROWS, first + blocks * MOST)
    for at in range(out.shape[1] // step):
        out[spill, at * step : (at + 1) * step] = dot(
            spill_picks(blocks, pieces, begin + at), extra
        ).astype(jnp.bfloat16)


def column_tile(width, tile):
    return pl.BlockSpec((width, tile), lambda i: (0, i))


def row_tile(tile, width):
    return pl.BlockSpec((tile, width), lambda i: (i, 0))


def tile_of(index, tile):
    return pl.ds(pl.multiple_of(index * tile, tile), tile)


def weight_copy(source, target, arrived, index, axis, tile):
    here = tile_of(index, tile)
    view = source.at[:, here] if axis else source.at[here, :]
    return pltpu.make_async_copy(view, target.at[index], arrived.at[index])


def halves(group, half, out):
    here = slice(half * ROWS, (half + 1) * ROWS)
    return [(block.at[here, :], out.at[at]) for at, block in enumerate(group)]


def hidden_grads(pre_gate, pre_up, d_hidden):
    sig = jax.nn.sigmoid(pre_gate)
    silu = pre_gate * sig
    hidden = (silu * pre_up).astype(jnp.bfloat16)
    d_gate = (d_hidden * pre_up * sig * (1.0 + pre_gate * (1.0 - sig))).astype(jnp.bfloat16)
    d_up = (d_hidden * silu).astype(jnp.bfloat16)
    return hidden, d_gate, d_up


def back(tile, share, me, part, group, gate_proj, up_proj, down_proj):
    blocks = len(group)
    width, hid = gate_proj.shape
    slots = blocks * MOST
    pieces, step = cut(width)
    tiles = hid // tile
    chunk = 2 * step
    chunks = width // chunk
    shape = (blocks, ROWS, width + step)
    given = 3 * hid + 2 * share

    def kernel(me_ref, part_ref, *refs):
        refs = list(refs)
        group_refs = [refs.pop(0) for _ in range(blocks)]
        gate_ref, up_ref, down_ref, out, kept, handed = [refs.pop(0) for _ in range(6)]
        x_held, dy_held, rows, scaled, factors, cuts = [refs.pop(0) for _ in range(6)]
        tail, staged, gate, up, down = [refs.pop(0) for _ in range(5)]
        x_in, dy_in, gate_in, up_in, down_in, gone, cut_in = refs
        now = pl.program_id(0)
        x_pairs, dy_pairs = halves(group_refs, 0, x_held), halves(group_refs, 1, dy_held)

        def column_copy(source, target, arrived, index):
            here = tile_of(index, tile)
            return pltpu.make_async_copy(
                source.at[:, here], target.at[:, here], arrived.at[index]
            )

        def fetch_x(index):
            column_copy(gate_ref, gate, gate_in, index).start()
            column_copy(up_ref, up, up_in, index).start()

        def fetch_dy(index):
            weight_copy(down_ref, down, down_in, index, 0, tile).start()

        def leave(index):
            columns = tile_of(index, chunk)
            return pltpu.make_async_copy(
                staged.at[:, :, columns], out.at[:, :, columns], gone.at[index]
            )

        def leave_factors():
            first, behind = slice(0, 3 * hid), slice(3 * hid, given)
            pairs = [(factors, kept.at[:, first]), (cuts.at[0], kept.at[:, behind])]
            return pairs + [(factors, handed.at[:, first]), (cuts.at[1], handed.at[:, behind])]

        @pl.when(now == 0)
        def _():
            start(x_pairs, x_in)
            fetch_x(0)
            wait(x_pairs, x_in)
            start(dy_pairs, dy_in)
            fetch_dy(0)
            unpack(x_held.at[:, :, :width], x_held.at[:, :, width:], pieces, 0, 0, rows)
            tail[...] = jnp.zeros_like(tail)

        @pl.when(now < tiles)
        def _():
            columns = tile_of(now, tile)
            column_copy(gate_ref, gate, gate_in, now).wait()
            pre_gate = dot(rows[...], gate[:, columns])

            @pl.when(now < tiles - 1)
            def _():
                fetch_x(now + 1)

            column_copy(up_ref, up, up_in, now).wait()
            pre_up = dot(rows[...], up[:, columns])

            @pl.when(now == 0)
            def _():
                wait(dy_pairs, dy_in)
                unpack(dy_held.at[:, :, :width], dy_held.at[:, :, width:], pieces, 0, 0, scaled)

            @pl.when(now < tiles - 1)
            def _():
                fetch_dy(now + 1)

            weight_copy(down_ref, down, down_in, now, 0, tile).wait()
            d_hidden = dot(scaled[...], down[now], BY_WIDTH)
            made, d_gate, d_up = hidden_grads(pre_gate, pre_up, d_hidden)
            factors[:, columns] = made
            factors[:, tile_of(tiles + now, tile)] = d_gate
            factors[:, tile_of(2 * tiles + now, tile)] = d_up

        @pl.when(now == tiles)
        def _():
            for at in range(2):
                columns = tile_of(part_ref[0] ^ at, share)
                cuts[at, :, :share] = rows[:, columns]
                cuts[at, :, share:] = scaled[:, columns]
            start(leave_factors(), cut_in)

        @pl.when(now >= tiles)
        def _():
            at = now - tiles
            here = tile_of(at, chunk)
            done = dot(factors[:, hid : 2 * hid], gate[here, :], BY_WIDTH)
            done += dot(factors[:, 2 * hid :], up[here, :], BY_WIDTH)
            done = done.astype(jnp.bfloat16)
            for block in range(blocks):
                staged[me_ref[0] ^ block, :, here] = done[block * ROWS : (block + 1) * ROWS]
            leave(at).start()
            for piece in range(chunk // step):
                tail[...] += dot(
                    spill_picks(blocks, pieces, at * (chunk // step) + piece),
                    done[blocks * ROWS :, piece * step : (piece + 1) * step],
                    BY_ROWS,
                )

        @pl.when(now == tiles + chunks - 1)
        def _():
            for block in range(blocks):
                part = tail[block * ROWS : (block + 1) * ROWS, :]
                staged[me_ref[0] ^ block, :, width:] = part.astype(jnp.bfloat16)
            last = pltpu.make_async_copy(
                staged.at[:, :, width:], out.at[:, :, width:], gone.at[chunks]
            )
            last.start()
            for at in range(chunks):
                leave(at).wait()
            wait(leave_factors(), cut_in)
            last.wait()

    return pl.pallas_call(
        kernel,
        grid=(tiles + chunks,),
        out_shape=[
            jax.ShapeDtypeStruct(shape, jnp.bfloat16),
            jax.ShapeDtypeStruct((slots, given), jnp.bfloat16),
            jax.ShapeDtypeStruct((slots, given), jnp.bfloat16),
        ],
        in_specs=[pl.BlockSpec(memory_space=pltpu.SMEM)] * 2 + anywhere(blocks + 3),
        out_specs=anywhere(3),
        scratch_shapes=[
            pltpu.VMEM(shape, jnp.bfloat16),
            pltpu.VMEM(shape, jnp.bfloat16),
            pltpu.VMEM((slots, width), jnp.bfloat16),
            pltpu.VMEM((slots, width), jnp.bfloat16),
            pltpu.VMEM((slots, 3 * hid), jnp.bfloat16),
            pltpu.VMEM((2, slots, 2 * share), jnp.bfloat16),
            pltpu.VMEM((blocks * ROWS, step), jnp.float32),
            pltpu.VMEM(shape, jnp.bfloat16),
            pltpu.VMEM((width, hid), jnp.bfloat16),
            pltpu.VMEM((width, hid), jnp.bfloat16),
            pltpu.VMEM((tiles, tile, width), jnp.bfloat16),
            pltpu.SemaphoreType.DMA((blocks,)),
            pltpu.SemaphoreType.DMA((blocks,)),
            pltpu.SemaphoreType.DMA((tiles,)),
            pltpu.SemaphoreType.DMA((tiles,)),
            pltpu.SemaphoreType.DMA((tiles,)),
            pltpu.SemaphoreType.DMA((chunks + 1,)),
            pltpu.SemaphoreType.DMA((4,)),
        ],
        compiler_params=params(),
        cost_estimate=cost(0, 4 * slots * width),
        name="back",
    )(me, part, *group, gate_proj, up_proj, down_proj)


def weight_grads(tile, share, part, known, groups, gate_proj, up_proj, down_proj):
    count, blocks = len(groups), len(groups[0])
    given = len(known)
    hid, width = down_proj.shape
    pieces, step = cut(width)
    slots = blocks * MOST
    total = (given + count) * slots
    tiles = hid // tile

    def kernel(part_ref, *refs):
        refs = list(refs)
        known_refs = [refs.pop(0) for _ in range(given)]
        group_refs = [[refs.pop(0) for _ in range(blocks)] for _ in range(count)]
        gate_ref, up_ref, down_ref = [refs.pop(0) for _ in range(3)]
        d_gate_ref, d_up_ref, d_down_ref = [refs.pop(0) for _ in range(3)]
        x_held, dy_held, x_all, dy_all = [refs.pop(0) for _ in range(4)]
        x_mine, dy_mine, factors = [refs.pop(0) for _ in range(3)]
        gate, up, down, x_in, dy_in, known_in, gate_in, up_in, down_in = refs
        now = pl.program_id(0)
        columns = tile_of(part_ref[0], share)
        x_pairs, dy_pairs, known_pairs = [], [], []
        for at in range(count):
            x_pairs += halves(group_refs[at], 0, x_held.at[at])
            dy_pairs += halves(group_refs[at], 1, dy_held.at[at])
        for at in range(given):
            here = slice(at * slots, (at + 1) * slots)
            behind = 3 * hid
            known_pairs += [
                (known_refs[at].at[:, :behind], factors.at[here, :]),
                (known_refs[at].at[:, behind : behind + share], x_mine.at[here, :]),
                (known_refs[at].at[:, behind + share :], dy_mine.at[here, :]),
            ]

        def arrange(held, rows_out, target):
            for at in range(count):
                unpack(
                    held.at[at, :, :, :width],
                    held.at[at, :, :, width:],
                    pieces,
                    0,
                    at * slots,
                    rows_out,
                )
            target[given * slots :, :] = rows_out[:, columns]

        def fetch_x(index):
            weight_copy(gate_ref, gate, gate_in, index, 1, tile).start()
            weight_copy(up_ref, up, up_in, index, 1, tile).start()

        def fetch_dy(index):
            weight_copy(down_ref, down, down_in, index, 0, tile).start()

        @pl.when(now == 0)
        def _():
            start(x_pairs, x_in)
            fetch_x(0)
            wait(x_pairs, x_in)
            start(dy_pairs, dy_in)
            fetch_dy(0)
            arrange(x_held, x_all, x_mine)

        weight_copy(gate_ref, gate, gate_in, now, 1, tile).wait()
        pre_gate = dot(x_all[...], gate[now])
        weight_copy(up_ref, up, up_in, now, 1, tile).wait()
        pre_up = dot(x_all[...], up[now])

        @pl.when(now == 0)
        def _():
            wait(dy_pairs, dy_in)
            start(known_pairs, known_in)
            arrange(dy_held, dy_all, dy_mine)

        @pl.when(now < tiles - 1)
        def _():
            fetch_x(now + 1)
            fetch_dy(now + 1)

        weight_copy(down_ref, down, down_in, now, 0, tile).wait()
        d_hidden = dot(dy_all[...], down[now], BY_WIDTH)
        made, d_gate, d_up = hidden_grads(pre_gate, pre_up, d_hidden)

        @pl.when(now == 0)
        def _():
            wait(known_pairs, known_in)

        made = jnp.concatenate([factors[:, tile_of(now, tile)], made], 0)
        d_gate = jnp.concatenate([factors[:, tile_of(tiles + now, tile)], d_gate], 0)
        d_up = jnp.concatenate([factors[:, tile_of(2 * tiles + now, tile)], d_up], 0)
        sums = dot(x_mine[...], jnp.concatenate([d_gate, d_up], 1), BY_ROWS)
        d_gate_ref[...] = sums[:, :tile]
        d_up_ref[...] = sums[:, tile:]
        d_down_ref[...] = dot(made, dy_mine[...], BY_ROWS)

    held = pltpu.VMEM((count, blocks, ROWS, width + step), jnp.bfloat16)
    arranged = pltpu.VMEM((count * slots, width), jnp.bfloat16)
    mine = pltpu.VMEM((total, share), jnp.bfloat16)
    return pl.pallas_call(
        kernel,
        grid=(tiles,),
        out_shape=[
            jax.ShapeDtypeStruct((share, hid), jnp.float32),
            jax.ShapeDtypeStruct((share, hid), jnp.float32),
            jax.ShapeDtypeStruct((hid, share), jnp.float32),
        ],
        in_specs=[pl.BlockSpec(memory_space=pltpu.SMEM)] + anywhere(given + count * blocks + 3),
        out_specs=[column_tile(share, tile), column_tile(share, tile), row_tile(tile, share)],
        scratch_shapes=[
            held,
            held,
            arranged,
            arranged,
            mine,
            mine,
            pltpu.VMEM((given * slots, 3 * hid), jnp.bfloat16),
            pltpu.VMEM((tiles, width, tile), jnp.bfloat16),
            pltpu.VMEM((tiles, width, tile), jnp.bfloat16),
            pltpu.VMEM((tiles, tile, width), jnp.bfloat16),
            pltpu.SemaphoreType.DMA((count * blocks,)),
            pltpu.SemaphoreType.DMA((count * blocks,)),
            pltpu.SemaphoreType.DMA((3 * given,)),
            pltpu.SemaphoreType.DMA((tiles,)),
            pltpu.SemaphoreType.DMA((tiles,)),
            pltpu.SemaphoreType.DMA((tiles,)),
        ],
        compiler_params=params(),
        cost_estimate=cost(0, 4 * slots * width),
        name="weight_grads",
    )(part, *known, *[block for group in groups for block in group], gate_proj, up_proj, down_proj)


def swap(value, axis, distance):
    size = lax.axis_size(axis)
    return lax.ppermute(value, axis, [(at, at ^ distance) for at in range(size)])


def exchange(blocks):
    return lax.all_to_all(blocks, "expert", split_axis=0, concat_axis=0, tiled=True)


def after(value, *earlier):
    return lax.optimization_barrier((value, *earlier))[0]


def gather_body(tokens, cotangent, routes, expert_gates, gate_proj, up_proj, down_proj):
    blocks = lax.axis_size("expert")
    tile, share = 256, tokens.shape[1] // lax.axis_size("dp")
    me = lax.axis_index("expert").astype(jnp.int32).reshape(1)
    part = lax.axis_index("dp").astype(jnp.int32).reshape(1)
    routes = routes.reshape(1, -1)
    gates = expert_gates.reshape(1, -1)
    weights = (gate_proj, up_proj, down_proj)
    received = list(pack(blocks, me, routes, gates, tokens, cotangent))
    for distance in reversed(range(1, blocks)):
        received[distance] = swap(received[distance], "expert", distance)
    far = [swap(block, "dp", 2) for block in received]
    sent, kept, handed = back(tile, share, me, part, received, *weights)
    returned = exchange(sent)
    far[4:] = after(far[4:], sent)
    last = [swap(block, "dp", 1) for block in far]
    known = [kept, swap(handed, "dp", 1)]
    grads = weight_grads(tile, share, part, known, [far, last], *weights)
    return (merge(routes, after(returned, *grads)), *grads)


def body(tokens, cotangent, routes, expert_gates, gate_proj, up_proj, down_proj):
    groups, blocks = lax.axis_size("dp"), lax.axis_size("expert")
    width, hid = gate_proj.shape
    rows_sent = (groups - 1) * 2 * blocks * MOST * width
    grads_sent = 3 * width * hid * (groups - 1) // groups
    fits = blocks == EXPERTS and groups == 4 and hid % 256 == 0
    fits = fits and tokens.shape[0] == 128 and routes.shape[1] == 1 and width // groups % 128 == 0
    chosen = gather_body if fits and rows_sent < grads_sent else scatter_body
    return chosen(tokens, cotangent, routes, expert_gates, gate_proj, up_proj, down_proj)


def solution(mesh):
    in_specs = (
        P(("dp", "expert"), None),
        P(("dp", "expert"), None),
        P(("dp", "expert"), None),
        P(("dp", "expert"), None),
        P(None, "expert"),
        P(None, "expert"),
        P("expert", None),
    )
    out_specs = (P(("dp", "expert"), None), P("dp", "expert"), P("dp", "expert"), P("expert", "dp"))
    return jax.shard_map(body, mesh=mesh, in_specs=in_specs, out_specs=out_specs, check_vma=False)
```

```python
import jax
import jax.numpy as jnp
from jax import lax
from jax.experimental import pallas as pl
from jax.experimental.pallas import tpu as pltpu
from jax.sharding import PartitionSpec as P

EXPERTS = 8
MOST = 18
ROWS = 16
VMEM_BYTES = (63 * 1024 + 768) * 1024


def build_slots(routes, capacity):
    flat_routes = routes.reshape(-1)
    one_hot = (flat_routes[:, None] == jnp.arange(EXPERTS, dtype=jnp.int32)[None, :]).astype(
        jnp.int32
    )
    before = jnp.cumsum(one_hot, axis=0) - one_hot
    position = jnp.sum(before * one_hot, axis=1)
    return flat_routes * capacity + position


def scatter_body(tokens, cotangent, routes, expert_gates, gate_proj, up_proj, down_proj):
    tok_dev, model_dim = tokens.shape
    top_k = routes.shape[1]
    expert_devs = lax.axis_size("expert")
    group_size = expert_devs // EXPERTS
    capacity = MOST
    slot_total = EXPERTS * capacity
    slot_of = build_slots(routes, capacity)
    owners = jnp.arange(tok_dev * top_k, dtype=jnp.int32) // top_k
    slot_table = jnp.full((slot_total,), tok_dev, jnp.int32).at[slot_of].set(owners)
    slot_gate = jnp.zeros((slot_total,), jnp.float32).at[slot_of].set(expert_gates.reshape(-1))
    x_slots = jnp.take(tokens, slot_table, axis=0, mode="fill", fill_value=0)
    dy_slots = (
        jnp.take(cotangent, slot_table, axis=0, mode="fill", fill_value=0).astype(jnp.float32)
        * slot_gate[:, None]
    ).astype(jnp.bfloat16)

    def copies(values):
        spread = values.reshape(EXPERTS, 1, capacity, model_dim)
        return jnp.broadcast_to(spread, (EXPERTS, group_size, capacity, model_dim)).reshape(
            expert_devs, capacity, model_dim
        )

    x_recv, dy_recv = (
        lax.all_to_all(copies(x_slots), "expert", split_axis=0, concat_axis=0, tiled=True),
        lax.all_to_all(copies(dy_slots), "expert", split_axis=0, concat_axis=0, tiled=True),
    )
    in_rows = x_recv.reshape(expert_devs * capacity, model_dim)
    scaled = dy_recv.reshape(expert_devs * capacity, model_dim)
    pre_gate = jnp.dot(in_rows, gate_proj, preferred_element_type=jnp.float32)
    pre_up = jnp.dot(in_rows, up_proj, preferred_element_type=jnp.float32)
    gate_sig = jax.nn.sigmoid(pre_gate)
    hidden = (pre_gate * gate_sig * pre_up).astype(jnp.bfloat16)
    by_width = (((1,), (1,)), ((), ()))
    by_rows = (((0,), (0,)), ((), ()))
    d_hidden = lax.dot_general(scaled, down_proj, by_width, preferred_element_type=jnp.float32)
    d_gate = (d_hidden * pre_up * gate_sig * (1.0 + pre_gate * (1.0 - gate_sig))).astype(
        jnp.bfloat16
    )
    d_up = (d_hidden * pre_gate * gate_sig).astype(jnp.bfloat16)
    grad_down = lax.dot_general(hidden, scaled, by_rows, preferred_element_type=jnp.float32)
    grad_gate = lax.dot_general(in_rows, d_gate, by_rows, preferred_element_type=jnp.float32)
    grad_up = lax.dot_general(in_rows, d_up, by_rows, preferred_element_type=jnp.float32)
    grad_gate, grad_up, grad_down = (
        lax.psum_scatter(
            grad_gate.astype(jnp.bfloat16), "dp", scatter_dimension=0, tiled=True
        ).astype(jnp.float32),
        lax.psum_scatter(
            grad_up.astype(jnp.bfloat16), "dp", scatter_dimension=0, tiled=True
        ).astype(jnp.float32),
        lax.psum_scatter(
            grad_down.astype(jnp.bfloat16), "dp", scatter_dimension=1, tiled=True
        ).astype(jnp.float32),
    )
    joined_grads = jnp.concatenate([d_gate, d_up], 1)
    joined_proj = jnp.concatenate([gate_proj, up_proj], 1)
    partial_value = lax.dot_general(
        joined_grads, joined_proj, by_width, preferred_element_type=jnp.float32
    ).astype(jnp.bfloat16)
    returned = lax.all_to_all(
        partial_value.reshape(expert_devs, capacity, model_dim),
        "expert",
        split_axis=0,
        concat_axis=0,
        tiled=True,
    )
    summed = jnp.sum(
        returned.reshape(EXPERTS, group_size, capacity, model_dim).astype(jnp.float32), axis=1
    )
    summed = summed.reshape(slot_total, model_dim)
    grad_input = jnp.take(summed, slot_of, axis=0).reshape(tok_dev, top_k, model_dim).sum(axis=1)
    return (grad_input.astype(jnp.bfloat16), grad_gate, grad_up, grad_down)


BY_WIDTH = (((1,), (1,)), ((), ()))
BY_ROWS = (((0,), (0,)), ((), ()))


def cut(width):
    pieces = ROWS // (MOST - ROWS)
    return pieces, width // pieces


def width_of(packed):
    pieces = ROWS // (MOST - ROWS)
    return packed.shape[2] * pieces // (pieces + 1)


def cost(flops, moved):
    return pl.CostEstimate(flops=flops, bytes_accessed=moved, transcendentals=0)


def params():
    return pltpu.CompilerParams(vmem_limit_bytes=VMEM_BYTES)


def anywhere(count):
    return [pl.BlockSpec(memory_space=pl.ANY)] * count


def dot(left, right, dims=(((1,), (0,)), ((), ()))):
    return lax.dot_general(left, right, dims, preferred_element_type=jnp.float32)


def ones(mask):
    return jnp.where(mask, 1.0, 0.0).astype(jnp.bfloat16)


def start(pairs, arrived, first=0):
    for at, (source, target) in enumerate(pairs):
        if at >= first:
            pltpu.make_async_copy(source, target, arrived.at[at]).start()


def wait(pairs, arrived, first=0):
    for at, (source, target) in enumerate(pairs):
        if at >= first:
            pltpu.make_async_copy(source, target, arrived.at[at]).wait()


def slot_masks(routes, blocks, width, me=0):
    tokens = routes.shape[1]
    pieces, _ = cut(width)
    experts = lax.broadcasted_iota(jnp.int32, (EXPERTS, tokens), 0)
    named = jnp.where(experts == routes, 1.0, 0.0)
    earlier = lax.broadcasted_iota(jnp.int32, (tokens, tokens), 0) < lax.broadcasted_iota(
        jnp.int32, (tokens, tokens), 1
    )
    before = dot(named.astype(jnp.bfloat16), ones(earlier))
    position = jnp.sum(before * named, axis=0, keepdims=True).astype(jnp.int32)
    slot = lax.broadcasted_iota(jnp.int32, (blocks * ROWS, tokens), 0)
    row = slot % ROWS
    mine = (slot // ROWS) ^ me == routes
    main = mine & (position == row)
    spill = mine & (position == ROWS + row // pieces)
    return main, spill, row % pieces


def pack(blocks, me, routes, gates, tokens, cotangent):
    count, width = tokens.shape
    pieces, step = cut(width)
    sources = (routes, gates, tokens, cotangent)

    def kernel(me_ref, *refs):
        outs, held, arrived = refs[4 : 4 + blocks], refs[4 + blocks : 8 + blocks], refs[-1]
        pairs = list(zip(refs[:4], held))
        start(pairs, arrived)
        wait(pairs[:2], arrived)
        main, spill, piece = slot_masks(held[0][...], blocks, width, me_ref[0])
        mains = ones(main)
        picks = [ones(spill & (piece == at)) for at in range(pieces)]
        main_scale = jnp.sum(jnp.where(main, held[1][...], 0.0), axis=1, keepdims=True)
        spill_scale = jnp.sum(jnp.where(spill, held[1][...], 0.0), axis=1, keepdims=True)
        for half in range(2):
            wait(pairs[: 3 + half], arrived, 2 + half)
            values = held[2 + half]
            rows = dot(mains, values[...])
            extra = jnp.zeros((blocks * ROWS, step), jnp.float32)
            for at in range(pieces):
                extra += dot(picks[at], values[:, at * step : (at + 1) * step])
            if half > 0:
                rows, extra = rows * main_scale, extra * spill_scale
            rows = rows.astype(jnp.bfloat16)
            extra = extra.astype(jnp.bfloat16)
            here = slice(half * ROWS, (half + 1) * ROWS)
            for block in range(blocks):
                part = slice(block * ROWS, (block + 1) * ROWS)
                outs[block][here, :width] = rows[part]
                outs[block][here, width:] = extra[part]

    inside = pl.BlockSpec(memory_space=pltpu.VMEM)
    return pl.pallas_call(
        kernel,
        out_shape=[jax.ShapeDtypeStruct((2 * ROWS, width + step), jnp.bfloat16)] * blocks,
        in_specs=[pl.BlockSpec(memory_space=pltpu.SMEM)] + anywhere(4),
        out_specs=[inside] * blocks,
        scratch_shapes=[pltpu.VMEM(source.shape, source.dtype) for source in sources]
        + [pltpu.SemaphoreType.DMA((4,))],
        compiler_params=params(),
        cost_estimate=cost(8 * blocks * ROWS * count * width, 8 * count * width),
        name="pack",
    )(me, *sources)


def join(received):
    count = len(received)

    def kernel(*refs):
        pairs = [(refs[at], refs[count].at[at]) for at in range(count)]
        start(pairs, refs[-1])
        wait(pairs, refs[-1])

    return pl.pallas_call(
        kernel,
        out_shape=jax.ShapeDtypeStruct((count,) + received[0].shape, jnp.bfloat16),
        in_specs=anywhere(count),
        out_specs=pl.BlockSpec(memory_space=pltpu.VMEM),
        scratch_shapes=[pltpu.SemaphoreType.DMA((count,))],
        compiler_params=params(),
        cost_estimate=cost(0, 4 * received[0].size * count),
        name="join",
    )(*received)


def merge(routes, returned):
    blocks = returned.shape[0]
    tokens = routes.shape[1]
    width = width_of(returned)
    pieces, step = cut(width)

    def kernel(routes_ref, back_ref, out, named, held, arrived):
        pairs = [(routes_ref, named), (back_ref, held)]
        start(pairs, arrived)
        wait(pairs[:1], arrived)
        main, spill, piece = slot_masks(named[...], blocks, width)
        mains = ones(main)
        picks = [ones(spill & (piece == at)) for at in range(pieces)]
        wait(pairs, arrived, 1)
        rows = jnp.concatenate([held[at, :, :width] for at in range(blocks)], 0)
        extra = jnp.concatenate([held[at, :, width:] for at in range(blocks)], 0)
        picked = dot(mains, rows, BY_ROWS)
        for at in range(pieces):
            columns = slice(at * step, (at + 1) * step)
            out[:, columns] = (picked[:, columns] + dot(picks[at], extra, BY_ROWS)).astype(
                jnp.bfloat16
            )

    return pl.pallas_call(
        kernel,
        out_shape=jax.ShapeDtypeStruct((tokens, width), jnp.bfloat16),
        in_specs=anywhere(2),
        out_specs=pl.BlockSpec(memory_space=pltpu.VMEM),
        scratch_shapes=[
            pltpu.VMEM(routes.shape, routes.dtype),
            pltpu.VMEM(returned.shape, returned.dtype),
            pltpu.SemaphoreType.DMA((2,)),
        ],
        compiler_params=params(),
        cost_estimate=cost(4 * blocks * ROWS * tokens * width, 4 * tokens * width),
        name="merge",
    )(routes, returned)


def spill_picks(blocks, pieces, at):
    shape = (blocks * (MOST - ROWS), blocks * ROWS)
    slot = lax.broadcasted_iota(jnp.int32, shape, 0)
    row = lax.broadcasted_iota(jnp.int32, shape, 1)
    return ones(row == slot * pieces + at)


def unpack(main, tail, pieces, begin, first, out):
    blocks = main.shape[0]
    step = tail.shape[2]
    for at in range(blocks):
        out[first + at * ROWS : first + (at + 1) * ROWS, :] = main[at]
    extra = jnp.concatenate([tail[at] for at in range(blocks)], 0)
    spill = slice(first + blocks * ROWS, first + blocks * MOST)
    for at in range(out.shape[1] // step):
        out[spill, at * step : (at + 1) * step] = dot(
            spill_picks(blocks, pieces, begin + at), extra
        ).astype(jnp.bfloat16)


def column_tile(width, tile):
    return pl.BlockSpec((width, tile), lambda i: (0, i))


def row_tile(tile, width):
    return pl.BlockSpec((tile, width), lambda i: (i, 0))


def tile_of(index, tile):
    return pl.ds(pl.multiple_of(index * tile, tile), tile)


def weight_copy(source, target, arrived, index, axis, tile):
    here = tile_of(index, tile)
    view = source.at[:, here] if axis else source.at[here, :]
    return pltpu.make_async_copy(view, target.at[index], arrived.at[index])


def halves(group, half, out):
    here = slice(half * ROWS, (half + 1) * ROWS)
    pairs, at = [], 0
    for item in group:
        if len(item.shape) == 2:
            pairs.append((item.at[here, :], out.at[at]))
            at += 1
        else:
            pairs.append((item.at[:, here, :], out.at[at : at + item.shape[0]]))
            at += item.shape[0]
    return pairs


def hidden_grads(pre_gate, pre_up, d_hidden):
    sig = jax.nn.sigmoid(pre_gate)
    silu = pre_gate * sig
    hidden = (silu * pre_up).astype(jnp.bfloat16)
    d_gate = (d_hidden * pre_up * sig * (1.0 + pre_gate * (1.0 - sig))).astype(jnp.bfloat16)
    d_up = (d_hidden * silu).astype(jnp.bfloat16)
    return hidden, d_gate, d_up


def back(tile, share, me, part, group, gate_proj, up_proj, down_proj):
    blocks = len(group)
    width, hid = gate_proj.shape
    slots = blocks * MOST
    pieces, step = cut(width)
    tiles = hid // tile
    chunk = 2 * step
    chunks = width // chunk
    shape = (blocks, ROWS, width + step)
    given = 3 * hid + 2 * share

    def kernel(me_ref, part_ref, *refs):
        refs = list(refs)
        group_refs = [refs.pop(0) for _ in range(blocks)]
        gate_ref, up_ref, down_ref, out, kept, handed = [refs.pop(0) for _ in range(6)]
        x_held, dy_held, rows, scaled, factors, cuts = [refs.pop(0) for _ in range(6)]
        tail, staged, gate, up, down = [refs.pop(0) for _ in range(5)]
        x_in, dy_in, gate_in, up_in, down_in, gone, cut_in = refs
        now = pl.program_id(0)
        x_pairs, dy_pairs = halves(group_refs, 0, x_held), halves(group_refs, 1, dy_held)

        def column_copy(source, target, arrived, index):
            here = tile_of(index, tile)
            return pltpu.make_async_copy(
                source.at[:, here], target.at[:, here], arrived.at[index]
            )

        def fetch_x(index):
            column_copy(gate_ref, gate, gate_in, index).start()
            column_copy(up_ref, up, up_in, index).start()

        def fetch_dy(index):
            weight_copy(down_ref, down, down_in, index, 0, tile).start()

        def leave(index):
            columns = tile_of(index, chunk)
            return pltpu.make_async_copy(
                staged.at[:, :, columns], out.at[:, :, columns], gone.at[index]
            )

        def leave_factors():
            first, behind = slice(0, 3 * hid), slice(3 * hid, given)
            pairs = [(factors, kept.at[:, first]), (cuts.at[0], kept.at[:, behind])]
            return pairs + [(factors, handed.at[:, first]), (cuts.at[1], handed.at[:, behind])]

        @pl.when(now == 0)
        def _():
            start(x_pairs, x_in)
            fetch_x(0)
            wait(x_pairs, x_in)
            start(dy_pairs, dy_in)
            fetch_dy(0)
            unpack(x_held.at[:, :, :width], x_held.at[:, :, width:], pieces, 0, 0, rows)
            tail[...] = jnp.zeros_like(tail)

        @pl.when(now < tiles)
        def _():
            columns = tile_of(now, tile)
            column_copy(gate_ref, gate, gate_in, now).wait()
            pre_gate = dot(rows[...], gate[:, columns])

            @pl.when(now < tiles - 1)
            def _():
                fetch_x(now + 1)

            column_copy(up_ref, up, up_in, now).wait()
            pre_up = dot(rows[...], up[:, columns])

            @pl.when(now == 0)
            def _():
                wait(dy_pairs, dy_in)
                unpack(dy_held.at[:, :, :width], dy_held.at[:, :, width:], pieces, 0, 0, scaled)

            @pl.when(now < tiles - 1)
            def _():
                fetch_dy(now + 1)

            weight_copy(down_ref, down, down_in, now, 0, tile).wait()
            d_hidden = dot(scaled[...], down[now], BY_WIDTH)
            made, d_gate, d_up = hidden_grads(pre_gate, pre_up, d_hidden)
            factors[:, columns] = made
            factors[:, tile_of(tiles + now, tile)] = d_gate
            factors[:, tile_of(2 * tiles + now, tile)] = d_up

        @pl.when(now == tiles)
        def _():
            for at in range(2):
                columns = tile_of(part_ref[0] ^ at, share)
                cuts[at, :, :share] = rows[:, columns]
                cuts[at, :, share:] = scaled[:, columns]
            start(leave_factors(), cut_in)

        @pl.when(now >= tiles)
        def _():
            at = now - tiles
            here = tile_of(at, chunk)
            done = dot(factors[:, hid : 2 * hid], gate[here, :], BY_WIDTH)
            done += dot(factors[:, 2 * hid :], up[here, :], BY_WIDTH)
            done = done.astype(jnp.bfloat16)
            for block in range(blocks):
                staged[me_ref[0] ^ block, :, here] = done[block * ROWS : (block + 1) * ROWS]
            leave(at).start()
            for piece in range(chunk // step):
                tail[...] += dot(
                    spill_picks(blocks, pieces, at * (chunk // step) + piece),
                    done[blocks * ROWS :, piece * step : (piece + 1) * step],
                    BY_ROWS,
                )

        @pl.when(now == tiles + chunks - 1)
        def _():
            for block in range(blocks):
                part = tail[block * ROWS : (block + 1) * ROWS, :]
                staged[me_ref[0] ^ block, :, width:] = part.astype(jnp.bfloat16)
            last = pltpu.make_async_copy(
                staged.at[:, :, width:], out.at[:, :, width:], gone.at[chunks]
            )
            last.start()
            for at in range(chunks):
                leave(at).wait()
            wait(leave_factors(), cut_in)
            last.wait()

    return pl.pallas_call(
        kernel,
        grid=(tiles + chunks,),
        out_shape=[
            jax.ShapeDtypeStruct(shape, jnp.bfloat16),
            jax.ShapeDtypeStruct((slots, given), jnp.bfloat16),
            jax.ShapeDtypeStruct((slots, given), jnp.bfloat16),
        ],
        in_specs=[pl.BlockSpec(memory_space=pltpu.SMEM)] * 2 + anywhere(blocks + 3),
        out_specs=anywhere(3),
        scratch_shapes=[
            pltpu.VMEM(shape, jnp.bfloat16),
            pltpu.VMEM(shape, jnp.bfloat16),
            pltpu.VMEM((slots, width), jnp.bfloat16),
            pltpu.VMEM((slots, width), jnp.bfloat16),
            pltpu.VMEM((slots, 3 * hid), jnp.bfloat16),
            pltpu.VMEM((2, slots, 2 * share), jnp.bfloat16),
            pltpu.VMEM((blocks * ROWS, step), jnp.float32),
            pltpu.VMEM(shape, jnp.bfloat16),
            pltpu.VMEM((width, hid), jnp.bfloat16),
            pltpu.VMEM((width, hid), jnp.bfloat16),
            pltpu.VMEM((tiles, tile, width), jnp.bfloat16),
            pltpu.SemaphoreType.DMA((blocks,)),
            pltpu.SemaphoreType.DMA((blocks,)),
            pltpu.SemaphoreType.DMA((tiles,)),
            pltpu.SemaphoreType.DMA((tiles,)),
            pltpu.SemaphoreType.DMA((tiles,)),
            pltpu.SemaphoreType.DMA((chunks + 1,)),
            pltpu.SemaphoreType.DMA((4,)),
        ],
        compiler_params=params(),
        cost_estimate=cost(10 * slots * width * hid, 4 * slots * width),
        name="back",
    )(me, part, *group, gate_proj, up_proj, down_proj)


def weight_grads(tile, share, part, known, groups, gate_proj, up_proj, down_proj):
    count, items = len(groups), len(groups[0])
    blocks = sum(item.shape[0] if item.ndim == 3 else 1 for item in groups[0])
    given = len(known)
    hid, width = down_proj.shape
    pieces, step = cut(width)
    slots = blocks * MOST
    total = (given + count) * slots
    tiles = hid // tile

    def kernel(part_ref, *refs):
        refs = list(refs)
        known_refs = [refs.pop(0) for _ in range(given)]
        group_refs = [[refs.pop(0) for _ in range(items)] for _ in range(count)]
        gate_ref, up_ref, down_ref = [refs.pop(0) for _ in range(3)]
        d_gate_ref, d_up_ref, d_down_ref = [refs.pop(0) for _ in range(3)]
        x_held, dy_held, x_all, dy_all = [refs.pop(0) for _ in range(4)]
        x_mine, dy_mine, factors = [refs.pop(0) for _ in range(3)]
        gate, up, down, x_in, dy_in, known_in, gate_in, up_in, down_in = refs
        now = pl.program_id(0)
        columns = tile_of(part_ref[0], share)
        x_pairs, dy_pairs, known_pairs = [], [], []
        for at in range(count):
            x_pairs += halves(group_refs[at], 0, x_held.at[at])
            dy_pairs += halves(group_refs[at], 1, dy_held.at[at])
        for at in range(given):
            here = slice(at * slots, (at + 1) * slots)
            behind = 3 * hid
            known_pairs += [
                (known_refs[at].at[:, :behind], factors.at[here, :]),
                (known_refs[at].at[:, behind : behind + share], x_mine.at[here, :]),
                (known_refs[at].at[:, behind + share :], dy_mine.at[here, :]),
            ]

        def arrange(held, rows_out, target):
            for at in range(count):
                unpack(
                    held.at[at, :, :, :width],
                    held.at[at, :, :, width:],
                    pieces,
                    0,
                    at * slots,
                    rows_out,
                )
            target[given * slots :, :] = rows_out[:, columns]

        def fetch_x(index):
            weight_copy(gate_ref, gate, gate_in, index, 1, tile).start()
            weight_copy(up_ref, up, up_in, index, 1, tile).start()

        def fetch_dy(index):
            weight_copy(down_ref, down, down_in, index, 0, tile).start()

        @pl.when(now == 0)
        def _():
            start(x_pairs, x_in)
            fetch_x(0)
            wait(x_pairs, x_in)
            start(dy_pairs, dy_in)
            fetch_dy(0)
            arrange(x_held, x_all, x_mine)

        weight_copy(gate_ref, gate, gate_in, now, 1, tile).wait()
        pre_gate = dot(x_all[...], gate[now])
        weight_copy(up_ref, up, up_in, now, 1, tile).wait()
        pre_up = dot(x_all[...], up[now])

        @pl.when(now == 0)
        def _():
            wait(dy_pairs, dy_in)
            start(known_pairs, known_in)
            arrange(dy_held, dy_all, dy_mine)

        @pl.when(now < tiles - 1)
        def _():
            fetch_x(now + 1)
            fetch_dy(now + 1)

        weight_copy(down_ref, down, down_in, now, 0, tile).wait()
        d_hidden = dot(dy_all[...], down[now], BY_WIDTH)
        made, d_gate, d_up = hidden_grads(pre_gate, pre_up, d_hidden)

        @pl.when(now == 0)
        def _():
            wait(known_pairs, known_in)

        made = jnp.concatenate([factors[:, tile_of(now, tile)], made], 0)
        d_gate = jnp.concatenate([factors[:, tile_of(tiles + now, tile)], d_gate], 0)
        d_up = jnp.concatenate([factors[:, tile_of(2 * tiles + now, tile)], d_up], 0)
        sums = dot(x_mine[...], jnp.concatenate([d_gate, d_up], 1), BY_ROWS)
        d_gate_ref[...] = sums[:, :tile]
        d_up_ref[...] = sums[:, tile:]
        d_down_ref[...] = dot(made, dy_mine[...], BY_ROWS)

    held = pltpu.VMEM((count, blocks, ROWS, width + step), jnp.bfloat16)
    arranged = pltpu.VMEM((count * slots, width), jnp.bfloat16)
    mine = pltpu.VMEM((total, share), jnp.bfloat16)
    return pl.pallas_call(
        kernel,
        grid=(tiles,),
        out_shape=[
            jax.ShapeDtypeStruct((share, hid), jnp.float32),
            jax.ShapeDtypeStruct((share, hid), jnp.float32),
            jax.ShapeDtypeStruct((hid, share), jnp.float32),
        ],
        in_specs=[pl.BlockSpec(memory_space=pltpu.SMEM)] + anywhere(given + count * items + 3),
        out_specs=[column_tile(share, tile), column_tile(share, tile), row_tile(tile, share)],
        scratch_shapes=[
            held,
            held,
            arranged,
            arranged,
            mine,
            mine,
            pltpu.VMEM((given * slots, 3 * hid), jnp.bfloat16),
            pltpu.VMEM((tiles, width, tile), jnp.bfloat16),
            pltpu.VMEM((tiles, width, tile), jnp.bfloat16),
            pltpu.VMEM((tiles, tile, width), jnp.bfloat16),
            pltpu.SemaphoreType.DMA((count * items,)),
            pltpu.SemaphoreType.DMA((count * items,)),
            pltpu.SemaphoreType.DMA((3 * given,)),
            pltpu.SemaphoreType.DMA((tiles,)),
            pltpu.SemaphoreType.DMA((tiles,)),
            pltpu.SemaphoreType.DMA((tiles,)),
        ],
        compiler_params=params(),
        cost_estimate=cost(0, 4 * slots * width),
        name="weight_grads",
    )(part, *known, *[item for group in groups for item in group], gate_proj, up_proj, down_proj)


def swap(value, axis, distance):
    size = lax.axis_size(axis)
    return lax.ppermute(value, axis, [(at, at ^ distance) for at in range(size)])


def exchange(blocks):
    return lax.all_to_all(blocks, "expert", split_axis=0, concat_axis=0, tiled=True)


def after(value, *earlier):
    return lax.optimization_barrier((value, *earlier))[0]


def gather_body(tokens, cotangent, routes, expert_gates, gate_proj, up_proj, down_proj):
    blocks = lax.axis_size("expert")
    tile, share = 256, tokens.shape[1] // lax.axis_size("dp")
    me = lax.axis_index("expert").astype(jnp.int32).reshape(1)
    part = lax.axis_index("dp").astype(jnp.int32).reshape(1)
    routes = routes.reshape(1, -1)
    gates = expert_gates.reshape(1, -1)
    weights = (gate_proj, up_proj, down_proj)
    received = list(pack(blocks, me, routes, gates, tokens, cotangent))
    for distance in reversed(range(1, blocks)):
        received[distance] = swap(received[distance], "expert", distance)
    half = blocks // 2
    far = swap(join(received[:half]), "dp", 2)
    far_half = swap(join(received[half:]), "dp", 2)
    sent, kept, handed = back(tile, share, me, part, received, *weights)
    sent, far = lax.optimization_barrier((sent, far))
    returned = exchange(sent)
    far = [far, after(far_half, sent)]
    last = [swap(item, "dp", 1) for item in far]
    known = [kept, swap(handed, "dp", 1)]
    grads = weight_grads(tile, share, part, known, [far, last], *weights)
    return (merge(routes, after(returned, *grads)), *grads)


def body(tokens, cotangent, routes, expert_gates, gate_proj, up_proj, down_proj):
    groups, blocks = lax.axis_size("dp"), lax.axis_size("expert")
    width, hid = gate_proj.shape
    rows_sent = (groups - 1) * 2 * blocks * MOST * width
    grads_sent = 3 * width * hid * (groups - 1) // groups
    fits = blocks == EXPERTS and groups == 4 and hid % 256 == 0
    fits = fits and tokens.shape[0] == 128 and routes.shape[1] == 1 and width // groups % 128 == 0
    chosen = gather_body if fits and rows_sent < grads_sent else scatter_body
    return chosen(tokens, cotangent, routes, expert_gates, gate_proj, up_proj, down_proj)


def solution(mesh):
    in_specs = (
        P(("dp", "expert"), None),
        P(("dp", "expert"), None),
        P(("dp", "expert"), None),
        P(("dp", "expert"), None),
        P(None, "expert"),
        P(None, "expert"),
        P("expert", None),
    )
    out_specs = (P(("dp", "expert"), None), P("dp", "expert"), P("dp", "expert"), P("expert", "dp"))
    return jax.shard_map(body, mesh=mesh, in_specs=in_specs, out_specs=out_specs, check_vma=False)
```

```python
import jax
import jax.numpy as jnp
from jax import lax
from jax.experimental import pallas as pl
from jax.experimental.pallas import tpu as pltpu
from jax.sharding import PartitionSpec as P

EXPERTS = 8
MOST = 18
ROWS = 16
VMEM_BYTES = (63 * 1024 + 768) * 1024


def build_slots(routes, capacity):
    flat_routes = routes.reshape(-1)
    one_hot = (flat_routes[:, None] == jnp.arange(EXPERTS, dtype=jnp.int32)[None, :]).astype(
        jnp.int32
    )
    before = jnp.cumsum(one_hot, axis=0) - one_hot
    position = jnp.sum(before * one_hot, axis=1)
    return flat_routes * capacity + position


def scatter_body(tokens, cotangent, routes, expert_gates, gate_proj, up_proj, down_proj):
    tok_dev, model_dim = tokens.shape
    top_k = routes.shape[1]
    expert_devs = lax.axis_size("expert")
    group_size = expert_devs // EXPERTS
    capacity = MOST
    slot_total = EXPERTS * capacity
    slot_of = build_slots(routes, capacity)
    owners = jnp.arange(tok_dev * top_k, dtype=jnp.int32) // top_k
    slot_table = jnp.full((slot_total,), tok_dev, jnp.int32).at[slot_of].set(owners)
    slot_gate = jnp.zeros((slot_total,), jnp.float32).at[slot_of].set(expert_gates.reshape(-1))
    x_slots = jnp.take(tokens, slot_table, axis=0, mode="fill", fill_value=0)
    dy_slots = (
        jnp.take(cotangent, slot_table, axis=0, mode="fill", fill_value=0).astype(jnp.float32)
        * slot_gate[:, None]
    ).astype(jnp.bfloat16)

    def copies(values):
        spread = values.reshape(EXPERTS, 1, capacity, model_dim)
        return jnp.broadcast_to(spread, (EXPERTS, group_size, capacity, model_dim)).reshape(
            expert_devs, capacity, model_dim
        )

    x_recv, dy_recv = (
        lax.all_to_all(copies(x_slots), "expert", split_axis=0, concat_axis=0, tiled=True),
        lax.all_to_all(copies(dy_slots), "expert", split_axis=0, concat_axis=0, tiled=True),
    )
    in_rows = x_recv.reshape(expert_devs * capacity, model_dim)
    scaled = dy_recv.reshape(expert_devs * capacity, model_dim)
    pre_gate = jnp.dot(in_rows, gate_proj, preferred_element_type=jnp.float32)
    pre_up = jnp.dot(in_rows, up_proj, preferred_element_type=jnp.float32)
    gate_sig = jax.nn.sigmoid(pre_gate)
    hidden = (pre_gate * gate_sig * pre_up).astype(jnp.bfloat16)
    by_width = (((1,), (1,)), ((), ()))
    by_rows = (((0,), (0,)), ((), ()))
    d_hidden = lax.dot_general(scaled, down_proj, by_width, preferred_element_type=jnp.float32)
    d_gate = (d_hidden * pre_up * gate_sig * (1.0 + pre_gate * (1.0 - gate_sig))).astype(
        jnp.bfloat16
    )
    d_up = (d_hidden * pre_gate * gate_sig).astype(jnp.bfloat16)
    grad_down = lax.dot_general(hidden, scaled, by_rows, preferred_element_type=jnp.float32)
    grad_gate = lax.dot_general(in_rows, d_gate, by_rows, preferred_element_type=jnp.float32)
    grad_up = lax.dot_general(in_rows, d_up, by_rows, preferred_element_type=jnp.float32)
    grad_gate, grad_up, grad_down = (
        lax.psum_scatter(
            grad_gate.astype(jnp.bfloat16), "dp", scatter_dimension=0, tiled=True
        ).astype(jnp.float32),
        lax.psum_scatter(
            grad_up.astype(jnp.bfloat16), "dp", scatter_dimension=0, tiled=True
        ).astype(jnp.float32),
        lax.psum_scatter(
            grad_down.astype(jnp.bfloat16), "dp", scatter_dimension=1, tiled=True
        ).astype(jnp.float32),
    )
    joined_grads = jnp.concatenate([d_gate, d_up], 1)
    joined_proj = jnp.concatenate([gate_proj, up_proj], 1)
    partial_value = lax.dot_general(
        joined_grads, joined_proj, by_width, preferred_element_type=jnp.float32
    ).astype(jnp.bfloat16)
    returned = lax.all_to_all(
        partial_value.reshape(expert_devs, capacity, model_dim),
        "expert",
        split_axis=0,
        concat_axis=0,
        tiled=True,
    )
    summed = jnp.sum(
        returned.reshape(EXPERTS, group_size, capacity, model_dim).astype(jnp.float32), axis=1
    )
    summed = summed.reshape(slot_total, model_dim)
    grad_input = jnp.take(summed, slot_of, axis=0).reshape(tok_dev, top_k, model_dim).sum(axis=1)
    return (grad_input.astype(jnp.bfloat16), grad_gate, grad_up, grad_down)


BY_WIDTH = (((1,), (1,)), ((), ()))
BY_ROWS = (((0,), (0,)), ((), ()))


def cut(width):
    pieces = ROWS // (MOST - ROWS)
    return pieces, width // pieces


def width_of(packed):
    pieces = ROWS // (MOST - ROWS)
    return packed.shape[2] * pieces // (pieces + 1)


def cost(flops, moved):
    return pl.CostEstimate(flops=flops, bytes_accessed=moved, transcendentals=0)


def params():
    return pltpu.CompilerParams(vmem_limit_bytes=VMEM_BYTES)


def anywhere(count):
    return [pl.BlockSpec(memory_space=pl.ANY)] * count


def dot(left, right, dims=(((1,), (0,)), ((), ()))):
    return lax.dot_general(left, right, dims, preferred_element_type=jnp.float32)


def ones(mask):
    return jnp.where(mask, 1.0, 0.0).astype(jnp.bfloat16)


def start(pairs, arrived, first=0):
    for at, (source, target) in enumerate(pairs):
        if at >= first:
            pltpu.make_async_copy(source, target, arrived.at[at]).start()


def wait(pairs, arrived, first=0):
    for at, (source, target) in enumerate(pairs):
        if at >= first:
            pltpu.make_async_copy(source, target, arrived.at[at]).wait()


def slot_masks(routes, blocks, width, me=0):
    tokens = routes.shape[1]
    pieces, _ = cut(width)
    experts = lax.broadcasted_iota(jnp.int32, (EXPERTS, tokens), 0)
    named = jnp.where(experts == routes, 1.0, 0.0)
    earlier = lax.broadcasted_iota(jnp.int32, (tokens, tokens), 0) < lax.broadcasted_iota(
        jnp.int32, (tokens, tokens), 1
    )
    before = dot(named.astype(jnp.bfloat16), ones(earlier))
    position = jnp.sum(before * named, axis=0, keepdims=True).astype(jnp.int32)
    slot = lax.broadcasted_iota(jnp.int32, (blocks * ROWS, tokens), 0)
    row = slot % ROWS
    mine = (slot // ROWS) ^ me == routes
    main = mine & (position == row)
    spill = mine & (position == ROWS + row // pieces)
    return main, spill, row % pieces


def pack(blocks, me, routes, gates, tokens, cotangent):
    count, width = tokens.shape
    pieces, step = cut(width)
    sources = (routes, gates, tokens, cotangent)

    def kernel(me_ref, *refs):
        outs, held, arrived = refs[4 : 4 + blocks], refs[4 + blocks : 8 + blocks], refs[-1]
        pairs = list(zip(refs[:4], held))
        start(pairs, arrived)
        wait(pairs[:2], arrived)
        main, spill, piece = slot_masks(held[0][...], blocks, width, me_ref[0])
        mains = ones(main)
        picks = [ones(spill & (piece == at)) for at in range(pieces)]
        main_scale = jnp.sum(jnp.where(main, held[1][...], 0.0), axis=1, keepdims=True)
        spill_scale = jnp.sum(jnp.where(spill, held[1][...], 0.0), axis=1, keepdims=True)
        for half in range(2):
            wait(pairs[: 3 + half], arrived, 2 + half)
            values = held[2 + half]
            rows = dot(mains, values[...])
            extra = jnp.zeros((blocks * ROWS, step), jnp.float32)
            for at in range(pieces):
                extra += dot(picks[at], values[:, at * step : (at + 1) * step])
            if half > 0:
                rows, extra = rows * main_scale, extra * spill_scale
            rows = rows.astype(jnp.bfloat16)
            extra = extra.astype(jnp.bfloat16)
            here = slice(half * ROWS, (half + 1) * ROWS)
            for block in range(blocks):
                part = slice(block * ROWS, (block + 1) * ROWS)
                outs[block][here, :width] = rows[part]
                outs[block][here, width:] = extra[part]

    inside = pl.BlockSpec(memory_space=pltpu.VMEM)
    return pl.pallas_call(
        kernel,
        out_shape=[jax.ShapeDtypeStruct((2 * ROWS, width + step), jnp.bfloat16)] * blocks,
        in_specs=[pl.BlockSpec(memory_space=pltpu.SMEM)] + anywhere(4),
        out_specs=[inside] * blocks,
        scratch_shapes=[pltpu.VMEM(source.shape, source.dtype) for source in sources]
        + [pltpu.SemaphoreType.DMA((4,))],
        compiler_params=params(),
        cost_estimate=cost(8 * blocks * ROWS * count * width, 8 * count * width),
        name="pack",
    )(me, *sources)


def join(received):
    count = len(received)

    def kernel(*refs):
        pairs = [(refs[at], refs[count].at[at]) for at in range(count)]
        start(pairs, refs[-1])
        wait(pairs, refs[-1])

    return pl.pallas_call(
        kernel,
        out_shape=jax.ShapeDtypeStruct((count,) + received[0].shape, jnp.bfloat16),
        in_specs=anywhere(count),
        out_specs=pl.BlockSpec(memory_space=pltpu.VMEM),
        scratch_shapes=[pltpu.SemaphoreType.DMA((count,))],
        compiler_params=params(),
        cost_estimate=cost(0, 4 * received[0].size * count),
        name="join",
    )(*received)


def merge(routes, returned):
    blocks = returned.shape[0]
    tokens = routes.shape[1]
    width = width_of(returned)
    pieces, step = cut(width)

    def kernel(routes_ref, back_ref, out, named, held, arrived):
        pairs = [(routes_ref, named), (back_ref, held)]
        start(pairs, arrived)
        wait(pairs[:1], arrived)
        main, spill, piece = slot_masks(named[...], blocks, width)
        mains = ones(main)
        picks = [ones(spill & (piece == at)) for at in range(pieces)]
        wait(pairs, arrived, 1)
        rows = jnp.concatenate([held[at, :, :width] for at in range(blocks)], 0)
        extra = jnp.concatenate([held[at, :, width:] for at in range(blocks)], 0)
        picked = dot(mains, rows, BY_ROWS)
        for at in range(pieces):
            columns = slice(at * step, (at + 1) * step)
            out[:, columns] = (picked[:, columns] + dot(picks[at], extra, BY_ROWS)).astype(
                jnp.bfloat16
            )

    return pl.pallas_call(
        kernel,
        out_shape=jax.ShapeDtypeStruct((tokens, width), jnp.bfloat16),
        in_specs=anywhere(2),
        out_specs=pl.BlockSpec(memory_space=pltpu.VMEM),
        scratch_shapes=[
            pltpu.VMEM(routes.shape, routes.dtype),
            pltpu.VMEM(returned.shape, returned.dtype),
            pltpu.SemaphoreType.DMA((2,)),
        ],
        compiler_params=params(),
        cost_estimate=cost(4 * blocks * ROWS * tokens * width, 4 * tokens * width),
        name="merge",
    )(routes, returned)


def spill_picks(blocks, pieces, at):
    shape = (blocks * (MOST - ROWS), blocks * ROWS)
    slot = lax.broadcasted_iota(jnp.int32, shape, 0)
    row = lax.broadcasted_iota(jnp.int32, shape, 1)
    return ones(row == slot * pieces + at)


def unpack(main, tail, pieces, begin, first, out):
    blocks = main.shape[0]
    step = tail.shape[2]
    for at in range(blocks):
        out[first + at * ROWS : first + (at + 1) * ROWS, :] = main[at]
    extra = jnp.concatenate([tail[at] for at in range(blocks)], 0)
    spill = slice(first + blocks * ROWS, first + blocks * MOST)
    for at in range(out.shape[1] // step):
        out[spill, at * step : (at + 1) * step] = dot(
            spill_picks(blocks, pieces, begin + at), extra
        ).astype(jnp.bfloat16)


def column_tile(width, tile):
    return pl.BlockSpec((width, tile), lambda i: (0, i))


def row_tile(tile, width):
    return pl.BlockSpec((tile, width), lambda i: (i, 0))


def tile_of(index, tile):
    return pl.ds(pl.multiple_of(index * tile, tile), tile)


def weight_copy(source, target, arrived, index, axis, tile):
    here = tile_of(index, tile)
    view = source.at[:, here] if axis else source.at[here, :]
    return pltpu.make_async_copy(view, target.at[index], arrived.at[index])


def halves(group, half, out):
    here = slice(half * ROWS, (half + 1) * ROWS)
    pairs, at = [], 0
    for item in group:
        if len(item.shape) == 2:
            pairs.append((item.at[here, :], out.at[at]))
            at += 1
        else:
            pairs.append((item.at[:, here, :], out.at[at : at + item.shape[0]]))
            at += item.shape[0]
    return pairs


def hidden_grads(pre_gate, pre_up, d_hidden):
    sig = jax.nn.sigmoid(pre_gate)
    silu = pre_gate * sig
    hidden = (silu * pre_up).astype(jnp.bfloat16)
    d_gate = (d_hidden * pre_up * sig * (1.0 + pre_gate * (1.0 - sig))).astype(jnp.bfloat16)
    d_up = (d_hidden * silu).astype(jnp.bfloat16)
    return hidden, d_gate, d_up


def back(tile, share, me, part, group, gate_proj, up_proj, down_proj):
    blocks = len(group)
    width, hid = gate_proj.shape
    slots = blocks * MOST
    pieces, step = cut(width)
    tiles = hid // tile
    chunk = 2 * step
    chunks = width // chunk
    shape = (blocks, ROWS, width + step)
    given = 3 * hid + 2 * share

    def kernel(me_ref, part_ref, *refs):
        refs = list(refs)
        group_refs = [refs.pop(0) for _ in range(blocks)]
        gate_ref, up_ref, down_ref, out, kept, handed = [refs.pop(0) for _ in range(6)]
        x_held, dy_held, rows, scaled, factors, cuts = [refs.pop(0) for _ in range(6)]
        tail, staged, gate, up, down = [refs.pop(0) for _ in range(5)]
        x_in, dy_in, gate_in, up_in, down_in, gone, cut_in = refs
        now = pl.program_id(0)
        x_pairs, dy_pairs = halves(group_refs, 0, x_held), halves(group_refs, 1, dy_held)

        def column_copy(source, target, arrived, index):
            here = tile_of(index, tile)
            return pltpu.make_async_copy(
                source.at[:, here], target.at[:, here], arrived.at[index]
            )

        def fetch_x(index):
            column_copy(gate_ref, gate, gate_in, index).start()
            column_copy(up_ref, up, up_in, index).start()

        def fetch_dy(index):
            weight_copy(down_ref, down, down_in, index, 0, tile).start()

        def leave(index):
            columns = tile_of(index, chunk)
            return pltpu.make_async_copy(
                staged.at[:, :, columns], out.at[:, :, columns], gone.at[index]
            )

        def leave_factors():
            first, behind = slice(0, 3 * hid), slice(3 * hid, given)
            pairs = [(factors, kept.at[:, first]), (cuts.at[0], kept.at[:, behind])]
            return pairs + [(factors, handed.at[:, first]), (cuts.at[1], handed.at[:, behind])]

        @pl.when(now == 0)
        def _():
            start(x_pairs, x_in)
            fetch_x(0)
            wait(x_pairs, x_in)
            start(dy_pairs, dy_in)
            fetch_dy(0)
            unpack(x_held.at[:, :, :width], x_held.at[:, :, width:], pieces, 0, 0, rows)
            tail[...] = jnp.zeros_like(tail)

        @pl.when(now < tiles)
        def _():
            columns = tile_of(now, tile)
            column_copy(gate_ref, gate, gate_in, now).wait()
            pre_gate = dot(rows[...], gate[:, columns])

            @pl.when(now < tiles - 1)
            def _():
                fetch_x(now + 1)

            column_copy(up_ref, up, up_in, now).wait()
            pre_up = dot(rows[...], up[:, columns])

            @pl.when(now == 0)
            def _():
                wait(dy_pairs, dy_in)
                unpack(dy_held.at[:, :, :width], dy_held.at[:, :, width:], pieces, 0, 0, scaled)

            @pl.when(now < tiles - 1)
            def _():
                fetch_dy(now + 1)

            weight_copy(down_ref, down, down_in, now, 0, tile).wait()
            d_hidden = dot(scaled[...], down[now], BY_WIDTH)
            made, d_gate, d_up = hidden_grads(pre_gate, pre_up, d_hidden)
            factors[:, columns] = made
            factors[:, tile_of(tiles + now, tile)] = d_gate
            factors[:, tile_of(2 * tiles + now, tile)] = d_up

        @pl.when(now == tiles)
        def _():
            for at in range(2):
                columns = tile_of(part_ref[0] ^ at, share)
                cuts[at, :, :share] = rows[:, columns]
                cuts[at, :, share:] = scaled[:, columns]
            start(leave_factors(), cut_in)

        @pl.when(now >= tiles)
        def _():
            at = now - tiles
            here = tile_of(at, chunk)
            done = dot(factors[:, hid : 2 * hid], gate[here, :], BY_WIDTH)
            done += dot(factors[:, 2 * hid :], up[here, :], BY_WIDTH)
            done = done.astype(jnp.bfloat16)
            for block in range(blocks):
                staged[me_ref[0] ^ block, :, here] = done[block * ROWS : (block + 1) * ROWS]
            leave(at).start()
            for piece in range(chunk // step):
                tail[...] += dot(
                    spill_picks(blocks, pieces, at * (chunk // step) + piece),
                    done[blocks * ROWS :, piece * step : (piece + 1) * step],
                    BY_ROWS,
                )

        @pl.when(now == tiles + chunks - 1)
        def _():
            for block in range(blocks):
                part = tail[block * ROWS : (block + 1) * ROWS, :]
                staged[me_ref[0] ^ block, :, width:] = part.astype(jnp.bfloat16)
            last = pltpu.make_async_copy(
                staged.at[:, :, width:], out.at[:, :, width:], gone.at[chunks]
            )
            last.start()
            for at in range(chunks):
                leave(at).wait()
            wait(leave_factors(), cut_in)
            last.wait()

    return pl.pallas_call(
        kernel,
        grid=(tiles + chunks,),
        out_shape=[
            jax.ShapeDtypeStruct(shape, jnp.bfloat16),
            jax.ShapeDtypeStruct((slots, given), jnp.bfloat16),
            jax.ShapeDtypeStruct((slots, given), jnp.bfloat16),
        ],
        in_specs=[pl.BlockSpec(memory_space=pltpu.SMEM)] * 2 + anywhere(blocks + 3),
        out_specs=anywhere(3),
        scratch_shapes=[
            pltpu.VMEM(shape, jnp.bfloat16),
            pltpu.VMEM(shape, jnp.bfloat16),
            pltpu.VMEM((slots, width), jnp.bfloat16),
            pltpu.VMEM((slots, width), jnp.bfloat16),
            pltpu.VMEM((slots, 3 * hid), jnp.bfloat16),
            pltpu.VMEM((2, slots, 2 * share), jnp.bfloat16),
            pltpu.VMEM((blocks * ROWS, step), jnp.float32),
            pltpu.VMEM(shape, jnp.bfloat16),
            pltpu.VMEM((width, hid), jnp.bfloat16),
            pltpu.VMEM((width, hid), jnp.bfloat16),
            pltpu.VMEM((tiles, tile, width), jnp.bfloat16),
            pltpu.SemaphoreType.DMA((blocks,)),
            pltpu.SemaphoreType.DMA((blocks,)),
            pltpu.SemaphoreType.DMA((tiles,)),
            pltpu.SemaphoreType.DMA((tiles,)),
            pltpu.SemaphoreType.DMA((tiles,)),
            pltpu.SemaphoreType.DMA((chunks + 1,)),
            pltpu.SemaphoreType.DMA((4,)),
        ],
        compiler_params=params(),
        cost_estimate=cost(50 * slots * width * hid, 4 * slots * width),
        name="back",
    )(me, part, *group, gate_proj, up_proj, down_proj)


def weight_grads(tile, share, part, known, groups, gate_proj, up_proj, down_proj):
    count, items = len(groups), len(groups[0])
    blocks = sum(item.shape[0] if item.ndim == 3 else 1 for item in groups[0])
    given = len(known)
    hid, width = down_proj.shape
    pieces, step = cut(width)
    slots = blocks * MOST
    total = (given + count) * slots
    tiles = hid // tile

    def kernel(part_ref, *refs):
        refs = list(refs)
        known_refs = [refs.pop(0) for _ in range(given)]
        group_refs = [[refs.pop(0) for _ in range(items)] for _ in range(count)]
        gate_ref, up_ref, down_ref = [refs.pop(0) for _ in range(3)]
        d_gate_ref, d_up_ref, d_down_ref = [refs.pop(0) for _ in range(3)]
        x_held, dy_held, x_all, dy_all = [refs.pop(0) for _ in range(4)]
        x_mine, dy_mine, factors = [refs.pop(0) for _ in range(3)]
        gate, up, down, x_in, dy_in, known_in, gate_in, up_in, down_in = refs
        now = pl.program_id(0)
        columns = tile_of(part_ref[0], share)
        x_pairs, dy_pairs, known_pairs = [], [], []
        for at in range(count):
            x_pairs += halves(group_refs[at], 0, x_held.at[at])
            dy_pairs += halves(group_refs[at], 1, dy_held.at[at])
        for at in range(given):
            here = slice(at * slots, (at + 1) * slots)
            behind = 3 * hid
            known_pairs += [
                (known_refs[at].at[:, :behind], factors.at[here, :]),
                (known_refs[at].at[:, behind : behind + share], x_mine.at[here, :]),
                (known_refs[at].at[:, behind + share :], dy_mine.at[here, :]),
            ]

        def arrange(held, rows_out, target):
            for at in range(count):
                unpack(
                    held.at[at, :, :, :width],
                    held.at[at, :, :, width:],
                    pieces,
                    0,
                    at * slots,
                    rows_out,
                )
            target[given * slots :, :] = rows_out[:, columns]

        def fetch_x(index):
            weight_copy(gate_ref, gate, gate_in, index, 1, tile).start()
            weight_copy(up_ref, up, up_in, index, 1, tile).start()

        def fetch_dy(index):
            weight_copy(down_ref, down, down_in, index, 0, tile).start()

        @pl.when(now == 0)
        def _():
            start(x_pairs, x_in)
            fetch_x(0)
            wait(x_pairs, x_in)
            start(dy_pairs, dy_in)
            fetch_dy(0)
            arrange(x_held, x_all, x_mine)

        weight_copy(gate_ref, gate, gate_in, now, 1, tile).wait()
        pre_gate = dot(x_all[...], gate[now])
        weight_copy(up_ref, up, up_in, now, 1, tile).wait()
        pre_up = dot(x_all[...], up[now])

        @pl.when(now == 0)
        def _():
            wait(dy_pairs, dy_in)
            start(known_pairs, known_in)
            arrange(dy_held, dy_all, dy_mine)

        @pl.when(now < tiles - 1)
        def _():
            fetch_x(now + 1)
            fetch_dy(now + 1)

        weight_copy(down_ref, down, down_in, now, 0, tile).wait()
        d_hidden = dot(dy_all[...], down[now], BY_WIDTH)
        made, d_gate, d_up = hidden_grads(pre_gate, pre_up, d_hidden)

        @pl.when(now == 0)
        def _():
            wait(known_pairs, known_in)

        made = jnp.concatenate([factors[:, tile_of(now, tile)], made], 0)
        d_gate = jnp.concatenate([factors[:, tile_of(tiles + now, tile)], d_gate], 0)
        d_up = jnp.concatenate([factors[:, tile_of(2 * tiles + now, tile)], d_up], 0)
        sums = dot(x_mine[...], jnp.concatenate([d_gate, d_up], 1), BY_ROWS)
        d_gate_ref[...] = sums[:, :tile]
        d_up_ref[...] = sums[:, tile:]
        d_down_ref[...] = dot(made, dy_mine[...], BY_ROWS)

    held = pltpu.VMEM((count, blocks, ROWS, width + step), jnp.bfloat16)
    arranged = pltpu.VMEM((count * slots, width), jnp.bfloat16)
    mine = pltpu.VMEM((total, share), jnp.bfloat16)
    return pl.pallas_call(
        kernel,
        grid=(tiles,),
        out_shape=[
            jax.ShapeDtypeStruct((share, hid), jnp.float32),
            jax.ShapeDtypeStruct((share, hid), jnp.float32),
            jax.ShapeDtypeStruct((hid, share), jnp.float32),
        ],
        in_specs=[pl.BlockSpec(memory_space=pltpu.SMEM)] + anywhere(given + count * items + 3),
        out_specs=[column_tile(share, tile), column_tile(share, tile), row_tile(tile, share)],
        scratch_shapes=[
            held,
            held,
            arranged,
            arranged,
            mine,
            mine,
            pltpu.VMEM((given * slots, 3 * hid), jnp.bfloat16),
            pltpu.VMEM((tiles, width, tile), jnp.bfloat16),
            pltpu.VMEM((tiles, width, tile), jnp.bfloat16),
            pltpu.VMEM((tiles, tile, width), jnp.bfloat16),
            pltpu.SemaphoreType.DMA((count * items,)),
            pltpu.SemaphoreType.DMA((count * items,)),
            pltpu.SemaphoreType.DMA((3 * given,)),
            pltpu.SemaphoreType.DMA((tiles,)),
            pltpu.SemaphoreType.DMA((tiles,)),
            pltpu.SemaphoreType.DMA((tiles,)),
        ],
        compiler_params=params(),
        cost_estimate=cost(0, 4 * slots * width),
        name="weight_grads",
    )(part, *known, *[item for group in groups for item in group], gate_proj, up_proj, down_proj)


def swap(value, axis, distance):
    size = lax.axis_size(axis)
    return lax.ppermute(value, axis, [(at, at ^ distance) for at in range(size)])


def exchange(blocks):
    return lax.all_to_all(blocks, "expert", split_axis=0, concat_axis=0, tiled=True)


def after(value, *earlier):
    return lax.optimization_barrier((value, *earlier))[0]


def gather_body(tokens, cotangent, routes, expert_gates, gate_proj, up_proj, down_proj):
    blocks = lax.axis_size("expert")
    tile, share = 256, tokens.shape[1] // lax.axis_size("dp")
    me = lax.axis_index("expert").astype(jnp.int32).reshape(1)
    part = lax.axis_index("dp").astype(jnp.int32).reshape(1)
    routes = routes.reshape(1, -1)
    gates = expert_gates.reshape(1, -1)
    weights = (gate_proj, up_proj, down_proj)
    received = list(pack(blocks, me, routes, gates, tokens, cotangent))
    for distance in reversed(range(1, blocks)):
        received[distance] = swap(received[distance], "expert", distance)
    half = blocks // 2
    far = swap(join(received[:half]), "dp", 2)
    far_half = swap(join(received[half:]), "dp", 2)
    sent, kept, handed = back(tile, share, me, part, received, *weights)
    sent, far = lax.optimization_barrier((sent, far))
    returned = exchange(sent)
    far = [far, after(far_half, sent)]
    last = [swap(item, "dp", 1) for item in far]
    known = [kept, swap(handed, "dp", 1)]
    grads = weight_grads(tile, share, part, known, [far, last], *weights)
    return (merge(routes, after(returned, *grads)), *grads)


def body(tokens, cotangent, routes, expert_gates, gate_proj, up_proj, down_proj):
    groups, blocks = lax.axis_size("dp"), lax.axis_size("expert")
    width, hid = gate_proj.shape
    rows_sent = (groups - 1) * 2 * blocks * MOST * width
    grads_sent = 3 * width * hid * (groups - 1) // groups
    fits = blocks == EXPERTS and groups == 4 and hid % 256 == 0
    fits = fits and tokens.shape[0] == 128 and routes.shape[1] == 1 and width // groups % 128 == 0
    chosen = gather_body if fits and rows_sent < grads_sent else scatter_body
    return chosen(tokens, cotangent, routes, expert_gates, gate_proj, up_proj, down_proj)


def solution(mesh):
    in_specs = (
        P(("dp", "expert"), None),
        P(("dp", "expert"), None),
        P(("dp", "expert"), None),
        P(("dp", "expert"), None),
        P(None, "expert"),
        P(None, "expert"),
        P("expert", None),
    )
    out_specs = (P(("dp", "expert"), None), P("dp", "expert"), P("dp", "expert"), P("expert", "dp"))
    return jax.shard_map(body, mesh=mesh, in_specs=in_specs, out_specs=out_specs, check_vma=False)
```

```python
import jax
import jax.numpy as jnp
from jax import lax
from jax.experimental import pallas as pl
from jax.experimental.pallas import tpu as pltpu
from jax.sharding import PartitionSpec as P

EXPERTS = 8
MOST = 18
ROWS = 16
VMEM_BYTES = (63 * 1024 + 768) * 1024


def build_slots(routes, capacity):
    flat_routes = routes.reshape(-1)
    one_hot = (flat_routes[:, None] == jnp.arange(EXPERTS, dtype=jnp.int32)[None, :]).astype(
        jnp.int32
    )
    before = jnp.cumsum(one_hot, axis=0) - one_hot
    position = jnp.sum(before * one_hot, axis=1)
    return flat_routes * capacity + position


def scatter_body(tokens, cotangent, routes, expert_gates, gate_proj, up_proj, down_proj):
    tok_dev, model_dim = tokens.shape
    top_k = routes.shape[1]
    expert_devs = lax.axis_size("expert")
    group_size = expert_devs // EXPERTS
    capacity = MOST
    slot_total = EXPERTS * capacity
    slot_of = build_slots(routes, capacity)
    owners = jnp.arange(tok_dev * top_k, dtype=jnp.int32) // top_k
    slot_table = jnp.full((slot_total,), tok_dev, jnp.int32).at[slot_of].set(owners)
    slot_gate = jnp.zeros((slot_total,), jnp.float32).at[slot_of].set(expert_gates.reshape(-1))
    x_slots = jnp.take(tokens, slot_table, axis=0, mode="fill", fill_value=0)
    dy_slots = (
        jnp.take(cotangent, slot_table, axis=0, mode="fill", fill_value=0).astype(jnp.float32)
        * slot_gate[:, None]
    ).astype(jnp.bfloat16)

    def copies(values):
        spread = values.reshape(EXPERTS, 1, capacity, model_dim)
        return jnp.broadcast_to(spread, (EXPERTS, group_size, capacity, model_dim)).reshape(
            expert_devs, capacity, model_dim
        )

    x_recv, dy_recv = (
        lax.all_to_all(copies(x_slots), "expert", split_axis=0, concat_axis=0, tiled=True),
        lax.all_to_all(copies(dy_slots), "expert", split_axis=0, concat_axis=0, tiled=True),
    )
    in_rows = x_recv.reshape(expert_devs * capacity, model_dim)
    scaled = dy_recv.reshape(expert_devs * capacity, model_dim)
    pre_gate = jnp.dot(in_rows, gate_proj, preferred_element_type=jnp.float32)
    pre_up = jnp.dot(in_rows, up_proj, preferred_element_type=jnp.float32)
    gate_sig = jax.nn.sigmoid(pre_gate)
    hidden = (pre_gate * gate_sig * pre_up).astype(jnp.bfloat16)
    by_width = (((1,), (1,)), ((), ()))
    by_rows = (((0,), (0,)), ((), ()))
    d_hidden = lax.dot_general(scaled, down_proj, by_width, preferred_element_type=jnp.float32)
    d_gate = (d_hidden * pre_up * gate_sig * (1.0 + pre_gate * (1.0 - gate_sig))).astype(
        jnp.bfloat16
    )
    d_up = (d_hidden * pre_gate * gate_sig).astype(jnp.bfloat16)
    grad_down = lax.dot_general(hidden, scaled, by_rows, preferred_element_type=jnp.float32)
    grad_gate = lax.dot_general(in_rows, d_gate, by_rows, preferred_element_type=jnp.float32)
    grad_up = lax.dot_general(in_rows, d_up, by_rows, preferred_element_type=jnp.float32)
    grad_gate, grad_up, grad_down = (
        lax.psum_scatter(
            grad_gate.astype(jnp.bfloat16), "dp", scatter_dimension=0, tiled=True
        ).astype(jnp.float32),
        lax.psum_scatter(
            grad_up.astype(jnp.bfloat16), "dp", scatter_dimension=0, tiled=True
        ).astype(jnp.float32),
        lax.psum_scatter(
            grad_down.astype(jnp.bfloat16), "dp", scatter_dimension=1, tiled=True
        ).astype(jnp.float32),
    )
    joined_grads = jnp.concatenate([d_gate, d_up], 1)
    joined_proj = jnp.concatenate([gate_proj, up_proj], 1)
    partial_value = lax.dot_general(
        joined_grads, joined_proj, by_width, preferred_element_type=jnp.float32
    ).astype(jnp.bfloat16)
    returned = lax.all_to_all(
        partial_value.reshape(expert_devs, capacity, model_dim),
        "expert",
        split_axis=0,
        concat_axis=0,
        tiled=True,
    )
    summed = jnp.sum(
        returned.reshape(EXPERTS, group_size, capacity, model_dim).astype(jnp.float32), axis=1
    )
    summed = summed.reshape(slot_total, model_dim)
    grad_input = jnp.take(summed, slot_of, axis=0).reshape(tok_dev, top_k, model_dim).sum(axis=1)
    return (grad_input.astype(jnp.bfloat16), grad_gate, grad_up, grad_down)


BY_WIDTH = (((1,), (1,)), ((), ()))
BY_ROWS = (((0,), (0,)), ((), ()))


def cut(width):
    pieces = ROWS // (MOST - ROWS)
    return pieces, width // pieces


def width_of(packed):
    pieces = ROWS // (MOST - ROWS)
    return packed.shape[2] * pieces // (pieces + 1)


def cost(flops, moved):
    return pl.CostEstimate(flops=flops, bytes_accessed=moved, transcendentals=0)


def params():
    return pltpu.CompilerParams(vmem_limit_bytes=VMEM_BYTES)


def anywhere(count):
    return [pl.BlockSpec(memory_space=pl.ANY)] * count


def dot(left, right, dims=(((1,), (0,)), ((), ()))):
    return lax.dot_general(left, right, dims, preferred_element_type=jnp.float32)


def ones(mask):
    return jnp.where(mask, 1.0, 0.0).astype(jnp.bfloat16)


def start(pairs, arrived, first=0):
    for at, (source, target) in enumerate(pairs):
        if at >= first:
            pltpu.make_async_copy(source, target, arrived.at[at]).start()


def wait(pairs, arrived, first=0):
    for at, (source, target) in enumerate(pairs):
        if at >= first:
            pltpu.make_async_copy(source, target, arrived.at[at]).wait()


def slot_masks(routes, blocks, width, me=0):
    tokens = routes.shape[1]
    pieces, _ = cut(width)
    experts = lax.broadcasted_iota(jnp.int32, (EXPERTS, tokens), 0)
    named = jnp.where(experts == routes, 1.0, 0.0)
    earlier = lax.broadcasted_iota(jnp.int32, (tokens, tokens), 0) < lax.broadcasted_iota(
        jnp.int32, (tokens, tokens), 1
    )
    before = dot(named.astype(jnp.bfloat16), ones(earlier))
    position = jnp.sum(before * named, axis=0, keepdims=True).astype(jnp.int32)
    slot = lax.broadcasted_iota(jnp.int32, (blocks * ROWS, tokens), 0)
    row = slot % ROWS
    mine = (slot // ROWS) ^ me == routes
    main = mine & (position == row)
    spill = mine & (position == ROWS + row // pieces)
    return main, spill, row % pieces


def pack(blocks, me, routes, gates, tokens, cotangent):
    count, width = tokens.shape
    pieces, step = cut(width)
    sources = (routes, gates, tokens, cotangent)

    def kernel(me_ref, *refs):
        outs, held, arrived = refs[4 : 4 + blocks], refs[4 + blocks : 8 + blocks], refs[-1]
        pairs = list(zip(refs[:4], held))
        start(pairs, arrived)
        wait(pairs[:2], arrived)
        main, spill, piece = slot_masks(held[0][...], blocks, width, me_ref[0])
        mains = ones(main)
        picks = [ones(spill & (piece == at)) for at in range(pieces)]
        main_scale = jnp.sum(jnp.where(main, held[1][...], 0.0), axis=1, keepdims=True)
        spill_scale = jnp.sum(jnp.where(spill, held[1][...], 0.0), axis=1, keepdims=True)
        for half in range(2):
            wait(pairs[: 3 + half], arrived, 2 + half)
            values = held[2 + half]
            rows = dot(mains, values[...])
            extra = jnp.zeros((blocks * ROWS, step), jnp.float32)
            for at in range(pieces):
                extra += dot(picks[at], values[:, at * step : (at + 1) * step])
            if half > 0:
                rows, extra = rows * main_scale, extra * spill_scale
            rows = rows.astype(jnp.bfloat16)
            extra = extra.astype(jnp.bfloat16)
            here = slice(half * ROWS, (half + 1) * ROWS)
            for block in range(blocks):
                part = slice(block * ROWS, (block + 1) * ROWS)
                outs[block][here, :width] = rows[part]
                outs[block][here, width:] = extra[part]

    inside = pl.BlockSpec(memory_space=pltpu.VMEM)
    return pl.pallas_call(
        kernel,
        out_shape=[jax.ShapeDtypeStruct((2 * ROWS, width + step), jnp.bfloat16)] * blocks,
        in_specs=[pl.BlockSpec(memory_space=pltpu.SMEM)] + anywhere(4),
        out_specs=[inside] * blocks,
        scratch_shapes=[pltpu.VMEM(source.shape, source.dtype) for source in sources]
        + [pltpu.SemaphoreType.DMA((4,))],
        compiler_params=params(),
        cost_estimate=cost(8 * blocks * ROWS * count * width, 8 * count * width),
        name="pack",
    )(me, *sources)


def join(received):
    count = len(received)

    def kernel(*refs):
        pairs = [(refs[at], refs[count].at[at]) for at in range(count)]
        start(pairs, refs[-1])
        wait(pairs, refs[-1])

    return pl.pallas_call(
        kernel,
        out_shape=jax.ShapeDtypeStruct((count,) + received[0].shape, jnp.bfloat16),
        in_specs=anywhere(count),
        out_specs=pl.BlockSpec(memory_space=pltpu.VMEM),
        scratch_shapes=[pltpu.SemaphoreType.DMA((count,))],
        compiler_params=params(),
        cost_estimate=cost(0, 4 * received[0].size * count),
        name="join",
    )(*received)


def merge(routes, returned):
    blocks = returned.shape[0]
    tokens = routes.shape[1]
    width = width_of(returned)
    pieces, step = cut(width)

    def kernel(routes_ref, back_ref, out, named, held, arrived):
        pairs = [(routes_ref, named), (back_ref, held)]
        start(pairs, arrived)
        wait(pairs[:1], arrived)
        main, spill, piece = slot_masks(named[...], blocks, width)
        mains = ones(main)
        picks = [ones(spill & (piece == at)) for at in range(pieces)]
        wait(pairs, arrived, 1)
        rows = jnp.concatenate([held[at, :, :width] for at in range(blocks)], 0)
        extra = jnp.concatenate([held[at, :, width:] for at in range(blocks)], 0)
        picked = dot(mains, rows, BY_ROWS)
        for at in range(pieces):
            columns = slice(at * step, (at + 1) * step)
            out[:, columns] = (picked[:, columns] + dot(picks[at], extra, BY_ROWS)).astype(
                jnp.bfloat16
            )

    return pl.pallas_call(
        kernel,
        out_shape=jax.ShapeDtypeStruct((tokens, width), jnp.bfloat16),
        in_specs=anywhere(2),
        out_specs=pl.BlockSpec(memory_space=pltpu.VMEM),
        scratch_shapes=[
            pltpu.VMEM(routes.shape, routes.dtype),
            pltpu.VMEM(returned.shape, returned.dtype),
            pltpu.SemaphoreType.DMA((2,)),
        ],
        compiler_params=params(),
        cost_estimate=cost(4 * blocks * ROWS * tokens * width, 4 * tokens * width),
        name="merge",
    )(routes, returned)


def spill_picks(blocks, pieces, at):
    shape = (blocks * (MOST - ROWS), blocks * ROWS)
    slot = lax.broadcasted_iota(jnp.int32, shape, 0)
    row = lax.broadcasted_iota(jnp.int32, shape, 1)
    return ones(row == slot * pieces + at)


def unpack(main, tail, pieces, begin, first, out):
    blocks = main.shape[0]
    step = tail.shape[2]
    for at in range(blocks):
        out[first + at * ROWS : first + (at + 1) * ROWS, :] = main[at]
    extra = jnp.concatenate([tail[at] for at in range(blocks)], 0)
    spill = slice(first + blocks * ROWS, first + blocks * MOST)
    for at in range(out.shape[1] // step):
        out[spill, at * step : (at + 1) * step] = dot(
            spill_picks(blocks, pieces, begin + at), extra
        ).astype(jnp.bfloat16)


def tile_of(index, tile):
    return pl.ds(pl.multiple_of(index * tile, tile), tile)


def weight_copy(source, target, arrived, index, axis, tile):
    here = tile_of(index, tile)
    view = source.at[:, here] if axis else source.at[here, :]
    return pltpu.make_async_copy(view, target.at[index], arrived.at[index])


def halves(group, half, out):
    here = slice(half * ROWS, (half + 1) * ROWS)
    pairs, at = [], 0
    for item in group:
        if len(item.shape) == 2:
            pairs.append((item.at[here, :], out.at[at]))
            at += 1
        else:
            pairs.append((item.at[:, here, :], out.at[at : at + item.shape[0]]))
            at += item.shape[0]
    return pairs


def hidden_grads(pre_gate, pre_up, d_hidden):
    sig = 0.5 * jnp.tanh(0.5 * pre_gate) + 0.5
    silu = pre_gate * sig
    hidden = (silu * pre_up).astype(jnp.bfloat16)
    d_gate = (d_hidden * pre_up * (sig + silu * (1.0 - sig))).astype(jnp.bfloat16)
    d_up = (d_hidden * silu).astype(jnp.bfloat16)
    return hidden, d_gate, d_up


def back(tile, share, me, part, group, gate_proj, up_proj, down_proj):
    blocks = len(group)
    width, hid = gate_proj.shape
    slots = blocks * MOST
    pieces, step = cut(width)
    tiles = hid // tile
    chunk = 2 * step
    chunks = width // chunk
    shape = (blocks, ROWS, width + step)
    given = 3 * hid + 2 * share

    def kernel(me_ref, part_ref, *refs):
        refs = list(refs)
        group_refs = [refs.pop(0) for _ in range(blocks)]
        gate_ref, up_ref, down_ref, out, kept, handed = [refs.pop(0) for _ in range(6)]
        x_held, dy_held, rows, scaled, factors, cuts = [refs.pop(0) for _ in range(6)]
        tail, staged, gate, up, down = [refs.pop(0) for _ in range(5)]
        x_in, dy_in, gate_in, up_in, down_in, gone, cut_in = refs
        now = pl.program_id(0)
        x_pairs, dy_pairs = halves(group_refs, 0, x_held), halves(group_refs, 1, dy_held)

        def column_copy(source, target, arrived, index):
            here = tile_of(index, tile)
            return pltpu.make_async_copy(
                source.at[:, here], target.at[:, here], arrived.at[index]
            )

        def fetch_x(index):
            column_copy(gate_ref, gate, gate_in, index).start()
            column_copy(up_ref, up, up_in, index).start()

        def fetch_dy(index):
            weight_copy(down_ref, down, down_in, index, 0, tile).start()

        def leave(index):
            columns = tile_of(index, chunk)
            return pltpu.make_async_copy(
                staged.at[:, :, columns], out.at[:, :, columns], gone.at[index]
            )

        def leave_factors():
            first, behind = slice(0, 3 * hid), slice(3 * hid, given)
            pairs = [(factors, kept.at[:, first]), (cuts.at[0], kept.at[:, behind])]
            return pairs + [(factors, handed.at[:, first]), (cuts.at[1], handed.at[:, behind])]

        @pl.when(now == 0)
        def _():
            start(x_pairs, x_in)
            fetch_x(0)
            wait(x_pairs, x_in)
            start(dy_pairs, dy_in)
            fetch_dy(0)
            unpack(x_held.at[:, :, :width], x_held.at[:, :, width:], pieces, 0, 0, rows)
            tail[...] = jnp.zeros_like(tail)

        @pl.when(now < tiles)
        def _():
            columns = tile_of(now, tile)
            column_copy(gate_ref, gate, gate_in, now).wait()
            pre_gate = dot(rows[...], gate[:, columns])

            @pl.when(now < tiles - 1)
            def _():
                fetch_x(now + 1)

            column_copy(up_ref, up, up_in, now).wait()
            pre_up = dot(rows[...], up[:, columns])

            @pl.when(now == 0)
            def _():
                wait(dy_pairs, dy_in)
                unpack(dy_held.at[:, :, :width], dy_held.at[:, :, width:], pieces, 0, 0, scaled)

            @pl.when(now < tiles - 1)
            def _():
                fetch_dy(now + 1)

            weight_copy(down_ref, down, down_in, now, 0, tile).wait()
            d_hidden = dot(scaled[...], down[now], BY_WIDTH)
            made, d_gate, d_up = hidden_grads(pre_gate, pre_up, d_hidden)
            factors[:, columns] = made
            factors[:, tile_of(tiles + now, tile)] = d_gate
            factors[:, tile_of(2 * tiles + now, tile)] = d_up

        @pl.when(now == tiles)
        def _():
            for at in range(2):
                columns = tile_of(part_ref[0] ^ at, share)
                cuts[at, :, :share] = rows[:, columns]
                cuts[at, :, share:] = scaled[:, columns]
            start(leave_factors(), cut_in)

        @pl.when(now >= tiles)
        def _():
            at = now - tiles
            here = tile_of(at, chunk)
            done = dot(factors[:, hid : 2 * hid], gate[here, :], BY_WIDTH)
            done += dot(factors[:, 2 * hid :], up[here, :], BY_WIDTH)
            done = done.astype(jnp.bfloat16)
            for block in range(blocks):
                staged[me_ref[0] ^ block, :, here] = done[block * ROWS : (block + 1) * ROWS]
            leave(at).start()
            for piece in range(chunk // step):
                tail[...] += dot(
                    spill_picks(blocks, pieces, at * (chunk // step) + piece),
                    done[blocks * ROWS :, piece * step : (piece + 1) * step],
                    BY_ROWS,
                )

        @pl.when(now == tiles + chunks - 1)
        def _():
            for block in range(blocks):
                part = tail[block * ROWS : (block + 1) * ROWS, :]
                staged[me_ref[0] ^ block, :, width:] = part.astype(jnp.bfloat16)
            last = pltpu.make_async_copy(
                staged.at[:, :, width:], out.at[:, :, width:], gone.at[chunks]
            )
            last.start()
            for at in range(chunks):
                leave(at).wait()
            wait(leave_factors(), cut_in)
            last.wait()

    return pl.pallas_call(
        kernel,
        grid=(tiles + chunks,),
        out_shape=[
            jax.ShapeDtypeStruct(shape, jnp.bfloat16),
            jax.ShapeDtypeStruct((slots, given), jnp.bfloat16),
            jax.ShapeDtypeStruct((slots, given), jnp.bfloat16),
        ],
        in_specs=[pl.BlockSpec(memory_space=pltpu.SMEM)] * 2 + anywhere(blocks + 3),
        out_specs=anywhere(3),
        scratch_shapes=[
            pltpu.VMEM(shape, jnp.bfloat16),
            pltpu.VMEM(shape, jnp.bfloat16),
            pltpu.VMEM((slots, width), jnp.bfloat16),
            pltpu.VMEM((slots, width), jnp.bfloat16),
            pltpu.VMEM((slots, 3 * hid), jnp.bfloat16),
            pltpu.VMEM((2, slots, 2 * share), jnp.bfloat16),
            pltpu.VMEM((blocks * ROWS, step), jnp.float32),
            pltpu.VMEM(shape, jnp.bfloat16),
            pltpu.VMEM((width, hid), jnp.bfloat16),
            pltpu.VMEM((width, hid), jnp.bfloat16),
            pltpu.VMEM((tiles, tile, width), jnp.bfloat16),
            pltpu.SemaphoreType.DMA((blocks,)),
            pltpu.SemaphoreType.DMA((blocks,)),
            pltpu.SemaphoreType.DMA((tiles,)),
            pltpu.SemaphoreType.DMA((tiles,)),
            pltpu.SemaphoreType.DMA((tiles,)),
            pltpu.SemaphoreType.DMA((chunks + 1,)),
            pltpu.SemaphoreType.DMA((4,)),
        ],
        compiler_params=params(),
        cost_estimate=cost(50 * slots * width * hid, 4 * slots * width),
        name="back",
    )(me, part, *group, gate_proj, up_proj, down_proj)


def weight_grads(tile, share, part, known, groups, gate_proj, up_proj, down_proj):
    count, items = len(groups), len(groups[0])
    blocks = sum(item.shape[0] if item.ndim == 3 else 1 for item in groups[0])
    given = len(known)
    hid, width = down_proj.shape
    pieces, step = cut(width)
    slots = blocks * MOST
    total = (given + count) * slots
    tiles = hid // tile

    def kernel(part_ref, *refs):
        refs = list(refs)
        known_refs = [refs.pop(0) for _ in range(given)]
        group_refs = [[refs.pop(0) for _ in range(items)] for _ in range(count)]
        gate_ref, up_ref, down_ref = [refs.pop(0) for _ in range(3)]
        d_gate_ref, d_up_ref, d_down_ref = [refs.pop(0) for _ in range(3)]
        x_held, dy_held, x_all, dy_all = [refs.pop(0) for _ in range(4)]
        x_mine, dy_mine, factors = [refs.pop(0) for _ in range(3)]
        gate, up, down, x_in, dy_in, known_in, gate_in, up_in, down_in = refs[:9]
        made_gate, made_up, made_down, gate_out, up_out, down_out = refs[9:]
        now = pl.program_id(0)
        columns = tile_of(part_ref[0], share)
        x_pairs, dy_pairs, known_pairs = [], [], []
        for at in range(count):
            x_pairs += halves(group_refs[at], 0, x_held.at[at])
            dy_pairs += halves(group_refs[at], 1, dy_held.at[at])
        for at in range(given):
            here = slice(at * slots, (at + 1) * slots)
            behind = 3 * hid
            known_pairs += [
                (known_refs[at].at[:, :behind], factors.at[here, :]),
                (known_refs[at].at[:, behind : behind + share], x_mine.at[here, :]),
                (known_refs[at].at[:, behind + share :], dy_mine.at[here, :]),
            ]

        def arrange(held, rows_out, target):
            for at in range(count):
                unpack(
                    held.at[at, :, :, :width],
                    held.at[at, :, :, width:],
                    pieces,
                    0,
                    at * slots,
                    rows_out,
                )
            target[given * slots :, :] = rows_out[:, columns]

        def leave(source, target, gone, index, axis):
            here = tile_of(index, tile)
            view = target.at[:, here] if axis else target.at[here, :]
            return pltpu.make_async_copy(source.at[index], view, gone.at[index])

        def fetch_x(index):
            weight_copy(gate_ref, gate, gate_in, index, 1, tile).start()
            weight_copy(up_ref, up, up_in, index, 1, tile).start()

        def fetch_dy(index):
            weight_copy(down_ref, down, down_in, index, 0, tile).start()

        @pl.when(now == 0)
        def _():
            start(x_pairs, x_in)
            fetch_x(0)
            wait(x_pairs, x_in)
            start(dy_pairs, dy_in)
            fetch_dy(0)
            arrange(x_held, x_all, x_mine)

        weight_copy(gate_ref, gate, gate_in, now, 1, tile).wait()
        pre_gate = dot(x_all[...], gate[now])
        weight_copy(up_ref, up, up_in, now, 1, tile).wait()
        pre_up = dot(x_all[...], up[now])

        @pl.when(now == 0)
        def _():
            wait(dy_pairs, dy_in)
            start(known_pairs, known_in)
            arrange(dy_held, dy_all, dy_mine)

        @pl.when(now < tiles - 1)
        def _():
            fetch_x(now + 1)
            fetch_dy(now + 1)

        weight_copy(down_ref, down, down_in, now, 0, tile).wait()
        d_hidden = dot(dy_all[...], down[now], BY_WIDTH)
        made, d_gate, d_up = hidden_grads(pre_gate, pre_up, d_hidden)

        @pl.when(now == 0)
        def _():
            wait(known_pairs, known_in)

        made = jnp.concatenate([factors[:, tile_of(now, tile)], made], 0)
        d_gate = jnp.concatenate([factors[:, tile_of(tiles + now, tile)], d_gate], 0)
        d_up = jnp.concatenate([factors[:, tile_of(2 * tiles + now, tile)], d_up], 0)
        sums = dot(x_mine[...], jnp.concatenate([d_gate, d_up], 1), BY_ROWS)
        made_gate[now] = sums[:, :tile]
        made_up[now] = sums[:, tile:]
        leave(made_gate, d_gate_ref, gate_out, now, 1).start()
        leave(made_up, d_up_ref, up_out, now, 1).start()
        made_down[now] = dot(made, dy_mine[...], BY_ROWS)
        leave(made_down, d_down_ref, down_out, now, 0).start()

        @pl.when(now == tiles - 1)
        def _():
            for at in range(tiles):
                leave(made_gate, d_gate_ref, gate_out, at, 1).wait()
                leave(made_up, d_up_ref, up_out, at, 1).wait()
                leave(made_down, d_down_ref, down_out, at, 0).wait()

    held = pltpu.VMEM((count, blocks, ROWS, width + step), jnp.bfloat16)
    arranged = pltpu.VMEM((count * slots, width), jnp.bfloat16)
    mine = pltpu.VMEM((total, share), jnp.bfloat16)
    return pl.pallas_call(
        kernel,
        grid=(tiles,),
        out_shape=[
            jax.ShapeDtypeStruct((share, hid), jnp.float32),
            jax.ShapeDtypeStruct((share, hid), jnp.float32),
            jax.ShapeDtypeStruct((hid, share), jnp.float32),
        ],
        in_specs=[pl.BlockSpec(memory_space=pltpu.SMEM)] + anywhere(given + count * items + 3),
        out_specs=anywhere(3),
        scratch_shapes=[
            held,
            held,
            arranged,
            arranged,
            mine,
            mine,
            pltpu.VMEM((given * slots, 3 * hid), jnp.bfloat16),
            pltpu.VMEM((tiles, width, tile), jnp.bfloat16),
            pltpu.VMEM((tiles, width, tile), jnp.bfloat16),
            pltpu.VMEM((tiles, tile, width), jnp.bfloat16),
            pltpu.SemaphoreType.DMA((count * items,)),
            pltpu.SemaphoreType.DMA((count * items,)),
            pltpu.SemaphoreType.DMA((3 * given,)),
            pltpu.SemaphoreType.DMA((tiles,)),
            pltpu.SemaphoreType.DMA((tiles,)),
            pltpu.SemaphoreType.DMA((tiles,)),
            pltpu.VMEM((tiles, share, tile), jnp.float32),
            pltpu.VMEM((tiles, share, tile), jnp.float32),
            pltpu.VMEM((tiles, tile, share), jnp.float32),
            pltpu.SemaphoreType.DMA((tiles,)),
            pltpu.SemaphoreType.DMA((tiles,)),
            pltpu.SemaphoreType.DMA((tiles,)),
        ],
        compiler_params=params(),
        cost_estimate=cost(0, 4 * slots * width),
        name="weight_grads",
    )(part, *known, *[item for group in groups for item in group], gate_proj, up_proj, down_proj)


def swap(value, axis, distance):
    size = lax.axis_size(axis)
    return lax.ppermute(value, axis, [(at, at ^ distance) for at in range(size)])


def exchange(blocks):
    return lax.all_to_all(blocks, "expert", split_axis=0, concat_axis=0, tiled=True)


def after(value, *earlier):
    return lax.optimization_barrier((value, *earlier))[0]


def gather_body(tokens, cotangent, routes, expert_gates, gate_proj, up_proj, down_proj):
    blocks = lax.axis_size("expert")
    tile, share = 256, tokens.shape[1] // lax.axis_size("dp")
    me = lax.axis_index("expert").astype(jnp.int32).reshape(1)
    part = lax.axis_index("dp").astype(jnp.int32).reshape(1)
    routes = routes.reshape(1, -1)
    gates = expert_gates.reshape(1, -1)
    weights = (gate_proj, up_proj, down_proj)
    received = list(pack(blocks, me, routes, gates, tokens, cotangent))
    for distance in reversed(range(1, blocks)):
        received[distance] = swap(received[distance], "expert", distance)
    half = blocks // 2
    far = swap(join(received[:half]), "dp", 2)
    far_half = swap(join(received[half:]), "dp", 2)
    sent, kept, handed = back(tile, share, me, part, received, *weights)
    sent, far = lax.optimization_barrier((sent, far))
    returned = exchange(sent)
    far = [far, after(far_half, sent)]
    last = [swap(item, "dp", 1) for item in far]
    known = [kept, swap(handed, "dp", 1)]
    grads = weight_grads(tile, share, part, known, [far, last], *weights)
    return (merge(routes, after(returned, *grads)), *grads)


def body(tokens, cotangent, routes, expert_gates, gate_proj, up_proj, down_proj):
    groups, blocks = lax.axis_size("dp"), lax.axis_size("expert")
    width, hid = gate_proj.shape
    rows_sent = (groups - 1) * 2 * blocks * MOST * width
    grads_sent = 3 * width * hid * (groups - 1) // groups
    fits = blocks == EXPERTS and groups == 4 and hid % 256 == 0
    fits = fits and tokens.shape[0] == 128 and routes.shape[1] == 1 and width // groups % 128 == 0
    chosen = gather_body if fits and rows_sent < grads_sent else scatter_body
    return chosen(tokens, cotangent, routes, expert_gates, gate_proj, up_proj, down_proj)


def solution(mesh):
    in_specs = (
        P(("dp", "expert"), None),
        P(("dp", "expert"), None),
        P(("dp", "expert"), None),
        P(("dp", "expert"), None),
        P(None, "expert"),
        P(None, "expert"),
        P("expert", None),
    )
    out_specs = (P(("dp", "expert"), None), P("dp", "expert"), P("dp", "expert"), P("expert", "dp"))
    return jax.shard_map(body, mesh=mesh, in_specs=in_specs, out_specs=out_specs, check_vma=False)
```

```python
import jax
import jax.numpy as jnp
from jax import lax
from jax.experimental import pallas as pl
from jax.experimental.pallas import tpu as pltpu
from jax.sharding import PartitionSpec as P

EXPERTS = 8
MOST = 18
ROWS = 16
VMEM_BYTES = (63 * 1024 + 768) * 1024


def build_slots(routes, capacity):
    flat_routes = routes.reshape(-1)
    one_hot = (flat_routes[:, None] == jnp.arange(EXPERTS, dtype=jnp.int32)[None, :]).astype(
        jnp.int32
    )
    before = jnp.cumsum(one_hot, axis=0) - one_hot
    position = jnp.sum(before * one_hot, axis=1)
    return flat_routes * capacity + position


def scatter_body(tokens, cotangent, routes, expert_gates, gate_proj, up_proj, down_proj):
    tok_dev, model_dim = tokens.shape
    top_k = routes.shape[1]
    expert_devs = lax.axis_size("expert")
    group_size = expert_devs // EXPERTS
    capacity = MOST
    slot_total = EXPERTS * capacity
    slot_of = build_slots(routes, capacity)
    owners = jnp.arange(tok_dev * top_k, dtype=jnp.int32) // top_k
    slot_table = jnp.full((slot_total,), tok_dev, jnp.int32).at[slot_of].set(owners)
    slot_gate = jnp.zeros((slot_total,), jnp.float32).at[slot_of].set(expert_gates.reshape(-1))
    x_slots = jnp.take(tokens, slot_table, axis=0, mode="fill", fill_value=0)
    dy_slots = (
        jnp.take(cotangent, slot_table, axis=0, mode="fill", fill_value=0).astype(jnp.float32)
        * slot_gate[:, None]
    ).astype(jnp.bfloat16)

    def copies(values):
        spread = values.reshape(EXPERTS, 1, capacity, model_dim)
        return jnp.broadcast_to(spread, (EXPERTS, group_size, capacity, model_dim)).reshape(
            expert_devs, capacity, model_dim
        )

    x_recv, dy_recv = (
        lax.all_to_all(copies(x_slots), "expert", split_axis=0, concat_axis=0, tiled=True),
        lax.all_to_all(copies(dy_slots), "expert", split_axis=0, concat_axis=0, tiled=True),
    )
    in_rows = x_recv.reshape(expert_devs * capacity, model_dim)
    scaled = dy_recv.reshape(expert_devs * capacity, model_dim)
    pre_gate = jnp.dot(in_rows, gate_proj, preferred_element_type=jnp.float32)
    pre_up = jnp.dot(in_rows, up_proj, preferred_element_type=jnp.float32)
    gate_sig = jax.nn.sigmoid(pre_gate)
    hidden = (pre_gate * gate_sig * pre_up).astype(jnp.bfloat16)
    by_width = (((1,), (1,)), ((), ()))
    by_rows = (((0,), (0,)), ((), ()))
    d_hidden = lax.dot_general(scaled, down_proj, by_width, preferred_element_type=jnp.float32)
    d_gate = (d_hidden * pre_up * gate_sig * (1.0 + pre_gate * (1.0 - gate_sig))).astype(
        jnp.bfloat16
    )
    d_up = (d_hidden * pre_gate * gate_sig).astype(jnp.bfloat16)
    grad_down = lax.dot_general(hidden, scaled, by_rows, preferred_element_type=jnp.float32)
    grad_gate = lax.dot_general(in_rows, d_gate, by_rows, preferred_element_type=jnp.float32)
    grad_up = lax.dot_general(in_rows, d_up, by_rows, preferred_element_type=jnp.float32)
    grad_gate, grad_up, grad_down = (
        lax.psum_scatter(
            grad_gate.astype(jnp.bfloat16), "dp", scatter_dimension=0, tiled=True
        ).astype(jnp.float32),
        lax.psum_scatter(
            grad_up.astype(jnp.bfloat16), "dp", scatter_dimension=0, tiled=True
        ).astype(jnp.float32),
        lax.psum_scatter(
            grad_down.astype(jnp.bfloat16), "dp", scatter_dimension=1, tiled=True
        ).astype(jnp.float32),
    )
    joined_grads = jnp.concatenate([d_gate, d_up], 1)
    joined_proj = jnp.concatenate([gate_proj, up_proj], 1)
    partial_value = lax.dot_general(
        joined_grads, joined_proj, by_width, preferred_element_type=jnp.float32
    ).astype(jnp.bfloat16)
    returned = lax.all_to_all(
        partial_value.reshape(expert_devs, capacity, model_dim),
        "expert",
        split_axis=0,
        concat_axis=0,
        tiled=True,
    )
    summed = jnp.sum(
        returned.reshape(EXPERTS, group_size, capacity, model_dim).astype(jnp.float32), axis=1
    )
    summed = summed.reshape(slot_total, model_dim)
    grad_input = jnp.take(summed, slot_of, axis=0).reshape(tok_dev, top_k, model_dim).sum(axis=1)
    return (grad_input.astype(jnp.bfloat16), grad_gate, grad_up, grad_down)


BY_WIDTH = (((1,), (1,)), ((), ()))
BY_ROWS = (((0,), (0,)), ((), ()))


def cut(width):
    pieces = ROWS // (MOST - ROWS)
    return pieces, width // pieces


def width_of(packed):
    pieces = ROWS // (MOST - ROWS)
    return packed.shape[2] * pieces // (pieces + 1)


def cost(flops, moved):
    return pl.CostEstimate(flops=flops, bytes_accessed=moved, transcendentals=0)


def params():
    return pltpu.CompilerParams(vmem_limit_bytes=VMEM_BYTES)


def anywhere(count):
    return [pl.BlockSpec(memory_space=pl.ANY)] * count


def dot(left, right, dims=(((1,), (0,)), ((), ()))):
    return lax.dot_general(left, right, dims, preferred_element_type=jnp.float32)


def ones(mask):
    return jnp.where(mask, 1.0, 0.0).astype(jnp.bfloat16)


def start(pairs, arrived, first=0):
    for at, (source, target) in enumerate(pairs):
        if at >= first:
            pltpu.make_async_copy(source, target, arrived.at[at]).start()


def wait(pairs, arrived, first=0):
    for at, (source, target) in enumerate(pairs):
        if at >= first:
            pltpu.make_async_copy(source, target, arrived.at[at]).wait()


def slot_masks(routes, blocks, width, me=0):
    tokens = routes.shape[1]
    pieces, _ = cut(width)
    experts = lax.broadcasted_iota(jnp.int32, (EXPERTS, tokens), 0)
    named = jnp.where(experts == routes, 1.0, 0.0)
    earlier = lax.broadcasted_iota(jnp.int32, (tokens, tokens), 0) < lax.broadcasted_iota(
        jnp.int32, (tokens, tokens), 1
    )
    before = dot(named.astype(jnp.bfloat16), ones(earlier))
    position = jnp.sum(before * named, axis=0, keepdims=True).astype(jnp.int32)
    slot = lax.broadcasted_iota(jnp.int32, (blocks * ROWS, tokens), 0)
    row = slot % ROWS
    mine = (slot // ROWS) ^ me == routes
    main = mine & (position == row)
    spill = mine & (position == ROWS + row // pieces)
    return main, spill, row % pieces


def pack(blocks, me, routes, gates, tokens, cotangent):
    count, width = tokens.shape
    pieces, step = cut(width)
    sources = (routes, gates, tokens, cotangent)

    def kernel(me_ref, *refs):
        outs, held, arrived = refs[4 : 4 + blocks], refs[4 + blocks : 8 + blocks], refs[-1]
        pairs = list(zip(refs[:4], held))
        start(pairs, arrived)
        wait(pairs[:2], arrived)
        main, spill, piece = slot_masks(held[0][...], blocks, width, me_ref[0])
        mains = ones(main)
        picks = [ones(spill & (piece == at)) for at in range(pieces)]
        main_scale = jnp.sum(jnp.where(main, held[1][...], 0.0), axis=1, keepdims=True)
        spill_scale = jnp.sum(jnp.where(spill, held[1][...], 0.0), axis=1, keepdims=True)
        for half in range(2):
            wait(pairs[: 3 + half], arrived, 2 + half)
            values = held[2 + half]
            rows = dot(mains, values[...])
            extra = jnp.zeros((blocks * ROWS, step), jnp.float32)
            for at in range(pieces):
                extra += dot(picks[at], values[:, at * step : (at + 1) * step])
            if half > 0:
                rows, extra = rows * main_scale, extra * spill_scale
            rows = rows.astype(jnp.bfloat16)
            extra = extra.astype(jnp.bfloat16)
            here = slice(half * ROWS, (half + 1) * ROWS)
            for block in range(blocks):
                part = slice(block * ROWS, (block + 1) * ROWS)
                outs[block][here, :width] = rows[part]
                outs[block][here, width:] = extra[part]

    inside = pl.BlockSpec(memory_space=pltpu.VMEM)
    return pl.pallas_call(
        kernel,
        out_shape=[jax.ShapeDtypeStruct((2 * ROWS, width + step), jnp.bfloat16)] * blocks,
        in_specs=[pl.BlockSpec(memory_space=pltpu.SMEM)] + anywhere(4),
        out_specs=[inside] * blocks,
        scratch_shapes=[pltpu.VMEM(source.shape, source.dtype) for source in sources]
        + [pltpu.SemaphoreType.DMA((4,))],
        compiler_params=params(),
        cost_estimate=cost(8 * blocks * ROWS * count * width, 8 * count * width),
        name="pack",
    )(me, *sources)


def join(received):
    count = len(received)

    def kernel(*refs):
        pairs = [(refs[at], refs[count].at[at]) for at in range(count)]
        start(pairs, refs[-1])
        wait(pairs, refs[-1])

    return pl.pallas_call(
        kernel,
        out_shape=jax.ShapeDtypeStruct((count,) + received[0].shape, jnp.bfloat16),
        in_specs=anywhere(count),
        out_specs=pl.BlockSpec(memory_space=pltpu.VMEM),
        scratch_shapes=[pltpu.SemaphoreType.DMA((count,))],
        compiler_params=params(),
        cost_estimate=cost(0, 4 * received[0].size * count),
        name="join",
    )(*received)


def merge(routes, returned):
    blocks = returned.shape[0]
    tokens = routes.shape[1]
    width = width_of(returned)
    pieces, step = cut(width)

    def kernel(routes_ref, back_ref, out, named, held, arrived):
        pairs = [(routes_ref, named), (back_ref, held)]
        start(pairs, arrived)
        wait(pairs[:1], arrived)
        main, spill, piece = slot_masks(named[...], blocks, width)
        mains = ones(main)
        picks = [ones(spill & (piece == at)) for at in range(pieces)]
        wait(pairs, arrived, 1)
        rows = jnp.concatenate([held[at, :, :width] for at in range(blocks)], 0)
        extra = jnp.concatenate([held[at, :, width:] for at in range(blocks)], 0)
        picked = dot(mains, rows, BY_ROWS)
        for at in range(pieces):
            columns = slice(at * step, (at + 1) * step)
            out[:, columns] = (picked[:, columns] + dot(picks[at], extra, BY_ROWS)).astype(
                jnp.bfloat16
            )

    return pl.pallas_call(
        kernel,
        out_shape=jax.ShapeDtypeStruct((tokens, width), jnp.bfloat16),
        in_specs=anywhere(2),
        out_specs=pl.BlockSpec(memory_space=pltpu.VMEM),
        scratch_shapes=[
            pltpu.VMEM(routes.shape, routes.dtype),
            pltpu.VMEM(returned.shape, returned.dtype),
            pltpu.SemaphoreType.DMA((2,)),
        ],
        compiler_params=params(),
        cost_estimate=cost(4 * blocks * ROWS * tokens * width, 4 * tokens * width),
        name="merge",
    )(routes, returned)


def spill_picks(blocks, pieces, at):
    shape = (blocks * (MOST - ROWS), blocks * ROWS)
    slot = lax.broadcasted_iota(jnp.int32, shape, 0)
    row = lax.broadcasted_iota(jnp.int32, shape, 1)
    return ones(row == slot * pieces + at)


def unpack(main, tail, pieces, begin, first, out):
    blocks = main.shape[0]
    step = tail.shape[2]
    for at in range(blocks):
        out[first + at * ROWS : first + (at + 1) * ROWS, :] = main[at]
    extra = jnp.concatenate([tail[at] for at in range(blocks)], 0)
    spill = slice(first + blocks * ROWS, first + blocks * MOST)
    for at in range(out.shape[1] // step):
        out[spill, at * step : (at + 1) * step] = dot(
            spill_picks(blocks, pieces, begin + at), extra
        ).astype(jnp.bfloat16)


def tile_of(index, tile):
    return pl.ds(pl.multiple_of(index * tile, tile), tile)


def weight_copy(source, target, arrived, index, axis, tile):
    here = tile_of(index, tile)
    view = source.at[:, here] if axis else source.at[here, :]
    return pltpu.make_async_copy(view, target.at[index], arrived.at[index])


def halves(group, half, out):
    here = slice(half * ROWS, (half + 1) * ROWS)
    pairs, at = [], 0
    for item in group:
        if len(item.shape) == 2:
            pairs.append((item.at[here, :], out.at[at]))
            at += 1
        else:
            pairs.append((item.at[:, here, :], out.at[at : at + item.shape[0]]))
            at += item.shape[0]
    return pairs


def hidden_grads(pre_gate, pre_up, d_hidden):
    sig = 0.5 * jnp.tanh(0.5 * pre_gate) + 0.5
    silu = pre_gate * sig
    hidden = (silu * pre_up).astype(jnp.bfloat16)
    d_gate = (d_hidden * pre_up * (sig + silu * (1.0 - sig))).astype(jnp.bfloat16)
    d_up = (d_hidden * silu).astype(jnp.bfloat16)
    return hidden, d_gate, d_up


def back(tile, share, me, part, group, gate_proj, up_proj, down_proj):
    blocks = len(group)
    width, hid = gate_proj.shape
    slots = blocks * MOST
    pieces, step = cut(width)
    tiles = hid // tile
    chunk = 2 * step
    chunks = width // chunk
    shape = (blocks, ROWS, width + step)
    given = 3 * hid + 2 * share

    def kernel(me_ref, part_ref, *refs):
        refs = list(refs)
        group_refs = [refs.pop(0) for _ in range(blocks)]
        gate_ref, up_ref, down_ref, out, kept, handed = [refs.pop(0) for _ in range(6)]
        x_held, dy_held, rows, scaled, factors, cuts = [refs.pop(0) for _ in range(6)]
        tail, staged, gate, up, down = [refs.pop(0) for _ in range(5)]
        x_in, dy_in, gate_in, up_in, down_in, gone, cut_in, turned = refs
        now = pl.program_id(0)
        x_pairs, dy_pairs = halves(group_refs, 0, x_held), halves(group_refs, 1, dy_held)

        def column_copy(source, target, arrived, index):
            here = tile_of(index, tile)
            return pltpu.make_async_copy(
                source.at[:, here], target.at[:, here], arrived.at[index]
            )

        def fetch_x(index):
            column_copy(gate_ref, gate, gate_in, index).start()
            column_copy(up_ref, up, up_in, index).start()

        def fetch_dy(index):
            weight_copy(down_ref, down, down_in, index, 0, tile).start()

        def leave(index):
            columns = tile_of(index, chunk)
            return pltpu.make_async_copy(
                staged.at[:, :, columns], out.at[:, :, columns], gone.at[index]
            )

        def leave_factors():
            first, behind = slice(0, 3 * hid), slice(3 * hid, given)
            pairs = [(factors, kept.at[:, first]), (cuts.at[0], kept.at[:, behind])]
            return pairs + [(factors, handed.at[:, first]), (cuts.at[1], handed.at[:, behind])]

        @pl.when(now == 0)
        def _():
            start(x_pairs, x_in)
            fetch_x(0)
            wait(x_pairs, x_in)
            start(dy_pairs, dy_in)
            fetch_dy(0)
            unpack(x_held.at[:, :, :width], x_held.at[:, :, width:], pieces, 0, 0, rows)
            tail[...] = jnp.zeros_like(tail)

        @pl.when(now < tiles)
        def _():
            columns = tile_of(now, tile)
            column_copy(gate_ref, gate, gate_in, now).wait()
            pre_gate = dot(rows[...], gate[:, columns])

            @pl.when(now < tiles - 1)
            def _():
                fetch_x(now + 1)

            column_copy(up_ref, up, up_in, now).wait()
            pre_up = dot(rows[...], up[:, columns])

            @pl.when(now == 0)
            def _():
                wait(dy_pairs, dy_in)
                unpack(dy_held.at[:, :, :width], dy_held.at[:, :, width:], pieces, 0, 0, scaled)

            @pl.when(now < tiles - 1)
            def _():
                fetch_dy(now + 1)

            weight_copy(down_ref, down, down_in, now, 0, tile).wait()
            d_hidden = dot(scaled[...], down[now], BY_WIDTH)
            made, d_gate, d_up = hidden_grads(pre_gate, pre_up, d_hidden)
            factors[:, columns] = made
            factors[:, tile_of(tiles + now, tile)] = d_gate
            factors[:, tile_of(2 * tiles + now, tile)] = d_up

        @pl.when(now == tiles)
        def _():
            for at in range(2):
                columns = tile_of(part_ref[0] ^ at, share)
                cuts[at, :, :share] = rows[:, columns]
                cuts[at, :, share:] = scaled[:, columns]
            start(leave_factors(), cut_in)
            turned[...] = factors[:, hid:].T

        @pl.when(now >= tiles)
        def _():
            at = now - tiles
            here = tile_of(at, chunk)
            done = dot(gate[here, :], turned[:hid, :]) + dot(up[here, :], turned[hid:, :])
            done = done.T.astype(jnp.bfloat16)
            for block in range(blocks):
                staged[me_ref[0] ^ block, :, here] = done[block * ROWS : (block + 1) * ROWS]
            leave(at).start()
            for piece in range(chunk // step):
                tail[...] += dot(
                    spill_picks(blocks, pieces, at * (chunk // step) + piece),
                    done[blocks * ROWS :, piece * step : (piece + 1) * step],
                    BY_ROWS,
                )

        @pl.when(now == tiles + chunks - 1)
        def _():
            for block in range(blocks):
                part = tail[block * ROWS : (block + 1) * ROWS, :]
                staged[me_ref[0] ^ block, :, width:] = part.astype(jnp.bfloat16)
            last = pltpu.make_async_copy(
                staged.at[:, :, width:], out.at[:, :, width:], gone.at[chunks]
            )
            last.start()
            for at in range(chunks):
                leave(at).wait()
            wait(leave_factors(), cut_in)
            last.wait()

    return pl.pallas_call(
        kernel,
        grid=(tiles + chunks,),
        out_shape=[
            jax.ShapeDtypeStruct(shape, jnp.bfloat16),
            jax.ShapeDtypeStruct((slots, given), jnp.bfloat16),
            jax.ShapeDtypeStruct((slots, given), jnp.bfloat16),
        ],
        in_specs=[pl.BlockSpec(memory_space=pltpu.SMEM)] * 2 + anywhere(blocks + 3),
        out_specs=anywhere(3),
        scratch_shapes=[
            pltpu.VMEM(shape, jnp.bfloat16),
            pltpu.VMEM(shape, jnp.bfloat16),
            pltpu.VMEM((slots, width), jnp.bfloat16),
            pltpu.VMEM((slots, width), jnp.bfloat16),
            pltpu.VMEM((slots, 3 * hid), jnp.bfloat16),
            pltpu.VMEM((2, slots, 2 * share), jnp.bfloat16),
            pltpu.VMEM((blocks * ROWS, step), jnp.float32),
            pltpu.VMEM(shape, jnp.bfloat16),
            pltpu.VMEM((width, hid), jnp.bfloat16),
            pltpu.VMEM((width, hid), jnp.bfloat16),
            pltpu.VMEM((tiles, tile, width), jnp.bfloat16),
            pltpu.SemaphoreType.DMA((blocks,)),
            pltpu.SemaphoreType.DMA((blocks,)),
            pltpu.SemaphoreType.DMA((tiles,)),
            pltpu.SemaphoreType.DMA((tiles,)),
            pltpu.SemaphoreType.DMA((tiles,)),
            pltpu.SemaphoreType.DMA((chunks + 1,)),
            pltpu.SemaphoreType.DMA((4,)),
            pltpu.VMEM((2 * hid, slots), jnp.bfloat16),
        ],
        compiler_params=params(),
        cost_estimate=cost(50 * slots * width * hid, 4 * slots * width),
        name="back",
    )(me, part, *group, gate_proj, up_proj, down_proj)


def weight_grads(tile, share, part, known, groups, gate_proj, up_proj, down_proj):
    count, items = len(groups), len(groups[0])
    blocks = sum(item.shape[0] if item.ndim == 3 else 1 for item in groups[0])
    given = len(known)
    hid, width = down_proj.shape
    pieces, step = cut(width)
    slots = blocks * MOST
    total = (given + count) * slots
    tiles = hid // tile

    def kernel(part_ref, *refs):
        refs = list(refs)
        known_refs = [refs.pop(0) for _ in range(given)]
        group_refs = [[refs.pop(0) for _ in range(items)] for _ in range(count)]
        gate_ref, up_ref, down_ref = [refs.pop(0) for _ in range(3)]
        d_gate_ref, d_up_ref, d_down_ref = [refs.pop(0) for _ in range(3)]
        x_held, dy_held, x_all, dy_all = [refs.pop(0) for _ in range(4)]
        x_mine, dy_mine, factors = [refs.pop(0) for _ in range(3)]
        gate, up, down, x_in, dy_in, known_in, gate_in, up_in, down_in = refs[:9]
        made_gate, made_up, made_down, gate_out, up_out, down_out, x_turned = refs[9:]
        now = pl.program_id(0)
        columns = tile_of(part_ref[0], share)
        x_pairs, dy_pairs, known_pairs = [], [], []
        for at in range(count):
            x_pairs += halves(group_refs[at], 0, x_held.at[at])
            dy_pairs += halves(group_refs[at], 1, dy_held.at[at])
        for at in range(given):
            here = slice(at * slots, (at + 1) * slots)
            behind = 3 * hid
            known_pairs += [
                (known_refs[at].at[:, :behind], factors.at[here, :]),
                (known_refs[at].at[:, behind : behind + share], x_mine.at[here, :]),
                (known_refs[at].at[:, behind + share :], dy_mine.at[here, :]),
            ]

        def arrange(held, rows_out, target):
            for at in range(count):
                unpack(
                    held.at[at, :, :, :width],
                    held.at[at, :, :, width:],
                    pieces,
                    0,
                    at * slots,
                    rows_out,
                )
            target[given * slots :, :] = rows_out[:, columns]

        def leave(source, target, gone, index, axis):
            here = tile_of(index, tile)
            view = target.at[:, here] if axis else target.at[here, :]
            return pltpu.make_async_copy(source.at[index], view, gone.at[index])

        def fetch_x(index):
            weight_copy(gate_ref, gate, gate_in, index, 1, tile).start()
            weight_copy(up_ref, up, up_in, index, 1, tile).start()

        def fetch_dy(index):
            weight_copy(down_ref, down, down_in, index, 0, tile).start()

        @pl.when(now == 0)
        def _():
            start(x_pairs, x_in)
            fetch_x(0)
            wait(x_pairs, x_in)
            start(dy_pairs, dy_in)
            fetch_dy(0)
            arrange(x_held, x_all, x_mine)

        weight_copy(gate_ref, gate, gate_in, now, 1, tile).wait()
        pre_gate = dot(x_all[...], gate[now])
        weight_copy(up_ref, up, up_in, now, 1, tile).wait()
        pre_up = dot(x_all[...], up[now])

        @pl.when(now == 0)
        def _():
            wait(dy_pairs, dy_in)
            start(known_pairs, known_in)
            arrange(dy_held, dy_all, dy_mine)

        @pl.when(now < tiles - 1)
        def _():
            fetch_x(now + 1)
            fetch_dy(now + 1)

        weight_copy(down_ref, down, down_in, now, 0, tile).wait()
        d_hidden = dot(dy_all[...], down[now], BY_WIDTH)
        made, d_gate, d_up = hidden_grads(pre_gate, pre_up, d_hidden)

        @pl.when(now == 0)
        def _():
            wait(known_pairs, known_in)
            x_turned[...] = x_mine[...].T

        made = jnp.concatenate([factors[:, tile_of(now, tile)], made], 0)
        d_gate = jnp.concatenate([factors[:, tile_of(tiles + now, tile)], d_gate], 0)
        d_up = jnp.concatenate([factors[:, tile_of(2 * tiles + now, tile)], d_up], 0)
        sums = dot(x_turned[...], jnp.concatenate([d_gate, d_up], 1))
        made_gate[now] = sums[:, :tile]
        made_up[now] = sums[:, tile:]
        leave(made_gate, d_gate_ref, gate_out, now, 1).start()
        leave(made_up, d_up_ref, up_out, now, 1).start()
        made_down[now] = dot(made, dy_mine[...], BY_ROWS)
        leave(made_down, d_down_ref, down_out, now, 0).start()

        @pl.when(now == tiles - 1)
        def _():
            for at in range(tiles):
                leave(made_gate, d_gate_ref, gate_out, at, 1).wait()
                leave(made_up, d_up_ref, up_out, at, 1).wait()
                leave(made_down, d_down_ref, down_out, at, 0).wait()

    held = pltpu.VMEM((count, blocks, ROWS, width + step), jnp.bfloat16)
    arranged = pltpu.VMEM((count * slots, width), jnp.bfloat16)
    mine = pltpu.VMEM((total, share), jnp.bfloat16)
    return pl.pallas_call(
        kernel,
        grid=(tiles,),
        out_shape=[
            jax.ShapeDtypeStruct((share, hid), jnp.float32),
            jax.ShapeDtypeStruct((share, hid), jnp.float32),
            jax.ShapeDtypeStruct((hid, share), jnp.float32),
        ],
        in_specs=[pl.BlockSpec(memory_space=pltpu.SMEM)] + anywhere(given + count * items + 3),
        out_specs=anywhere(3),
        scratch_shapes=[
            held,
            held,
            arranged,
            arranged,
            mine,
            mine,
            pltpu.VMEM((given * slots, 3 * hid), jnp.bfloat16),
            pltpu.VMEM((tiles, width, tile), jnp.bfloat16),
            pltpu.VMEM((tiles, width, tile), jnp.bfloat16),
            pltpu.VMEM((tiles, tile, width), jnp.bfloat16),
            pltpu.SemaphoreType.DMA((count * items,)),
            pltpu.SemaphoreType.DMA((count * items,)),
            pltpu.SemaphoreType.DMA((3 * given,)),
            pltpu.SemaphoreType.DMA((tiles,)),
            pltpu.SemaphoreType.DMA((tiles,)),
            pltpu.SemaphoreType.DMA((tiles,)),
            pltpu.VMEM((tiles, share, tile), jnp.float32),
            pltpu.VMEM((tiles, share, tile), jnp.float32),
            pltpu.VMEM((tiles, tile, share), jnp.float32),
            pltpu.SemaphoreType.DMA((tiles,)),
            pltpu.SemaphoreType.DMA((tiles,)),
            pltpu.SemaphoreType.DMA((tiles,)),
            pltpu.VMEM((share, total), jnp.bfloat16),
        ],
        compiler_params=params(),
        cost_estimate=cost(0, 4 * slots * width),
        name="weight_grads",
    )(part, *known, *[item for group in groups for item in group], gate_proj, up_proj, down_proj)


def swap(value, axis, distance):
    size = lax.axis_size(axis)
    return lax.ppermute(value, axis, [(at, at ^ distance) for at in range(size)])


def exchange(blocks):
    return lax.all_to_all(blocks, "expert", split_axis=0, concat_axis=0, tiled=True)


def after(value, *earlier):
    return lax.optimization_barrier((value, *earlier))[0]


def gather_body(tokens, cotangent, routes, expert_gates, gate_proj, up_proj, down_proj):
    blocks = lax.axis_size("expert")
    tile, share = 256, tokens.shape[1] // lax.axis_size("dp")
    me = lax.axis_index("expert").astype(jnp.int32).reshape(1)
    part = lax.axis_index("dp").astype(jnp.int32).reshape(1)
    routes = routes.reshape(1, -1)
    gates = expert_gates.reshape(1, -1)
    weights = (gate_proj, up_proj, down_proj)
    received = list(pack(blocks, me, routes, gates, tokens, cotangent))
    for distance in reversed(range(1, blocks)):
        received[distance] = swap(received[distance], "expert", distance)
    half = blocks // 2
    far = swap(join(received[:half]), "dp", 2)
    far_half = swap(join(received[half:]), "dp", 2)
    sent, kept, handed = back(tile, share, me, part, received, *weights)
    sent, far = lax.optimization_barrier((sent, far))
    returned = exchange(sent)
    far = [far, after(far_half, sent)]
    last = [swap(item, "dp", 1) for item in far]
    known = [kept, swap(handed, "dp", 1)]
    grads = weight_grads(tile, share, part, known, [far, last], *weights)
    return (merge(routes, after(returned, *grads)), *grads)


def body(tokens, cotangent, routes, expert_gates, gate_proj, up_proj, down_proj):
    groups, blocks = lax.axis_size("dp"), lax.axis_size("expert")
    width, hid = gate_proj.shape
    rows_sent = (groups - 1) * 2 * blocks * MOST * width
    grads_sent = 3 * width * hid * (groups - 1) // groups
    fits = blocks == EXPERTS and groups == 4 and hid % 256 == 0
    fits = fits and tokens.shape[0] == 128 and routes.shape[1] == 1 and width // groups % 128 == 0
    chosen = gather_body if fits and rows_sent < grads_sent else scatter_body
    return chosen(tokens, cotangent, routes, expert_gates, gate_proj, up_proj, down_proj)


def solution(mesh):
    in_specs = (
        P(("dp", "expert"), None),
        P(("dp", "expert"), None),
        P(("dp", "expert"), None),
        P(("dp", "expert"), None),
        P(None, "expert"),
        P(None, "expert"),
        P("expert", None),
    )
    out_specs = (P(("dp", "expert"), None), P("dp", "expert"), P("dp", "expert"), P("expert", "dp"))
    return jax.shard_map(body, mesh=mesh, in_specs=in_specs, out_specs=out_specs, check_vma=False)
```

```python
import jax
import jax.numpy as jnp
from jax import lax
from jax.experimental import pallas as pl
from jax.experimental.pallas import tpu as pltpu
from jax.sharding import PartitionSpec as P

EXPERTS = 8
MOST = 18
ROWS = 16
VMEM_BYTES = (63 * 1024 + 768) * 1024


def build_slots(routes, capacity):
    flat_routes = routes.reshape(-1)
    one_hot = (flat_routes[:, None] == jnp.arange(EXPERTS, dtype=jnp.int32)[None, :]).astype(
        jnp.int32
    )
    before = jnp.cumsum(one_hot, axis=0) - one_hot
    position = jnp.sum(before * one_hot, axis=1)
    return flat_routes * capacity + position


def scatter_body(tokens, cotangent, routes, expert_gates, gate_proj, up_proj, down_proj):
    tok_dev, model_dim = tokens.shape
    top_k = routes.shape[1]
    expert_devs = lax.axis_size("expert")
    group_size = expert_devs // EXPERTS
    capacity = MOST
    slot_total = EXPERTS * capacity
    slot_of = build_slots(routes, capacity)
    owners = jnp.arange(tok_dev * top_k, dtype=jnp.int32) // top_k
    slot_table = jnp.full((slot_total,), tok_dev, jnp.int32).at[slot_of].set(owners)
    slot_gate = jnp.zeros((slot_total,), jnp.float32).at[slot_of].set(expert_gates.reshape(-1))
    x_slots = jnp.take(tokens, slot_table, axis=0, mode="fill", fill_value=0)
    dy_slots = (
        jnp.take(cotangent, slot_table, axis=0, mode="fill", fill_value=0).astype(jnp.float32)
        * slot_gate[:, None]
    ).astype(jnp.bfloat16)

    def copies(values):
        spread = values.reshape(EXPERTS, 1, capacity, model_dim)
        return jnp.broadcast_to(spread, (EXPERTS, group_size, capacity, model_dim)).reshape(
            expert_devs, capacity, model_dim
        )

    x_recv, dy_recv = (
        lax.all_to_all(copies(x_slots), "expert", split_axis=0, concat_axis=0, tiled=True),
        lax.all_to_all(copies(dy_slots), "expert", split_axis=0, concat_axis=0, tiled=True),
    )
    in_rows = x_recv.reshape(expert_devs * capacity, model_dim)
    scaled = dy_recv.reshape(expert_devs * capacity, model_dim)
    pre_gate = jnp.dot(in_rows, gate_proj, preferred_element_type=jnp.float32)
    pre_up = jnp.dot(in_rows, up_proj, preferred_element_type=jnp.float32)
    gate_sig = jax.nn.sigmoid(pre_gate)
    hidden = (pre_gate * gate_sig * pre_up).astype(jnp.bfloat16)
    by_width = (((1,), (1,)), ((), ()))
    by_rows = (((0,), (0,)), ((), ()))
    d_hidden = lax.dot_general(scaled, down_proj, by_width, preferred_element_type=jnp.float32)
    d_gate = (d_hidden * pre_up * gate_sig * (1.0 + pre_gate * (1.0 - gate_sig))).astype(
        jnp.bfloat16
    )
    d_up = (d_hidden * pre_gate * gate_sig).astype(jnp.bfloat16)
    grad_down = lax.dot_general(hidden, scaled, by_rows, preferred_element_type=jnp.float32)
    grad_gate = lax.dot_general(in_rows, d_gate, by_rows, preferred_element_type=jnp.float32)
    grad_up = lax.dot_general(in_rows, d_up, by_rows, preferred_element_type=jnp.float32)
    grad_gate, grad_up, grad_down = (
        lax.psum_scatter(
            grad_gate.astype(jnp.bfloat16), "dp", scatter_dimension=0, tiled=True
        ).astype(jnp.float32),
        lax.psum_scatter(
            grad_up.astype(jnp.bfloat16), "dp", scatter_dimension=0, tiled=True
        ).astype(jnp.float32),
        lax.psum_scatter(
            grad_down.astype(jnp.bfloat16), "dp", scatter_dimension=1, tiled=True
        ).astype(jnp.float32),
    )
    joined_grads = jnp.concatenate([d_gate, d_up], 1)
    joined_proj = jnp.concatenate([gate_proj, up_proj], 1)
    partial_value = lax.dot_general(
        joined_grads, joined_proj, by_width, preferred_element_type=jnp.float32
    ).astype(jnp.bfloat16)
    returned = lax.all_to_all(
        partial_value.reshape(expert_devs, capacity, model_dim),
        "expert",
        split_axis=0,
        concat_axis=0,
        tiled=True,
    )
    summed = jnp.sum(
        returned.reshape(EXPERTS, group_size, capacity, model_dim).astype(jnp.float32), axis=1
    )
    summed = summed.reshape(slot_total, model_dim)
    grad_input = jnp.take(summed, slot_of, axis=0).reshape(tok_dev, top_k, model_dim).sum(axis=1)
    return (grad_input.astype(jnp.bfloat16), grad_gate, grad_up, grad_down)


BY_WIDTH = (((1,), (1,)), ((), ()))
BY_ROWS = (((0,), (0,)), ((), ()))


def cut(width):
    pieces = ROWS // (MOST - ROWS)
    return pieces, width // pieces


def width_of(packed):
    pieces = ROWS // (MOST - ROWS)
    return packed.shape[2] * pieces // (pieces + 1)


def cost(flops, moved):
    return pl.CostEstimate(flops=flops, bytes_accessed=moved, transcendentals=0)


def params():
    return pltpu.CompilerParams(vmem_limit_bytes=VMEM_BYTES)


def anywhere(count):
    return [pl.BlockSpec(memory_space=pl.ANY)] * count


def dot(left, right, dims=(((1,), (0,)), ((), ()))):
    return lax.dot_general(left, right, dims, preferred_element_type=jnp.float32)


def ones(mask):
    return jnp.where(mask, 1.0, 0.0).astype(jnp.bfloat16)


def start(pairs, arrived, first=0):
    for at, (source, target) in enumerate(pairs):
        if at >= first:
            pltpu.make_async_copy(source, target, arrived.at[at]).start()


def wait(pairs, arrived, first=0):
    for at, (source, target) in enumerate(pairs):
        if at >= first:
            pltpu.make_async_copy(source, target, arrived.at[at]).wait()


def slot_masks(routes, blocks, width, me=0):
    tokens = routes.shape[1]
    pieces, _ = cut(width)
    experts = lax.broadcasted_iota(jnp.int32, (EXPERTS, tokens), 0)
    named = jnp.where(experts == routes, 1.0, 0.0)
    earlier = lax.broadcasted_iota(jnp.int32, (tokens, tokens), 0) < lax.broadcasted_iota(
        jnp.int32, (tokens, tokens), 1
    )
    before = dot(named.astype(jnp.bfloat16), ones(earlier))
    position = jnp.sum(before * named, axis=0, keepdims=True).astype(jnp.int32)
    slot = lax.broadcasted_iota(jnp.int32, (blocks * ROWS, tokens), 0)
    row = slot % ROWS
    mine = (slot // ROWS) ^ me == routes
    main = mine & (position == row)
    spill = mine & (position == ROWS + row // pieces)
    return main, spill, row % pieces


def pack(blocks, me, routes, gates, tokens, cotangent):
    count, width = tokens.shape
    pieces, step = cut(width)
    sources = (routes, gates, tokens, cotangent)

    def kernel(me_ref, *refs):
        outs, held, arrived = refs[4 : 4 + blocks], refs[4 + blocks : 8 + blocks], refs[-1]
        pairs = list(zip(refs[:4], held))
        start(pairs, arrived)
        wait(pairs[:2], arrived)
        main, spill, piece = slot_masks(held[0][...], blocks, width, me_ref[0])
        mains = ones(main)
        picks = [ones(spill & (piece == at)) for at in range(pieces)]
        main_scale = jnp.sum(jnp.where(main, held[1][...], 0.0), axis=1, keepdims=True)
        spill_scale = jnp.sum(jnp.where(spill, held[1][...], 0.0), axis=1, keepdims=True)
        for half in range(2):
            wait(pairs[: 3 + half], arrived, 2 + half)
            values = held[2 + half]
            rows = dot(mains, values[...])
            extra = jnp.zeros((blocks * ROWS, step), jnp.float32)
            for at in range(pieces):
                extra += dot(picks[at], values[:, at * step : (at + 1) * step])
            if half > 0:
                rows, extra = rows * main_scale, extra * spill_scale
            rows = rows.astype(jnp.bfloat16)
            extra = extra.astype(jnp.bfloat16)
            here = slice(half * ROWS, (half + 1) * ROWS)
            for block in range(blocks):
                part = slice(block * ROWS, (block + 1) * ROWS)
                outs[block][here, :width] = rows[part]
                outs[block][here, width:] = extra[part]

    inside = pl.BlockSpec(memory_space=pltpu.VMEM)
    return pl.pallas_call(
        kernel,
        out_shape=[jax.ShapeDtypeStruct((2 * ROWS, width + step), jnp.bfloat16)] * blocks,
        in_specs=[pl.BlockSpec(memory_space=pltpu.SMEM)] + anywhere(4),
        out_specs=[inside] * blocks,
        scratch_shapes=[pltpu.VMEM(source.shape, source.dtype) for source in sources]
        + [pltpu.SemaphoreType.DMA((4,))],
        compiler_params=params(),
        cost_estimate=cost(8 * blocks * ROWS * count * width, 8 * count * width),
        name="pack",
    )(me, *sources)


def join(received):
    count = len(received)

    def kernel(*refs):
        pairs = [(refs[at], refs[count].at[at]) for at in range(count)]
        start(pairs, refs[-1])
        wait(pairs, refs[-1])

    return pl.pallas_call(
        kernel,
        out_shape=jax.ShapeDtypeStruct((count,) + received[0].shape, jnp.bfloat16),
        in_specs=anywhere(count),
        out_specs=pl.BlockSpec(memory_space=pltpu.VMEM),
        scratch_shapes=[pltpu.SemaphoreType.DMA((count,))],
        compiler_params=params(),
        cost_estimate=cost(0, 4 * received[0].size * count),
        name="join",
    )(*received)


def merge(routes, returned):
    blocks = returned.shape[0]
    tokens = routes.shape[1]
    width = width_of(returned)
    pieces, step = cut(width)

    def kernel(routes_ref, back_ref, out, named, held, arrived):
        pairs = [(routes_ref, named), (back_ref, held)]
        start(pairs, arrived)
        wait(pairs[:1], arrived)
        main, spill, piece = slot_masks(named[...], blocks, width)
        mains = ones(main)
        picks = [ones(spill & (piece == at)) for at in range(pieces)]
        wait(pairs, arrived, 1)
        rows = jnp.concatenate([held[at, :, :width] for at in range(blocks)], 0)
        extra = jnp.concatenate([held[at, :, width:] for at in range(blocks)], 0)
        picked = dot(mains, rows, BY_ROWS)
        for at in range(pieces):
            columns = slice(at * step, (at + 1) * step)
            out[:, columns] = (picked[:, columns] + dot(picks[at], extra, BY_ROWS)).astype(
                jnp.bfloat16
            )

    return pl.pallas_call(
        kernel,
        out_shape=jax.ShapeDtypeStruct((tokens, width), jnp.bfloat16),
        in_specs=anywhere(2),
        out_specs=pl.BlockSpec(memory_space=pltpu.VMEM),
        scratch_shapes=[
            pltpu.VMEM(routes.shape, routes.dtype),
            pltpu.VMEM(returned.shape, returned.dtype),
            pltpu.SemaphoreType.DMA((2,)),
        ],
        compiler_params=params(),
        cost_estimate=cost(4 * blocks * ROWS * tokens * width, 4 * tokens * width),
        name="merge",
    )(routes, returned)


def spill_picks(blocks, pieces):
    extras = blocks * (MOST - ROWS)
    shape = (pieces * extras, blocks * ROWS)
    index = lax.broadcasted_iota(jnp.int32, shape, 0)
    row = lax.broadcasted_iota(jnp.int32, shape, 1)
    return ones(row == (index % extras) * pieces + index // extras)


def unpack(packed, first, out):
    blocks, width = packed.shape[0], out.shape[1]
    pieces, step = cut(width)
    extras = blocks * (MOST - ROWS)
    for at in range(blocks):
        out[first + at * ROWS : first + (at + 1) * ROWS, :] = packed[at, :, :width]
    tails = jnp.concatenate([packed[at, :, width:] for at in range(blocks)], 0)
    placed = dot(spill_picks(blocks, pieces), tails).astype(jnp.bfloat16)
    spill = slice(first + blocks * ROWS, first + blocks * MOST)
    for at in range(pieces):
        out[spill, at * step : (at + 1) * step] = placed[at * extras : (at + 1) * extras]


def tile_of(index, tile):
    return pl.ds(pl.multiple_of(index * tile, tile), tile)


def weight_copy(source, target, arrived, index, axis, tile):
    here = tile_of(index, tile)
    view = source.at[:, here] if axis else source.at[here, :]
    return pltpu.make_async_copy(view, target.at[index], arrived.at[index])


def halves(group, half, out):
    here = slice(half * ROWS, (half + 1) * ROWS)
    pairs, at = [], 0
    for item in group:
        if len(item.shape) == 2:
            pairs.append((item.at[here, :], out.at[at]))
            at += 1
        else:
            pairs.append((item.at[:, here, :], out.at[at : at + item.shape[0]]))
            at += item.shape[0]
    return pairs


def hidden_grads(pre_gate, pre_up, d_hidden):
    sig = 0.5 * jnp.tanh(0.5 * pre_gate) + 0.5
    silu = pre_gate * sig
    hidden = (silu * pre_up).astype(jnp.bfloat16)
    d_gate = (d_hidden * pre_up * (sig + silu * (1.0 - sig))).astype(jnp.bfloat16)
    d_up = (d_hidden * silu).astype(jnp.bfloat16)
    return hidden, d_gate, d_up


def back(tile, share, me, part, group, gate_proj, up_proj, down_proj):
    blocks = len(group)
    width, hid = gate_proj.shape
    slots = blocks * MOST
    pieces, step = cut(width)
    tiles = hid // tile
    chunk = 2 * step
    chunks = width // chunk
    shape = (blocks, ROWS, width + step)
    given = 3 * hid + 2 * share

    def kernel(me_ref, part_ref, *refs):
        refs = list(refs)
        group_refs = [refs.pop(0) for _ in range(blocks)]
        gate_ref, up_ref, down_ref, out, kept, handed = [refs.pop(0) for _ in range(6)]
        x_held, dy_held, rows, scaled, factors, cuts = [refs.pop(0) for _ in range(6)]
        staged, gate, up, down = [refs.pop(0) for _ in range(4)]
        x_in, dy_in, gate_in, up_in, down_in, gone, cut_in = refs
        x_pairs, dy_pairs = halves(group_refs, 0, x_held), halves(group_refs, 1, dy_held)

        def column_copy(source, target, arrived, index):
            here = slice(index * tile, (index + 1) * tile)
            return pltpu.make_async_copy(
                source.at[:, here], target.at[:, here], arrived.at[index]
            )

        def fetch_x(index):
            column_copy(gate_ref, gate, gate_in, index).start()
            column_copy(up_ref, up, up_in, index).start()

        def fetch_dy(index):
            weight_copy(down_ref, down, down_in, index, 0, tile).start()

        def leave(index):
            columns = slice(index * chunk, (index + 1) * chunk)
            return pltpu.make_async_copy(
                staged.at[:, :, columns], out.at[:, :, columns], gone.at[index]
            )

        first, behind = slice(0, 3 * hid), slice(3 * hid, given)
        leaving = [(factors, kept.at[:, first]), (cuts.at[0], kept.at[:, behind])]
        leaving += [(factors, handed.at[:, first]), (cuts.at[1], handed.at[:, behind])]

        start(x_pairs, x_in)
        fetch_x(0)
        wait(x_pairs, x_in)
        start(dy_pairs, dy_in)
        fetch_dy(0)
        unpack(x_held, 0, rows)
        for now in range(tiles):
            columns = slice(now * tile, (now + 1) * tile)
            column_copy(gate_ref, gate, gate_in, now).wait()
            pre_gate = dot(rows[...], gate[:, columns])
            if now < tiles - 1:
                fetch_x(now + 1)
            column_copy(up_ref, up, up_in, now).wait()
            pre_up = dot(rows[...], up[:, columns])
            if now == 0:
                wait(dy_pairs, dy_in)
                unpack(dy_held, 0, scaled)
            if now < tiles - 1:
                fetch_dy(now + 1)
            weight_copy(down_ref, down, down_in, now, 0, tile).wait()
            d_hidden = dot(scaled[...], down[now], BY_WIDTH)
            made, d_gate, d_up = hidden_grads(pre_gate, pre_up, d_hidden)
            factors[:, columns] = made
            factors[:, hid + now * tile : hid + (now + 1) * tile] = d_gate
            factors[:, 2 * hid + now * tile : 2 * hid + (now + 1) * tile] = d_up

        for at in range(2):
            columns = tile_of(part_ref[0] ^ at, share)
            cuts[at, :, :share] = rows[:, columns]
            cuts[at, :, share:] = scaled[:, columns]
        start(leaving, cut_in)
        extras = []
        for at in range(chunks):
            here = slice(at * chunk, (at + 1) * chunk)
            done = dot(factors[:, hid : 2 * hid], gate[here, :], BY_WIDTH)
            done += dot(factors[:, 2 * hid :], up[here, :], BY_WIDTH)
            done = done.astype(jnp.bfloat16)
            for block in range(blocks):
                staged[me_ref[0] ^ block, :, here] = done[block * ROWS : (block + 1) * ROWS]
            leave(at).start()
            extras += [done[blocks * ROWS :, :step], done[blocks * ROWS :, step:]]
        tail = dot(spill_picks(blocks, pieces), jnp.concatenate(extras, 0), BY_ROWS)
        tail = tail.astype(jnp.bfloat16)
        for block in range(blocks):
            staged[me_ref[0] ^ block, :, width:] = tail[block * ROWS : (block + 1) * ROWS]
        last = pltpu.make_async_copy(
            staged.at[:, :, width:], out.at[:, :, width:], gone.at[chunks]
        )
        last.start()
        for at in range(chunks):
            leave(at).wait()
        wait(leaving, cut_in)
        last.wait()

    return pl.pallas_call(
        kernel,
        out_shape=[
            jax.ShapeDtypeStruct(shape, jnp.bfloat16),
            jax.ShapeDtypeStruct((slots, given), jnp.bfloat16),
            jax.ShapeDtypeStruct((slots, given), jnp.bfloat16),
        ],
        in_specs=[pl.BlockSpec(memory_space=pltpu.SMEM)] * 2 + anywhere(blocks + 3),
        out_specs=anywhere(3),
        scratch_shapes=[
            pltpu.VMEM(shape, jnp.bfloat16),
            pltpu.VMEM(shape, jnp.bfloat16),
            pltpu.VMEM((slots, width), jnp.bfloat16),
            pltpu.VMEM((slots, width), jnp.bfloat16),
            pltpu.VMEM((slots, 3 * hid), jnp.bfloat16),
            pltpu.VMEM((2, slots, 2 * share), jnp.bfloat16),
            pltpu.VMEM(shape, jnp.bfloat16),
            pltpu.VMEM((width, hid), jnp.bfloat16),
            pltpu.VMEM((width, hid), jnp.bfloat16),
            pltpu.VMEM((tiles, tile, width), jnp.bfloat16),
            pltpu.SemaphoreType.DMA((blocks,)),
            pltpu.SemaphoreType.DMA((blocks,)),
            pltpu.SemaphoreType.DMA((tiles,)),
            pltpu.SemaphoreType.DMA((tiles,)),
            pltpu.SemaphoreType.DMA((tiles,)),
            pltpu.SemaphoreType.DMA((chunks + 1,)),
            pltpu.SemaphoreType.DMA((4,)),
        ],
        compiler_params=params(),
        cost_estimate=cost(50 * slots * width * hid, 4 * slots * width),
        name="back",
    )(me, part, *group, gate_proj, up_proj, down_proj)


def weight_grads(tile, share, part, known, groups, gate_proj, up_proj, down_proj):
    count, items = len(groups), len(groups[0])
    blocks = sum(item.shape[0] if item.ndim == 3 else 1 for item in groups[0])
    given = len(known)
    hid, width = down_proj.shape
    pieces, step = cut(width)
    slots = blocks * MOST
    total = (given + count) * slots
    tiles = hid // tile

    def kernel(part_ref, *refs):
        refs = list(refs)
        known_refs = [refs.pop(0) for _ in range(given)]
        group_refs = [[refs.pop(0) for _ in range(items)] for _ in range(count)]
        gate_ref, up_ref, down_ref = [refs.pop(0) for _ in range(3)]
        d_gate_ref, d_up_ref, d_down_ref = [refs.pop(0) for _ in range(3)]
        x_held, dy_held, x_all, dy_all = [refs.pop(0) for _ in range(4)]
        x_mine, dy_mine, factors = [refs.pop(0) for _ in range(3)]
        gate, up, down, x_in, dy_in, known_in, gate_in, up_in, down_in = refs[:9]
        made_gate, made_up, made_down, gate_out, up_out, down_out = refs[9:]
        now = pl.program_id(0)
        columns = tile_of(part_ref[0], share)
        x_pairs, dy_pairs, known_pairs = [], [], []
        for at in range(count):
            x_pairs += halves(group_refs[at], 0, x_held.at[at])
            dy_pairs += halves(group_refs[at], 1, dy_held.at[at])
        for at in range(given):
            here = slice(at * slots, (at + 1) * slots)
            behind = 3 * hid
            known_pairs += [
                (known_refs[at].at[:, :behind], factors.at[here, :]),
                (known_refs[at].at[:, behind : behind + share], x_mine.at[here, :]),
                (known_refs[at].at[:, behind + share :], dy_mine.at[here, :]),
            ]

        def arrange(held, rows_out, target):
            for at in range(count):
                unpack(held.at[at], at * slots, rows_out)
            target[given * slots :, :] = rows_out[:, columns]

        def leave(source, target, gone, index, axis):
            here = tile_of(index, tile)
            view = target.at[:, here] if axis else target.at[here, :]
            return pltpu.make_async_copy(source.at[index], view, gone.at[index])

        def fetch_x(index):
            weight_copy(gate_ref, gate, gate_in, index, 1, tile).start()
            weight_copy(up_ref, up, up_in, index, 1, tile).start()

        def fetch_dy(index):
            weight_copy(down_ref, down, down_in, index, 0, tile).start()

        @pl.when(now == 0)
        def _():
            start(x_pairs, x_in)
            fetch_x(0)
            wait(x_pairs, x_in)
            start(dy_pairs, dy_in)
            fetch_dy(0)
            arrange(x_held, x_all, x_mine)

        weight_copy(gate_ref, gate, gate_in, now, 1, tile).wait()
        pre_gate = dot(x_all[...], gate[now])
        weight_copy(up_ref, up, up_in, now, 1, tile).wait()
        pre_up = dot(x_all[...], up[now])

        @pl.when(now == 0)
        def _():
            wait(dy_pairs, dy_in)
            start(known_pairs, known_in)
            arrange(dy_held, dy_all, dy_mine)

        @pl.when(now < tiles - 1)
        def _():
            fetch_x(now + 1)
            fetch_dy(now + 1)

        weight_copy(down_ref, down, down_in, now, 0, tile).wait()
        d_hidden = dot(dy_all[...], down[now], BY_WIDTH)
        made, d_gate, d_up = hidden_grads(pre_gate, pre_up, d_hidden)

        @pl.when(now == 0)
        def _():
            wait(known_pairs, known_in)

        made = jnp.concatenate([factors[:, tile_of(now, tile)], made], 0)
        d_gate = jnp.concatenate([factors[:, tile_of(tiles + now, tile)], d_gate], 0)
        d_up = jnp.concatenate([factors[:, tile_of(2 * tiles + now, tile)], d_up], 0)
        sums = dot(x_mine[...], jnp.concatenate([d_gate, d_up], 1), BY_ROWS)
        made_gate[now] = sums[:, :tile]
        made_up[now] = sums[:, tile:]
        leave(made_gate, d_gate_ref, gate_out, now, 1).start()
        leave(made_up, d_up_ref, up_out, now, 1).start()
        made_down[now] = dot(made, dy_mine[...], BY_ROWS)
        leave(made_down, d_down_ref, down_out, now, 0).start()

        @pl.when(now == tiles - 1)
        def _():
            for at in range(tiles):
                leave(made_gate, d_gate_ref, gate_out, at, 1).wait()
                leave(made_up, d_up_ref, up_out, at, 1).wait()
                leave(made_down, d_down_ref, down_out, at, 0).wait()

    held = pltpu.VMEM((count, blocks, ROWS, width + step), jnp.bfloat16)
    arranged = pltpu.VMEM((count * slots, width), jnp.bfloat16)
    mine = pltpu.VMEM((total, share), jnp.bfloat16)
    return pl.pallas_call(
        kernel,
        grid=(tiles,),
        out_shape=[
            jax.ShapeDtypeStruct((share, hid), jnp.float32),
            jax.ShapeDtypeStruct((share, hid), jnp.float32),
            jax.ShapeDtypeStruct((hid, share), jnp.float32),
        ],
        in_specs=[pl.BlockSpec(memory_space=pltpu.SMEM)] + anywhere(given + count * items + 3),
        out_specs=anywhere(3),
        scratch_shapes=[
            held,
            held,
            arranged,
            arranged,
            mine,
            mine,
            pltpu.VMEM((given * slots, 3 * hid), jnp.bfloat16),
            pltpu.VMEM((tiles, width, tile), jnp.bfloat16),
            pltpu.VMEM((tiles, width, tile), jnp.bfloat16),
            pltpu.VMEM((tiles, tile, width), jnp.bfloat16),
            pltpu.SemaphoreType.DMA((count * items,)),
            pltpu.SemaphoreType.DMA((count * items,)),
            pltpu.SemaphoreType.DMA((3 * given,)),
            pltpu.SemaphoreType.DMA((tiles,)),
            pltpu.SemaphoreType.DMA((tiles,)),
            pltpu.SemaphoreType.DMA((tiles,)),
            pltpu.VMEM((tiles, share, tile), jnp.float32),
            pltpu.VMEM((tiles, share, tile), jnp.float32),
            pltpu.VMEM((tiles, tile, share), jnp.float32),
            pltpu.SemaphoreType.DMA((tiles,)),
            pltpu.SemaphoreType.DMA((tiles,)),
            pltpu.SemaphoreType.DMA((tiles,)),
        ],
        compiler_params=params(),
        cost_estimate=cost(0, 4 * slots * width),
        name="weight_grads",
    )(part, *known, *[item for group in groups for item in group], gate_proj, up_proj, down_proj)


def swap(value, axis, distance):
    size = lax.axis_size(axis)
    return lax.ppermute(value, axis, [(at, at ^ distance) for at in range(size)])


def exchange(blocks):
    return lax.all_to_all(blocks, "expert", split_axis=0, concat_axis=0, tiled=True)


def after(value, *earlier):
    return lax.optimization_barrier((value, *earlier))[0]


def gather_body(tokens, cotangent, routes, expert_gates, gate_proj, up_proj, down_proj):
    blocks = lax.axis_size("expert")
    tile, share = 256, tokens.shape[1] // lax.axis_size("dp")
    me = lax.axis_index("expert").astype(jnp.int32).reshape(1)
    part = lax.axis_index("dp").astype(jnp.int32).reshape(1)
    routes = routes.reshape(1, -1)
    gates = expert_gates.reshape(1, -1)
    weights = (gate_proj, up_proj, down_proj)
    received = list(pack(blocks, me, routes, gates, tokens, cotangent))
    for distance in reversed(range(1, blocks)):
        received[distance] = swap(received[distance], "expert", distance)
    half = blocks // 2
    far = swap(join(received[:half]), "dp", 2)
    far_half = swap(join(received[half:]), "dp", 2)
    sent, kept, handed = back(tile, share, me, part, received, *weights)
    sent, far = lax.optimization_barrier((sent, far))
    returned = exchange(sent)
    far = [far, after(far_half, sent)]
    last = [swap(item, "dp", 1) for item in far]
    known = [kept, swap(handed, "dp", 1)]
    grads = weight_grads(tile, share, part, known, [far, last], *weights)
    return (merge(routes, after(returned, *grads)), *grads)


def body(tokens, cotangent, routes, expert_gates, gate_proj, up_proj, down_proj):
    groups, blocks = lax.axis_size("dp"), lax.axis_size("expert")
    width, hid = gate_proj.shape
    rows_sent = (groups - 1) * 2 * blocks * MOST * width
    grads_sent = 3 * width * hid * (groups - 1) // groups
    fits = blocks == EXPERTS and groups == 4 and hid % 256 == 0
    fits = fits and tokens.shape[0] == 128 and routes.shape[1] == 1 and width // groups % 128 == 0
    chosen = gather_body if fits and rows_sent < grads_sent else scatter_body
    return chosen(tokens, cotangent, routes, expert_gates, gate_proj, up_proj, down_proj)


def solution(mesh):
    in_specs = (
        P(("dp", "expert"), None),
        P(("dp", "expert"), None),
        P(("dp", "expert"), None),
        P(("dp", "expert"), None),
        P(None, "expert"),
        P(None, "expert"),
        P("expert", None),
    )
    out_specs = (P(("dp", "expert"), None), P("dp", "expert"), P("dp", "expert"), P("expert", "dp"))
    return jax.shard_map(body, mesh=mesh, in_specs=in_specs, out_specs=out_specs, check_vma=False)
```

```python
import jax
import jax.numpy as jnp
from jax import lax
from jax.experimental import pallas as pl
from jax.experimental.pallas import tpu as pltpu
from jax.sharding import PartitionSpec as P

EXPERTS = 8
MOST = 18
ROWS = 16
VMEM_BYTES = (63 * 1024 + 768) * 1024


def build_slots(routes, capacity):
    flat_routes = routes.reshape(-1)
    one_hot = (flat_routes[:, None] == jnp.arange(EXPERTS, dtype=jnp.int32)[None, :]).astype(
        jnp.int32
    )
    before = jnp.cumsum(one_hot, axis=0) - one_hot
    position = jnp.sum(before * one_hot, axis=1)
    return flat_routes * capacity + position


def scatter_body(tokens, cotangent, routes, expert_gates, gate_proj, up_proj, down_proj):
    tok_dev, model_dim = tokens.shape
    top_k = routes.shape[1]
    expert_devs = lax.axis_size("expert")
    group_size = expert_devs // EXPERTS
    capacity = MOST
    slot_total = EXPERTS * capacity
    slot_of = build_slots(routes, capacity)
    owners = jnp.arange(tok_dev * top_k, dtype=jnp.int32) // top_k
    slot_table = jnp.full((slot_total,), tok_dev, jnp.int32).at[slot_of].set(owners)
    slot_gate = jnp.zeros((slot_total,), jnp.float32).at[slot_of].set(expert_gates.reshape(-1))
    x_slots = jnp.take(tokens, slot_table, axis=0, mode="fill", fill_value=0)
    dy_slots = (
        jnp.take(cotangent, slot_table, axis=0, mode="fill", fill_value=0).astype(jnp.float32)
        * slot_gate[:, None]
    ).astype(jnp.bfloat16)

    def copies(values):
        spread = values.reshape(EXPERTS, 1, capacity, model_dim)
        return jnp.broadcast_to(spread, (EXPERTS, group_size, capacity, model_dim)).reshape(
            expert_devs, capacity, model_dim
        )

    x_recv, dy_recv = (
        lax.all_to_all(copies(x_slots), "expert", split_axis=0, concat_axis=0, tiled=True),
        lax.all_to_all(copies(dy_slots), "expert", split_axis=0, concat_axis=0, tiled=True),
    )
    in_rows = x_recv.reshape(expert_devs * capacity, model_dim)
    scaled = dy_recv.reshape(expert_devs * capacity, model_dim)
    pre_gate = jnp.dot(in_rows, gate_proj, preferred_element_type=jnp.float32)
    pre_up = jnp.dot(in_rows, up_proj, preferred_element_type=jnp.float32)
    gate_sig = jax.nn.sigmoid(pre_gate)
    hidden = (pre_gate * gate_sig * pre_up).astype(jnp.bfloat16)
    by_width = (((1,), (1,)), ((), ()))
    by_rows = (((0,), (0,)), ((), ()))
    d_hidden = lax.dot_general(scaled, down_proj, by_width, preferred_element_type=jnp.float32)
    d_gate = (d_hidden * pre_up * gate_sig * (1.0 + pre_gate * (1.0 - gate_sig))).astype(
        jnp.bfloat16
    )
    d_up = (d_hidden * pre_gate * gate_sig).astype(jnp.bfloat16)
    grad_down = lax.dot_general(hidden, scaled, by_rows, preferred_element_type=jnp.float32)
    grad_gate = lax.dot_general(in_rows, d_gate, by_rows, preferred_element_type=jnp.float32)
    grad_up = lax.dot_general(in_rows, d_up, by_rows, preferred_element_type=jnp.float32)
    grad_gate, grad_up, grad_down = (
        lax.psum_scatter(
            grad_gate.astype(jnp.bfloat16), "dp", scatter_dimension=0, tiled=True
        ).astype(jnp.float32),
        lax.psum_scatter(
            grad_up.astype(jnp.bfloat16), "dp", scatter_dimension=0, tiled=True
        ).astype(jnp.float32),
        lax.psum_scatter(
            grad_down.astype(jnp.bfloat16), "dp", scatter_dimension=1, tiled=True
        ).astype(jnp.float32),
    )
    joined_grads = jnp.concatenate([d_gate, d_up], 1)
    joined_proj = jnp.concatenate([gate_proj, up_proj], 1)
    partial_value = lax.dot_general(
        joined_grads, joined_proj, by_width, preferred_element_type=jnp.float32
    ).astype(jnp.bfloat16)
    returned = lax.all_to_all(
        partial_value.reshape(expert_devs, capacity, model_dim),
        "expert",
        split_axis=0,
        concat_axis=0,
        tiled=True,
    )
    summed = jnp.sum(
        returned.reshape(EXPERTS, group_size, capacity, model_dim).astype(jnp.float32), axis=1
    )
    summed = summed.reshape(slot_total, model_dim)
    grad_input = jnp.take(summed, slot_of, axis=0).reshape(tok_dev, top_k, model_dim).sum(axis=1)
    return (grad_input.astype(jnp.bfloat16), grad_gate, grad_up, grad_down)


BY_WIDTH = (((1,), (1,)), ((), ()))
BY_ROWS = (((0,), (0,)), ((), ()))


def cut(width):
    pieces = ROWS // (MOST - ROWS)
    return pieces, width // pieces


def width_of(packed):
    pieces = ROWS // (MOST - ROWS)
    return packed.shape[2] * pieces // (pieces + 1)


def cost(flops, moved):
    return pl.CostEstimate(flops=flops, bytes_accessed=moved, transcendentals=0)


def params():
    return pltpu.CompilerParams(vmem_limit_bytes=VMEM_BYTES)


def anywhere(count):
    return [pl.BlockSpec(memory_space=pl.ANY)] * count


def dot(left, right, dims=(((1,), (0,)), ((), ()))):
    return lax.dot_general(left, right, dims, preferred_element_type=jnp.float32)


def ones(mask):
    return jnp.where(mask, 1.0, 0.0).astype(jnp.bfloat16)


def start(pairs, arrived, first=0):
    for at, (source, target) in enumerate(pairs):
        if at >= first:
            pltpu.make_async_copy(source, target, arrived.at[at]).start()


def wait(pairs, arrived, first=0):
    for at, (source, target) in enumerate(pairs):
        if at >= first:
            pltpu.make_async_copy(source, target, arrived.at[at]).wait()


def slot_masks(routes, blocks, width, me=0):
    tokens = routes.shape[1]
    pieces, _ = cut(width)
    experts = lax.broadcasted_iota(jnp.int32, (EXPERTS, tokens), 0)
    named = jnp.where(experts == routes, 1.0, 0.0)
    earlier = lax.broadcasted_iota(jnp.int32, (tokens, tokens), 0) < lax.broadcasted_iota(
        jnp.int32, (tokens, tokens), 1
    )
    before = dot(named.astype(jnp.bfloat16), ones(earlier))
    position = jnp.sum(before * named, axis=0, keepdims=True).astype(jnp.int32)
    slot = lax.broadcasted_iota(jnp.int32, (blocks * ROWS, tokens), 0)
    row = slot % ROWS
    mine = (slot // ROWS) ^ me == routes
    main = mine & (position == row)
    spill = mine & (position == ROWS + row // pieces)
    return main, spill, row % pieces


def pack(blocks, me, routes, gates, tokens, cotangent):
    count, width = tokens.shape
    pieces, step = cut(width)
    sources = (routes, gates, tokens, cotangent)

    def kernel(me_ref, *refs):
        outs, held, arrived = refs[4 : 4 + blocks], refs[4 + blocks : 8 + blocks], refs[-1]
        pairs = list(zip(refs[:4], held))
        start(pairs, arrived)
        wait(pairs[:2], arrived)
        main, spill, piece = slot_masks(held[0][...], blocks, width, me_ref[0])
        mains = ones(main)
        picks = [ones(spill & (piece == at)) for at in range(pieces)]
        main_scale = jnp.sum(jnp.where(main, held[1][...], 0.0), axis=1, keepdims=True)
        spill_scale = jnp.sum(jnp.where(spill, held[1][...], 0.0), axis=1, keepdims=True)
        for half in range(2):
            wait(pairs[: 3 + half], arrived, 2 + half)
            values = held[2 + half]
            rows = dot(mains, values[...])
            extra = jnp.zeros((blocks * ROWS, step), jnp.float32)
            for at in range(pieces):
                extra += dot(picks[at], values[:, at * step : (at + 1) * step])
            if half > 0:
                rows, extra = rows * main_scale, extra * spill_scale
            rows = rows.astype(jnp.bfloat16)
            extra = extra.astype(jnp.bfloat16)
            here = slice(half * ROWS, (half + 1) * ROWS)
            for block in range(blocks):
                part = slice(block * ROWS, (block + 1) * ROWS)
                outs[block][here, :width] = rows[part]
                outs[block][here, width:] = extra[part]

    inside = pl.BlockSpec(memory_space=pltpu.VMEM)
    return pl.pallas_call(
        kernel,
        out_shape=[jax.ShapeDtypeStruct((2 * ROWS, width + step), jnp.bfloat16)] * blocks,
        in_specs=[pl.BlockSpec(memory_space=pltpu.SMEM)] + anywhere(4),
        out_specs=[inside] * blocks,
        scratch_shapes=[pltpu.VMEM(source.shape, source.dtype) for source in sources]
        + [pltpu.SemaphoreType.DMA((4,))],
        compiler_params=params(),
        cost_estimate=cost(8 * blocks * ROWS * count * width, 8 * count * width),
        name="pack",
    )(me, *sources)


def join(received):
    count = len(received)

    def kernel(*refs):
        pairs = [(refs[at], refs[count].at[at]) for at in range(count)]
        start(pairs, refs[-1])
        wait(pairs, refs[-1])

    return pl.pallas_call(
        kernel,
        out_shape=jax.ShapeDtypeStruct((count,) + received[0].shape, jnp.bfloat16),
        in_specs=anywhere(count),
        out_specs=pl.BlockSpec(memory_space=pltpu.VMEM),
        scratch_shapes=[pltpu.SemaphoreType.DMA((count,))],
        compiler_params=params(),
        cost_estimate=cost(0, 4 * received[0].size * count),
        name="join",
    )(*received)


def merge(routes, returned):
    blocks = returned.shape[0]
    tokens = routes.shape[1]
    width = width_of(returned)
    pieces, step = cut(width)

    def kernel(routes_ref, back_ref, out, named, held, arrived):
        pairs = [(routes_ref, named), (back_ref, held)]
        start(pairs, arrived)
        wait(pairs[:1], arrived)
        main, spill, piece = slot_masks(named[...], blocks, width)
        mains = ones(main)
        picks = [ones(spill & (piece == at)) for at in range(pieces)]
        wait(pairs, arrived, 1)
        rows = jnp.concatenate([held[at, :, :width] for at in range(blocks)], 0)
        extra = jnp.concatenate([held[at, :, width:] for at in range(blocks)], 0)
        picked = dot(mains, rows, BY_ROWS)
        for at in range(pieces):
            columns = slice(at * step, (at + 1) * step)
            out[:, columns] = (picked[:, columns] + dot(picks[at], extra, BY_ROWS)).astype(
                jnp.bfloat16
            )

    return pl.pallas_call(
        kernel,
        out_shape=jax.ShapeDtypeStruct((tokens, width), jnp.bfloat16),
        in_specs=anywhere(2),
        out_specs=pl.BlockSpec(memory_space=pltpu.VMEM),
        scratch_shapes=[
            pltpu.VMEM(routes.shape, routes.dtype),
            pltpu.VMEM(returned.shape, returned.dtype),
            pltpu.SemaphoreType.DMA((2,)),
        ],
        compiler_params=params(),
        cost_estimate=cost(4 * blocks * ROWS * tokens * width, 4 * tokens * width),
        name="merge",
    )(routes, returned)


def spill_picks(blocks, pieces):
    extras = blocks * (MOST - ROWS)
    shape = (pieces * extras, blocks * ROWS)
    index = lax.broadcasted_iota(jnp.int32, shape, 0)
    row = lax.broadcasted_iota(jnp.int32, shape, 1)
    return ones(row == (index % extras) * pieces + index // extras)


def unpack(packed, first, out):
    blocks, width = packed.shape[0], out.shape[1]
    pieces, step = cut(width)
    extras = blocks * (MOST - ROWS)
    for at in range(blocks):
        out[first + at * ROWS : first + (at + 1) * ROWS, :] = packed[at, :, :width]
    tails = jnp.concatenate([packed[at, :, width:] for at in range(blocks)], 0)
    placed = dot(spill_picks(blocks, pieces), tails).astype(jnp.bfloat16)
    spill = slice(first + blocks * ROWS, first + blocks * MOST)
    for at in range(pieces):
        out[spill, at * step : (at + 1) * step] = placed[at * extras : (at + 1) * extras]


def tile_of(index, tile):
    return pl.ds(pl.multiple_of(index * tile, tile), tile)


def weight_copy(source, target, arrived, index, axis, tile):
    here = tile_of(index, tile)
    view = source.at[:, here] if axis else source.at[here, :]
    return pltpu.make_async_copy(view, target.at[index], arrived.at[index])


def halves(group, half, out):
    here = slice(half * ROWS, (half + 1) * ROWS)
    pairs, at = [], 0
    for item in group:
        if len(item.shape) == 2:
            pairs.append((item.at[here, :], out.at[at]))
            at += 1
        else:
            pairs.append((item.at[:, here, :], out.at[at : at + item.shape[0]]))
            at += item.shape[0]
    return pairs


def hidden_grads(pre_gate, pre_up, d_hidden):
    sig = 0.5 * jnp.tanh(0.5 * pre_gate) + 0.5
    silu = pre_gate * sig
    hidden = (silu * pre_up).astype(jnp.bfloat16)
    d_gate = (d_hidden * pre_up * (sig + silu * (1.0 - sig))).astype(jnp.bfloat16)
    d_up = (d_hidden * silu).astype(jnp.bfloat16)
    return hidden, d_gate, d_up


def back(tile, share, me, part, group, gate_proj, up_proj, down_proj):
    blocks = len(group)
    width, hid = gate_proj.shape
    slots = blocks * MOST
    pieces, step = cut(width)
    tiles = hid // tile
    chunk = 2 * step
    chunks = width // chunk
    shape = (blocks, ROWS, width + step)
    given = 3 * hid + 2 * share

    def kernel(me_ref, part_ref, *refs):
        refs = list(refs)
        group_refs = [refs.pop(0) for _ in range(blocks)]
        gate_ref, up_ref, down_ref, out, kept, handed = [refs.pop(0) for _ in range(6)]
        x_held, dy_held, rows, scaled, factors, cuts = [refs.pop(0) for _ in range(6)]
        staged, gate, up, down = [refs.pop(0) for _ in range(4)]
        x_in, dy_in, gate_in, up_in, down_in, gone, cut_in = refs
        x_pairs, dy_pairs = halves(group_refs, 0, x_held), halves(group_refs, 1, dy_held)

        def column_copy(source, target, arrived, index):
            here = slice(index * tile, (index + 1) * tile)
            return pltpu.make_async_copy(
                source.at[:, here], target.at[:, here], arrived.at[index]
            )

        def fetch_x(index):
            column_copy(gate_ref, gate, gate_in, index).start()
            column_copy(up_ref, up, up_in, index).start()

        def fetch_dy(index):
            weight_copy(down_ref, down, down_in, index, 0, tile).start()

        def leave(index):
            columns = slice(index * chunk, (index + 1) * chunk)
            return pltpu.make_async_copy(
                staged.at[:, :, columns], out.at[:, :, columns], gone.at[index]
            )

        first, behind = slice(0, 3 * hid), slice(3 * hid, given)
        leaving = [(factors, kept.at[:, first]), (cuts.at[0], kept.at[:, behind])]
        leaving += [(factors, handed.at[:, first]), (cuts.at[1], handed.at[:, behind])]

        start(x_pairs, x_in)
        fetch_x(0)
        wait(x_pairs, x_in)
        start(dy_pairs, dy_in)
        fetch_dy(0)
        unpack(x_held, 0, rows)
        for now in range(tiles):
            columns = slice(now * tile, (now + 1) * tile)
            column_copy(gate_ref, gate, gate_in, now).wait()
            pre_gate = dot(rows[...], gate[:, columns])
            if now < tiles - 1:
                fetch_x(now + 1)
            column_copy(up_ref, up, up_in, now).wait()
            pre_up = dot(rows[...], up[:, columns])
            if now == 0:
                wait(dy_pairs, dy_in)
                unpack(dy_held, 0, scaled)
            if now < tiles - 1:
                fetch_dy(now + 1)
            weight_copy(down_ref, down, down_in, now, 0, tile).wait()
            d_hidden = dot(scaled[...], down[now], BY_WIDTH)
            made, d_gate, d_up = hidden_grads(pre_gate, pre_up, d_hidden)
            factors[:, columns] = made
            factors[:, hid + now * tile : hid + (now + 1) * tile] = d_gate
            factors[:, 2 * hid + now * tile : 2 * hid + (now + 1) * tile] = d_up

        for at in range(2):
            columns = tile_of(part_ref[0] ^ at, share)
            cuts[at, :, :share] = rows[:, columns]
            cuts[at, :, share:] = scaled[:, columns]
        start(leaving, cut_in)
        extras = []
        for at in range(chunks):
            here = slice(at * chunk, (at + 1) * chunk)
            done = dot(factors[:, hid : 2 * hid], gate[here, :], BY_WIDTH)
            done += dot(factors[:, 2 * hid :], up[here, :], BY_WIDTH)
            done = done.astype(jnp.bfloat16)
            for block in range(blocks):
                staged[me_ref[0] ^ block, :, here] = done[block * ROWS : (block + 1) * ROWS]
            leave(at).start()
            extras += [done[blocks * ROWS :, :step], done[blocks * ROWS :, step:]]
        tail = dot(spill_picks(blocks, pieces), jnp.concatenate(extras, 0), BY_ROWS)
        tail = tail.astype(jnp.bfloat16)
        for block in range(blocks):
            staged[me_ref[0] ^ block, :, width:] = tail[block * ROWS : (block + 1) * ROWS]
        last = pltpu.make_async_copy(
            staged.at[:, :, width:], out.at[:, :, width:], gone.at[chunks]
        )
        last.start()
        for at in range(chunks):
            leave(at).wait()
        wait(leaving, cut_in)
        last.wait()

    return pl.pallas_call(
        kernel,
        out_shape=[
            jax.ShapeDtypeStruct(shape, jnp.bfloat16),
            jax.ShapeDtypeStruct((slots, given), jnp.bfloat16),
            jax.ShapeDtypeStruct((slots, given), jnp.bfloat16),
        ],
        in_specs=[pl.BlockSpec(memory_space=pltpu.SMEM)] * 2 + anywhere(blocks + 3),
        out_specs=anywhere(3),
        scratch_shapes=[
            pltpu.VMEM(shape, jnp.bfloat16),
            pltpu.VMEM(shape, jnp.bfloat16),
            pltpu.VMEM((slots, width), jnp.bfloat16),
            pltpu.VMEM((slots, width), jnp.bfloat16),
            pltpu.VMEM((slots, 3 * hid), jnp.bfloat16),
            pltpu.VMEM((2, slots, 2 * share), jnp.bfloat16),
            pltpu.VMEM(shape, jnp.bfloat16),
            pltpu.VMEM((width, hid), jnp.bfloat16),
            pltpu.VMEM((width, hid), jnp.bfloat16),
            pltpu.VMEM((tiles, tile, width), jnp.bfloat16),
            pltpu.SemaphoreType.DMA((blocks,)),
            pltpu.SemaphoreType.DMA((blocks,)),
            pltpu.SemaphoreType.DMA((tiles,)),
            pltpu.SemaphoreType.DMA((tiles,)),
            pltpu.SemaphoreType.DMA((tiles,)),
            pltpu.SemaphoreType.DMA((chunks + 1,)),
            pltpu.SemaphoreType.DMA((4,)),
        ],
        compiler_params=params(),
        cost_estimate=cost(50 * slots * width * hid, 4 * slots * width),
        name="back",
    )(me, part, *group, gate_proj, up_proj, down_proj)


def weight_grads(tile, share, part, known, groups, gate_proj, up_proj, down_proj):
    count, items = len(groups), len(groups[0])
    blocks = sum(item.shape[0] if item.ndim == 3 else 1 for item in groups[0])
    given = len(known)
    hid, width = down_proj.shape
    pieces, step = cut(width)
    slots = blocks * MOST
    total = (given + count) * slots
    tiles = hid // tile

    def kernel(part_ref, *refs):
        refs = list(refs)
        known_refs = [refs.pop(0) for _ in range(given)]
        group_refs = [[refs.pop(0) for _ in range(items)] for _ in range(count)]
        gate_ref, up_ref, down_ref = [refs.pop(0) for _ in range(3)]
        d_gate_ref, d_up_ref, d_down_ref = [refs.pop(0) for _ in range(3)]
        x_held, dy_held, x_all, dy_all = [refs.pop(0) for _ in range(4)]
        x_mine, dy_mine, factors = [refs.pop(0) for _ in range(3)]
        gate, up, down, x_in, dy_in, known_in, gate_in, up_in, down_in = refs[:9]
        made_gate, made_up, made_down, gate_out, up_out, down_out = refs[9:]
        columns = tile_of(part_ref[0], share)
        x_pairs, dy_pairs, known_pairs = [], [], []
        for at in range(count):
            x_pairs += halves(group_refs[at], 0, x_held.at[at])
            dy_pairs += halves(group_refs[at], 1, dy_held.at[at])
        for at in range(given):
            here = slice(at * slots, (at + 1) * slots)
            behind = 3 * hid
            known_pairs += [
                (known_refs[at].at[:, :behind], factors.at[here, :]),
                (known_refs[at].at[:, behind : behind + share], x_mine.at[here, :]),
                (known_refs[at].at[:, behind + share :], dy_mine.at[here, :]),
            ]

        def arrange(held, rows_out, target):
            for at in range(count):
                unpack(held.at[at], at * slots, rows_out)
            target[given * slots :, :] = rows_out[:, columns]

        def leave(source, target, gone, index, axis):
            here = tile_of(index, tile)
            view = target.at[:, here] if axis else target.at[here, :]
            return pltpu.make_async_copy(source.at[index], view, gone.at[index])

        def fetch_x(index):
            weight_copy(gate_ref, gate, gate_in, index, 1, tile).start()
            weight_copy(up_ref, up, up_in, index, 1, tile).start()

        def fetch_dy(index):
            weight_copy(down_ref, down, down_in, index, 0, tile).start()

        start(x_pairs, x_in)
        fetch_x(0)
        wait(x_pairs, x_in)
        start(dy_pairs, dy_in)
        fetch_dy(0)
        arrange(x_held, x_all, x_mine)
        for now in range(tiles):
            here = slice(now * tile, (now + 1) * tile)
            weight_copy(gate_ref, gate, gate_in, now, 1, tile).wait()
            pre_gate = dot(x_all[...], gate[now])
            weight_copy(up_ref, up, up_in, now, 1, tile).wait()
            pre_up = dot(x_all[...], up[now])
            if now == 0:
                wait(dy_pairs, dy_in)
                start(known_pairs, known_in)
                arrange(dy_held, dy_all, dy_mine)
            if now < tiles - 1:
                fetch_x(now + 1)
                fetch_dy(now + 1)
            weight_copy(down_ref, down, down_in, now, 0, tile).wait()
            d_hidden = dot(dy_all[...], down[now], BY_WIDTH)
            made, d_gate, d_up = hidden_grads(pre_gate, pre_up, d_hidden)
            if now == 0:
                wait(known_pairs, known_in)
            made = jnp.concatenate([factors[:, here], made], 0)
            d_gate = jnp.concatenate([factors[:, hid + here.start : hid + here.stop], d_gate], 0)
            d_up = jnp.concatenate(
                [factors[:, 2 * hid + here.start : 2 * hid + here.stop], d_up], 0
            )
            sums = dot(x_mine[...], jnp.concatenate([d_gate, d_up], 1), BY_ROWS)
            made_gate[now] = sums[:, :tile]
            made_up[now] = sums[:, tile:]
            leave(made_gate, d_gate_ref, gate_out, now, 1).start()
            leave(made_up, d_up_ref, up_out, now, 1).start()
            made_down[now] = dot(made, dy_mine[...], BY_ROWS)
            leave(made_down, d_down_ref, down_out, now, 0).start()
        for at in range(tiles):
            leave(made_gate, d_gate_ref, gate_out, at, 1).wait()
            leave(made_up, d_up_ref, up_out, at, 1).wait()
            leave(made_down, d_down_ref, down_out, at, 0).wait()

    held = pltpu.VMEM((count, blocks, ROWS, width + step), jnp.bfloat16)
    arranged = pltpu.VMEM((count * slots, width), jnp.bfloat16)
    mine = pltpu.VMEM((total, share), jnp.bfloat16)
    return pl.pallas_call(
        kernel,
        out_shape=[
            jax.ShapeDtypeStruct((share, hid), jnp.float32),
            jax.ShapeDtypeStruct((share, hid), jnp.float32),
            jax.ShapeDtypeStruct((hid, share), jnp.float32),
        ],
        in_specs=[pl.BlockSpec(memory_space=pltpu.SMEM)] + anywhere(given + count * items + 3),
        out_specs=anywhere(3),
        scratch_shapes=[
            held,
            held,
            arranged,
            arranged,
            mine,
            mine,
            pltpu.VMEM((given * slots, 3 * hid), jnp.bfloat16),
            pltpu.VMEM((tiles, width, tile), jnp.bfloat16),
            pltpu.VMEM((tiles, width, tile), jnp.bfloat16),
            pltpu.VMEM((tiles, tile, width), jnp.bfloat16),
            pltpu.SemaphoreType.DMA((count * items,)),
            pltpu.SemaphoreType.DMA((count * items,)),
            pltpu.SemaphoreType.DMA((3 * given,)),
            pltpu.SemaphoreType.DMA((tiles,)),
            pltpu.SemaphoreType.DMA((tiles,)),
            pltpu.SemaphoreType.DMA((tiles,)),
            pltpu.VMEM((tiles, share, tile), jnp.float32),
            pltpu.VMEM((tiles, share, tile), jnp.float32),
            pltpu.VMEM((tiles, tile, share), jnp.float32),
            pltpu.SemaphoreType.DMA((tiles,)),
            pltpu.SemaphoreType.DMA((tiles,)),
            pltpu.SemaphoreType.DMA((tiles,)),
        ],
        compiler_params=params(),
        cost_estimate=cost(0, 4 * slots * width),
        name="weight_grads",
    )(part, *known, *[item for group in groups for item in group], gate_proj, up_proj, down_proj)


def swap(value, axis, distance):
    size = lax.axis_size(axis)
    return lax.ppermute(value, axis, [(at, at ^ distance) for at in range(size)])


def exchange(blocks):
    return lax.all_to_all(blocks, "expert", split_axis=0, concat_axis=0, tiled=True)


def after(value, *earlier):
    return lax.optimization_barrier((value, *earlier))[0]


def gather_body(tokens, cotangent, routes, expert_gates, gate_proj, up_proj, down_proj):
    blocks = lax.axis_size("expert")
    tile, share = 256, tokens.shape[1] // lax.axis_size("dp")
    me = lax.axis_index("expert").astype(jnp.int32).reshape(1)
    part = lax.axis_index("dp").astype(jnp.int32).reshape(1)
    routes = routes.reshape(1, -1)
    gates = expert_gates.reshape(1, -1)
    weights = (gate_proj, up_proj, down_proj)
    received = list(pack(blocks, me, routes, gates, tokens, cotangent))
    for distance in reversed(range(1, blocks)):
        received[distance] = swap(received[distance], "expert", distance)
    half = blocks // 2
    far = swap(join(received[:half]), "dp", 2)
    far_half = swap(join(received[half:]), "dp", 2)
    sent, kept, handed = back(tile, share, me, part, received, *weights)
    sent, far = lax.optimization_barrier((sent, far))
    returned = exchange(sent)
    far = [far, after(far_half, sent)]
    last = [swap(item, "dp", 1) for item in far]
    known = [kept, swap(handed, "dp", 1)]
    grads = weight_grads(tile, share, part, known, [far, last], *weights)
    return (merge(routes, after(returned, *grads)), *grads)


def body(tokens, cotangent, routes, expert_gates, gate_proj, up_proj, down_proj):
    groups, blocks = lax.axis_size("dp"), lax.axis_size("expert")
    width, hid = gate_proj.shape
    rows_sent = (groups - 1) * 2 * blocks * MOST * width
    grads_sent = 3 * width * hid * (groups - 1) // groups
    fits = blocks == EXPERTS and groups == 4 and hid % 256 == 0
    fits = fits and tokens.shape[0] == 128 and routes.shape[1] == 1 and width // groups % 128 == 0
    chosen = gather_body if fits and rows_sent < grads_sent else scatter_body
    return chosen(tokens, cotangent, routes, expert_gates, gate_proj, up_proj, down_proj)


def solution(mesh):
    in_specs = (
        P(("dp", "expert"), None),
        P(("dp", "expert"), None),
        P(("dp", "expert"), None),
        P(("dp", "expert"), None),
        P(None, "expert"),
        P(None, "expert"),
        P("expert", None),
    )
    out_specs = (P(("dp", "expert"), None), P("dp", "expert"), P("dp", "expert"), P("expert", "dp"))
    return jax.shard_map(body, mesh=mesh, in_specs=in_specs, out_specs=out_specs, check_vma=False)
```

```python
import jax
import jax.numpy as jnp
from jax import lax
from jax.experimental import pallas as pl
from jax.experimental.pallas import tpu as pltpu
from jax.sharding import PartitionSpec as P

EXPERTS = 8
MOST = 18
ROWS = 16
VMEM_BYTES = (63 * 1024 + 768) * 1024


def build_slots(routes, capacity):
    flat_routes = routes.reshape(-1)
    one_hot = (flat_routes[:, None] == jnp.arange(EXPERTS, dtype=jnp.int32)[None, :]).astype(
        jnp.int32
    )
    before = jnp.cumsum(one_hot, axis=0) - one_hot
    position = jnp.sum(before * one_hot, axis=1)
    return flat_routes * capacity + position


def scatter_body(tokens, cotangent, routes, expert_gates, gate_proj, up_proj, down_proj):
    tok_dev, model_dim = tokens.shape
    top_k = routes.shape[1]
    expert_devs = lax.axis_size("expert")
    group_size = expert_devs // EXPERTS
    capacity = MOST
    slot_total = EXPERTS * capacity
    slot_of = build_slots(routes, capacity)
    owners = jnp.arange(tok_dev * top_k, dtype=jnp.int32) // top_k
    slot_table = jnp.full((slot_total,), tok_dev, jnp.int32).at[slot_of].set(owners)
    slot_gate = jnp.zeros((slot_total,), jnp.float32).at[slot_of].set(expert_gates.reshape(-1))
    x_slots = jnp.take(tokens, slot_table, axis=0, mode="fill", fill_value=0)
    dy_slots = (
        jnp.take(cotangent, slot_table, axis=0, mode="fill", fill_value=0).astype(jnp.float32)
        * slot_gate[:, None]
    ).astype(jnp.bfloat16)

    def copies(values):
        spread = values.reshape(EXPERTS, 1, capacity, model_dim)
        return jnp.broadcast_to(spread, (EXPERTS, group_size, capacity, model_dim)).reshape(
            expert_devs, capacity, model_dim
        )

    x_recv, dy_recv = (
        lax.all_to_all(copies(x_slots), "expert", split_axis=0, concat_axis=0, tiled=True),
        lax.all_to_all(copies(dy_slots), "expert", split_axis=0, concat_axis=0, tiled=True),
    )
    in_rows = x_recv.reshape(expert_devs * capacity, model_dim)
    scaled = dy_recv.reshape(expert_devs * capacity, model_dim)
    pre_gate = jnp.dot(in_rows, gate_proj, preferred_element_type=jnp.float32)
    pre_up = jnp.dot(in_rows, up_proj, preferred_element_type=jnp.float32)
    gate_sig = jax.nn.sigmoid(pre_gate)
    hidden = (pre_gate * gate_sig * pre_up).astype(jnp.bfloat16)
    by_width = (((1,), (1,)), ((), ()))
    by_rows = (((0,), (0,)), ((), ()))
    d_hidden = lax.dot_general(scaled, down_proj, by_width, preferred_element_type=jnp.float32)
    d_gate = (d_hidden * pre_up * gate_sig * (1.0 + pre_gate * (1.0 - gate_sig))).astype(
        jnp.bfloat16
    )
    d_up = (d_hidden * pre_gate * gate_sig).astype(jnp.bfloat16)
    grad_down = lax.dot_general(hidden, scaled, by_rows, preferred_element_type=jnp.float32)
    grad_gate = lax.dot_general(in_rows, d_gate, by_rows, preferred_element_type=jnp.float32)
    grad_up = lax.dot_general(in_rows, d_up, by_rows, preferred_element_type=jnp.float32)
    grad_gate, grad_up, grad_down = (
        lax.psum_scatter(
            grad_gate.astype(jnp.bfloat16), "dp", scatter_dimension=0, tiled=True
        ).astype(jnp.float32),
        lax.psum_scatter(
            grad_up.astype(jnp.bfloat16), "dp", scatter_dimension=0, tiled=True
        ).astype(jnp.float32),
        lax.psum_scatter(
            grad_down.astype(jnp.bfloat16), "dp", scatter_dimension=1, tiled=True
        ).astype(jnp.float32),
    )
    joined_grads = jnp.concatenate([d_gate, d_up], 1)
    joined_proj = jnp.concatenate([gate_proj, up_proj], 1)
    partial_value = lax.dot_general(
        joined_grads, joined_proj, by_width, preferred_element_type=jnp.float32
    ).astype(jnp.bfloat16)
    returned = lax.all_to_all(
        partial_value.reshape(expert_devs, capacity, model_dim),
        "expert",
        split_axis=0,
        concat_axis=0,
        tiled=True,
    )
    summed = jnp.sum(
        returned.reshape(EXPERTS, group_size, capacity, model_dim).astype(jnp.float32), axis=1
    )
    summed = summed.reshape(slot_total, model_dim)
    grad_input = jnp.take(summed, slot_of, axis=0).reshape(tok_dev, top_k, model_dim).sum(axis=1)
    return (grad_input.astype(jnp.bfloat16), grad_gate, grad_up, grad_down)


BY_WIDTH = (((1,), (1,)), ((), ()))
BY_ROWS = (((0,), (0,)), ((), ()))


def cut(width):
    pieces = ROWS // (MOST - ROWS)
    return pieces, width // pieces


def width_of(packed):
    pieces = ROWS // (MOST - ROWS)
    return packed.shape[2] * pieces // (pieces + 1)


def cost(flops, moved):
    return pl.CostEstimate(flops=flops, bytes_accessed=moved, transcendentals=0)


def params():
    return pltpu.CompilerParams(vmem_limit_bytes=VMEM_BYTES)


def anywhere(count):
    return [pl.BlockSpec(memory_space=pl.ANY)] * count


def dot(left, right, dims=(((1,), (0,)), ((), ()))):
    return lax.dot_general(left, right, dims, preferred_element_type=jnp.float32)


def ones(mask):
    return jnp.where(mask, 1.0, 0.0).astype(jnp.bfloat16)


def start(pairs, arrived, first=0):
    for at, (source, target) in enumerate(pairs):
        if at >= first:
            pltpu.make_async_copy(source, target, arrived.at[at]).start()


def wait(pairs, arrived, first=0):
    for at, (source, target) in enumerate(pairs):
        if at >= first:
            pltpu.make_async_copy(source, target, arrived.at[at]).wait()


def slot_masks(routes, blocks, width, me=0):
    tokens = routes.shape[1]
    pieces, _ = cut(width)
    experts = lax.broadcasted_iota(jnp.int32, (EXPERTS, tokens), 0)
    named = jnp.where(experts == routes, 1.0, 0.0)
    earlier = lax.broadcasted_iota(jnp.int32, (tokens, tokens), 0) < lax.broadcasted_iota(
        jnp.int32, (tokens, tokens), 1
    )
    before = dot(named.astype(jnp.bfloat16), ones(earlier))
    position = jnp.sum(before * named, axis=0, keepdims=True).astype(jnp.int32)
    slot = lax.broadcasted_iota(jnp.int32, (blocks * ROWS, tokens), 0)
    row = slot % ROWS
    mine = (slot // ROWS) ^ me == routes
    main = mine & (position == row)
    spill = mine & (position == ROWS + row // pieces)
    return main, spill, row % pieces


def pack(blocks, me, routes, gates, tokens, cotangent):
    count, width = tokens.shape
    pieces, step = cut(width)
    sources = (routes, gates, tokens, cotangent)
    block_shape = (2 * ROWS, width + step)

    def kernel(me_ref, *refs):
        outs, held = refs[4 : 4 + blocks], refs[4 + blocks : 8 + blocks]
        staged, arrived, gone = refs[8 + blocks :]
        pairs = list(zip(refs[:4], held))
        start(pairs, arrived)
        wait(pairs[:2], arrived)
        main, spill, piece = slot_masks(held[0][...], blocks, width, me_ref[0])
        mains = ones(main)
        picks = jnp.concatenate([ones(spill & (piece == at)) for at in range(pieces)], 1)
        main_scale = jnp.sum(jnp.where(main, held[1][...], 0.0), axis=1, keepdims=True)
        spill_scale = jnp.sum(jnp.where(spill, held[1][...], 0.0), axis=1, keepdims=True)
        leaving = []
        for half in range(2):
            wait(pairs[: 3 + half], arrived, 2 + half)
            values = held[2 + half]
            rows = dot(mains, values[...])
            cuts = [values[:, at * step : (at + 1) * step] for at in range(pieces)]
            extra = dot(picks, jnp.concatenate(cuts, 0))
            if half > 0:
                rows, extra = rows * main_scale, extra * spill_scale
            rows = rows.astype(jnp.bfloat16)
            extra = extra.astype(jnp.bfloat16)
            here = slice(half * ROWS, (half + 1) * ROWS)
            for block in range(blocks):
                part = slice(block * ROWS, (block + 1) * ROWS)
                staged[block, here, :width] = rows[part]
                staged[block, here, width:] = extra[part]
            sent = [(staged.at[at, here], outs[at].at[here, :]) for at in range(blocks)]
            leaving += sent
            start(leaving, gone, half * blocks)
        wait(leaving, gone)

    return pl.pallas_call(
        kernel,
        out_shape=[jax.ShapeDtypeStruct(block_shape, jnp.bfloat16)] * blocks,
        in_specs=[pl.BlockSpec(memory_space=pltpu.SMEM)] + anywhere(4),
        out_specs=anywhere(blocks),
        scratch_shapes=[pltpu.VMEM(source.shape, source.dtype) for source in sources]
        + [
            pltpu.VMEM((blocks,) + block_shape, jnp.bfloat16),
            pltpu.SemaphoreType.DMA((4,)),
            pltpu.SemaphoreType.DMA((2 * blocks,)),
        ],
        compiler_params=params(),
        cost_estimate=cost(8 * blocks * ROWS * count * width, 8 * count * width),
        name="pack",
    )(me, *sources)


def join(received):
    count = len(received)
    shape = (count,) + received[0].shape

    def kernel(*refs):
        out, held, arrived, gone = refs[count:]
        pairs = [(refs[at], held.at[at]) for at in range(count)]
        leaving = [(held.at[at], out.at[at]) for at in range(count)]
        start(pairs, arrived)
        for at in range(count):
            wait(pairs[: at + 1], arrived, at)
            start(leaving[: at + 1], gone, at)
        wait(leaving, gone)

    return pl.pallas_call(
        kernel,
        out_shape=jax.ShapeDtypeStruct(shape, jnp.bfloat16),
        in_specs=anywhere(count),
        out_specs=pl.BlockSpec(memory_space=pl.ANY),
        scratch_shapes=[
            pltpu.VMEM(shape, jnp.bfloat16),
            pltpu.SemaphoreType.DMA((count,)),
            pltpu.SemaphoreType.DMA((count,)),
        ],
        compiler_params=params(),
        cost_estimate=cost(0, 4 * received[0].size * count),
        name="join",
    )(*received)


def merge(routes, returned):
    blocks = returned.shape[0]
    tokens = routes.shape[1]
    width = width_of(returned)
    pieces, step = cut(width)
    chunk = 2 * step

    def kernel(routes_ref, back_ref, out, named, held, made, arrived, gone):
        spans = [slice(width, width + step)]
        spans += [slice(at, at + chunk) for at in range(0, width, chunk)]
        pairs = [(routes_ref, named)]
        pairs += [(back_ref.at[:, :, span], held.at[:, :, span]) for span in spans]
        leaving = [(made.at[:, span], out.at[:, span]) for span in spans[1:]]
        start(pairs, arrived)
        wait(pairs[:1], arrived)
        main, spill, piece = slot_masks(named[...], blocks, width)
        mains = ones(main)
        picks = jnp.concatenate([ones(spill & (piece == at)) for at in range(pieces)], 1)
        wait(pairs[:2], arrived, 1)
        tails = jnp.concatenate([held[at, :, width:] for at in range(blocks)], 0)
        extra = dot(picks, tails, BY_ROWS)
        for at, span in enumerate(spans[1:]):
            wait(pairs[: at + 3], arrived, at + 2)
            rows = jnp.concatenate([held[block, :, span] for block in range(blocks)], 0)
            here = [extra[(2 * at + side) * tokens :][:tokens] for side in range(2)]
            picked = dot(mains, rows, BY_ROWS) + jnp.concatenate(here, 1)
            made[:, span] = picked.astype(jnp.bfloat16)
            start(leaving[: at + 1], gone, at)
        wait(leaving, gone)

    chunks = width // chunk
    return pl.pallas_call(
        kernel,
        out_shape=jax.ShapeDtypeStruct((tokens, width), jnp.bfloat16),
        in_specs=anywhere(2),
        out_specs=pl.BlockSpec(memory_space=pl.ANY),
        scratch_shapes=[
            pltpu.VMEM(routes.shape, routes.dtype),
            pltpu.VMEM(returned.shape, returned.dtype),
            pltpu.VMEM((tokens, width), jnp.bfloat16),
            pltpu.SemaphoreType.DMA((chunks + 2,)),
            pltpu.SemaphoreType.DMA((chunks,)),
        ],
        compiler_params=params(),
        cost_estimate=cost(4 * blocks * ROWS * tokens * width, 4 * tokens * width),
        name="merge",
    )(routes, returned)


def spill_picks(blocks, pieces):
    extras = blocks * (MOST - ROWS)
    shape = (pieces * extras, blocks * ROWS)
    index = lax.broadcasted_iota(jnp.int32, shape, 0)
    row = lax.broadcasted_iota(jnp.int32, shape, 1)
    return ones(row == (index % extras) * pieces + index // extras)


def unpack(packed, first, out):
    blocks, width = packed.shape[0], out.shape[1]
    pieces, step = cut(width)
    extras = blocks * (MOST - ROWS)
    for at in range(blocks):
        out[first + at * ROWS : first + (at + 1) * ROWS, :] = packed[at, :, :width]
    tails = jnp.concatenate([packed[at, :, width:] for at in range(blocks)], 0)
    placed = dot(spill_picks(blocks, pieces), tails).astype(jnp.bfloat16)
    spill = slice(first + blocks * ROWS, first + blocks * MOST)
    for at in range(pieces):
        out[spill, at * step : (at + 1) * step] = placed[at * extras : (at + 1) * extras]


def tile_of(index, tile):
    return pl.ds(pl.multiple_of(index * tile, tile), tile)


def weight_copy(source, target, arrived, index, axis, tile):
    here = tile_of(index, tile)
    view = source.at[:, here] if axis else source.at[here, :]
    return pltpu.make_async_copy(view, target.at[index], arrived.at[index])


def halves(group, half, out):
    here = slice(half * ROWS, (half + 1) * ROWS)
    pairs, at = [], 0
    for item in group:
        if len(item.shape) == 2:
            pairs.append((item.at[here, :], out.at[at]))
            at += 1
        else:
            pairs.append((item.at[:, here, :], out.at[at : at + item.shape[0]]))
            at += item.shape[0]
    return pairs


def hidden_grads(pre_gate, pre_up, d_hidden):
    sig = 0.5 * jnp.tanh(0.5 * pre_gate) + 0.5
    silu = pre_gate * sig
    hidden = (silu * pre_up).astype(jnp.bfloat16)
    d_gate = (d_hidden * pre_up * (sig + silu * (1.0 - sig))).astype(jnp.bfloat16)
    d_up = (d_hidden * silu).astype(jnp.bfloat16)
    return hidden, d_gate, d_up


def back(tile, share, me, part, group, gate_proj, up_proj, down_proj):
    blocks = len(group)
    width, hid = gate_proj.shape
    slots = blocks * MOST
    pieces, step = cut(width)
    tiles = hid // tile
    chunk = 2 * step
    chunks = width // chunk
    shape = (blocks, ROWS, width + step)
    given = 3 * hid + 2 * share

    def kernel(me_ref, part_ref, *refs):
        refs = list(refs)
        group_refs = [refs.pop(0) for _ in range(blocks)]
        gate_ref, up_ref, down_ref, out, kept, handed = [refs.pop(0) for _ in range(6)]
        x_held, dy_held, rows, scaled, factors, cuts = [refs.pop(0) for _ in range(6)]
        staged, gate, up, down = [refs.pop(0) for _ in range(4)]
        x_in, dy_in, gate_in, up_in, down_in, gone, cut_in = refs
        x_pairs, dy_pairs = halves(group_refs, 0, x_held), halves(group_refs, 1, dy_held)

        def column_copy(source, target, arrived, index):
            here = slice(index * tile, (index + 1) * tile)
            return pltpu.make_async_copy(
                source.at[:, here], target.at[:, here], arrived.at[index]
            )

        def fetch_x(index):
            column_copy(gate_ref, gate, gate_in, index).start()
            column_copy(up_ref, up, up_in, index).start()

        def fetch_dy(index):
            weight_copy(down_ref, down, down_in, index, 0, tile).start()

        def leave(index):
            columns = slice(index * chunk, (index + 1) * chunk)
            return pltpu.make_async_copy(
                staged.at[:, :, columns], out.at[:, :, columns], gone.at[index]
            )

        first, behind = slice(0, 3 * hid), slice(3 * hid, given)
        leaving = [(factors, kept.at[:, first]), (cuts.at[0], kept.at[:, behind])]
        leaving += [(factors, handed.at[:, first]), (cuts.at[1], handed.at[:, behind])]

        start(x_pairs, x_in)
        fetch_x(0)
        wait(x_pairs, x_in)
        start(dy_pairs, dy_in)
        fetch_dy(0)
        unpack(x_held, 0, rows)
        for now in range(tiles):
            columns = slice(now * tile, (now + 1) * tile)
            column_copy(gate_ref, gate, gate_in, now).wait()
            pre_gate = dot(rows[...], gate[:, columns])
            if now < tiles - 1:
                fetch_x(now + 1)
            column_copy(up_ref, up, up_in, now).wait()
            pre_up = dot(rows[...], up[:, columns])
            if now == 0:
                wait(dy_pairs, dy_in)
                unpack(dy_held, 0, scaled)
            if now < tiles - 1:
                fetch_dy(now + 1)
            weight_copy(down_ref, down, down_in, now, 0, tile).wait()
            d_hidden = dot(scaled[...], down[now], BY_WIDTH)
            made, d_gate, d_up = hidden_grads(pre_gate, pre_up, d_hidden)
            factors[:, columns] = made
            factors[:, hid + now * tile : hid + (now + 1) * tile] = d_gate
            factors[:, 2 * hid + now * tile : 2 * hid + (now + 1) * tile] = d_up

        for at in range(2):
            columns = tile_of(part_ref[0] ^ at, share)
            cuts[at, :, :share] = rows[:, columns]
            cuts[at, :, share:] = scaled[:, columns]
        start(leaving, cut_in)
        extras = []
        for at in range(chunks):
            here = slice(at * chunk, (at + 1) * chunk)
            done = dot(factors[:, hid : 2 * hid], gate[here, :], BY_WIDTH)
            done += dot(factors[:, 2 * hid :], up[here, :], BY_WIDTH)
            done = done.astype(jnp.bfloat16)
            for block in range(blocks):
                staged[me_ref[0] ^ block, :, here] = done[block * ROWS : (block + 1) * ROWS]
            leave(at).start()
            extras += [done[blocks * ROWS :, :step], done[blocks * ROWS :, step:]]
        tail = dot(spill_picks(blocks, pieces), jnp.concatenate(extras, 0), BY_ROWS)
        tail = tail.astype(jnp.bfloat16)
        for block in range(blocks):
            staged[me_ref[0] ^ block, :, width:] = tail[block * ROWS : (block + 1) * ROWS]
        last = pltpu.make_async_copy(
            staged.at[:, :, width:], out.at[:, :, width:], gone.at[chunks]
        )
        last.start()
        for at in range(chunks):
            leave(at).wait()
        wait(leaving, cut_in)
        last.wait()

    return pl.pallas_call(
        kernel,
        out_shape=[
            jax.ShapeDtypeStruct(shape, jnp.bfloat16),
            jax.ShapeDtypeStruct((slots, given), jnp.bfloat16),
            jax.ShapeDtypeStruct((slots, given), jnp.bfloat16),
        ],
        in_specs=[pl.BlockSpec(memory_space=pltpu.SMEM)] * 2 + anywhere(blocks + 3),
        out_specs=anywhere(3),
        scratch_shapes=[
            pltpu.VMEM(shape, jnp.bfloat16),
            pltpu.VMEM(shape, jnp.bfloat16),
            pltpu.VMEM((slots, width), jnp.bfloat16),
            pltpu.VMEM((slots, width), jnp.bfloat16),
            pltpu.VMEM((slots, 3 * hid), jnp.bfloat16),
            pltpu.VMEM((2, slots, 2 * share), jnp.bfloat16),
            pltpu.VMEM(shape, jnp.bfloat16),
            pltpu.VMEM((width, hid), jnp.bfloat16),
            pltpu.VMEM((width, hid), jnp.bfloat16),
            pltpu.VMEM((tiles, tile, width), jnp.bfloat16),
            pltpu.SemaphoreType.DMA((blocks,)),
            pltpu.SemaphoreType.DMA((blocks,)),
            pltpu.SemaphoreType.DMA((tiles,)),
            pltpu.SemaphoreType.DMA((tiles,)),
            pltpu.SemaphoreType.DMA((tiles,)),
            pltpu.SemaphoreType.DMA((chunks + 1,)),
            pltpu.SemaphoreType.DMA((4,)),
        ],
        compiler_params=params(),
        cost_estimate=cost(50 * slots * width * hid, 4 * slots * width),
        name="back",
    )(me, part, *group, gate_proj, up_proj, down_proj)


def weight_grads(tile, share, part, known, groups, gate_proj, up_proj, down_proj):
    count, items = len(groups), len(groups[0])
    blocks = sum(item.shape[0] if item.ndim == 3 else 1 for item in groups[0])
    given = len(known)
    hid, width = down_proj.shape
    pieces, step = cut(width)
    slots = blocks * MOST
    total = (given + count) * slots
    tiles = hid // tile

    def kernel(part_ref, *refs):
        refs = list(refs)
        known_refs = [refs.pop(0) for _ in range(given)]
        group_refs = [[refs.pop(0) for _ in range(items)] for _ in range(count)]
        gate_ref, up_ref, down_ref = [refs.pop(0) for _ in range(3)]
        d_gate_ref, d_up_ref, d_down_ref = [refs.pop(0) for _ in range(3)]
        x_held, dy_held, x_all, dy_all = [refs.pop(0) for _ in range(4)]
        x_mine, dy_mine, factors = [refs.pop(0) for _ in range(3)]
        gate, up, down, x_in, dy_in, known_in, gate_in, up_in, down_in = refs[:9]
        made_gate, made_up, made_down, gate_out, up_out, down_out = refs[9:]
        columns = tile_of(part_ref[0], share)
        x_pairs, dy_pairs, known_pairs = [], [], []
        for at in range(count):
            x_pairs += halves(group_refs[at], 0, x_held.at[at])
            dy_pairs += halves(group_refs[at], 1, dy_held.at[at])
        for at in range(given):
            here = slice(at * slots, (at + 1) * slots)
            behind = 3 * hid
            known_pairs += [
                (known_refs[at].at[:, :behind], factors.at[here, :]),
                (known_refs[at].at[:, behind : behind + share], x_mine.at[here, :]),
                (known_refs[at].at[:, behind + share :], dy_mine.at[here, :]),
            ]

        def arrange(held, rows_out, target):
            for at in range(count):
                unpack(held.at[at], at * slots, rows_out)
            target[given * slots :, :] = rows_out[:, columns]

        def leave(source, target, gone, index, axis):
            here = tile_of(index, tile)
            view = target.at[:, here] if axis else target.at[here, :]
            return pltpu.make_async_copy(source.at[index], view, gone.at[index])

        def fetch_x(index):
            weight_copy(gate_ref, gate, gate_in, index, 1, tile).start()
            weight_copy(up_ref, up, up_in, index, 1, tile).start()

        def fetch_dy(index):
            weight_copy(down_ref, down, down_in, index, 0, tile).start()

        start(x_pairs, x_in)
        fetch_x(0)
        wait(x_pairs, x_in)
        start(dy_pairs, dy_in)
        fetch_dy(0)
        arrange(x_held, x_all, x_mine)
        for now in range(tiles):
            here = slice(now * tile, (now + 1) * tile)
            weight_copy(gate_ref, gate, gate_in, now, 1, tile).wait()
            pre_gate = dot(x_all[...], gate[now])
            weight_copy(up_ref, up, up_in, now, 1, tile).wait()
            pre_up = dot(x_all[...], up[now])
            if now == 0:
                wait(dy_pairs, dy_in)
                start(known_pairs, known_in)
                arrange(dy_held, dy_all, dy_mine)
            if now < tiles - 1:
                fetch_x(now + 1)
                fetch_dy(now + 1)
            weight_copy(down_ref, down, down_in, now, 0, tile).wait()
            d_hidden = dot(dy_all[...], down[now], BY_WIDTH)
            made, d_gate, d_up = hidden_grads(pre_gate, pre_up, d_hidden)
            if now == 0:
                wait(known_pairs, known_in)
            made = jnp.concatenate([factors[:, here], made], 0)
            d_gate = jnp.concatenate([factors[:, hid + here.start : hid + here.stop], d_gate], 0)
            d_up = jnp.concatenate(
                [factors[:, 2 * hid + here.start : 2 * hid + here.stop], d_up], 0
            )
            sums = dot(x_mine[...], jnp.concatenate([d_gate, d_up], 1), BY_ROWS)
            made_gate[now] = sums[:, :tile]
            made_up[now] = sums[:, tile:]
            leave(made_gate, d_gate_ref, gate_out, now, 1).start()
            leave(made_up, d_up_ref, up_out, now, 1).start()
            made_down[now] = dot(made, dy_mine[...], BY_ROWS)
            leave(made_down, d_down_ref, down_out, now, 0).start()
        for at in range(tiles):
            leave(made_gate, d_gate_ref, gate_out, at, 1).wait()
            leave(made_up, d_up_ref, up_out, at, 1).wait()
            leave(made_down, d_down_ref, down_out, at, 0).wait()

    held = pltpu.VMEM((count, blocks, ROWS, width + step), jnp.bfloat16)
    arranged = pltpu.VMEM((count * slots, width), jnp.bfloat16)
    mine = pltpu.VMEM((total, share), jnp.bfloat16)
    return pl.pallas_call(
        kernel,
        out_shape=[
            jax.ShapeDtypeStruct((share, hid), jnp.float32),
            jax.ShapeDtypeStruct((share, hid), jnp.float32),
            jax.ShapeDtypeStruct((hid, share), jnp.float32),
        ],
        in_specs=[pl.BlockSpec(memory_space=pltpu.SMEM)] + anywhere(given + count * items + 3),
        out_specs=anywhere(3),
        scratch_shapes=[
            held,
            held,
            arranged,
            arranged,
            mine,
            mine,
            pltpu.VMEM((given * slots, 3 * hid), jnp.bfloat16),
            pltpu.VMEM((tiles, width, tile), jnp.bfloat16),
            pltpu.VMEM((tiles, width, tile), jnp.bfloat16),
            pltpu.VMEM((tiles, tile, width), jnp.bfloat16),
            pltpu.SemaphoreType.DMA((count * items,)),
            pltpu.SemaphoreType.DMA((count * items,)),
            pltpu.SemaphoreType.DMA((3 * given,)),
            pltpu.SemaphoreType.DMA((tiles,)),
            pltpu.SemaphoreType.DMA((tiles,)),
            pltpu.SemaphoreType.DMA((tiles,)),
            pltpu.VMEM((tiles, share, tile), jnp.float32),
            pltpu.VMEM((tiles, share, tile), jnp.float32),
            pltpu.VMEM((tiles, tile, share), jnp.float32),
            pltpu.SemaphoreType.DMA((tiles,)),
            pltpu.SemaphoreType.DMA((tiles,)),
            pltpu.SemaphoreType.DMA((tiles,)),
        ],
        compiler_params=params(),
        cost_estimate=cost(0, 4 * slots * width),
        name="weight_grads",
    )(part, *known, *[item for group in groups for item in group], gate_proj, up_proj, down_proj)


def swap(value, axis, distance):
    size = lax.axis_size(axis)
    return lax.ppermute(value, axis, [(at, at ^ distance) for at in range(size)])


def exchange(blocks):
    return lax.all_to_all(blocks, "expert", split_axis=0, concat_axis=0, tiled=True)


def after(value, *earlier):
    return lax.optimization_barrier((value, *earlier))[0]


def gather_body(tokens, cotangent, routes, expert_gates, gate_proj, up_proj, down_proj):
    blocks = lax.axis_size("expert")
    tile, share = 256, tokens.shape[1] // lax.axis_size("dp")
    me = lax.axis_index("expert").astype(jnp.int32).reshape(1)
    part = lax.axis_index("dp").astype(jnp.int32).reshape(1)
    routes = routes.reshape(1, -1)
    gates = expert_gates.reshape(1, -1)
    weights = (gate_proj, up_proj, down_proj)
    received = list(pack(blocks, me, routes, gates, tokens, cotangent))
    for distance in reversed(range(1, blocks)):
        received[distance] = swap(received[distance], "expert", distance)
    half = blocks // 2
    far = swap(join(received[:half]), "dp", 2)
    far_half = swap(join(received[half:]), "dp", 2)
    sent, kept, handed = back(tile, share, me, part, received, *weights)
    sent, far = lax.optimization_barrier((sent, far))
    returned = exchange(sent)
    far = [far, after(far_half, sent)]
    last = [swap(item, "dp", 1) for item in far]
    known = [kept, swap(handed, "dp", 1)]
    grads = weight_grads(tile, share, part, known, [far, last], *weights)
    return (merge(routes, after(returned, *grads)), *grads)


def body(tokens, cotangent, routes, expert_gates, gate_proj, up_proj, down_proj):
    groups, blocks = lax.axis_size("dp"), lax.axis_size("expert")
    width, hid = gate_proj.shape
    rows_sent = (groups - 1) * 2 * blocks * MOST * width
    grads_sent = 3 * width * hid * (groups - 1) // groups
    fits = blocks == EXPERTS and groups == 4 and hid % 256 == 0
    fits = fits and tokens.shape[0] == 128 and routes.shape[1] == 1 and width // groups % 128 == 0
    chosen = gather_body if fits and rows_sent < grads_sent else scatter_body
    return chosen(tokens, cotangent, routes, expert_gates, gate_proj, up_proj, down_proj)


def solution(mesh):
    in_specs = (
        P(("dp", "expert"), None),
        P(("dp", "expert"), None),
        P(("dp", "expert"), None),
        P(("dp", "expert"), None),
        P(None, "expert"),
        P(None, "expert"),
        P("expert", None),
    )
    out_specs = (P(("dp", "expert"), None), P("dp", "expert"), P("dp", "expert"), P("expert", "dp"))
    return jax.shard_map(body, mesh=mesh, in_specs=in_specs, out_specs=out_specs, check_vma=False)
```

```python
import jax
import jax.numpy as jnp
from jax import lax
from jax.experimental import pallas as pl
from jax.experimental.pallas import tpu as pltpu
from jax.sharding import PartitionSpec as P

EXPERTS = 8
MOST = 18
ROWS = 16
VMEM_BYTES = (63 * 1024 + 768) * 1024


def build_slots(routes, capacity):
    flat_routes = routes.reshape(-1)
    one_hot = (flat_routes[:, None] == jnp.arange(EXPERTS, dtype=jnp.int32)[None, :]).astype(
        jnp.int32
    )
    before = jnp.cumsum(one_hot, axis=0) - one_hot
    position = jnp.sum(before * one_hot, axis=1)
    return flat_routes * capacity + position


def scatter_body(tokens, cotangent, routes, expert_gates, gate_proj, up_proj, down_proj):
    tok_dev, model_dim = tokens.shape
    top_k = routes.shape[1]
    expert_devs = lax.axis_size("expert")
    group_size = expert_devs // EXPERTS
    capacity = MOST
    slot_total = EXPERTS * capacity
    slot_of = build_slots(routes, capacity)
    owners = jnp.arange(tok_dev * top_k, dtype=jnp.int32) // top_k
    slot_table = jnp.full((slot_total,), tok_dev, jnp.int32).at[slot_of].set(owners)
    slot_gate = jnp.zeros((slot_total,), jnp.float32).at[slot_of].set(expert_gates.reshape(-1))
    x_slots = jnp.take(tokens, slot_table, axis=0, mode="fill", fill_value=0)
    dy_slots = (
        jnp.take(cotangent, slot_table, axis=0, mode="fill", fill_value=0).astype(jnp.float32)
        * slot_gate[:, None]
    ).astype(jnp.bfloat16)

    def copies(values):
        spread = values.reshape(EXPERTS, 1, capacity, model_dim)
        return jnp.broadcast_to(spread, (EXPERTS, group_size, capacity, model_dim)).reshape(
            expert_devs, capacity, model_dim
        )

    x_recv, dy_recv = (
        lax.all_to_all(copies(x_slots), "expert", split_axis=0, concat_axis=0, tiled=True),
        lax.all_to_all(copies(dy_slots), "expert", split_axis=0, concat_axis=0, tiled=True),
    )
    in_rows = x_recv.reshape(expert_devs * capacity, model_dim)
    scaled = dy_recv.reshape(expert_devs * capacity, model_dim)
    pre_gate = jnp.dot(in_rows, gate_proj, preferred_element_type=jnp.float32)
    pre_up = jnp.dot(in_rows, up_proj, preferred_element_type=jnp.float32)
    gate_sig = jax.nn.sigmoid(pre_gate)
    hidden = (pre_gate * gate_sig * pre_up).astype(jnp.bfloat16)
    by_width = (((1,), (1,)), ((), ()))
    by_rows = (((0,), (0,)), ((), ()))
    d_hidden = lax.dot_general(scaled, down_proj, by_width, preferred_element_type=jnp.float32)
    d_gate = (d_hidden * pre_up * gate_sig * (1.0 + pre_gate * (1.0 - gate_sig))).astype(
        jnp.bfloat16
    )
    d_up = (d_hidden * pre_gate * gate_sig).astype(jnp.bfloat16)
    grad_down = lax.dot_general(hidden, scaled, by_rows, preferred_element_type=jnp.float32)
    grad_gate = lax.dot_general(in_rows, d_gate, by_rows, preferred_element_type=jnp.float32)
    grad_up = lax.dot_general(in_rows, d_up, by_rows, preferred_element_type=jnp.float32)
    grad_gate, grad_up, grad_down = (
        lax.psum_scatter(
            grad_gate.astype(jnp.bfloat16), "dp", scatter_dimension=0, tiled=True
        ).astype(jnp.float32),
        lax.psum_scatter(
            grad_up.astype(jnp.bfloat16), "dp", scatter_dimension=0, tiled=True
        ).astype(jnp.float32),
        lax.psum_scatter(
            grad_down.astype(jnp.bfloat16), "dp", scatter_dimension=1, tiled=True
        ).astype(jnp.float32),
    )
    joined_grads = jnp.concatenate([d_gate, d_up], 1)
    joined_proj = jnp.concatenate([gate_proj, up_proj], 1)
    partial_value = lax.dot_general(
        joined_grads, joined_proj, by_width, preferred_element_type=jnp.float32
    ).astype(jnp.bfloat16)
    returned = lax.all_to_all(
        partial_value.reshape(expert_devs, capacity, model_dim),
        "expert",
        split_axis=0,
        concat_axis=0,
        tiled=True,
    )
    summed = jnp.sum(
        returned.reshape(EXPERTS, group_size, capacity, model_dim).astype(jnp.float32), axis=1
    )
    summed = summed.reshape(slot_total, model_dim)
    grad_input = jnp.take(summed, slot_of, axis=0).reshape(tok_dev, top_k, model_dim).sum(axis=1)
    return (grad_input.astype(jnp.bfloat16), grad_gate, grad_up, grad_down)


BY_WIDTH = (((1,), (1,)), ((), ()))
BY_ROWS = (((0,), (0,)), ((), ()))


def cut(width):
    pieces = ROWS // (MOST - ROWS)
    return pieces, width // pieces


def width_of(packed):
    pieces = ROWS // (MOST - ROWS)
    return packed.shape[2] * pieces // (pieces + 1)


def cost(flops, moved):
    return pl.CostEstimate(flops=flops, bytes_accessed=moved, transcendentals=0)


def params():
    return pltpu.CompilerParams(vmem_limit_bytes=VMEM_BYTES)


def anywhere(count):
    return [pl.BlockSpec(memory_space=pl.ANY)] * count


def dot(left, right, dims=(((1,), (0,)), ((), ()))):
    return lax.dot_general(left, right, dims, preferred_element_type=jnp.float32)


def ones(mask):
    return jnp.where(mask, 1.0, 0.0).astype(jnp.bfloat16)


def start(pairs, arrived, first=0):
    for at, (source, target) in enumerate(pairs):
        if at >= first:
            pltpu.make_async_copy(source, target, arrived.at[at]).start()


def wait(pairs, arrived, first=0):
    for at, (source, target) in enumerate(pairs):
        if at >= first:
            pltpu.make_async_copy(source, target, arrived.at[at]).wait()


def slot_masks(routes, blocks, width, me=0):
    tokens = routes.shape[1]
    pieces, _ = cut(width)
    experts = lax.broadcasted_iota(jnp.int32, (EXPERTS, tokens), 0)
    named = jnp.where(experts == routes, 1.0, 0.0)
    earlier = lax.broadcasted_iota(jnp.int32, (tokens, tokens), 0) < lax.broadcasted_iota(
        jnp.int32, (tokens, tokens), 1
    )
    before = dot(named.astype(jnp.bfloat16), ones(earlier))
    position = jnp.sum(before * named, axis=0, keepdims=True).astype(jnp.int32)
    slot = lax.broadcasted_iota(jnp.int32, (blocks * ROWS, tokens), 0)
    row = slot % ROWS
    mine = (slot // ROWS) ^ me == routes
    main = mine & (position == row)
    spill = mine & (position == ROWS + row // pieces)
    return main, spill, row % pieces


def pack(blocks, me, routes, gates, tokens, cotangent):
    count, width = tokens.shape
    pieces, step = cut(width)
    sources = (routes, gates, tokens, cotangent)
    block_shape = (2 * ROWS, width + step)

    def kernel(me_ref, *refs):
        outs, held = refs[4 : 4 + blocks], refs[4 + blocks : 8 + blocks]
        staged, arrived, gone = refs[8 + blocks :]
        pairs = list(zip(refs[:4], held))
        start(pairs, arrived)
        wait(pairs[:2], arrived)
        main, spill, piece = slot_masks(held[0][...], blocks, width, me_ref[0])
        mains = ones(main)
        picks = jnp.concatenate([ones(spill & (piece == at)) for at in range(pieces)], 1)
        main_scale = jnp.sum(jnp.where(main, held[1][...], 0.0), axis=1, keepdims=True)
        spill_scale = jnp.sum(jnp.where(spill, held[1][...], 0.0), axis=1, keepdims=True)
        leaving = []
        for half in range(2):
            wait(pairs[: 3 + half], arrived, 2 + half)
            values = held[2 + half]
            rows = dot(mains, values[...])
            cuts = [values[:, at * step : (at + 1) * step] for at in range(pieces)]
            extra = dot(picks, jnp.concatenate(cuts, 0))
            if half > 0:
                rows, extra = rows * main_scale, extra * spill_scale
            rows = rows.astype(jnp.bfloat16)
            extra = extra.astype(jnp.bfloat16)
            here = slice(half * ROWS, (half + 1) * ROWS)
            for block in range(blocks):
                part = slice(block * ROWS, (block + 1) * ROWS)
                staged[block, here, :width] = rows[part]
                staged[block, here, width:] = extra[part]
            sent = [(staged.at[at, here], outs[at].at[here, :]) for at in range(blocks)]
            leaving += sent
            start(leaving, gone, half * blocks)
        wait(leaving, gone)

    return pl.pallas_call(
        kernel,
        out_shape=[jax.ShapeDtypeStruct(block_shape, jnp.bfloat16)] * blocks,
        in_specs=[pl.BlockSpec(memory_space=pltpu.SMEM)] + anywhere(4),
        out_specs=anywhere(blocks),
        scratch_shapes=[pltpu.VMEM(source.shape, source.dtype) for source in sources]
        + [
            pltpu.VMEM((blocks,) + block_shape, jnp.bfloat16),
            pltpu.SemaphoreType.DMA((4,)),
            pltpu.SemaphoreType.DMA((2 * blocks,)),
        ],
        compiler_params=params(),
        cost_estimate=cost(8 * blocks * ROWS * count * width, 8 * count * width),
        name="pack",
    )(me, *sources)


def join(received, flops=0):
    count = len(received)
    shape = (count,) + received[0].shape

    def kernel(*refs):
        out, held, arrived, gone = refs[count:]
        pairs = [(refs[at], held.at[at]) for at in range(count)]
        leaving = [(held.at[at], out.at[at]) for at in range(count)]
        start(pairs, arrived)
        for at in range(count):
            wait(pairs[: at + 1], arrived, at)
            start(leaving[: at + 1], gone, at)
        wait(leaving, gone)

    return pl.pallas_call(
        kernel,
        out_shape=jax.ShapeDtypeStruct(shape, jnp.bfloat16),
        in_specs=anywhere(count),
        out_specs=pl.BlockSpec(memory_space=pl.ANY),
        scratch_shapes=[
            pltpu.VMEM(shape, jnp.bfloat16),
            pltpu.SemaphoreType.DMA((count,)),
            pltpu.SemaphoreType.DMA((count,)),
        ],
        compiler_params=params(),
        cost_estimate=cost(flops, 4 * received[0].size * count),
        name="join",
    )(*received)


def merge(routes, returned):
    blocks = returned.shape[0]
    tokens = routes.shape[1]
    width = width_of(returned)
    pieces, step = cut(width)

    def kernel(routes_ref, back_ref, out, named, held, arrived):
        pairs = [(routes_ref, named), (back_ref, held)]
        start(pairs, arrived)
        wait(pairs[:1], arrived)
        main, spill, piece = slot_masks(named[...], blocks, width)
        mains = ones(main)
        picks = [ones(spill & (piece == at)) for at in range(pieces)]
        wait(pairs, arrived, 1)
        rows = jnp.concatenate([held[at, :, :width] for at in range(blocks)], 0)
        extra = jnp.concatenate([held[at, :, width:] for at in range(blocks)], 0)
        picked = dot(mains, rows, BY_ROWS)
        for at in range(pieces):
            columns = slice(at * step, (at + 1) * step)
            out[:, columns] = (picked[:, columns] + dot(picks[at], extra, BY_ROWS)).astype(
                jnp.bfloat16
            )

    return pl.pallas_call(
        kernel,
        out_shape=jax.ShapeDtypeStruct((tokens, width), jnp.bfloat16),
        in_specs=anywhere(2),
        out_specs=pl.BlockSpec(memory_space=pltpu.VMEM),
        scratch_shapes=[
            pltpu.VMEM(routes.shape, routes.dtype),
            pltpu.VMEM(returned.shape, returned.dtype),
            pltpu.SemaphoreType.DMA((2,)),
        ],
        compiler_params=params(),
        cost_estimate=cost(4 * blocks * ROWS * tokens * width, 4 * tokens * width),
        name="merge",
    )(routes, returned)


def spill_picks(blocks, pieces):
    extras = blocks * (MOST - ROWS)
    shape = (pieces * extras, blocks * ROWS)
    index = lax.broadcasted_iota(jnp.int32, shape, 0)
    row = lax.broadcasted_iota(jnp.int32, shape, 1)
    return ones(row == (index % extras) * pieces + index // extras)


def unpack(packed, first, out):
    blocks, width = packed.shape[0], out.shape[1]
    pieces, step = cut(width)
    extras = blocks * (MOST - ROWS)
    for at in range(blocks):
        out[first + at * ROWS : first + (at + 1) * ROWS, :] = packed[at, :, :width]
    tails = jnp.concatenate([packed[at, :, width:] for at in range(blocks)], 0)
    placed = dot(spill_picks(blocks, pieces), tails).astype(jnp.bfloat16)
    spill = slice(first + blocks * ROWS, first + blocks * MOST)
    for at in range(pieces):
        out[spill, at * step : (at + 1) * step] = placed[at * extras : (at + 1) * extras]


def tile_of(index, tile):
    return pl.ds(pl.multiple_of(index * tile, tile), tile)


def weight_copy(source, target, arrived, index, axis, tile):
    here = tile_of(index, tile)
    view = source.at[:, here] if axis else source.at[here, :]
    return pltpu.make_async_copy(view, target.at[index], arrived.at[index])


def halves(group, half, out):
    here = slice(half * ROWS, (half + 1) * ROWS)
    pairs, at = [], 0
    for item in group:
        if len(item.shape) == 2:
            pairs.append((item.at[here, :], out.at[at]))
            at += 1
        else:
            pairs.append((item.at[:, here, :], out.at[at : at + item.shape[0]]))
            at += item.shape[0]
    return pairs


def hidden_grads(pre_gate, pre_up, d_hidden):
    sig = 0.5 * jnp.tanh(0.5 * pre_gate) + 0.5
    silu = pre_gate * sig
    hidden = (silu * pre_up).astype(jnp.bfloat16)
    d_gate = (d_hidden * pre_up * (sig + silu * (1.0 - sig))).astype(jnp.bfloat16)
    d_up = (d_hidden * silu).astype(jnp.bfloat16)
    return hidden, d_gate, d_up


def back(tile, share, me, part, group, gate_proj, up_proj, down_proj):
    blocks = len(group)
    width, hid = gate_proj.shape
    slots = blocks * MOST
    pieces, step = cut(width)
    tiles = hid // tile
    chunk = 2 * step
    chunks = width // chunk
    shape = (blocks, ROWS, width + step)
    given = 3 * hid + 2 * share

    def kernel(me_ref, part_ref, *refs):
        refs = list(refs)
        group_refs = [refs.pop(0) for _ in range(blocks)]
        gate_ref, up_ref, down_ref, out, kept, handed = [refs.pop(0) for _ in range(6)]
        x_held, dy_held, rows, scaled, factors, cuts = [refs.pop(0) for _ in range(6)]
        staged, gate, up, down = [refs.pop(0) for _ in range(4)]
        x_in, dy_in, gate_in, up_in, down_in, gone, cut_in = refs
        x_pairs, dy_pairs = halves(group_refs, 0, x_held), halves(group_refs, 1, dy_held)

        def column_copy(source, target, arrived, index):
            here = slice(index * tile, (index + 1) * tile)
            return pltpu.make_async_copy(
                source.at[:, here], target.at[:, here], arrived.at[index]
            )

        def fetch_x(index):
            column_copy(gate_ref, gate, gate_in, index).start()
            column_copy(up_ref, up, up_in, index).start()

        def fetch_dy(index):
            weight_copy(down_ref, down, down_in, index, 0, tile).start()

        def leave(index):
            columns = slice(index * chunk, (index + 1) * chunk)
            return pltpu.make_async_copy(
                staged.at[:, :, columns], out.at[:, :, columns], gone.at[index]
            )

        first, behind = slice(0, 3 * hid), slice(3 * hid, given)
        leaving = [(factors, kept.at[:, first]), (cuts.at[0], kept.at[:, behind])]
        leaving += [(factors, handed.at[:, first]), (cuts.at[1], handed.at[:, behind])]

        start(x_pairs, x_in)
        fetch_x(0)
        wait(x_pairs, x_in)
        start(dy_pairs, dy_in)
        fetch_dy(0)
        unpack(x_held, 0, rows)
        for now in range(tiles):
            columns = slice(now * tile, (now + 1) * tile)
            column_copy(gate_ref, gate, gate_in, now).wait()
            pre_gate = dot(rows[...], gate[:, columns])
            if now < tiles - 1:
                fetch_x(now + 1)
            column_copy(up_ref, up, up_in, now).wait()
            pre_up = dot(rows[...], up[:, columns])
            if now == 0:
                wait(dy_pairs, dy_in)
                unpack(dy_held, 0, scaled)
            if now < tiles - 1:
                fetch_dy(now + 1)
            weight_copy(down_ref, down, down_in, now, 0, tile).wait()
            d_hidden = dot(scaled[...], down[now], BY_WIDTH)
            made, d_gate, d_up = hidden_grads(pre_gate, pre_up, d_hidden)
            factors[:, columns] = made
            factors[:, hid + now * tile : hid + (now + 1) * tile] = d_gate
            factors[:, 2 * hid + now * tile : 2 * hid + (now + 1) * tile] = d_up

        for at in range(2):
            columns = tile_of(part_ref[0] ^ at, share)
            cuts[at, :, :share] = rows[:, columns]
            cuts[at, :, share:] = scaled[:, columns]
        start(leaving, cut_in)
        extras = []
        for at in range(chunks):
            here = slice(at * chunk, (at + 1) * chunk)
            done = dot(factors[:, hid : 2 * hid], gate[here, :], BY_WIDTH)
            done += dot(factors[:, 2 * hid :], up[here, :], BY_WIDTH)
            done = done.astype(jnp.bfloat16)
            for block in range(blocks):
                staged[me_ref[0] ^ block, :, here] = done[block * ROWS : (block + 1) * ROWS]
            leave(at).start()
            extras += [done[blocks * ROWS :, :step], done[blocks * ROWS :, step:]]
        tail = dot(spill_picks(blocks, pieces), jnp.concatenate(extras, 0), BY_ROWS)
        tail = tail.astype(jnp.bfloat16)
        for block in range(blocks):
            staged[me_ref[0] ^ block, :, width:] = tail[block * ROWS : (block + 1) * ROWS]
        last = pltpu.make_async_copy(
            staged.at[:, :, width:], out.at[:, :, width:], gone.at[chunks]
        )
        last.start()
        for at in range(chunks):
            leave(at).wait()
        wait(leaving, cut_in)
        last.wait()

    return pl.pallas_call(
        kernel,
        out_shape=[
            jax.ShapeDtypeStruct(shape, jnp.bfloat16),
            jax.ShapeDtypeStruct((slots, given), jnp.bfloat16),
            jax.ShapeDtypeStruct((slots, given), jnp.bfloat16),
        ],
        in_specs=[pl.BlockSpec(memory_space=pltpu.SMEM)] * 2 + anywhere(blocks + 3),
        out_specs=anywhere(3),
        scratch_shapes=[
            pltpu.VMEM(shape, jnp.bfloat16),
            pltpu.VMEM(shape, jnp.bfloat16),
            pltpu.VMEM((slots, width), jnp.bfloat16),
            pltpu.VMEM((slots, width), jnp.bfloat16),
            pltpu.VMEM((slots, 3 * hid), jnp.bfloat16),
            pltpu.VMEM((2, slots, 2 * share), jnp.bfloat16),
            pltpu.VMEM(shape, jnp.bfloat16),
            pltpu.VMEM((width, hid), jnp.bfloat16),
            pltpu.VMEM((width, hid), jnp.bfloat16),
            pltpu.VMEM((tiles, tile, width), jnp.bfloat16),
            pltpu.SemaphoreType.DMA((blocks,)),
            pltpu.SemaphoreType.DMA((blocks,)),
            pltpu.SemaphoreType.DMA((tiles,)),
            pltpu.SemaphoreType.DMA((tiles,)),
            pltpu.SemaphoreType.DMA((tiles,)),
            pltpu.SemaphoreType.DMA((chunks + 1,)),
            pltpu.SemaphoreType.DMA((4,)),
        ],
        compiler_params=params(),
        cost_estimate=cost(50 * slots * width * hid, 4 * slots * width),
        name="back",
    )(me, part, *group, gate_proj, up_proj, down_proj)


def weight_grads(tile, share, part, known, groups, gate_proj, up_proj, down_proj):
    count, items = len(groups), len(groups[0])
    blocks = sum(item.shape[0] if item.ndim == 3 else 1 for item in groups[0])
    given = len(known)
    hid, width = down_proj.shape
    pieces, step = cut(width)
    slots = blocks * MOST
    total = (given + count) * slots
    tiles = hid // tile

    def kernel(part_ref, *refs):
        refs = list(refs)
        known_refs = [refs.pop(0) for _ in range(given)]
        group_refs = [[refs.pop(0) for _ in range(items)] for _ in range(count)]
        gate_ref, up_ref, down_ref = [refs.pop(0) for _ in range(3)]
        d_gate_ref, d_up_ref, d_down_ref = [refs.pop(0) for _ in range(3)]
        x_held, dy_held, x_all, dy_all = [refs.pop(0) for _ in range(4)]
        x_mine, dy_mine, factors = [refs.pop(0) for _ in range(3)]
        gate, up, down, x_in, dy_in, known_in, gate_in, up_in, down_in = refs[:9]
        made_gate, made_up, made_down, gate_out, up_out, down_out = refs[9:]
        columns = tile_of(part_ref[0], share)
        x_pairs, dy_pairs, known_pairs = [], [], []
        for at in range(count):
            x_pairs += halves(group_refs[at], 0, x_held.at[at])
            dy_pairs += halves(group_refs[at], 1, dy_held.at[at])
        for at in range(given):
            here = slice(at * slots, (at + 1) * slots)
            behind = 3 * hid
            known_pairs += [
                (known_refs[at].at[:, :behind], factors.at[here, :]),
                (known_refs[at].at[:, behind : behind + share], x_mine.at[here, :]),
                (known_refs[at].at[:, behind + share :], dy_mine.at[here, :]),
            ]

        def arrange(held, rows_out, target):
            for at in range(count):
                unpack(held.at[at], at * slots, rows_out)
            target[given * slots :, :] = rows_out[:, columns]

        def leave(source, target, gone, index, axis):
            here = tile_of(index, tile)
            view = target.at[:, here] if axis else target.at[here, :]
            return pltpu.make_async_copy(source.at[index], view, gone.at[index])

        def fetch_x(index):
            weight_copy(gate_ref, gate, gate_in, index, 1, tile).start()
            weight_copy(up_ref, up, up_in, index, 1, tile).start()

        def fetch_dy(index):
            weight_copy(down_ref, down, down_in, index, 0, tile).start()

        start(x_pairs, x_in)
        fetch_x(0)
        wait(x_pairs, x_in)
        start(dy_pairs, dy_in)
        fetch_dy(0)
        arrange(x_held, x_all, x_mine)
        for now in range(tiles):
            here = slice(now * tile, (now + 1) * tile)
            weight_copy(gate_ref, gate, gate_in, now, 1, tile).wait()
            pre_gate = dot(x_all[...], gate[now])
            weight_copy(up_ref, up, up_in, now, 1, tile).wait()
            pre_up = dot(x_all[...], up[now])
            if now == 0:
                wait(dy_pairs, dy_in)
                start(known_pairs, known_in)
                arrange(dy_held, dy_all, dy_mine)
            if now < tiles - 1:
                fetch_x(now + 1)
                fetch_dy(now + 1)
            weight_copy(down_ref, down, down_in, now, 0, tile).wait()
            d_hidden = dot(dy_all[...], down[now], BY_WIDTH)
            made, d_gate, d_up = hidden_grads(pre_gate, pre_up, d_hidden)
            if now == 0:
                wait(known_pairs, known_in)
            made = jnp.concatenate([factors[:, here], made], 0)
            d_gate = jnp.concatenate([factors[:, hid + here.start : hid + here.stop], d_gate], 0)
            d_up = jnp.concatenate(
                [factors[:, 2 * hid + here.start : 2 * hid + here.stop], d_up], 0
            )
            sums = dot(x_mine[...], jnp.concatenate([d_gate, d_up], 1), BY_ROWS)
            made_gate[now] = sums[:, :tile]
            made_up[now] = sums[:, tile:]
            leave(made_gate, d_gate_ref, gate_out, now, 1).start()
            leave(made_up, d_up_ref, up_out, now, 1).start()
            made_down[now] = dot(made, dy_mine[...], BY_ROWS)
            leave(made_down, d_down_ref, down_out, now, 0).start()
        for at in range(tiles):
            leave(made_gate, d_gate_ref, gate_out, at, 1).wait()
            leave(made_up, d_up_ref, up_out, at, 1).wait()
            leave(made_down, d_down_ref, down_out, at, 0).wait()

    held = pltpu.VMEM((count, blocks, ROWS, width + step), jnp.bfloat16)
    arranged = pltpu.VMEM((count * slots, width), jnp.bfloat16)
    mine = pltpu.VMEM((total, share), jnp.bfloat16)
    return pl.pallas_call(
        kernel,
        out_shape=[
            jax.ShapeDtypeStruct((share, hid), jnp.float32),
            jax.ShapeDtypeStruct((share, hid), jnp.float32),
            jax.ShapeDtypeStruct((hid, share), jnp.float32),
        ],
        in_specs=[pl.BlockSpec(memory_space=pltpu.SMEM)] + anywhere(given + count * items + 3),
        out_specs=anywhere(3),
        scratch_shapes=[
            held,
            held,
            arranged,
            arranged,
            mine,
            mine,
            pltpu.VMEM((given * slots, 3 * hid), jnp.bfloat16),
            pltpu.VMEM((tiles, width, tile), jnp.bfloat16),
            pltpu.VMEM((tiles, width, tile), jnp.bfloat16),
            pltpu.VMEM((tiles, tile, width), jnp.bfloat16),
            pltpu.SemaphoreType.DMA((count * items,)),
            pltpu.SemaphoreType.DMA((count * items,)),
            pltpu.SemaphoreType.DMA((3 * given,)),
            pltpu.SemaphoreType.DMA((tiles,)),
            pltpu.SemaphoreType.DMA((tiles,)),
            pltpu.SemaphoreType.DMA((tiles,)),
            pltpu.VMEM((tiles, share, tile), jnp.float32),
            pltpu.VMEM((tiles, share, tile), jnp.float32),
            pltpu.VMEM((tiles, tile, share), jnp.float32),
            pltpu.SemaphoreType.DMA((tiles,)),
            pltpu.SemaphoreType.DMA((tiles,)),
            pltpu.SemaphoreType.DMA((tiles,)),
        ],
        compiler_params=params(),
        cost_estimate=cost(0, 4 * slots * width),
        name="weight_grads",
    )(part, *known, *[item for group in groups for item in group], gate_proj, up_proj, down_proj)


def swap(value, axis, distance):
    size = lax.axis_size(axis)
    return lax.ppermute(value, axis, [(at, at ^ distance) for at in range(size)])


def exchange(blocks):
    return lax.all_to_all(blocks, "expert", split_axis=0, concat_axis=0, tiled=True)


def after(value, *earlier):
    return lax.optimization_barrier((value, *earlier))[0]


def gather_body(tokens, cotangent, routes, expert_gates, gate_proj, up_proj, down_proj):
    blocks = lax.axis_size("expert")
    tile, share = 256, tokens.shape[1] // lax.axis_size("dp")
    me = lax.axis_index("expert").astype(jnp.int32).reshape(1)
    part = lax.axis_index("dp").astype(jnp.int32).reshape(1)
    routes = routes.reshape(1, -1)
    gates = expert_gates.reshape(1, -1)
    weights = (gate_proj, up_proj, down_proj)
    received = list(pack(blocks, me, routes, gates, tokens, cotangent))
    for distance in reversed(range(1, blocks)):
        received[distance] = swap(received[distance], "expert", distance)
    half = blocks // 2
    far = swap(join(received[:half]), "dp", 2)
    work = 50 * blocks * MOST * gate_proj.size
    far_half = swap(join(received[half:], work), "dp", 2)
    sent, kept, handed = back(tile, share, me, part, received, *weights)
    last = swap(far, "dp", 1)
    sent, last = lax.optimization_barrier((sent, last))
    returned = exchange(sent)
    far = [far, after(far_half, sent)]
    last = [last, swap(far[1], "dp", 1)]
    known = [kept, swap(handed, "dp", 1)]
    grads = weight_grads(tile, share, part, known, [far, last], *weights)
    return (merge(routes, after(returned, *grads)), *grads)


def body(tokens, cotangent, routes, expert_gates, gate_proj, up_proj, down_proj):
    groups, blocks = lax.axis_size("dp"), lax.axis_size("expert")
    width, hid = gate_proj.shape
    rows_sent = (groups - 1) * 2 * blocks * MOST * width
    grads_sent = 3 * width * hid * (groups - 1) // groups
    fits = blocks == EXPERTS and groups == 4 and hid % 256 == 0
    fits = fits and tokens.shape[0] == 128 and routes.shape[1] == 1 and width // groups % 128 == 0
    chosen = gather_body if fits and rows_sent < grads_sent else scatter_body
    return chosen(tokens, cotangent, routes, expert_gates, gate_proj, up_proj, down_proj)


def solution(mesh):
    in_specs = (
        P(("dp", "expert"), None),
        P(("dp", "expert"), None),
        P(("dp", "expert"), None),
        P(("dp", "expert"), None),
        P(None, "expert"),
        P(None, "expert"),
        P("expert", None),
    )
    out_specs = (P(("dp", "expert"), None), P("dp", "expert"), P("dp", "expert"), P("expert", "dp"))
    return jax.shard_map(body, mesh=mesh, in_specs=in_specs, out_specs=out_specs, check_vma=False)
```

```python
import jax
import jax.numpy as jnp
from jax import lax
from jax.experimental import pallas as pl
from jax.experimental.pallas import tpu as pltpu
from jax.sharding import PartitionSpec as P

EXPERTS = 8
MOST = 18
ROWS = 16
VMEM_BYTES = (63 * 1024 + 768) * 1024


def build_slots(routes, capacity):
    flat_routes = routes.reshape(-1)
    one_hot = (flat_routes[:, None] == jnp.arange(EXPERTS, dtype=jnp.int32)[None, :]).astype(
        jnp.int32
    )
    before = jnp.cumsum(one_hot, axis=0) - one_hot
    position = jnp.sum(before * one_hot, axis=1)
    return flat_routes * capacity + position


def scatter_body(tokens, cotangent, routes, expert_gates, gate_proj, up_proj, down_proj):
    tok_dev, model_dim = tokens.shape
    top_k = routes.shape[1]
    expert_devs = lax.axis_size("expert")
    group_size = expert_devs // EXPERTS
    capacity = MOST
    slot_total = EXPERTS * capacity
    slot_of = build_slots(routes, capacity)
    owners = jnp.arange(tok_dev * top_k, dtype=jnp.int32) // top_k
    slot_table = jnp.full((slot_total,), tok_dev, jnp.int32).at[slot_of].set(owners)
    slot_gate = jnp.zeros((slot_total,), jnp.float32).at[slot_of].set(expert_gates.reshape(-1))
    x_slots = jnp.take(tokens, slot_table, axis=0, mode="fill", fill_value=0)
    dy_slots = (
        jnp.take(cotangent, slot_table, axis=0, mode="fill", fill_value=0).astype(jnp.float32)
        * slot_gate[:, None]
    ).astype(jnp.bfloat16)

    def copies(values):
        spread = values.reshape(EXPERTS, 1, capacity, model_dim)
        return jnp.broadcast_to(spread, (EXPERTS, group_size, capacity, model_dim)).reshape(
            expert_devs, capacity, model_dim
        )

    x_recv, dy_recv = (
        lax.all_to_all(copies(x_slots), "expert", split_axis=0, concat_axis=0, tiled=True),
        lax.all_to_all(copies(dy_slots), "expert", split_axis=0, concat_axis=0, tiled=True),
    )
    in_rows = x_recv.reshape(expert_devs * capacity, model_dim)
    scaled = dy_recv.reshape(expert_devs * capacity, model_dim)
    pre_gate = jnp.dot(in_rows, gate_proj, preferred_element_type=jnp.float32)
    pre_up = jnp.dot(in_rows, up_proj, preferred_element_type=jnp.float32)
    gate_sig = jax.nn.sigmoid(pre_gate)
    hidden = (pre_gate * gate_sig * pre_up).astype(jnp.bfloat16)
    by_width = (((1,), (1,)), ((), ()))
    by_rows = (((0,), (0,)), ((), ()))
    d_hidden = lax.dot_general(scaled, down_proj, by_width, preferred_element_type=jnp.float32)
    d_gate = (d_hidden * pre_up * gate_sig * (1.0 + pre_gate * (1.0 - gate_sig))).astype(
        jnp.bfloat16
    )
    d_up = (d_hidden * pre_gate * gate_sig).astype(jnp.bfloat16)
    grad_down = lax.dot_general(hidden, scaled, by_rows, preferred_element_type=jnp.float32)
    grad_gate = lax.dot_general(in_rows, d_gate, by_rows, preferred_element_type=jnp.float32)
    grad_up = lax.dot_general(in_rows, d_up, by_rows, preferred_element_type=jnp.float32)
    grad_gate, grad_up, grad_down = (
        lax.psum_scatter(
            grad_gate.astype(jnp.bfloat16), "dp", scatter_dimension=0, tiled=True
        ).astype(jnp.float32),
        lax.psum_scatter(
            grad_up.astype(jnp.bfloat16), "dp", scatter_dimension=0, tiled=True
        ).astype(jnp.float32),
        lax.psum_scatter(
            grad_down.astype(jnp.bfloat16), "dp", scatter_dimension=1, tiled=True
        ).astype(jnp.float32),
    )
    joined_grads = jnp.concatenate([d_gate, d_up], 1)
    joined_proj = jnp.concatenate([gate_proj, up_proj], 1)
    partial_value = lax.dot_general(
        joined_grads, joined_proj, by_width, preferred_element_type=jnp.float32
    ).astype(jnp.bfloat16)
    returned = lax.all_to_all(
        partial_value.reshape(expert_devs, capacity, model_dim),
        "expert",
        split_axis=0,
        concat_axis=0,
        tiled=True,
    )
    summed = jnp.sum(
        returned.reshape(EXPERTS, group_size, capacity, model_dim).astype(jnp.float32), axis=1
    )
    summed = summed.reshape(slot_total, model_dim)
    grad_input = jnp.take(summed, slot_of, axis=0).reshape(tok_dev, top_k, model_dim).sum(axis=1)
    return (grad_input.astype(jnp.bfloat16), grad_gate, grad_up, grad_down)


BY_WIDTH = (((1,), (1,)), ((), ()))
BY_ROWS = (((0,), (0,)), ((), ()))


def cut(width):
    pieces = ROWS // (MOST - ROWS)
    return pieces, width // pieces


def width_of(packed):
    pieces = ROWS // (MOST - ROWS)
    return packed.shape[2] * pieces // (pieces + 1)


def cost(flops, moved):
    return pl.CostEstimate(flops=flops, bytes_accessed=moved, transcendentals=0)


def params():
    return pltpu.CompilerParams(vmem_limit_bytes=VMEM_BYTES)


def anywhere(count):
    return [pl.BlockSpec(memory_space=pl.ANY)] * count


def dot(left, right, dims=(((1,), (0,)), ((), ()))):
    return lax.dot_general(left, right, dims, preferred_element_type=jnp.float32)


def ones(mask):
    return jnp.where(mask, 1.0, 0.0).astype(jnp.bfloat16)


def start(pairs, arrived, first=0):
    for at, (source, target) in enumerate(pairs):
        if at >= first:
            pltpu.make_async_copy(source, target, arrived.at[at]).start()


def wait(pairs, arrived, first=0):
    for at, (source, target) in enumerate(pairs):
        if at >= first:
            pltpu.make_async_copy(source, target, arrived.at[at]).wait()


def slot_masks(routes, blocks, width, me=0):
    tokens = routes.shape[1]
    pieces, _ = cut(width)
    experts = lax.broadcasted_iota(jnp.int32, (EXPERTS, tokens), 0)
    named = jnp.where(experts == routes, 1.0, 0.0)
    earlier = lax.broadcasted_iota(jnp.int32, (tokens, tokens), 0) < lax.broadcasted_iota(
        jnp.int32, (tokens, tokens), 1
    )
    before = dot(named.astype(jnp.bfloat16), ones(earlier))
    position = jnp.sum(before * named, axis=0, keepdims=True).astype(jnp.int32)
    slot = lax.broadcasted_iota(jnp.int32, (blocks * ROWS, tokens), 0)
    row = slot % ROWS
    mine = (slot // ROWS) ^ me == routes
    main = mine & (position == row)
    spill = mine & (position == ROWS + row // pieces)
    return main, spill, row % pieces


def pack(blocks, me, routes, gates, tokens, cotangent):
    count, width = tokens.shape
    pieces, step = cut(width)
    sources = (routes, gates, tokens, cotangent)
    block_shape = (2 * ROWS, width + step)

    def kernel(me_ref, *refs):
        outs, held = refs[4 : 4 + blocks], refs[4 + blocks : 8 + blocks]
        staged, arrived, gone = refs[8 + blocks :]
        pairs = list(zip(refs[:4], held))
        start(pairs, arrived)
        wait(pairs[:2], arrived)
        main, spill, piece = slot_masks(held[0][...], blocks, width, me_ref[0])
        mains = ones(main)
        picks = jnp.concatenate([ones(spill & (piece == at)) for at in range(pieces)], 1)
        main_scale = jnp.sum(jnp.where(main, held[1][...], 0.0), axis=1, keepdims=True)
        spill_scale = jnp.sum(jnp.where(spill, held[1][...], 0.0), axis=1, keepdims=True)
        leaving = []
        for half in range(2):
            wait(pairs[: 3 + half], arrived, 2 + half)
            values = held[2 + half]
            rows = dot(mains, values[...])
            cuts = [values[:, at * step : (at + 1) * step] for at in range(pieces)]
            extra = dot(picks, jnp.concatenate(cuts, 0))
            if half > 0:
                rows, extra = rows * main_scale, extra * spill_scale
            rows = rows.astype(jnp.bfloat16)
            extra = extra.astype(jnp.bfloat16)
            here = slice(half * ROWS, (half + 1) * ROWS)
            for block in range(blocks):
                part = slice(block * ROWS, (block + 1) * ROWS)
                staged[block, here, :width] = rows[part]
                staged[block, here, width:] = extra[part]
            sent = [(staged.at[at, here], outs[at].at[here, :]) for at in range(blocks)]
            leaving += sent
            start(leaving, gone, half * blocks)
        wait(leaving, gone)

    return pl.pallas_call(
        kernel,
        out_shape=[jax.ShapeDtypeStruct(block_shape, jnp.bfloat16)] * blocks,
        in_specs=[pl.BlockSpec(memory_space=pltpu.SMEM)] + anywhere(4),
        out_specs=anywhere(blocks),
        scratch_shapes=[pltpu.VMEM(source.shape, source.dtype) for source in sources]
        + [
            pltpu.VMEM((blocks,) + block_shape, jnp.bfloat16),
            pltpu.SemaphoreType.DMA((4,)),
            pltpu.SemaphoreType.DMA((2 * blocks,)),
        ],
        compiler_params=params(),
        cost_estimate=cost(8 * blocks * ROWS * count * width, 8 * count * width),
        name="pack",
    )(me, *sources)


def join(received, flops=0):
    count = len(received)
    shape = (count,) + received[0].shape

    def kernel(*refs):
        out, held, arrived, gone = refs[count:]
        pairs = [(refs[at], held.at[at]) for at in range(count)]
        leaving = [(held.at[at], out.at[at]) for at in range(count)]
        start(pairs, arrived)
        for at in range(count):
            wait(pairs[: at + 1], arrived, at)
            start(leaving[: at + 1], gone, at)
        wait(leaving, gone)

    return pl.pallas_call(
        kernel,
        out_shape=jax.ShapeDtypeStruct(shape, jnp.bfloat16),
        in_specs=anywhere(count),
        out_specs=pl.BlockSpec(memory_space=pl.ANY),
        scratch_shapes=[
            pltpu.VMEM(shape, jnp.bfloat16),
            pltpu.SemaphoreType.DMA((count,)),
            pltpu.SemaphoreType.DMA((count,)),
        ],
        compiler_params=params(),
        cost_estimate=cost(flops, 4 * received[0].size * count),
        name="join",
    )(*received)


def merge(routes, returned):
    blocks = returned.shape[0]
    tokens = routes.shape[1]
    width = width_of(returned)
    pieces, step = cut(width)

    def kernel(routes_ref, back_ref, out, named, held, arrived):
        pairs = [(routes_ref, named), (back_ref, held)]
        start(pairs, arrived)
        wait(pairs[:1], arrived)
        main, spill, piece = slot_masks(named[...], blocks, width)
        mains = ones(main)
        picks = [ones(spill & (piece == at)) for at in range(pieces)]
        wait(pairs, arrived, 1)
        rows = jnp.concatenate([held[at, :, :width] for at in range(blocks)], 0)
        extra = jnp.concatenate([held[at, :, width:] for at in range(blocks)], 0)
        picked = dot(mains, rows, BY_ROWS)
        for at in range(pieces):
            columns = slice(at * step, (at + 1) * step)
            out[:, columns] = (picked[:, columns] + dot(picks[at], extra, BY_ROWS)).astype(
                jnp.bfloat16
            )

    return pl.pallas_call(
        kernel,
        out_shape=jax.ShapeDtypeStruct((tokens, width), jnp.bfloat16),
        in_specs=anywhere(2),
        out_specs=pl.BlockSpec(memory_space=pltpu.VMEM),
        scratch_shapes=[
            pltpu.VMEM(routes.shape, routes.dtype),
            pltpu.VMEM(returned.shape, returned.dtype),
            pltpu.SemaphoreType.DMA((2,)),
        ],
        compiler_params=params(),
        cost_estimate=cost(4 * blocks * ROWS * tokens * width, 4 * tokens * width),
        name="merge",
    )(routes, returned)


def spill_picks(blocks, pieces):
    extras = blocks * (MOST - ROWS)
    shape = (pieces * extras, blocks * ROWS)
    index = lax.broadcasted_iota(jnp.int32, shape, 0)
    row = lax.broadcasted_iota(jnp.int32, shape, 1)
    return ones(row == (index % extras) * pieces + index // extras)


def unpack(packed, first, out):
    blocks, width = packed.shape[0], out.shape[1]
    pieces, step = cut(width)
    extras = blocks * (MOST - ROWS)
    for at in range(blocks):
        out[first + at * ROWS : first + (at + 1) * ROWS, :] = packed[at, :, :width]
    tails = jnp.concatenate([packed[at, :, width:] for at in range(blocks)], 0)
    placed = dot(spill_picks(blocks, pieces), tails).astype(jnp.bfloat16)
    spill = slice(first + blocks * ROWS, first + blocks * MOST)
    for at in range(pieces):
        out[spill, at * step : (at + 1) * step] = placed[at * extras : (at + 1) * extras]


def tile_of(index, tile):
    return pl.ds(pl.multiple_of(index * tile, tile), tile)


def weight_copy(source, target, arrived, index, axis, tile):
    here = tile_of(index, tile)
    view = source.at[:, here] if axis else source.at[here, :]
    return pltpu.make_async_copy(view, target.at[index], arrived.at[index])


def halves(group, half, out):
    here = slice(half * ROWS, (half + 1) * ROWS)
    pairs, at = [], 0
    for item in group:
        if len(item.shape) == 2:
            pairs.append((item.at[here, :], out.at[at]))
            at += 1
        else:
            pairs.append((item.at[:, here, :], out.at[at : at + item.shape[0]]))
            at += item.shape[0]
    return pairs


def hidden_grads(pre_gate, pre_up, d_hidden):
    sig = 0.5 * jnp.tanh(0.5 * pre_gate) + 0.5
    silu = pre_gate * sig
    hidden = (silu * pre_up).astype(jnp.bfloat16)
    d_gate = (d_hidden * pre_up * (sig + silu * (1.0 - sig))).astype(jnp.bfloat16)
    d_up = (d_hidden * silu).astype(jnp.bfloat16)
    return hidden, d_gate, d_up


def back(tile, share, me, part, order, group, gate_proj, up_proj, down_proj):
    blocks = len(group)
    width, hid = gate_proj.shape
    slots = blocks * MOST
    pieces, step = cut(width)
    tiles = hid // tile
    chunk = 2 * step
    chunks = width // chunk
    shape = (blocks, ROWS, width + step)
    given = 3 * hid + 2 * share

    def kernel(me_ref, part_ref, *refs):
        refs = list(refs)
        group_refs = [refs.pop(0) for _ in range(blocks)]
        gate_ref, up_ref, down_ref, out, kept, handed = [refs.pop(0) for _ in range(6)]
        x_held, dy_held, rows, scaled, factors, cuts = [refs.pop(0) for _ in range(6)]
        staged, gate, up, down = [refs.pop(0) for _ in range(4)]
        x_in, dy_in, gate_in, up_in, down_in, gone, cut_in = refs
        x_pairs, dy_pairs = halves(group_refs, 0, x_held), halves(group_refs, 1, dy_held)

        def column_copy(source, target, arrived, index):
            here = slice(index * tile, (index + 1) * tile)
            return pltpu.make_async_copy(
                source.at[:, here], target.at[:, here], arrived.at[index]
            )

        def fetch_x(index):
            column_copy(gate_ref, gate, gate_in, index).start()
            column_copy(up_ref, up, up_in, index).start()

        def fetch_dy(index):
            weight_copy(down_ref, down, down_in, index, 0, tile).start()

        def leave(index):
            columns = slice(index * chunk, (index + 1) * chunk)
            return pltpu.make_async_copy(
                staged.at[:, :, columns], out.at[:, :, columns], gone.at[index]
            )

        first, behind = slice(0, 3 * hid), slice(3 * hid, given)
        leaving = [(factors, kept.at[:, first]), (cuts.at[0], kept.at[:, behind])]
        leaving += [(factors, handed.at[:, first]), (cuts.at[1], handed.at[:, behind])]

        start(x_pairs, x_in)
        fetch_x(0)
        wait(x_pairs, x_in)
        start(dy_pairs, dy_in)
        fetch_dy(0)
        unpack(x_held, 0, rows)
        for now in range(tiles):
            columns = slice(now * tile, (now + 1) * tile)
            column_copy(gate_ref, gate, gate_in, now).wait()
            pre_gate = dot(rows[...], gate[:, columns])
            if now < tiles - 1:
                fetch_x(now + 1)
            column_copy(up_ref, up, up_in, now).wait()
            pre_up = dot(rows[...], up[:, columns])
            if now == 0:
                wait(dy_pairs, dy_in)
                unpack(dy_held, 0, scaled)
            if now < tiles - 1:
                fetch_dy(now + 1)
            weight_copy(down_ref, down, down_in, now, 0, tile).wait()
            d_hidden = dot(scaled[...], down[now], BY_WIDTH)
            made, d_gate, d_up = hidden_grads(pre_gate, pre_up, d_hidden)
            factors[:, columns] = made
            factors[:, hid + now * tile : hid + (now + 1) * tile] = d_gate
            factors[:, 2 * hid + now * tile : 2 * hid + (now + 1) * tile] = d_up

        for at in range(2):
            columns = tile_of(part_ref[0] ^ at, share)
            cuts[at, :, :share] = rows[:, columns]
            cuts[at, :, share:] = scaled[:, columns]
        start(leaving, cut_in)
        extras = []
        for at in range(chunks):
            here = slice(at * chunk, (at + 1) * chunk)
            done = dot(factors[:, hid : 2 * hid], gate[here, :], BY_WIDTH)
            done += dot(factors[:, 2 * hid :], up[here, :], BY_WIDTH)
            done = done.astype(jnp.bfloat16)
            for block in range(blocks):
                staged[me_ref[0] ^ order[block], :, here] = done[block * ROWS : (block + 1) * ROWS]
            leave(at).start()
            extras += [done[blocks * ROWS :, :step], done[blocks * ROWS :, step:]]
        tail = dot(spill_picks(blocks, pieces), jnp.concatenate(extras, 0), BY_ROWS)
        tail = tail.astype(jnp.bfloat16)
        for block in range(blocks):
            staged[me_ref[0] ^ order[block], :, width:] = tail[block * ROWS : (block + 1) * ROWS]
        last = pltpu.make_async_copy(
            staged.at[:, :, width:], out.at[:, :, width:], gone.at[chunks]
        )
        last.start()
        for at in range(chunks):
            leave(at).wait()
        wait(leaving, cut_in)
        last.wait()

    return pl.pallas_call(
        kernel,
        out_shape=[
            jax.ShapeDtypeStruct(shape, jnp.bfloat16),
            jax.ShapeDtypeStruct((slots, given), jnp.bfloat16),
            jax.ShapeDtypeStruct((slots, given), jnp.bfloat16),
        ],
        in_specs=[pl.BlockSpec(memory_space=pltpu.SMEM)] * 2 + anywhere(blocks + 3),
        out_specs=anywhere(3),
        scratch_shapes=[
            pltpu.VMEM(shape, jnp.bfloat16),
            pltpu.VMEM(shape, jnp.bfloat16),
            pltpu.VMEM((slots, width), jnp.bfloat16),
            pltpu.VMEM((slots, width), jnp.bfloat16),
            pltpu.VMEM((slots, 3 * hid), jnp.bfloat16),
            pltpu.VMEM((2, slots, 2 * share), jnp.bfloat16),
            pltpu.VMEM(shape, jnp.bfloat16),
            pltpu.VMEM((width, hid), jnp.bfloat16),
            pltpu.VMEM((width, hid), jnp.bfloat16),
            pltpu.VMEM((tiles, tile, width), jnp.bfloat16),
            pltpu.SemaphoreType.DMA((blocks,)),
            pltpu.SemaphoreType.DMA((blocks,)),
            pltpu.SemaphoreType.DMA((tiles,)),
            pltpu.SemaphoreType.DMA((tiles,)),
            pltpu.SemaphoreType.DMA((tiles,)),
            pltpu.SemaphoreType.DMA((chunks + 1,)),
            pltpu.SemaphoreType.DMA((4,)),
        ],
        compiler_params=params(),
        cost_estimate=cost(50 * slots * width * hid, 4 * slots * width),
        name="back",
    )(me, part, *group, gate_proj, up_proj, down_proj)


def weight_grads(tile, share, part, known, groups, gate_proj, up_proj, down_proj):
    count, items = len(groups), len(groups[0])
    blocks = sum(item.shape[0] if item.ndim == 3 else 1 for item in groups[0])
    given = len(known)
    hid, width = down_proj.shape
    pieces, step = cut(width)
    slots = blocks * MOST
    total = (given + count) * slots
    tiles = hid // tile

    def kernel(part_ref, *refs):
        refs = list(refs)
        known_refs = [refs.pop(0) for _ in range(given)]
        group_refs = [[refs.pop(0) for _ in range(items)] for _ in range(count)]
        gate_ref, up_ref, down_ref = [refs.pop(0) for _ in range(3)]
        d_gate_ref, d_up_ref, d_down_ref = [refs.pop(0) for _ in range(3)]
        x_held, dy_held, x_all, dy_all = [refs.pop(0) for _ in range(4)]
        x_mine, dy_mine, factors = [refs.pop(0) for _ in range(3)]
        gate, up, down, x_in, dy_in, known_in, gate_in, up_in, down_in = refs[:9]
        made_gate, made_up, made_down, gate_out, up_out, down_out = refs[9:]
        columns = tile_of(part_ref[0], share)
        x_pairs, dy_pairs, known_pairs = [], [], []
        for at in range(count):
            x_pairs += halves(group_refs[at], 0, x_held.at[at])
            dy_pairs += halves(group_refs[at], 1, dy_held.at[at])
        for at in range(given):
            here = slice(at * slots, (at + 1) * slots)
            behind = 3 * hid
            known_pairs += [
                (known_refs[at].at[:, :behind], factors.at[here, :]),
                (known_refs[at].at[:, behind : behind + share], x_mine.at[here, :]),
                (known_refs[at].at[:, behind + share :], dy_mine.at[here, :]),
            ]

        def arrange(held, rows_out, target):
            for at in range(count):
                unpack(held.at[at], at * slots, rows_out)
            target[given * slots :, :] = rows_out[:, columns]

        def leave(source, target, gone, index, axis):
            here = tile_of(index, tile)
            view = target.at[:, here] if axis else target.at[here, :]
            return pltpu.make_async_copy(source.at[index], view, gone.at[index])

        def fetch_x(index):
            weight_copy(gate_ref, gate, gate_in, index, 1, tile).start()
            weight_copy(up_ref, up, up_in, index, 1, tile).start()

        def fetch_dy(index):
            weight_copy(down_ref, down, down_in, index, 0, tile).start()

        start(x_pairs, x_in)
        fetch_x(0)
        wait(x_pairs, x_in)
        start(dy_pairs, dy_in)
        fetch_dy(0)
        arrange(x_held, x_all, x_mine)
        for now in range(tiles):
            here = slice(now * tile, (now + 1) * tile)
            weight_copy(gate_ref, gate, gate_in, now, 1, tile).wait()
            pre_gate = dot(x_all[...], gate[now])
            weight_copy(up_ref, up, up_in, now, 1, tile).wait()
            pre_up = dot(x_all[...], up[now])
            if now == 0:
                wait(dy_pairs, dy_in)
                start(known_pairs, known_in)
                arrange(dy_held, dy_all, dy_mine)
            if now < tiles - 1:
                fetch_x(now + 1)
                fetch_dy(now + 1)
            weight_copy(down_ref, down, down_in, now, 0, tile).wait()
            d_hidden = dot(dy_all[...], down[now], BY_WIDTH)
            made, d_gate, d_up = hidden_grads(pre_gate, pre_up, d_hidden)
            if now == 0:
                wait(known_pairs, known_in)
            made = jnp.concatenate([factors[:, here], made], 0)
            d_gate = jnp.concatenate([factors[:, hid + here.start : hid + here.stop], d_gate], 0)
            d_up = jnp.concatenate(
                [factors[:, 2 * hid + here.start : 2 * hid + here.stop], d_up], 0
            )
            sums = dot(x_mine[...], jnp.concatenate([d_gate, d_up], 1), BY_ROWS)
            made_gate[now] = sums[:, :tile]
            made_up[now] = sums[:, tile:]
            leave(made_gate, d_gate_ref, gate_out, now, 1).start()
            leave(made_up, d_up_ref, up_out, now, 1).start()
            made_down[now] = dot(made, dy_mine[...], BY_ROWS)
            leave(made_down, d_down_ref, down_out, now, 0).start()
        for at in range(tiles):
            leave(made_gate, d_gate_ref, gate_out, at, 1).wait()
            leave(made_up, d_up_ref, up_out, at, 1).wait()
            leave(made_down, d_down_ref, down_out, at, 0).wait()

    held = pltpu.VMEM((count, blocks, ROWS, width + step), jnp.bfloat16)
    arranged = pltpu.VMEM((count * slots, width), jnp.bfloat16)
    mine = pltpu.VMEM((total, share), jnp.bfloat16)
    return pl.pallas_call(
        kernel,
        out_shape=[
            jax.ShapeDtypeStruct((share, hid), jnp.float32),
            jax.ShapeDtypeStruct((share, hid), jnp.float32),
            jax.ShapeDtypeStruct((hid, share), jnp.float32),
        ],
        in_specs=[pl.BlockSpec(memory_space=pltpu.SMEM)] + anywhere(given + count * items + 3),
        out_specs=anywhere(3),
        scratch_shapes=[
            held,
            held,
            arranged,
            arranged,
            mine,
            mine,
            pltpu.VMEM((given * slots, 3 * hid), jnp.bfloat16),
            pltpu.VMEM((tiles, width, tile), jnp.bfloat16),
            pltpu.VMEM((tiles, width, tile), jnp.bfloat16),
            pltpu.VMEM((tiles, tile, width), jnp.bfloat16),
            pltpu.SemaphoreType.DMA((count * items,)),
            pltpu.SemaphoreType.DMA((count * items,)),
            pltpu.SemaphoreType.DMA((3 * given,)),
            pltpu.SemaphoreType.DMA((tiles,)),
            pltpu.SemaphoreType.DMA((tiles,)),
            pltpu.SemaphoreType.DMA((tiles,)),
            pltpu.VMEM((tiles, share, tile), jnp.float32),
            pltpu.VMEM((tiles, share, tile), jnp.float32),
            pltpu.VMEM((tiles, tile, share), jnp.float32),
            pltpu.SemaphoreType.DMA((tiles,)),
            pltpu.SemaphoreType.DMA((tiles,)),
            pltpu.SemaphoreType.DMA((tiles,)),
        ],
        compiler_params=params(),
        cost_estimate=cost(0, 4 * slots * width),
        name="weight_grads",
    )(part, *known, *[item for group in groups for item in group], gate_proj, up_proj, down_proj)


def swap(value, axis, distance):
    size = lax.axis_size(axis)
    return lax.ppermute(value, axis, [(at, at ^ distance) for at in range(size)])


def exchange(blocks):
    return lax.all_to_all(blocks, "expert", split_axis=0, concat_axis=0, tiled=True)


def after(value, *earlier):
    return lax.optimization_barrier((value, *earlier))[0]


def gather_body(tokens, cotangent, routes, expert_gates, gate_proj, up_proj, down_proj):
    blocks = lax.axis_size("expert")
    tile, share = 256, tokens.shape[1] // lax.axis_size("dp")
    me = lax.axis_index("expert").astype(jnp.int32).reshape(1)
    part = lax.axis_index("dp").astype(jnp.int32).reshape(1)
    routes = routes.reshape(1, -1)
    gates = expert_gates.reshape(1, -1)
    weights = (gate_proj, up_proj, down_proj)
    received = list(pack(blocks, me, routes, gates, tokens, cotangent))
    for distance in reversed(range(1, blocks)):
        received[distance] = swap(received[distance], "expert", distance)
    order = [0, 1, 2, 4, 5, 6, 7, 3]
    early = 3
    received = [received[index] for index in order]
    far = swap(join(received[:early]), "dp", 2)
    work = 50 * blocks * MOST * gate_proj.size
    far_rest = swap(join(received[early:], work), "dp", 2)
    sent, kept, handed = back(tile, share, me, part, order, received, *weights)
    last = swap(far, "dp", 1)
    sent, last = lax.optimization_barrier((sent, last))
    returned = exchange(sent)
    far = [far, after(far_rest, sent)]
    last = [last, swap(far[1], "dp", 1)]
    known = [kept, swap(handed, "dp", 1)]
    grads = weight_grads(tile, share, part, known, [far, last], *weights)
    return (merge(routes, after(returned, *grads)), *grads)


def body(tokens, cotangent, routes, expert_gates, gate_proj, up_proj, down_proj):
    groups, blocks = lax.axis_size("dp"), lax.axis_size("expert")
    width, hid = gate_proj.shape
    rows_sent = (groups - 1) * 2 * blocks * MOST * width
    grads_sent = 3 * width * hid * (groups - 1) // groups
    fits = blocks == EXPERTS and groups == 4 and hid % 256 == 0
    fits = fits and tokens.shape[0] == 128 and routes.shape[1] == 1 and width // groups % 128 == 0
    chosen = gather_body if fits and rows_sent < grads_sent else scatter_body
    return chosen(tokens, cotangent, routes, expert_gates, gate_proj, up_proj, down_proj)


def solution(mesh):
    in_specs = (
        P(("dp", "expert"), None),
        P(("dp", "expert"), None),
        P(("dp", "expert"), None),
        P(("dp", "expert"), None),
        P(None, "expert"),
        P(None, "expert"),
        P("expert", None),
    )
    out_specs = (P(("dp", "expert"), None), P("dp", "expert"), P("dp", "expert"), P("expert", "dp"))
    return jax.shard_map(body, mesh=mesh, in_specs=in_specs, out_specs=out_specs, check_vma=False)
```

```python
import jax
import jax.numpy as jnp
from jax import lax
from jax.experimental import pallas as pl
from jax.experimental.pallas import tpu as pltpu
from jax.sharding import PartitionSpec as P

EXPERTS = 8
MOST = 18
ROWS = 16
VMEM_BYTES = (63 * 1024 + 768) * 1024


def build_slots(routes, capacity):
    flat_routes = routes.reshape(-1)
    one_hot = (flat_routes[:, None] == jnp.arange(EXPERTS, dtype=jnp.int32)[None, :]).astype(
        jnp.int32
    )
    before = jnp.cumsum(one_hot, axis=0) - one_hot
    position = jnp.sum(before * one_hot, axis=1)
    return flat_routes * capacity + position


def scatter_body(tokens, cotangent, routes, expert_gates, gate_proj, up_proj, down_proj):
    tok_dev, model_dim = tokens.shape
    top_k = routes.shape[1]
    expert_devs = lax.axis_size("expert")
    group_size = expert_devs // EXPERTS
    capacity = MOST
    slot_total = EXPERTS * capacity
    slot_of = build_slots(routes, capacity)
    owners = jnp.arange(tok_dev * top_k, dtype=jnp.int32) // top_k
    slot_table = jnp.full((slot_total,), tok_dev, jnp.int32).at[slot_of].set(owners)
    slot_gate = jnp.zeros((slot_total,), jnp.float32).at[slot_of].set(expert_gates.reshape(-1))
    x_slots = jnp.take(tokens, slot_table, axis=0, mode="fill", fill_value=0)
    dy_slots = (
        jnp.take(cotangent, slot_table, axis=0, mode="fill", fill_value=0).astype(jnp.float32)
        * slot_gate[:, None]
    ).astype(jnp.bfloat16)

    def copies(values):
        spread = values.reshape(EXPERTS, 1, capacity, model_dim)
        return jnp.broadcast_to(spread, (EXPERTS, group_size, capacity, model_dim)).reshape(
            expert_devs, capacity, model_dim
        )

    x_recv, dy_recv = (
        lax.all_to_all(copies(x_slots), "expert", split_axis=0, concat_axis=0, tiled=True),
        lax.all_to_all(copies(dy_slots), "expert", split_axis=0, concat_axis=0, tiled=True),
    )
    in_rows = x_recv.reshape(expert_devs * capacity, model_dim)
    scaled = dy_recv.reshape(expert_devs * capacity, model_dim)
    pre_gate = jnp.dot(in_rows, gate_proj, preferred_element_type=jnp.float32)
    pre_up = jnp.dot(in_rows, up_proj, preferred_element_type=jnp.float32)
    gate_sig = jax.nn.sigmoid(pre_gate)
    hidden = (pre_gate * gate_sig * pre_up).astype(jnp.bfloat16)
    by_width = (((1,), (1,)), ((), ()))
    by_rows = (((0,), (0,)), ((), ()))
    d_hidden = lax.dot_general(scaled, down_proj, by_width, preferred_element_type=jnp.float32)
    d_gate = (d_hidden * pre_up * gate_sig * (1.0 + pre_gate * (1.0 - gate_sig))).astype(
        jnp.bfloat16
    )
    d_up = (d_hidden * pre_gate * gate_sig).astype(jnp.bfloat16)
    grad_down = lax.dot_general(hidden, scaled, by_rows, preferred_element_type=jnp.float32)
    grad_gate = lax.dot_general(in_rows, d_gate, by_rows, preferred_element_type=jnp.float32)
    grad_up = lax.dot_general(in_rows, d_up, by_rows, preferred_element_type=jnp.float32)
    grad_gate, grad_up, grad_down = (
        lax.psum_scatter(
            grad_gate.astype(jnp.bfloat16), "dp", scatter_dimension=0, tiled=True
        ).astype(jnp.float32),
        lax.psum_scatter(
            grad_up.astype(jnp.bfloat16), "dp", scatter_dimension=0, tiled=True
        ).astype(jnp.float32),
        lax.psum_scatter(
            grad_down.astype(jnp.bfloat16), "dp", scatter_dimension=1, tiled=True
        ).astype(jnp.float32),
    )
    joined_grads = jnp.concatenate([d_gate, d_up], 1)
    joined_proj = jnp.concatenate([gate_proj, up_proj], 1)
    partial_value = lax.dot_general(
        joined_grads, joined_proj, by_width, preferred_element_type=jnp.float32
    ).astype(jnp.bfloat16)
    returned = lax.all_to_all(
        partial_value.reshape(expert_devs, capacity, model_dim),
        "expert",
        split_axis=0,
        concat_axis=0,
        tiled=True,
    )
    summed = jnp.sum(
        returned.reshape(EXPERTS, group_size, capacity, model_dim).astype(jnp.float32), axis=1
    )
    summed = summed.reshape(slot_total, model_dim)
    grad_input = jnp.take(summed, slot_of, axis=0).reshape(tok_dev, top_k, model_dim).sum(axis=1)
    return (grad_input.astype(jnp.bfloat16), grad_gate, grad_up, grad_down)


BY_WIDTH = (((1,), (1,)), ((), ()))
BY_ROWS = (((0,), (0,)), ((), ()))


def cut(width):
    pieces = ROWS // (MOST - ROWS)
    return pieces, width // pieces


def width_of(packed):
    pieces = ROWS // (MOST - ROWS)
    return packed.shape[2] * pieces // (pieces + 1)


def cost(flops, moved):
    return pl.CostEstimate(flops=flops, bytes_accessed=moved, transcendentals=0)


def params():
    return pltpu.CompilerParams(vmem_limit_bytes=VMEM_BYTES)


def anywhere(count):
    return [pl.BlockSpec(memory_space=pl.ANY)] * count


def dot(left, right, dims=(((1,), (0,)), ((), ()))):
    return lax.dot_general(left, right, dims, preferred_element_type=jnp.float32)


def ones(mask):
    return jnp.where(mask, 1.0, 0.0).astype(jnp.bfloat16)


def start(pairs, arrived, first=0):
    for at, (source, target) in enumerate(pairs):
        if at >= first:
            pltpu.make_async_copy(source, target, arrived.at[at]).start()


def wait(pairs, arrived, first=0):
    for at, (source, target) in enumerate(pairs):
        if at >= first:
            pltpu.make_async_copy(source, target, arrived.at[at]).wait()


def slot_masks(routes, blocks, width, me=0):
    tokens = routes.shape[1]
    pieces, _ = cut(width)
    experts = lax.broadcasted_iota(jnp.int32, (EXPERTS, tokens), 0)
    named = jnp.where(experts == routes, 1.0, 0.0)
    earlier = lax.broadcasted_iota(jnp.int32, (tokens, tokens), 0) < lax.broadcasted_iota(
        jnp.int32, (tokens, tokens), 1
    )
    before = dot(named.astype(jnp.bfloat16), ones(earlier))
    position = jnp.sum(before * named, axis=0, keepdims=True).astype(jnp.int32)
    slot = lax.broadcasted_iota(jnp.int32, (blocks * ROWS, tokens), 0)
    row = slot % ROWS
    mine = (slot // ROWS) ^ me == routes
    main = mine & (position == row)
    spill = mine & (position == ROWS + row // pieces)
    return main, spill, row % pieces


def pack(blocks, me, routes, gates, tokens, cotangent):
    near = blocks // 2
    count, width = tokens.shape
    pieces, step = cut(width)
    sources = (routes, gates, tokens, cotangent)
    block_shape = (2 * ROWS, width + step)

    def kernel(me_ref, *refs):
        outs, held = refs[4 : 5 + near], refs[5 + near : 9 + near]
        staged, arrived, gone = refs[9 + near :]
        targets = [outs[0].at[(me_ref[0] & (near - 1)) ^ at] for at in range(near)]
        targets += outs[1:]
        pairs = list(zip(refs[:4], held))
        start(pairs, arrived)
        wait(pairs[:2], arrived)
        main, spill, piece = slot_masks(held[0][...], blocks, width, me_ref[0])
        mains = ones(main)
        picks = jnp.concatenate([ones(spill & (piece == at)) for at in range(pieces)], 1)
        main_scale = jnp.sum(jnp.where(main, held[1][...], 0.0), axis=1, keepdims=True)
        spill_scale = jnp.sum(jnp.where(spill, held[1][...], 0.0), axis=1, keepdims=True)
        leaving = []
        for half in range(2):
            wait(pairs[: 3 + half], arrived, 2 + half)
            values = held[2 + half]
            rows = dot(mains, values[...])
            cuts = [values[:, at * step : (at + 1) * step] for at in range(pieces)]
            extra = dot(picks, jnp.concatenate(cuts, 0))
            if half > 0:
                rows, extra = rows * main_scale, extra * spill_scale
            rows = rows.astype(jnp.bfloat16)
            extra = extra.astype(jnp.bfloat16)
            here = slice(half * ROWS, (half + 1) * ROWS)
            for block in range(blocks):
                part = slice(block * ROWS, (block + 1) * ROWS)
                staged[block, here, :width] = rows[part]
                staged[block, here, width:] = extra[part]
            sent = [(staged.at[at, here], targets[at].at[here, :]) for at in range(blocks)]
            leaving += sent
            start(leaving, gone, half * blocks)
        wait(leaving, gone)

    return pl.pallas_call(
        kernel,
        out_shape=[jax.ShapeDtypeStruct((near,) + block_shape, jnp.bfloat16)]
        + [jax.ShapeDtypeStruct(block_shape, jnp.bfloat16)] * (blocks - near),
        in_specs=[pl.BlockSpec(memory_space=pltpu.SMEM)] + anywhere(4),
        out_specs=anywhere(1 + blocks - near),
        scratch_shapes=[pltpu.VMEM(source.shape, source.dtype) for source in sources]
        + [
            pltpu.VMEM((blocks,) + block_shape, jnp.bfloat16),
            pltpu.SemaphoreType.DMA((4,)),
            pltpu.SemaphoreType.DMA((2 * blocks,)),
        ],
        compiler_params=params(),
        cost_estimate=cost(8 * blocks * ROWS * count * width, 8 * count * width),
        name="pack",
    )(me, *sources)


def join(received, flops=0):
    count = len(received)
    shape = (count,) + received[0].shape

    def kernel(*refs):
        out, held, arrived, gone = refs[count:]
        pairs = [(refs[at], held.at[at]) for at in range(count)]
        leaving = [(held.at[at], out.at[at]) for at in range(count)]
        start(pairs, arrived)
        for at in range(count):
            wait(pairs[: at + 1], arrived, at)
            start(leaving[: at + 1], gone, at)
        wait(leaving, gone)

    return pl.pallas_call(
        kernel,
        out_shape=jax.ShapeDtypeStruct(shape, jnp.bfloat16),
        in_specs=anywhere(count),
        out_specs=pl.BlockSpec(memory_space=pl.ANY),
        scratch_shapes=[
            pltpu.VMEM(shape, jnp.bfloat16),
            pltpu.SemaphoreType.DMA((count,)),
            pltpu.SemaphoreType.DMA((count,)),
        ],
        compiler_params=params(),
        cost_estimate=cost(flops, 4 * received[0].size * count),
        name="join",
    )(*received)


def merge(routes, returned):
    blocks = returned.shape[0]
    tokens = routes.shape[1]
    width = width_of(returned)
    pieces, step = cut(width)

    def kernel(routes_ref, back_ref, out, named, held, arrived):
        pairs = [(routes_ref, named), (back_ref, held)]
        start(pairs, arrived)
        wait(pairs[:1], arrived)
        main, spill, piece = slot_masks(named[...], blocks, width)
        mains = ones(main)
        picks = [ones(spill & (piece == at)) for at in range(pieces)]
        wait(pairs, arrived, 1)
        rows = jnp.concatenate([held[at, :, :width] for at in range(blocks)], 0)
        extra = jnp.concatenate([held[at, :, width:] for at in range(blocks)], 0)
        picked = dot(mains, rows, BY_ROWS)
        for at in range(pieces):
            columns = slice(at * step, (at + 1) * step)
            out[:, columns] = (picked[:, columns] + dot(picks[at], extra, BY_ROWS)).astype(
                jnp.bfloat16
            )

    return pl.pallas_call(
        kernel,
        out_shape=jax.ShapeDtypeStruct((tokens, width), jnp.bfloat16),
        in_specs=anywhere(2),
        out_specs=pl.BlockSpec(memory_space=pltpu.VMEM),
        scratch_shapes=[
            pltpu.VMEM(routes.shape, routes.dtype),
            pltpu.VMEM(returned.shape, returned.dtype),
            pltpu.SemaphoreType.DMA((2,)),
        ],
        compiler_params=params(),
        cost_estimate=cost(4 * blocks * ROWS * tokens * width, 4 * tokens * width),
        name="merge",
    )(routes, returned)


def spill_picks(blocks, pieces):
    extras = blocks * (MOST - ROWS)
    shape = (pieces * extras, blocks * ROWS)
    index = lax.broadcasted_iota(jnp.int32, shape, 0)
    row = lax.broadcasted_iota(jnp.int32, shape, 1)
    return ones(row == (index % extras) * pieces + index // extras)


def unpack(packed, first, out):
    blocks, width = packed.shape[0], out.shape[1]
    pieces, step = cut(width)
    extras = blocks * (MOST - ROWS)
    for at in range(blocks):
        out[first + at * ROWS : first + (at + 1) * ROWS, :] = packed[at, :, :width]
    tails = jnp.concatenate([packed[at, :, width:] for at in range(blocks)], 0)
    placed = dot(spill_picks(blocks, pieces), tails).astype(jnp.bfloat16)
    spill = slice(first + blocks * ROWS, first + blocks * MOST)
    for at in range(pieces):
        out[spill, at * step : (at + 1) * step] = placed[at * extras : (at + 1) * extras]


def tile_of(index, tile):
    return pl.ds(pl.multiple_of(index * tile, tile), tile)


def weight_copy(source, target, arrived, index, axis, tile):
    here = tile_of(index, tile)
    view = source.at[:, here] if axis else source.at[here, :]
    return pltpu.make_async_copy(view, target.at[index], arrived.at[index])


def halves(group, half, out):
    here = slice(half * ROWS, (half + 1) * ROWS)
    pairs, at = [], 0
    for item in group:
        if len(item.shape) == 2:
            pairs.append((item.at[here, :], out.at[at]))
            at += 1
        else:
            pairs.append((item.at[:, here, :], out.at[at : at + item.shape[0]]))
            at += item.shape[0]
    return pairs


def hidden_grads(pre_gate, pre_up, d_hidden):
    sig = 0.5 * jnp.tanh(0.5 * pre_gate) + 0.5
    silu = pre_gate * sig
    hidden = (silu * pre_up).astype(jnp.bfloat16)
    d_gate = (d_hidden * pre_up * (sig + silu * (1.0 - sig))).astype(jnp.bfloat16)
    d_up = (d_hidden * silu).astype(jnp.bfloat16)
    return hidden, d_gate, d_up


def back(tile, share, me, part, group, gate_proj, up_proj, down_proj):
    items, near = len(group), group[0].shape[0]
    blocks = near + items - 1
    width, hid = gate_proj.shape
    slots = blocks * MOST
    pieces, step = cut(width)
    tiles = hid // tile
    chunk = 2 * step
    chunks = width // chunk
    shape = (blocks, ROWS, width + step)
    given = 3 * hid + 2 * share

    def kernel(me_ref, part_ref, *refs):
        refs = list(refs)
        group_refs = [refs.pop(0) for _ in range(items)]
        gate_ref, up_ref, down_ref, out, kept, handed = [refs.pop(0) for _ in range(6)]
        x_held, dy_held, rows, scaled, factors, cuts = [refs.pop(0) for _ in range(6)]
        staged, gate, up, down = [refs.pop(0) for _ in range(4)]
        x_in, dy_in, gate_in, up_in, down_in, gone, cut_in = refs
        x_pairs, dy_pairs = halves(group_refs, 0, x_held), halves(group_refs, 1, dy_held)

        def column_copy(source, target, arrived, index):
            here = slice(index * tile, (index + 1) * tile)
            return pltpu.make_async_copy(
                source.at[:, here], target.at[:, here], arrived.at[index]
            )

        def fetch_x(index):
            column_copy(gate_ref, gate, gate_in, index).start()
            column_copy(up_ref, up, up_in, index).start()

        def fetch_dy(index):
            weight_copy(down_ref, down, down_in, index, 0, tile).start()

        def leave(index):
            columns = slice(index * chunk, (index + 1) * chunk)
            return pltpu.make_async_copy(
                staged.at[:, :, columns], out.at[:, :, columns], gone.at[index]
            )

        senders = [me_ref[0] - (me_ref[0] & (near - 1)) + at for at in range(near)]
        senders += [me_ref[0] ^ at for at in range(near, blocks)]
        first, behind = slice(0, 3 * hid), slice(3 * hid, given)
        leaving = [(factors, kept.at[:, first]), (cuts.at[0], kept.at[:, behind])]
        leaving += [(factors, handed.at[:, first]), (cuts.at[1], handed.at[:, behind])]

        start(x_pairs, x_in)
        fetch_x(0)
        wait(x_pairs, x_in)
        start(dy_pairs, dy_in)
        fetch_dy(0)
        unpack(x_held, 0, rows)
        for now in range(tiles):
            columns = slice(now * tile, (now + 1) * tile)
            column_copy(gate_ref, gate, gate_in, now).wait()
            pre_gate = dot(rows[...], gate[:, columns])
            if now < tiles - 1:
                fetch_x(now + 1)
            column_copy(up_ref, up, up_in, now).wait()
            pre_up = dot(rows[...], up[:, columns])
            if now == 0:
                wait(dy_pairs, dy_in)
                unpack(dy_held, 0, scaled)
            if now < tiles - 1:
                fetch_dy(now + 1)
            weight_copy(down_ref, down, down_in, now, 0, tile).wait()
            d_hidden = dot(scaled[...], down[now], BY_WIDTH)
            made, d_gate, d_up = hidden_grads(pre_gate, pre_up, d_hidden)
            factors[:, columns] = made
            factors[:, hid + now * tile : hid + (now + 1) * tile] = d_gate
            factors[:, 2 * hid + now * tile : 2 * hid + (now + 1) * tile] = d_up

        for at in range(2):
            columns = tile_of(part_ref[0] ^ at, share)
            cuts[at, :, :share] = rows[:, columns]
            cuts[at, :, share:] = scaled[:, columns]
        start(leaving, cut_in)
        extras = []
        for at in range(chunks):
            here = slice(at * chunk, (at + 1) * chunk)
            done = dot(factors[:, hid : 2 * hid], gate[here, :], BY_WIDTH)
            done += dot(factors[:, 2 * hid :], up[here, :], BY_WIDTH)
            done = done.astype(jnp.bfloat16)
            for block in range(blocks):
                staged[senders[block], :, here] = done[block * ROWS : (block + 1) * ROWS]
            leave(at).start()
            extras += [done[blocks * ROWS :, :step], done[blocks * ROWS :, step:]]
        tail = dot(spill_picks(blocks, pieces), jnp.concatenate(extras, 0), BY_ROWS)
        tail = tail.astype(jnp.bfloat16)
        for block in range(blocks):
            staged[senders[block], :, width:] = tail[block * ROWS : (block + 1) * ROWS]
        last = pltpu.make_async_copy(
            staged.at[:, :, width:], out.at[:, :, width:], gone.at[chunks]
        )
        last.start()
        for at in range(chunks):
            leave(at).wait()
        wait(leaving, cut_in)
        last.wait()

    return pl.pallas_call(
        kernel,
        out_shape=[
            jax.ShapeDtypeStruct(shape, jnp.bfloat16),
            jax.ShapeDtypeStruct((slots, given), jnp.bfloat16),
            jax.ShapeDtypeStruct((slots, given), jnp.bfloat16),
        ],
        in_specs=[pl.BlockSpec(memory_space=pltpu.SMEM)] * 2 + anywhere(items + 3),
        out_specs=anywhere(3),
        scratch_shapes=[
            pltpu.VMEM(shape, jnp.bfloat16),
            pltpu.VMEM(shape, jnp.bfloat16),
            pltpu.VMEM((slots, width), jnp.bfloat16),
            pltpu.VMEM((slots, width), jnp.bfloat16),
            pltpu.VMEM((slots, 3 * hid), jnp.bfloat16),
            pltpu.VMEM((2, slots, 2 * share), jnp.bfloat16),
            pltpu.VMEM(shape, jnp.bfloat16),
            pltpu.VMEM((width, hid), jnp.bfloat16),
            pltpu.VMEM((width, hid), jnp.bfloat16),
            pltpu.VMEM((tiles, tile, width), jnp.bfloat16),
            pltpu.SemaphoreType.DMA((items,)),
            pltpu.SemaphoreType.DMA((items,)),
            pltpu.SemaphoreType.DMA((tiles,)),
            pltpu.SemaphoreType.DMA((tiles,)),
            pltpu.SemaphoreType.DMA((tiles,)),
            pltpu.SemaphoreType.DMA((chunks + 1,)),
            pltpu.SemaphoreType.DMA((4,)),
        ],
        compiler_params=params(),
        cost_estimate=cost(50 * slots * width * hid, 4 * slots * width),
        name="back",
    )(me, part, *group, gate_proj, up_proj, down_proj)


def weight_grads(tile, share, part, known, groups, gate_proj, up_proj, down_proj):
    count, items = len(groups), len(groups[0])
    blocks = sum(item.shape[0] if item.ndim == 3 else 1 for item in groups[0])
    given = len(known)
    hid, width = down_proj.shape
    pieces, step = cut(width)
    slots = blocks * MOST
    total = (given + count) * slots
    tiles = hid // tile

    def kernel(part_ref, *refs):
        refs = list(refs)
        known_refs = [refs.pop(0) for _ in range(given)]
        group_refs = [[refs.pop(0) for _ in range(items)] for _ in range(count)]
        gate_ref, up_ref, down_ref = [refs.pop(0) for _ in range(3)]
        d_gate_ref, d_up_ref, d_down_ref = [refs.pop(0) for _ in range(3)]
        x_held, dy_held, x_all, dy_all = [refs.pop(0) for _ in range(4)]
        x_mine, dy_mine, factors = [refs.pop(0) for _ in range(3)]
        gate, up, down, x_in, dy_in, known_in, gate_in, up_in, down_in = refs[:9]
        made_gate, made_up, made_down, gate_out, up_out, down_out = refs[9:]
        columns = tile_of(part_ref[0], share)
        x_pairs, dy_pairs, known_pairs = [], [], []
        for at in range(count):
            x_pairs += halves(group_refs[at], 0, x_held.at[at])
            dy_pairs += halves(group_refs[at], 1, dy_held.at[at])
        for at in range(given):
            here = slice(at * slots, (at + 1) * slots)
            behind = 3 * hid
            known_pairs += [
                (known_refs[at].at[:, :behind], factors.at[here, :]),
                (known_refs[at].at[:, behind : behind + share], x_mine.at[here, :]),
                (known_refs[at].at[:, behind + share :], dy_mine.at[here, :]),
            ]

        def arrange(held, rows_out, target):
            for at in range(count):
                unpack(held.at[at], at * slots, rows_out)
            target[given * slots :, :] = rows_out[:, columns]

        def leave(source, target, gone, index, axis):
            here = tile_of(index, tile)
            view = target.at[:, here] if axis else target.at[here, :]
            return pltpu.make_async_copy(source.at[index], view, gone.at[index])

        def fetch_x(index):
            weight_copy(gate_ref, gate, gate_in, index, 1, tile).start()
            weight_copy(up_ref, up, up_in, index, 1, tile).start()

        def fetch_dy(index):
            weight_copy(down_ref, down, down_in, index, 0, tile).start()

        start(x_pairs, x_in)
        fetch_x(0)
        wait(x_pairs, x_in)
        start(dy_pairs, dy_in)
        fetch_dy(0)
        arrange(x_held, x_all, x_mine)
        for now in range(tiles):
            here = slice(now * tile, (now + 1) * tile)
            weight_copy(gate_ref, gate, gate_in, now, 1, tile).wait()
            pre_gate = dot(x_all[...], gate[now])
            weight_copy(up_ref, up, up_in, now, 1, tile).wait()
            pre_up = dot(x_all[...], up[now])
            if now == 0:
                wait(dy_pairs, dy_in)
                start(known_pairs, known_in)
                arrange(dy_held, dy_all, dy_mine)
            if now < tiles - 1:
                fetch_x(now + 1)
                fetch_dy(now + 1)
            weight_copy(down_ref, down, down_in, now, 0, tile).wait()
            d_hidden = dot(dy_all[...], down[now], BY_WIDTH)
            made, d_gate, d_up = hidden_grads(pre_gate, pre_up, d_hidden)
            if now == 0:
                wait(known_pairs, known_in)
            made = jnp.concatenate([factors[:, here], made], 0)
            d_gate = jnp.concatenate([factors[:, hid + here.start : hid + here.stop], d_gate], 0)
            d_up = jnp.concatenate(
                [factors[:, 2 * hid + here.start : 2 * hid + here.stop], d_up], 0
            )
            sums = dot(x_mine[...], jnp.concatenate([d_gate, d_up], 1), BY_ROWS)
            made_gate[now] = sums[:, :tile]
            made_up[now] = sums[:, tile:]
            leave(made_gate, d_gate_ref, gate_out, now, 1).start()
            leave(made_up, d_up_ref, up_out, now, 1).start()
            made_down[now] = dot(made, dy_mine[...], BY_ROWS)
            leave(made_down, d_down_ref, down_out, now, 0).start()
        for at in range(tiles):
            leave(made_gate, d_gate_ref, gate_out, at, 1).wait()
            leave(made_up, d_up_ref, up_out, at, 1).wait()
            leave(made_down, d_down_ref, down_out, at, 0).wait()

    held = pltpu.VMEM((count, blocks, ROWS, width + step), jnp.bfloat16)
    arranged = pltpu.VMEM((count * slots, width), jnp.bfloat16)
    mine = pltpu.VMEM((total, share), jnp.bfloat16)
    return pl.pallas_call(
        kernel,
        out_shape=[
            jax.ShapeDtypeStruct((share, hid), jnp.float32),
            jax.ShapeDtypeStruct((share, hid), jnp.float32),
            jax.ShapeDtypeStruct((hid, share), jnp.float32),
        ],
        in_specs=[pl.BlockSpec(memory_space=pltpu.SMEM)] + anywhere(given + count * items + 3),
        out_specs=anywhere(3),
        scratch_shapes=[
            held,
            held,
            arranged,
            arranged,
            mine,
            mine,
            pltpu.VMEM((given * slots, 3 * hid), jnp.bfloat16),
            pltpu.VMEM((tiles, width, tile), jnp.bfloat16),
            pltpu.VMEM((tiles, width, tile), jnp.bfloat16),
            pltpu.VMEM((tiles, tile, width), jnp.bfloat16),
            pltpu.SemaphoreType.DMA((count * items,)),
            pltpu.SemaphoreType.DMA((count * items,)),
            pltpu.SemaphoreType.DMA((3 * given,)),
            pltpu.SemaphoreType.DMA((tiles,)),
            pltpu.SemaphoreType.DMA((tiles,)),
            pltpu.SemaphoreType.DMA((tiles,)),
            pltpu.VMEM((tiles, share, tile), jnp.float32),
            pltpu.VMEM((tiles, share, tile), jnp.float32),
            pltpu.VMEM((tiles, tile, share), jnp.float32),
            pltpu.SemaphoreType.DMA((tiles,)),
            pltpu.SemaphoreType.DMA((tiles,)),
            pltpu.SemaphoreType.DMA((tiles,)),
        ],
        compiler_params=params(),
        cost_estimate=cost(0, 4 * slots * width),
        name="weight_grads",
    )(part, *known, *[item for group in groups for item in group], gate_proj, up_proj, down_proj)


def swap(value, axis, distance):
    size = lax.axis_size(axis)
    return lax.ppermute(value, axis, [(at, at ^ distance) for at in range(size)])


def exchange(blocks, groups=None):
    return lax.all_to_all(
        blocks, "expert", split_axis=0, concat_axis=0, tiled=True, axis_index_groups=groups
    )


def after(value, *earlier):
    return lax.optimization_barrier((value, *earlier))[0]


def gather_body(tokens, cotangent, routes, expert_gates, gate_proj, up_proj, down_proj):
    blocks = lax.axis_size("expert")
    tile, share = 256, tokens.shape[1] // lax.axis_size("dp")
    me = lax.axis_index("expert").astype(jnp.int32).reshape(1)
    part = lax.axis_index("dp").astype(jnp.int32).reshape(1)
    routes = routes.reshape(1, -1)
    gates = expert_gates.reshape(1, -1)
    weights = (gate_proj, up_proj, down_proj)
    first, *received = pack(blocks, me, routes, gates, tokens, cotangent)
    half = blocks // 2
    groups = [list(range(at, at + half)) for at in range(0, blocks, half)]
    first = exchange(first, groups)
    received = [swap(block, "expert", half + at) for at, block in enumerate(received)]
    far = swap(first, "dp", 2)
    work = 50 * blocks * MOST * gate_proj.size
    far_rest = swap(join(received, work), "dp", 2)
    sent, kept, handed = back(tile, share, me, part, [first, *received], *weights)
    last = swap(far, "dp", 1)
    sent, last = lax.optimization_barrier((sent, last))
    returned = exchange(sent)
    far = [far, after(far_rest, sent)]
    last = [last, swap(far[1], "dp", 1)]
    known = [kept, swap(handed, "dp", 1)]
    grads = weight_grads(tile, share, part, known, [far, last], *weights)
    return (merge(routes, after(returned, *grads)), *grads)


def body(tokens, cotangent, routes, expert_gates, gate_proj, up_proj, down_proj):
    groups, blocks = lax.axis_size("dp"), lax.axis_size("expert")
    width, hid = gate_proj.shape
    rows_sent = (groups - 1) * 2 * blocks * MOST * width
    grads_sent = 3 * width * hid * (groups - 1) // groups
    fits = blocks == EXPERTS and groups == 4 and hid % 256 == 0
    fits = fits and tokens.shape[0] == 128 and routes.shape[1] == 1 and width // groups % 128 == 0
    chosen = gather_body if fits and rows_sent < grads_sent else scatter_body
    return chosen(tokens, cotangent, routes, expert_gates, gate_proj, up_proj, down_proj)


def solution(mesh):
    in_specs = (
        P(("dp", "expert"), None),
        P(("dp", "expert"), None),
        P(("dp", "expert"), None),
        P(("dp", "expert"), None),
        P(None, "expert"),
        P(None, "expert"),
        P("expert", None),
    )
    out_specs = (P(("dp", "expert"), None), P("dp", "expert"), P("dp", "expert"), P("expert", "dp"))
    return jax.shard_map(body, mesh=mesh, in_specs=in_specs, out_specs=out_specs, check_vma=False)
```

```python
import jax
import jax.numpy as jnp
from jax import lax
from jax.experimental import pallas as pl
from jax.experimental.pallas import tpu as pltpu
from jax.sharding import PartitionSpec as P

EXPERTS = 8
MOST = 18
ROWS = 16
VMEM_BYTES = (63 * 1024 + 768) * 1024


def build_slots(routes, capacity):
    flat_routes = routes.reshape(-1)
    one_hot = (flat_routes[:, None] == jnp.arange(EXPERTS, dtype=jnp.int32)[None, :]).astype(
        jnp.int32
    )
    before = jnp.cumsum(one_hot, axis=0) - one_hot
    position = jnp.sum(before * one_hot, axis=1)
    return flat_routes * capacity + position


def scatter_body(tokens, cotangent, routes, expert_gates, gate_proj, up_proj, down_proj):
    tok_dev, model_dim = tokens.shape
    top_k = routes.shape[1]
    expert_devs = lax.axis_size("expert")
    group_size = expert_devs // EXPERTS
    capacity = MOST
    slot_total = EXPERTS * capacity
    slot_of = build_slots(routes, capacity)
    owners = jnp.arange(tok_dev * top_k, dtype=jnp.int32) // top_k
    slot_table = jnp.full((slot_total,), tok_dev, jnp.int32).at[slot_of].set(owners)
    slot_gate = jnp.zeros((slot_total,), jnp.float32).at[slot_of].set(expert_gates.reshape(-1))
    x_slots = jnp.take(tokens, slot_table, axis=0, mode="fill", fill_value=0)
    dy_slots = (
        jnp.take(cotangent, slot_table, axis=0, mode="fill", fill_value=0).astype(jnp.float32)
        * slot_gate[:, None]
    ).astype(jnp.bfloat16)

    def copies(values):
        spread = values.reshape(EXPERTS, 1, capacity, model_dim)
        return jnp.broadcast_to(spread, (EXPERTS, group_size, capacity, model_dim)).reshape(
            expert_devs, capacity, model_dim
        )

    x_recv, dy_recv = (
        lax.all_to_all(copies(x_slots), "expert", split_axis=0, concat_axis=0, tiled=True),
        lax.all_to_all(copies(dy_slots), "expert", split_axis=0, concat_axis=0, tiled=True),
    )
    in_rows = x_recv.reshape(expert_devs * capacity, model_dim)
    scaled = dy_recv.reshape(expert_devs * capacity, model_dim)
    pre_gate = jnp.dot(in_rows, gate_proj, preferred_element_type=jnp.float32)
    pre_up = jnp.dot(in_rows, up_proj, preferred_element_type=jnp.float32)
    gate_sig = jax.nn.sigmoid(pre_gate)
    hidden = (pre_gate * gate_sig * pre_up).astype(jnp.bfloat16)
    by_width = (((1,), (1,)), ((), ()))
    by_rows = (((0,), (0,)), ((), ()))
    d_hidden = lax.dot_general(scaled, down_proj, by_width, preferred_element_type=jnp.float32)
    d_gate = (d_hidden * pre_up * gate_sig * (1.0 + pre_gate * (1.0 - gate_sig))).astype(
        jnp.bfloat16
    )
    d_up = (d_hidden * pre_gate * gate_sig).astype(jnp.bfloat16)
    grad_down = lax.dot_general(hidden, scaled, by_rows, preferred_element_type=jnp.float32)
    grad_gate = lax.dot_general(in_rows, d_gate, by_rows, preferred_element_type=jnp.float32)
    grad_up = lax.dot_general(in_rows, d_up, by_rows, preferred_element_type=jnp.float32)
    grad_gate, grad_up, grad_down = (
        lax.psum_scatter(
            grad_gate.astype(jnp.bfloat16), "dp", scatter_dimension=0, tiled=True
        ).astype(jnp.float32),
        lax.psum_scatter(
            grad_up.astype(jnp.bfloat16), "dp", scatter_dimension=0, tiled=True
        ).astype(jnp.float32),
        lax.psum_scatter(
            grad_down.astype(jnp.bfloat16), "dp", scatter_dimension=1, tiled=True
        ).astype(jnp.float32),
    )
    joined_grads = jnp.concatenate([d_gate, d_up], 1)
    joined_proj = jnp.concatenate([gate_proj, up_proj], 1)
    partial_value = lax.dot_general(
        joined_grads, joined_proj, by_width, preferred_element_type=jnp.float32
    ).astype(jnp.bfloat16)
    returned = lax.all_to_all(
        partial_value.reshape(expert_devs, capacity, model_dim),
        "expert",
        split_axis=0,
        concat_axis=0,
        tiled=True,
    )
    summed = jnp.sum(
        returned.reshape(EXPERTS, group_size, capacity, model_dim).astype(jnp.float32), axis=1
    )
    summed = summed.reshape(slot_total, model_dim)
    grad_input = jnp.take(summed, slot_of, axis=0).reshape(tok_dev, top_k, model_dim).sum(axis=1)
    return (grad_input.astype(jnp.bfloat16), grad_gate, grad_up, grad_down)


BY_WIDTH = (((1,), (1,)), ((), ()))
BY_ROWS = (((0,), (0,)), ((), ()))


def cut(width):
    pieces = ROWS // (MOST - ROWS)
    return pieces, width // pieces


def width_of(packed):
    pieces = ROWS // (MOST - ROWS)
    return packed.shape[2] * pieces // (pieces + 1)


def cost(flops, moved):
    return pl.CostEstimate(flops=flops, bytes_accessed=moved, transcendentals=0)


def params():
    return pltpu.CompilerParams(vmem_limit_bytes=VMEM_BYTES)


def anywhere(count):
    return [pl.BlockSpec(memory_space=pl.ANY)] * count


def dot(left, right, dims=(((1,), (0,)), ((), ()))):
    return lax.dot_general(left, right, dims, preferred_element_type=jnp.float32)


def ones(mask):
    return jnp.where(mask, 1.0, 0.0).astype(jnp.bfloat16)


def start(pairs, arrived, first=0):
    for at, (source, target) in enumerate(pairs):
        if at >= first:
            pltpu.make_async_copy(source, target, arrived.at[at]).start()


def wait(pairs, arrived, first=0):
    for at, (source, target) in enumerate(pairs):
        if at >= first:
            pltpu.make_async_copy(source, target, arrived.at[at]).wait()


def slot_masks(routes, blocks, width, me=0):
    tokens = routes.shape[1]
    pieces, _ = cut(width)
    experts = lax.broadcasted_iota(jnp.int32, (EXPERTS, tokens), 0)
    named = jnp.where(experts == routes, 1.0, 0.0)
    earlier = lax.broadcasted_iota(jnp.int32, (tokens, tokens), 0) < lax.broadcasted_iota(
        jnp.int32, (tokens, tokens), 1
    )
    before = dot(named.astype(jnp.bfloat16), ones(earlier))
    position = jnp.sum(before * named, axis=0, keepdims=True).astype(jnp.int32)
    slot = lax.broadcasted_iota(jnp.int32, (blocks * ROWS, tokens), 0)
    row = slot % ROWS
    mine = (slot // ROWS) ^ me == routes
    main = mine & (position == row)
    spill = mine & (position == ROWS + row // pieces)
    return main, spill, row % pieces


def pack(blocks, me, routes, gates, tokens, cotangent):
    count, width = tokens.shape
    pieces, step = cut(width)
    sources = (routes, gates, tokens, cotangent)
    block_shape = (2 * ROWS, width + step)

    def kernel(me_ref, *refs):
        outs, held = refs[4 : 4 + blocks], refs[4 + blocks : 8 + blocks]
        staged, arrived, gone = refs[8 + blocks :]
        pairs = list(zip(refs[:4], held))
        start(pairs, arrived)
        wait(pairs[:2], arrived)
        main, spill, piece = slot_masks(held[0][...], blocks, width, me_ref[0])
        mains = ones(main)
        picks = jnp.concatenate([ones(spill & (piece == at)) for at in range(pieces)], 1)
        main_scale = jnp.sum(jnp.where(main, held[1][...], 0.0), axis=1, keepdims=True)
        spill_scale = jnp.sum(jnp.where(spill, held[1][...], 0.0), axis=1, keepdims=True)
        leaving = []
        for half in range(2):
            wait(pairs[: 3 + half], arrived, 2 + half)
            values = held[2 + half]
            rows = dot(mains, values[...])
            cuts = [values[:, at * step : (at + 1) * step] for at in range(pieces)]
            extra = dot(picks, jnp.concatenate(cuts, 0))
            if half > 0:
                rows, extra = rows * main_scale, extra * spill_scale
            rows = rows.astype(jnp.bfloat16)
            extra = extra.astype(jnp.bfloat16)
            here = slice(half * ROWS, (half + 1) * ROWS)
            for block in range(blocks):
                part = slice(block * ROWS, (block + 1) * ROWS)
                staged[block, here, :width] = rows[part]
                staged[block, here, width:] = extra[part]
            sent = [(staged.at[at, here], outs[at].at[here, :]) for at in range(blocks)]
            leaving += sent
            start(leaving, gone, half * blocks)
        wait(leaving, gone)

    return pl.pallas_call(
        kernel,
        out_shape=[jax.ShapeDtypeStruct(block_shape, jnp.bfloat16)] * blocks,
        in_specs=[pl.BlockSpec(memory_space=pltpu.SMEM)] + anywhere(4),
        out_specs=anywhere(blocks),
        scratch_shapes=[pltpu.VMEM(source.shape, source.dtype) for source in sources]
        + [
            pltpu.VMEM((blocks,) + block_shape, jnp.bfloat16),
            pltpu.SemaphoreType.DMA((4,)),
            pltpu.SemaphoreType.DMA((2 * blocks,)),
        ],
        compiler_params=params(),
        cost_estimate=cost(8 * blocks * ROWS * count * width, 8 * count * width),
        name="pack",
    )(me, *sources)


def join(received, flops=0):
    count = len(received)
    shape = (count,) + received[0].shape

    def kernel(*refs):
        out, held, arrived, gone = refs[count:]
        pairs = [(refs[at], held.at[at]) for at in range(count)]
        leaving = [(held.at[at], out.at[at]) for at in range(count)]
        start(pairs, arrived)
        for at in range(count):
            wait(pairs[: at + 1], arrived, at)
            start(leaving[: at + 1], gone, at)
        wait(leaving, gone)

    return pl.pallas_call(
        kernel,
        out_shape=jax.ShapeDtypeStruct(shape, jnp.bfloat16),
        in_specs=anywhere(count),
        out_specs=pl.BlockSpec(memory_space=pl.ANY),
        scratch_shapes=[
            pltpu.VMEM(shape, jnp.bfloat16),
            pltpu.SemaphoreType.DMA((count,)),
            pltpu.SemaphoreType.DMA((count,)),
        ],
        compiler_params=params(),
        cost_estimate=cost(flops, 4 * received[0].size * count),
        name="join",
    )(*received)


def merge(routes, returned):
    blocks = returned.shape[0]
    tokens = routes.shape[1]
    width = width_of(returned)
    pieces, step = cut(width)

    def kernel(routes_ref, back_ref, out, named, held, arrived):
        pairs = [(routes_ref, named), (back_ref, held)]
        start(pairs, arrived)
        wait(pairs[:1], arrived)
        main, spill, piece = slot_masks(named[...], blocks, width)
        mains = ones(main)
        picks = [ones(spill & (piece == at)) for at in range(pieces)]
        wait(pairs, arrived, 1)
        rows = jnp.concatenate([held[at, :, :width] for at in range(blocks)], 0)
        extra = jnp.concatenate([held[at, :, width:] for at in range(blocks)], 0)
        picked = dot(mains, rows, BY_ROWS)
        for at in range(pieces):
            columns = slice(at * step, (at + 1) * step)
            out[:, columns] = (picked[:, columns] + dot(picks[at], extra, BY_ROWS)).astype(
                jnp.bfloat16
            )

    return pl.pallas_call(
        kernel,
        out_shape=jax.ShapeDtypeStruct((tokens, width), jnp.bfloat16),
        in_specs=anywhere(2),
        out_specs=pl.BlockSpec(memory_space=pltpu.VMEM),
        scratch_shapes=[
            pltpu.VMEM(routes.shape, routes.dtype),
            pltpu.VMEM(returned.shape, returned.dtype),
            pltpu.SemaphoreType.DMA((2,)),
        ],
        compiler_params=params(),
        cost_estimate=cost(4 * blocks * ROWS * tokens * width, 4 * tokens * width),
        name="merge",
    )(routes, returned)


def spill_picks(blocks, pieces):
    extras = blocks * (MOST - ROWS)
    shape = (pieces * extras, blocks * ROWS)
    index = lax.broadcasted_iota(jnp.int32, shape, 0)
    row = lax.broadcasted_iota(jnp.int32, shape, 1)
    return ones(row == (index % extras) * pieces + index // extras)


def unpack(packed, first, out):
    blocks, width = packed.shape[0], out.shape[1]
    pieces, step = cut(width)
    extras = blocks * (MOST - ROWS)
    for at in range(blocks):
        out[first + at * ROWS : first + (at + 1) * ROWS, :] = packed[at, :, :width]
    tails = jnp.concatenate([packed[at, :, width:] for at in range(blocks)], 0)
    placed = dot(spill_picks(blocks, pieces), tails).astype(jnp.bfloat16)
    spill = slice(first + blocks * ROWS, first + blocks * MOST)
    for at in range(pieces):
        out[spill, at * step : (at + 1) * step] = placed[at * extras : (at + 1) * extras]


def tile_of(index, tile):
    return pl.ds(pl.multiple_of(index * tile, tile), tile)


def weight_copy(source, target, arrived, index, axis, tile):
    here = tile_of(index, tile)
    view = source.at[:, here] if axis else source.at[here, :]
    return pltpu.make_async_copy(view, target.at[index], arrived.at[index])


def halves(group, half, out):
    here = slice(half * ROWS, (half + 1) * ROWS)
    pairs, at = [], 0
    for item in group:
        if len(item.shape) == 2:
            pairs.append((item.at[here, :], out.at[at]))
            at += 1
        else:
            pairs.append((item.at[:, here, :], out.at[at : at + item.shape[0]]))
            at += item.shape[0]
    return pairs


def hidden_grads(pre_gate, pre_up, d_hidden):
    sig = 0.5 * jnp.tanh(0.5 * pre_gate) + 0.5
    silu = pre_gate * sig
    hidden = (silu * pre_up).astype(jnp.bfloat16)
    d_gate = (d_hidden * pre_up * (sig + silu * (1.0 - sig))).astype(jnp.bfloat16)
    d_up = (d_hidden * silu).astype(jnp.bfloat16)
    return hidden, d_gate, d_up


def back(tile, share, me, part, order, group, gate_proj, up_proj, down_proj):
    blocks = len(group)
    width, hid = gate_proj.shape
    slots = blocks * MOST
    pieces, step = cut(width)
    tiles = hid // tile
    chunk = 2 * step
    chunks = width // chunk
    shape = (blocks, ROWS, width + step)
    given = 3 * hid + 2 * share

    def kernel(me_ref, part_ref, *refs):
        refs = list(refs)
        group_refs = [refs.pop(0) for _ in range(blocks)]
        gate_ref, up_ref, down_ref, out, kept, handed = [refs.pop(0) for _ in range(6)]
        x_held, dy_held, rows, scaled, factors, cuts = [refs.pop(0) for _ in range(6)]
        staged, gate, up, down = [refs.pop(0) for _ in range(4)]
        x_in, dy_in, gate_in, up_in, down_in, gone, cut_in = refs
        x_pairs, dy_pairs = halves(group_refs, 0, x_held), halves(group_refs, 1, dy_held)

        def column_copy(source, target, arrived, index):
            here = slice(index * tile, (index + 1) * tile)
            return pltpu.make_async_copy(
                source.at[:, here], target.at[:, here], arrived.at[index]
            )

        def fetch_x(index):
            column_copy(gate_ref, gate, gate_in, index).start()
            column_copy(up_ref, up, up_in, index).start()

        def fetch_dy(index):
            weight_copy(down_ref, down, down_in, index, 0, tile).start()

        def leave(index):
            columns = slice(index * chunk, (index + 1) * chunk)
            return pltpu.make_async_copy(
                staged.at[:, :, columns], out.at[:, :, columns], gone.at[index]
            )

        first, behind = slice(0, 3 * hid), slice(3 * hid, given)
        leaving = [(factors, kept.at[:, first]), (cuts.at[0], kept.at[:, behind])]
        leaving += [(factors, handed.at[:, first]), (cuts.at[1], handed.at[:, behind])]

        start(x_pairs, x_in)
        fetch_x(0)
        wait(x_pairs, x_in)
        start(dy_pairs, dy_in)
        fetch_dy(0)
        unpack(x_held, 0, rows)
        for now in range(tiles):
            columns = slice(now * tile, (now + 1) * tile)
            column_copy(gate_ref, gate, gate_in, now).wait()
            pre_gate = dot(rows[...], gate[:, columns])
            if now < tiles - 1:
                fetch_x(now + 1)
            column_copy(up_ref, up, up_in, now).wait()
            pre_up = dot(rows[...], up[:, columns])
            if now == 0:
                wait(dy_pairs, dy_in)
                unpack(dy_held, 0, scaled)
            if now < tiles - 1:
                fetch_dy(now + 1)
            weight_copy(down_ref, down, down_in, now, 0, tile).wait()
            d_hidden = dot(scaled[...], down[now], BY_WIDTH)
            made, d_gate, d_up = hidden_grads(pre_gate, pre_up, d_hidden)
            factors[:, columns] = made
            factors[:, hid + now * tile : hid + (now + 1) * tile] = d_gate
            factors[:, 2 * hid + now * tile : 2 * hid + (now + 1) * tile] = d_up

        for at in range(2):
            columns = tile_of(part_ref[0] ^ at, share)
            cuts[at, :, :share] = rows[:, columns]
            cuts[at, :, share:] = scaled[:, columns]
        start(leaving, cut_in)
        extras = []
        for at in range(chunks):
            here = slice(at * chunk, (at + 1) * chunk)
            done = dot(factors[:, hid : 2 * hid], gate[here, :], BY_WIDTH)
            done += dot(factors[:, 2 * hid :], up[here, :], BY_WIDTH)
            done = done.astype(jnp.bfloat16)
            for block in range(blocks):
                staged[me_ref[0] ^ order[block], :, here] = done[block * ROWS : (block + 1) * ROWS]
            leave(at).start()
            extras += [done[blocks * ROWS :, :step], done[blocks * ROWS :, step:]]
        tail = dot(spill_picks(blocks, pieces), jnp.concatenate(extras, 0), BY_ROWS)
        tail = tail.astype(jnp.bfloat16)
        for block in range(blocks):
            staged[me_ref[0] ^ order[block], :, width:] = tail[block * ROWS : (block + 1) * ROWS]
        last = pltpu.make_async_copy(
            staged.at[:, :, width:], out.at[:, :, width:], gone.at[chunks]
        )
        last.start()
        for at in range(chunks):
            leave(at).wait()
        wait(leaving, cut_in)
        last.wait()

    return pl.pallas_call(
        kernel,
        out_shape=[
            jax.ShapeDtypeStruct(shape, jnp.bfloat16),
            jax.ShapeDtypeStruct((slots, given), jnp.bfloat16),
            jax.ShapeDtypeStruct((slots, given), jnp.bfloat16),
        ],
        in_specs=[pl.BlockSpec(memory_space=pltpu.SMEM)] * 2 + anywhere(blocks + 3),
        out_specs=anywhere(3),
        scratch_shapes=[
            pltpu.VMEM(shape, jnp.bfloat16),
            pltpu.VMEM(shape, jnp.bfloat16),
            pltpu.VMEM((slots, width), jnp.bfloat16),
            pltpu.VMEM((slots, width), jnp.bfloat16),
            pltpu.VMEM((slots, 3 * hid), jnp.bfloat16),
            pltpu.VMEM((2, slots, 2 * share), jnp.bfloat16),
            pltpu.VMEM(shape, jnp.bfloat16),
            pltpu.VMEM((width, hid), jnp.bfloat16),
            pltpu.VMEM((width, hid), jnp.bfloat16),
            pltpu.VMEM((tiles, tile, width), jnp.bfloat16),
            pltpu.SemaphoreType.DMA((blocks,)),
            pltpu.SemaphoreType.DMA((blocks,)),
            pltpu.SemaphoreType.DMA((tiles,)),
            pltpu.SemaphoreType.DMA((tiles,)),
            pltpu.SemaphoreType.DMA((tiles,)),
            pltpu.SemaphoreType.DMA((chunks + 1,)),
            pltpu.SemaphoreType.DMA((4,)),
        ],
        compiler_params=params(),
        cost_estimate=cost(50 * slots * width * hid, 4 * slots * width),
        name="back",
    )(me, part, *group, gate_proj, up_proj, down_proj)


def weight_grads(tile, share, part, known, groups, gate_proj, up_proj, down_proj):
    count, items = len(groups), len(groups[0])
    blocks = sum(item.shape[0] if item.ndim == 3 else 1 for item in groups[0])
    given = len(known)
    hid, width = down_proj.shape
    pieces, step = cut(width)
    slots = blocks * MOST
    total = (given + count) * slots
    tiles = hid // tile

    def kernel(part_ref, *refs):
        refs = list(refs)
        known_refs = [refs.pop(0) for _ in range(given)]
        group_refs = [[refs.pop(0) for _ in range(items)] for _ in range(count)]
        gate_ref, up_ref, down_ref = [refs.pop(0) for _ in range(3)]
        d_gate_ref, d_up_ref, d_down_ref = [refs.pop(0) for _ in range(3)]
        x_held, dy_held, x_all, dy_all = [refs.pop(0) for _ in range(4)]
        x_mine, dy_mine, factors = [refs.pop(0) for _ in range(3)]
        gate, up, down, x_in, dy_in, known_in, gate_in, up_in, down_in = refs[:9]
        made_gate, made_up, made_down, gate_out, up_out, down_out = refs[9:]
        columns = tile_of(part_ref[0], share)
        x_pairs, dy_pairs, known_pairs = [], [], []
        for at in range(count):
            x_pairs += halves(group_refs[at], 0, x_held.at[at])
            dy_pairs += halves(group_refs[at], 1, dy_held.at[at])
        for at in range(given):
            here = slice(at * slots, (at + 1) * slots)
            behind = 3 * hid
            known_pairs += [
                (known_refs[at].at[:, :behind], factors.at[here, :]),
                (known_refs[at].at[:, behind : behind + share], x_mine.at[here, :]),
                (known_refs[at].at[:, behind + share :], dy_mine.at[here, :]),
            ]

        def arrange(held, rows_out, target):
            for at in range(count):
                unpack(held.at[at], at * slots, rows_out)
            target[given * slots :, :] = rows_out[:, columns]

        def leave(source, target, gone, index, axis):
            here = tile_of(index, tile)
            view = target.at[:, here] if axis else target.at[here, :]
            return pltpu.make_async_copy(source.at[index], view, gone.at[index])

        def fetch_x(index):
            weight_copy(gate_ref, gate, gate_in, index, 1, tile).start()
            weight_copy(up_ref, up, up_in, index, 1, tile).start()

        def fetch_dy(index):
            weight_copy(down_ref, down, down_in, index, 0, tile).start()

        start(x_pairs, x_in)
        fetch_x(0)
        wait(x_pairs, x_in)
        start(dy_pairs, dy_in)
        fetch_dy(0)
        arrange(x_held, x_all, x_mine)
        for now in range(tiles):
            here = slice(now * tile, (now + 1) * tile)
            weight_copy(gate_ref, gate, gate_in, now, 1, tile).wait()
            pre_gate = dot(x_all[...], gate[now])
            weight_copy(up_ref, up, up_in, now, 1, tile).wait()
            pre_up = dot(x_all[...], up[now])
            if now == 0:
                wait(dy_pairs, dy_in)
                start(known_pairs, known_in)
                arrange(dy_held, dy_all, dy_mine)
            if now < tiles - 1:
                fetch_x(now + 1)
                fetch_dy(now + 1)
            weight_copy(down_ref, down, down_in, now, 0, tile).wait()
            d_hidden = dot(dy_all[...], down[now], BY_WIDTH)
            made, d_gate, d_up = hidden_grads(pre_gate, pre_up, d_hidden)
            if now == 0:
                wait(known_pairs, known_in)
            made = jnp.concatenate([factors[:, here], made], 0)
            d_gate = jnp.concatenate([factors[:, hid + here.start : hid + here.stop], d_gate], 0)
            d_up = jnp.concatenate(
                [factors[:, 2 * hid + here.start : 2 * hid + here.stop], d_up], 0
            )
            sums = dot(x_mine[...], jnp.concatenate([d_gate, d_up], 1), BY_ROWS)
            made_gate[now] = sums[:, :tile]
            made_up[now] = sums[:, tile:]
            leave(made_gate, d_gate_ref, gate_out, now, 1).start()
            leave(made_up, d_up_ref, up_out, now, 1).start()
            made_down[now] = dot(made, dy_mine[...], BY_ROWS)
            leave(made_down, d_down_ref, down_out, now, 0).start()
        for at in range(tiles):
            leave(made_gate, d_gate_ref, gate_out, at, 1).wait()
            leave(made_up, d_up_ref, up_out, at, 1).wait()
            leave(made_down, d_down_ref, down_out, at, 0).wait()

    held = pltpu.VMEM((count, blocks, ROWS, width + step), jnp.bfloat16)
    arranged = pltpu.VMEM((count * slots, width), jnp.bfloat16)
    mine = pltpu.VMEM((total, share), jnp.bfloat16)
    return pl.pallas_call(
        kernel,
        out_shape=[
            jax.ShapeDtypeStruct((share, hid), jnp.float32),
            jax.ShapeDtypeStruct((share, hid), jnp.float32),
            jax.ShapeDtypeStruct((hid, share), jnp.float32),
        ],
        in_specs=[pl.BlockSpec(memory_space=pltpu.SMEM)] + anywhere(given + count * items + 3),
        out_specs=anywhere(3),
        scratch_shapes=[
            held,
            held,
            arranged,
            arranged,
            mine,
            mine,
            pltpu.VMEM((given * slots, 3 * hid), jnp.bfloat16),
            pltpu.VMEM((tiles, width, tile), jnp.bfloat16),
            pltpu.VMEM((tiles, width, tile), jnp.bfloat16),
            pltpu.VMEM((tiles, tile, width), jnp.bfloat16),
            pltpu.SemaphoreType.DMA((count * items,)),
            pltpu.SemaphoreType.DMA((count * items,)),
            pltpu.SemaphoreType.DMA((3 * given,)),
            pltpu.SemaphoreType.DMA((tiles,)),
            pltpu.SemaphoreType.DMA((tiles,)),
            pltpu.SemaphoreType.DMA((tiles,)),
            pltpu.VMEM((tiles, share, tile), jnp.float32),
            pltpu.VMEM((tiles, share, tile), jnp.float32),
            pltpu.VMEM((tiles, tile, share), jnp.float32),
            pltpu.SemaphoreType.DMA((tiles,)),
            pltpu.SemaphoreType.DMA((tiles,)),
            pltpu.SemaphoreType.DMA((tiles,)),
        ],
        compiler_params=params(),
        cost_estimate=cost(0, 4 * slots * width),
        name="weight_grads",
    )(part, *known, *[item for group in groups for item in group], gate_proj, up_proj, down_proj)


def swap(value, axis, distance):
    size = lax.axis_size(axis)
    return lax.ppermute(value, axis, [(at, at ^ distance) for at in range(size)])


def exchange(blocks):
    return lax.all_to_all(blocks, "expert", split_axis=0, concat_axis=0, tiled=True)


def after(value, *earlier):
    return lax.optimization_barrier((value, *earlier))[0]


def gather_body(tokens, cotangent, routes, expert_gates, gate_proj, up_proj, down_proj):
    blocks = lax.axis_size("expert")
    tile, share = 256, tokens.shape[1] // lax.axis_size("dp")
    me = lax.axis_index("expert").astype(jnp.int32).reshape(1)
    part = lax.axis_index("dp").astype(jnp.int32).reshape(1)
    routes = routes.reshape(1, -1)
    gates = expert_gates.reshape(1, -1)
    weights = (gate_proj, up_proj, down_proj)
    received = list(pack(blocks, me, routes, gates, tokens, cotangent))
    for distance in reversed(range(1, blocks)):
        received[distance] = swap(received[distance], "expert", distance)
    order = [0, 1, 2, 6, 7, 4, 5, 3]
    early = 3
    received = [received[index] for index in order]
    far = swap(join(received[:early]), "dp", 2)
    work = 50 * blocks * MOST * gate_proj.size
    far_rest = swap(join(received[early:], work), "dp", 2)
    sent, kept, handed = back(tile, share, me, part, order, received, *weights)
    last = swap(far, "dp", 1)
    sent, last = lax.optimization_barrier((sent, last))
    returned = exchange(sent)
    far = [far, after(far_rest, sent)]
    last = [last, swap(far[1], "dp", 1)]
    known = [kept, swap(handed, "dp", 1)]
    grads = weight_grads(tile, share, part, known, [far, last], *weights)
    return (merge(routes, after(returned, *grads)), *grads)


def body(tokens, cotangent, routes, expert_gates, gate_proj, up_proj, down_proj):
    groups, blocks = lax.axis_size("dp"), lax.axis_size("expert")
    width, hid = gate_proj.shape
    rows_sent = (groups - 1) * 2 * blocks * MOST * width
    grads_sent = 3 * width * hid * (groups - 1) // groups
    fits = blocks == EXPERTS and groups == 4 and hid % 256 == 0
    fits = fits and tokens.shape[0] == 128 and routes.shape[1] == 1 and width // groups % 128 == 0
    chosen = gather_body if fits and rows_sent < grads_sent else scatter_body
    return chosen(tokens, cotangent, routes, expert_gates, gate_proj, up_proj, down_proj)


def solution(mesh):
    in_specs = (
        P(("dp", "expert"), None),
        P(("dp", "expert"), None),
        P(("dp", "expert"), None),
        P(("dp", "expert"), None),
        P(None, "expert"),
        P(None, "expert"),
        P("expert", None),
    )
    out_specs = (P(("dp", "expert"), None), P("dp", "expert"), P("dp", "expert"), P("expert", "dp"))
    return jax.shard_map(body, mesh=mesh, in_specs=in_specs, out_specs=out_specs, check_vma=False)
```

```python
import jax
import jax.numpy as jnp
from jax import lax
from jax.experimental import pallas as pl
from jax.experimental.pallas import tpu as pltpu
from jax.sharding import PartitionSpec as P

EXPERTS = 8
MOST = 18
ROWS = 16
VMEM_BYTES = (63 * 1024 + 768) * 1024


def build_slots(routes, capacity):
    flat_routes = routes.reshape(-1)
    one_hot = (flat_routes[:, None] == jnp.arange(EXPERTS, dtype=jnp.int32)[None, :]).astype(
        jnp.int32
    )
    before = jnp.cumsum(one_hot, axis=0) - one_hot
    position = jnp.sum(before * one_hot, axis=1)
    return flat_routes * capacity + position


def scatter_body(tokens, cotangent, routes, expert_gates, gate_proj, up_proj, down_proj):
    tok_dev, model_dim = tokens.shape
    top_k = routes.shape[1]
    expert_devs = lax.axis_size("expert")
    group_size = expert_devs // EXPERTS
    capacity = MOST
    slot_total = EXPERTS * capacity
    slot_of = build_slots(routes, capacity)
    owners = jnp.arange(tok_dev * top_k, dtype=jnp.int32) // top_k
    slot_table = jnp.full((slot_total,), tok_dev, jnp.int32).at[slot_of].set(owners)
    slot_gate = jnp.zeros((slot_total,), jnp.float32).at[slot_of].set(expert_gates.reshape(-1))
    x_slots = jnp.take(tokens, slot_table, axis=0, mode="fill", fill_value=0)
    dy_slots = (
        jnp.take(cotangent, slot_table, axis=0, mode="fill", fill_value=0).astype(jnp.float32)
        * slot_gate[:, None]
    ).astype(jnp.bfloat16)

    def copies(values):
        spread = values.reshape(EXPERTS, 1, capacity, model_dim)
        return jnp.broadcast_to(spread, (EXPERTS, group_size, capacity, model_dim)).reshape(
            expert_devs, capacity, model_dim
        )

    x_recv, dy_recv = (
        lax.all_to_all(copies(x_slots), "expert", split_axis=0, concat_axis=0, tiled=True),
        lax.all_to_all(copies(dy_slots), "expert", split_axis=0, concat_axis=0, tiled=True),
    )
    in_rows = x_recv.reshape(expert_devs * capacity, model_dim)
    scaled = dy_recv.reshape(expert_devs * capacity, model_dim)
    pre_gate = jnp.dot(in_rows, gate_proj, preferred_element_type=jnp.float32)
    pre_up = jnp.dot(in_rows, up_proj, preferred_element_type=jnp.float32)
    gate_sig = jax.nn.sigmoid(pre_gate)
    hidden = (pre_gate * gate_sig * pre_up).astype(jnp.bfloat16)
    by_width = (((1,), (1,)), ((), ()))
    by_rows = (((0,), (0,)), ((), ()))
    d_hidden = lax.dot_general(scaled, down_proj, by_width, preferred_element_type=jnp.float32)
    d_gate = (d_hidden * pre_up * gate_sig * (1.0 + pre_gate * (1.0 - gate_sig))).astype(
        jnp.bfloat16
    )
    d_up = (d_hidden * pre_gate * gate_sig).astype(jnp.bfloat16)
    grad_down = lax.dot_general(hidden, scaled, by_rows, preferred_element_type=jnp.float32)
    grad_gate = lax.dot_general(in_rows, d_gate, by_rows, preferred_element_type=jnp.float32)
    grad_up = lax.dot_general(in_rows, d_up, by_rows, preferred_element_type=jnp.float32)
    grad_gate, grad_up, grad_down = (
        lax.psum_scatter(
            grad_gate.astype(jnp.bfloat16), "dp", scatter_dimension=0, tiled=True
        ).astype(jnp.float32),
        lax.psum_scatter(
            grad_up.astype(jnp.bfloat16), "dp", scatter_dimension=0, tiled=True
        ).astype(jnp.float32),
        lax.psum_scatter(
            grad_down.astype(jnp.bfloat16), "dp", scatter_dimension=1, tiled=True
        ).astype(jnp.float32),
    )
    joined_grads = jnp.concatenate([d_gate, d_up], 1)
    joined_proj = jnp.concatenate([gate_proj, up_proj], 1)
    partial_value = lax.dot_general(
        joined_grads, joined_proj, by_width, preferred_element_type=jnp.float32
    ).astype(jnp.bfloat16)
    returned = lax.all_to_all(
        partial_value.reshape(expert_devs, capacity, model_dim),
        "expert",
        split_axis=0,
        concat_axis=0,
        tiled=True,
    )
    summed = jnp.sum(
        returned.reshape(EXPERTS, group_size, capacity, model_dim).astype(jnp.float32), axis=1
    )
    summed = summed.reshape(slot_total, model_dim)
    grad_input = jnp.take(summed, slot_of, axis=0).reshape(tok_dev, top_k, model_dim).sum(axis=1)
    return (grad_input.astype(jnp.bfloat16), grad_gate, grad_up, grad_down)


BY_WIDTH = (((1,), (1,)), ((), ()))
BY_ROWS = (((0,), (0,)), ((), ()))


def cut(width):
    pieces = ROWS // (MOST - ROWS)
    return pieces, width // pieces


def width_of(packed):
    pieces = ROWS // (MOST - ROWS)
    return packed.shape[2] * pieces // (pieces + 1)


def cost(flops, moved):
    return pl.CostEstimate(flops=flops, bytes_accessed=moved, transcendentals=0)


def params():
    return pltpu.CompilerParams(vmem_limit_bytes=VMEM_BYTES)


def anywhere(count):
    return [pl.BlockSpec(memory_space=pl.ANY)] * count


def dot(left, right, dims=(((1,), (0,)), ((), ()))):
    return lax.dot_general(left, right, dims, preferred_element_type=jnp.float32)


def ones(mask):
    return jnp.where(mask, 1.0, 0.0).astype(jnp.bfloat16)


def start(pairs, arrived, first=0):
    for at, (source, target) in enumerate(pairs):
        if at >= first:
            pltpu.make_async_copy(source, target, arrived.at[at]).start()


def wait(pairs, arrived, first=0):
    for at, (source, target) in enumerate(pairs):
        if at >= first:
            pltpu.make_async_copy(source, target, arrived.at[at]).wait()


def slot_masks(routes, blocks, width, me=0):
    tokens = routes.shape[1]
    pieces, _ = cut(width)
    experts = lax.broadcasted_iota(jnp.int32, (EXPERTS, tokens), 0)
    named = jnp.where(experts == routes, 1.0, 0.0)
    earlier = lax.broadcasted_iota(jnp.int32, (tokens, tokens), 0) < lax.broadcasted_iota(
        jnp.int32, (tokens, tokens), 1
    )
    before = dot(named.astype(jnp.bfloat16), ones(earlier))
    position = jnp.sum(before * named, axis=0, keepdims=True).astype(jnp.int32)
    slot = lax.broadcasted_iota(jnp.int32, (blocks * ROWS, tokens), 0)
    row = slot % ROWS
    mine = (slot // ROWS) ^ me == routes
    main = mine & (position == row)
    spill = mine & (position == ROWS + row // pieces)
    return main, spill, row % pieces


def pack(blocks, me, routes, gates, tokens, cotangent):
    count, width = tokens.shape
    pieces, step = cut(width)
    sources = (routes, gates, tokens, cotangent)
    block_shape = (2 * ROWS, width + step)

    def kernel(me_ref, *refs):
        outs, held = refs[4 : 4 + blocks], refs[4 + blocks : 8 + blocks]
        staged, arrived, gone = refs[8 + blocks :]
        pairs = list(zip(refs[:4], held))
        start(pairs, arrived)
        wait(pairs[:2], arrived)
        main, spill, piece = slot_masks(held[0][...], blocks, width, me_ref[0])
        mains = ones(main)
        picks = jnp.concatenate([ones(spill & (piece == at)) for at in range(pieces)], 1)
        main_scale = jnp.sum(jnp.where(main, held[1][...], 0.0), axis=1, keepdims=True)
        spill_scale = jnp.sum(jnp.where(spill, held[1][...], 0.0), axis=1, keepdims=True)
        leaving = []
        for half in range(2):
            wait(pairs[: 3 + half], arrived, 2 + half)
            values = held[2 + half]
            rows = dot(mains, values[...])
            cuts = [values[:, at * step : (at + 1) * step] for at in range(pieces)]
            extra = dot(picks, jnp.concatenate(cuts, 0))
            if half > 0:
                rows, extra = rows * main_scale, extra * spill_scale
            rows = rows.astype(jnp.bfloat16)
            extra = extra.astype(jnp.bfloat16)
            here = slice(half * ROWS, (half + 1) * ROWS)
            for block in range(blocks):
                part = slice(block * ROWS, (block + 1) * ROWS)
                staged[block, here, :width] = rows[part]
                staged[block, here, width:] = extra[part]
            sent = [(staged.at[at, here], outs[at].at[here, :]) for at in range(blocks)]
            leaving += sent
            start(leaving, gone, half * blocks)
        wait(leaving, gone)

    return pl.pallas_call(
        kernel,
        out_shape=[jax.ShapeDtypeStruct(block_shape, jnp.bfloat16)] * blocks,
        in_specs=[pl.BlockSpec(memory_space=pltpu.SMEM)] + anywhere(4),
        out_specs=anywhere(blocks),
        scratch_shapes=[pltpu.VMEM(source.shape, source.dtype) for source in sources]
        + [
            pltpu.VMEM((blocks,) + block_shape, jnp.bfloat16),
            pltpu.SemaphoreType.DMA((4,)),
            pltpu.SemaphoreType.DMA((2 * blocks,)),
        ],
        compiler_params=params(),
        cost_estimate=cost(8 * blocks * ROWS * count * width, 8 * count * width),
        name="pack",
    )(me, *sources)


def join(received, flops=0):
    count = len(received)
    shape = (count,) + received[0].shape

    def kernel(*refs):
        out, held, arrived, gone = refs[count:]
        pairs = [(refs[at], held.at[at]) for at in range(count)]
        leaving = [(held.at[at], out.at[at]) for at in range(count)]
        start(pairs, arrived)
        for at in range(count):
            wait(pairs[: at + 1], arrived, at)
            start(leaving[: at + 1], gone, at)
        wait(leaving, gone)

    return pl.pallas_call(
        kernel,
        out_shape=jax.ShapeDtypeStruct(shape, jnp.bfloat16),
        in_specs=anywhere(count),
        out_specs=pl.BlockSpec(memory_space=pl.ANY),
        scratch_shapes=[
            pltpu.VMEM(shape, jnp.bfloat16),
            pltpu.SemaphoreType.DMA((count,)),
            pltpu.SemaphoreType.DMA((count,)),
        ],
        compiler_params=params(),
        cost_estimate=cost(flops, 4 * received[0].size * count),
        name="join",
    )(*received)


def merge(routes, returned):
    blocks = returned.shape[0]
    tokens = routes.shape[1]
    width = width_of(returned)
    pieces, step = cut(width)

    def kernel(routes_ref, back_ref, out, named, held, arrived):
        pairs = [(routes_ref, named), (back_ref, held)]
        start(pairs, arrived)
        wait(pairs[:1], arrived)
        main, spill, piece = slot_masks(named[...], blocks, width)
        mains = ones(main)
        picks = [ones(spill & (piece == at)) for at in range(pieces)]
        wait(pairs, arrived, 1)
        rows = jnp.concatenate([held[at, :, :width] for at in range(blocks)], 0)
        extra = jnp.concatenate([held[at, :, width:] for at in range(blocks)], 0)
        picked = dot(mains, rows, BY_ROWS)
        for at in range(pieces):
            columns = slice(at * step, (at + 1) * step)
            out[:, columns] = (picked[:, columns] + dot(picks[at], extra, BY_ROWS)).astype(
                jnp.bfloat16
            )

    return pl.pallas_call(
        kernel,
        out_shape=jax.ShapeDtypeStruct((tokens, width), jnp.bfloat16),
        in_specs=anywhere(2),
        out_specs=pl.BlockSpec(memory_space=pltpu.VMEM),
        scratch_shapes=[
            pltpu.VMEM(routes.shape, routes.dtype),
            pltpu.VMEM(returned.shape, returned.dtype),
            pltpu.SemaphoreType.DMA((2,)),
        ],
        compiler_params=params(),
        cost_estimate=cost(4 * blocks * ROWS * tokens * width, 4 * tokens * width),
        name="merge",
    )(routes, returned)


def spill_picks(blocks, pieces):
    extras = blocks * (MOST - ROWS)
    shape = (pieces * extras, blocks * ROWS)
    index = lax.broadcasted_iota(jnp.int32, shape, 0)
    row = lax.broadcasted_iota(jnp.int32, shape, 1)
    return ones(row == (index % extras) * pieces + index // extras)


def unpack(packed, first, out):
    blocks, width = packed.shape[0], out.shape[1]
    pieces, step = cut(width)
    extras = blocks * (MOST - ROWS)
    for at in range(blocks):
        out[first + at * ROWS : first + (at + 1) * ROWS, :] = packed[at, :, :width]
    tails = jnp.concatenate([packed[at, :, width:] for at in range(blocks)], 0)
    placed = dot(spill_picks(blocks, pieces), tails).astype(jnp.bfloat16)
    spill = slice(first + blocks * ROWS, first + blocks * MOST)
    for at in range(pieces):
        out[spill, at * step : (at + 1) * step] = placed[at * extras : (at + 1) * extras]


def tile_of(index, tile):
    return pl.ds(pl.multiple_of(index * tile, tile), tile)


def weight_copy(source, target, arrived, index, axis, tile):
    here = tile_of(index, tile)
    view = source.at[:, here] if axis else source.at[here, :]
    return pltpu.make_async_copy(view, target.at[index], arrived.at[index])


def halves(group, half, out):
    here = slice(half * ROWS, (half + 1) * ROWS)
    pairs, at = [], 0
    for item in group:
        if len(item.shape) == 2:
            pairs.append((item.at[here, :], out.at[at]))
            at += 1
        else:
            pairs.append((item.at[:, here, :], out.at[at : at + item.shape[0]]))
            at += item.shape[0]
    return pairs


def hidden_grads(pre_gate, pre_up, d_hidden):
    sig = 0.5 * jnp.tanh(0.5 * pre_gate) + 0.5
    silu = pre_gate * sig
    hidden = (silu * pre_up).astype(jnp.bfloat16)
    d_gate = (d_hidden * pre_up * (sig + silu * (1.0 - sig))).astype(jnp.bfloat16)
    d_up = (d_hidden * silu).astype(jnp.bfloat16)
    return hidden, d_gate, d_up


def back(tile, share, me, part, order, group, gate_proj, up_proj, down_proj):
    blocks = len(group)
    width, hid = gate_proj.shape
    slots = blocks * MOST
    pieces, step = cut(width)
    tiles = hid // tile
    chunk = 2 * step
    chunks = width // chunk
    shape = (blocks, ROWS, width + step)
    given = 3 * hid + 2 * share

    def kernel(me_ref, part_ref, *refs):
        refs = list(refs)
        group_refs = [refs.pop(0) for _ in range(blocks)]
        gate_ref, up_ref, down_ref, out, kept, handed = [refs.pop(0) for _ in range(6)]
        x_held, dy_held, rows, scaled, factors, cuts = [refs.pop(0) for _ in range(6)]
        staged, gate, up, down = [refs.pop(0) for _ in range(4)]
        x_in, dy_in, gate_in, up_in, down_in, gone, cut_in = refs
        x_pairs, dy_pairs = halves(group_refs, 0, x_held), halves(group_refs, 1, dy_held)

        def column_copy(source, target, arrived, index):
            here = slice(index * tile, (index + 1) * tile)
            return pltpu.make_async_copy(
                source.at[:, here], target.at[:, here], arrived.at[index]
            )

        def fetch_x(index):
            column_copy(gate_ref, gate, gate_in, index).start()
            column_copy(up_ref, up, up_in, index).start()

        def fetch_dy(index):
            weight_copy(down_ref, down, down_in, index, 0, tile).start()

        def leave(index):
            columns = slice(index * chunk, (index + 1) * chunk)
            return pltpu.make_async_copy(
                staged.at[:, :, columns], out.at[:, :, columns], gone.at[index]
            )

        first, behind = slice(0, 3 * hid), slice(3 * hid, given)
        leaving = [(factors, kept.at[:, first]), (cuts.at[0], kept.at[:, behind])]
        leaving += [(factors, handed.at[:, first]), (cuts.at[1], handed.at[:, behind])]

        start(x_pairs, x_in)
        fetch_x(0)
        wait(x_pairs, x_in)
        start(dy_pairs, dy_in)
        fetch_dy(0)
        unpack(x_held, 0, rows)
        for now in range(tiles):
            columns = slice(now * tile, (now + 1) * tile)
            column_copy(gate_ref, gate, gate_in, now).wait()
            pre_gate = dot(rows[...], gate[:, columns])
            if now < tiles - 1:
                fetch_x(now + 1)
            column_copy(up_ref, up, up_in, now).wait()
            pre_up = dot(rows[...], up[:, columns])
            if now == 0:
                wait(dy_pairs, dy_in)
                unpack(dy_held, 0, scaled)
            if now < tiles - 1:
                fetch_dy(now + 1)
            weight_copy(down_ref, down, down_in, now, 0, tile).wait()
            d_hidden = dot(scaled[...], down[now], BY_WIDTH)
            made, d_gate, d_up = hidden_grads(pre_gate, pre_up, d_hidden)
            factors[:, columns] = made
            factors[:, hid + now * tile : hid + (now + 1) * tile] = d_gate
            factors[:, 2 * hid + now * tile : 2 * hid + (now + 1) * tile] = d_up

        for at in range(2):
            columns = tile_of(part_ref[0] ^ at, share)
            cuts[at, :, :share] = rows[:, columns]
            cuts[at, :, share:] = scaled[:, columns]
        start(leaving, cut_in)
        extras = []
        for at in range(chunks):
            here = slice(at * chunk, (at + 1) * chunk)
            done = dot(factors[:, hid : 2 * hid], gate[here, :], BY_WIDTH)
            done += dot(factors[:, 2 * hid :], up[here, :], BY_WIDTH)
            done = done.astype(jnp.bfloat16)
            for block in range(blocks):
                staged[me_ref[0] ^ order[block], :, here] = done[block * ROWS : (block + 1) * ROWS]
            leave(at).start()
            extras += [done[blocks * ROWS :, :step], done[blocks * ROWS :, step:]]
        tail = dot(spill_picks(blocks, pieces), jnp.concatenate(extras, 0), BY_ROWS)
        tail = tail.astype(jnp.bfloat16)
        for block in range(blocks):
            staged[me_ref[0] ^ order[block], :, width:] = tail[block * ROWS : (block + 1) * ROWS]
        last = pltpu.make_async_copy(
            staged.at[:, :, width:], out.at[:, :, width:], gone.at[chunks]
        )
        last.start()
        for at in range(chunks):
            leave(at).wait()
        wait(leaving, cut_in)
        last.wait()

    return pl.pallas_call(
        kernel,
        out_shape=[
            jax.ShapeDtypeStruct(shape, jnp.bfloat16),
            jax.ShapeDtypeStruct((slots, given), jnp.bfloat16),
            jax.ShapeDtypeStruct((slots, given), jnp.bfloat16),
        ],
        in_specs=[pl.BlockSpec(memory_space=pltpu.SMEM)] * 2 + anywhere(blocks + 3),
        out_specs=anywhere(3),
        scratch_shapes=[
            pltpu.VMEM(shape, jnp.bfloat16),
            pltpu.VMEM(shape, jnp.bfloat16),
            pltpu.VMEM((slots, width), jnp.bfloat16),
            pltpu.VMEM((slots, width), jnp.bfloat16),
            pltpu.VMEM((slots, 3 * hid), jnp.bfloat16),
            pltpu.VMEM((2, slots, 2 * share), jnp.bfloat16),
            pltpu.VMEM(shape, jnp.bfloat16),
            pltpu.VMEM((width, hid), jnp.bfloat16),
            pltpu.VMEM((width, hid), jnp.bfloat16),
            pltpu.VMEM((tiles, tile, width), jnp.bfloat16),
            pltpu.SemaphoreType.DMA((blocks,)),
            pltpu.SemaphoreType.DMA((blocks,)),
            pltpu.SemaphoreType.DMA((tiles,)),
            pltpu.SemaphoreType.DMA((tiles,)),
            pltpu.SemaphoreType.DMA((tiles,)),
            pltpu.SemaphoreType.DMA((chunks + 1,)),
            pltpu.SemaphoreType.DMA((4,)),
        ],
        compiler_params=params(),
        cost_estimate=cost(50 * slots * width * hid, 4 * slots * width),
        name="back",
    )(me, part, *group, gate_proj, up_proj, down_proj)


def weight_grads(tile, share, part, known, groups, gate_proj, up_proj, down_proj):
    count, items = len(groups), len(groups[0])
    blocks = sum(item.shape[0] if item.ndim == 3 else 1 for item in groups[0])
    given = len(known)
    hid, width = down_proj.shape
    pieces, step = cut(width)
    slots = blocks * MOST
    total = (given + count) * slots
    tiles = hid // tile

    def kernel(part_ref, *refs):
        refs = list(refs)
        known_refs = [refs.pop(0) for _ in range(given)]
        group_refs = [[refs.pop(0) for _ in range(items)] for _ in range(count)]
        gate_ref, up_ref, down_ref = [refs.pop(0) for _ in range(3)]
        d_gate_ref, d_up_ref, d_down_ref = [refs.pop(0) for _ in range(3)]
        x_held, dy_held, x_all, dy_all = [refs.pop(0) for _ in range(4)]
        x_mine, dy_mine, factors = [refs.pop(0) for _ in range(3)]
        gate, up, down, x_in, dy_in, known_in, gate_in, up_in, down_in = refs[:9]
        made_gate, made_up, made_down, gate_out, up_out, down_out = refs[9:]
        columns = tile_of(part_ref[0], share)
        x_pairs, dy_pairs, known_pairs = [], [], []
        for at in range(count):
            x_pairs += halves(group_refs[at], 0, x_held.at[at])
            dy_pairs += halves(group_refs[at], 1, dy_held.at[at])
        for at in range(given):
            here = slice(at * slots, (at + 1) * slots)
            behind = 3 * hid
            known_pairs += [
                (known_refs[at].at[:, :behind], factors.at[here, :]),
                (known_refs[at].at[:, behind : behind + share], x_mine.at[here, :]),
                (known_refs[at].at[:, behind + share :], dy_mine.at[here, :]),
            ]

        def arrange(held, rows_out, target):
            for at in range(count):
                unpack(held.at[at], at * slots, rows_out)
            target[given * slots :, :] = rows_out[:, columns]

        def leave(source, target, gone, index, axis):
            here = tile_of(index, tile)
            view = target.at[:, here] if axis else target.at[here, :]
            return pltpu.make_async_copy(source.at[index], view, gone.at[index])

        def fetch_x(index):
            weight_copy(gate_ref, gate, gate_in, index, 1, tile).start()
            weight_copy(up_ref, up, up_in, index, 1, tile).start()

        def fetch_dy(index):
            weight_copy(down_ref, down, down_in, index, 0, tile).start()

        start(x_pairs, x_in)
        fetch_x(0)
        wait(x_pairs, x_in)
        start(dy_pairs, dy_in)
        fetch_dy(0)
        arrange(x_held, x_all, x_mine)
        for now in range(tiles):
            here = slice(now * tile, (now + 1) * tile)
            weight_copy(gate_ref, gate, gate_in, now, 1, tile).wait()
            pre_gate = dot(x_all[...], gate[now])
            weight_copy(up_ref, up, up_in, now, 1, tile).wait()
            pre_up = dot(x_all[...], up[now])
            if now == 0:
                wait(dy_pairs, dy_in)
                start(known_pairs, known_in)
                arrange(dy_held, dy_all, dy_mine)
            if now < tiles - 1:
                fetch_x(now + 1)
                fetch_dy(now + 1)
            weight_copy(down_ref, down, down_in, now, 0, tile).wait()
            d_hidden = dot(dy_all[...], down[now], BY_WIDTH)
            made, d_gate, d_up = hidden_grads(pre_gate, pre_up, d_hidden)
            if now == 0:
                wait(known_pairs, known_in)
            made = jnp.concatenate([factors[:, here], made], 0)
            d_gate = jnp.concatenate([factors[:, hid + here.start : hid + here.stop], d_gate], 0)
            d_up = jnp.concatenate(
                [factors[:, 2 * hid + here.start : 2 * hid + here.stop], d_up], 0
            )
            sums = dot(x_mine[...], jnp.concatenate([d_gate, d_up], 1), BY_ROWS)
            made_gate[now] = sums[:, :tile]
            made_up[now] = sums[:, tile:]
            leave(made_gate, d_gate_ref, gate_out, now, 1).start()
            leave(made_up, d_up_ref, up_out, now, 1).start()
            made_down[now] = dot(made, dy_mine[...], BY_ROWS)
            leave(made_down, d_down_ref, down_out, now, 0).start()
        for at in range(tiles):
            leave(made_gate, d_gate_ref, gate_out, at, 1).wait()
            leave(made_up, d_up_ref, up_out, at, 1).wait()
            leave(made_down, d_down_ref, down_out, at, 0).wait()

    held = pltpu.VMEM((count, blocks, ROWS, width + step), jnp.bfloat16)
    arranged = pltpu.VMEM((count * slots, width), jnp.bfloat16)
    mine = pltpu.VMEM((total, share), jnp.bfloat16)
    return pl.pallas_call(
        kernel,
        out_shape=[
            jax.ShapeDtypeStruct((share, hid), jnp.float32),
            jax.ShapeDtypeStruct((share, hid), jnp.float32),
            jax.ShapeDtypeStruct((hid, share), jnp.float32),
        ],
        in_specs=[pl.BlockSpec(memory_space=pltpu.SMEM)] + anywhere(given + count * items + 3),
        out_specs=anywhere(3),
        scratch_shapes=[
            held,
            held,
            arranged,
            arranged,
            mine,
            mine,
            pltpu.VMEM((given * slots, 3 * hid), jnp.bfloat16),
            pltpu.VMEM((tiles, width, tile), jnp.bfloat16),
            pltpu.VMEM((tiles, width, tile), jnp.bfloat16),
            pltpu.VMEM((tiles, tile, width), jnp.bfloat16),
            pltpu.SemaphoreType.DMA((count * items,)),
            pltpu.SemaphoreType.DMA((count * items,)),
            pltpu.SemaphoreType.DMA((3 * given,)),
            pltpu.SemaphoreType.DMA((tiles,)),
            pltpu.SemaphoreType.DMA((tiles,)),
            pltpu.SemaphoreType.DMA((tiles,)),
            pltpu.VMEM((tiles, share, tile), jnp.float32),
            pltpu.VMEM((tiles, share, tile), jnp.float32),
            pltpu.VMEM((tiles, tile, share), jnp.float32),
            pltpu.SemaphoreType.DMA((tiles,)),
            pltpu.SemaphoreType.DMA((tiles,)),
            pltpu.SemaphoreType.DMA((tiles,)),
        ],
        compiler_params=params(),
        cost_estimate=cost(0, 4 * slots * width),
        name="weight_grads",
    )(part, *known, *[item for group in groups for item in group], gate_proj, up_proj, down_proj)


def swap(value, axis, distance):
    size = lax.axis_size(axis)
    return lax.ppermute(value, axis, [(at, at ^ distance) for at in range(size)])


def exchange(blocks):
    return lax.all_to_all(blocks, "expert", split_axis=0, concat_axis=0, tiled=True)


def after(value, *earlier):
    return lax.optimization_barrier((value, *earlier))[0]


def gather_body(tokens, cotangent, routes, expert_gates, gate_proj, up_proj, down_proj):
    blocks = lax.axis_size("expert")
    tile, share = 256, tokens.shape[1] // lax.axis_size("dp")
    me = lax.axis_index("expert").astype(jnp.int32).reshape(1)
    part = lax.axis_index("dp").astype(jnp.int32).reshape(1)
    routes = routes.reshape(1, -1)
    gates = expert_gates.reshape(1, -1)
    weights = (gate_proj, up_proj, down_proj)
    received = list(pack(blocks, me, routes, gates, tokens, cotangent))
    for distance in reversed(range(1, blocks)):
        received[distance] = swap(received[distance], "expert", distance)
    order = [0, 1, 2, 6, 4, 7, 5, 3]
    early = 3
    received = [received[index] for index in order]
    far = swap(join(received[:early]), "dp", 2)
    work = 50 * blocks * MOST * gate_proj.size
    far_rest = swap(join(received[early:], work), "dp", 2)
    sent, kept, handed = back(tile, share, me, part, order, received, *weights)
    last = swap(far, "dp", 1)
    sent, last = lax.optimization_barrier((sent, last))
    returned = exchange(sent)
    far = [far, after(far_rest, sent)]
    last = [last, swap(far[1], "dp", 1)]
    known = [kept, swap(handed, "dp", 1)]
    grads = weight_grads(tile, share, part, known, [far, last], *weights)
    return (merge(routes, after(returned, *grads)), *grads)


def body(tokens, cotangent, routes, expert_gates, gate_proj, up_proj, down_proj):
    groups, blocks = lax.axis_size("dp"), lax.axis_size("expert")
    width, hid = gate_proj.shape
    rows_sent = (groups - 1) * 2 * blocks * MOST * width
    grads_sent = 3 * width * hid * (groups - 1) // groups
    fits = blocks == EXPERTS and groups == 4 and hid % 256 == 0
    fits = fits and tokens.shape[0] == 128 and routes.shape[1] == 1 and width // groups % 128 == 0
    chosen = gather_body if fits and rows_sent < grads_sent else scatter_body
    return chosen(tokens, cotangent, routes, expert_gates, gate_proj, up_proj, down_proj)


def solution(mesh):
    in_specs = (
        P(("dp", "expert"), None),
        P(("dp", "expert"), None),
        P(("dp", "expert"), None),
        P(("dp", "expert"), None),
        P(None, "expert"),
        P(None, "expert"),
        P("expert", None),
    )
    out_specs = (P(("dp", "expert"), None), P("dp", "expert"), P("dp", "expert"), P("expert", "dp"))
    return jax.shard_map(body, mesh=mesh, in_specs=in_specs, out_specs=out_specs, check_vma=False)
```

```python
import jax
import jax.numpy as jnp
from jax import lax
from jax.experimental import pallas as pl
from jax.experimental.pallas import tpu as pltpu
from jax.sharding import PartitionSpec as P

EXPERTS = 8
MOST = 18
ROWS = 16
VMEM_BYTES = (63 * 1024 + 768) * 1024


def build_slots(routes, capacity):
    flat_routes = routes.reshape(-1)
    one_hot = (flat_routes[:, None] == jnp.arange(EXPERTS, dtype=jnp.int32)[None, :]).astype(
        jnp.int32
    )
    before = jnp.cumsum(one_hot, axis=0) - one_hot
    position = jnp.sum(before * one_hot, axis=1)
    return flat_routes * capacity + position


def scatter_body(tokens, cotangent, routes, expert_gates, gate_proj, up_proj, down_proj):
    tok_dev, model_dim = tokens.shape
    top_k = routes.shape[1]
    expert_devs = lax.axis_size("expert")
    group_size = expert_devs // EXPERTS
    capacity = MOST
    slot_total = EXPERTS * capacity
    slot_of = build_slots(routes, capacity)
    owners = jnp.arange(tok_dev * top_k, dtype=jnp.int32) // top_k
    slot_table = jnp.full((slot_total,), tok_dev, jnp.int32).at[slot_of].set(owners)
    slot_gate = jnp.zeros((slot_total,), jnp.float32).at[slot_of].set(expert_gates.reshape(-1))
    x_slots = jnp.take(tokens, slot_table, axis=0, mode="fill", fill_value=0)
    dy_slots = (
        jnp.take(cotangent, slot_table, axis=0, mode="fill", fill_value=0).astype(jnp.float32)
        * slot_gate[:, None]
    ).astype(jnp.bfloat16)

    def copies(values):
        spread = values.reshape(EXPERTS, 1, capacity, model_dim)
        return jnp.broadcast_to(spread, (EXPERTS, group_size, capacity, model_dim)).reshape(
            expert_devs, capacity, model_dim
        )

    x_recv, dy_recv = (
        lax.all_to_all(copies(x_slots), "expert", split_axis=0, concat_axis=0, tiled=True),
        lax.all_to_all(copies(dy_slots), "expert", split_axis=0, concat_axis=0, tiled=True),
    )
    in_rows = x_recv.reshape(expert_devs * capacity, model_dim)
    scaled = dy_recv.reshape(expert_devs * capacity, model_dim)
    pre_gate = jnp.dot(in_rows, gate_proj, preferred_element_type=jnp.float32)
    pre_up = jnp.dot(in_rows, up_proj, preferred_element_type=jnp.float32)
    gate_sig = jax.nn.sigmoid(pre_gate)
    hidden = (pre_gate * gate_sig * pre_up).astype(jnp.bfloat16)
    by_width = (((1,), (1,)), ((), ()))
    by_rows = (((0,), (0,)), ((), ()))
    d_hidden = lax.dot_general(scaled, down_proj, by_width, preferred_element_type=jnp.float32)
    d_gate = (d_hidden * pre_up * gate_sig * (1.0 + pre_gate * (1.0 - gate_sig))).astype(
        jnp.bfloat16
    )
    d_up = (d_hidden * pre_gate * gate_sig).astype(jnp.bfloat16)
    grad_down = lax.dot_general(hidden, scaled, by_rows, preferred_element_type=jnp.float32)
    grad_gate = lax.dot_general(in_rows, d_gate, by_rows, preferred_element_type=jnp.float32)
    grad_up = lax.dot_general(in_rows, d_up, by_rows, preferred_element_type=jnp.float32)
    grad_gate, grad_up, grad_down = (
        lax.psum_scatter(
            grad_gate.astype(jnp.bfloat16), "dp", scatter_dimension=0, tiled=True
        ).astype(jnp.float32),
        lax.psum_scatter(
            grad_up.astype(jnp.bfloat16), "dp", scatter_dimension=0, tiled=True
        ).astype(jnp.float32),
        lax.psum_scatter(
            grad_down.astype(jnp.bfloat16), "dp", scatter_dimension=1, tiled=True
        ).astype(jnp.float32),
    )
    joined_grads = jnp.concatenate([d_gate, d_up], 1)
    joined_proj = jnp.concatenate([gate_proj, up_proj], 1)
    partial_value = lax.dot_general(
        joined_grads, joined_proj, by_width, preferred_element_type=jnp.float32
    ).astype(jnp.bfloat16)
    returned = lax.all_to_all(
        partial_value.reshape(expert_devs, capacity, model_dim),
        "expert",
        split_axis=0,
        concat_axis=0,
        tiled=True,
    )
    summed = jnp.sum(
        returned.reshape(EXPERTS, group_size, capacity, model_dim).astype(jnp.float32), axis=1
    )
    summed = summed.reshape(slot_total, model_dim)
    grad_input = jnp.take(summed, slot_of, axis=0).reshape(tok_dev, top_k, model_dim).sum(axis=1)
    return (grad_input.astype(jnp.bfloat16), grad_gate, grad_up, grad_down)


BY_WIDTH = (((1,), (1,)), ((), ()))
BY_ROWS = (((0,), (0,)), ((), ()))


def cut(width):
    pieces = ROWS // (MOST - ROWS)
    return pieces, width // pieces


def width_of(packed):
    pieces = ROWS // (MOST - ROWS)
    return packed.shape[2] * pieces // (pieces + 1)


def cost(flops, moved):
    return pl.CostEstimate(flops=flops, bytes_accessed=moved, transcendentals=0)


def params():
    return pltpu.CompilerParams(vmem_limit_bytes=VMEM_BYTES)


def anywhere(count):
    return [pl.BlockSpec(memory_space=pl.ANY)] * count


def dot(left, right, dims=(((1,), (0,)), ((), ()))):
    return lax.dot_general(left, right, dims, preferred_element_type=jnp.float32)


def ones(mask):
    return jnp.where(mask, 1.0, 0.0).astype(jnp.bfloat16)


def start(pairs, arrived, first=0):
    for at, (source, target) in enumerate(pairs):
        if at >= first:
            pltpu.make_async_copy(source, target, arrived.at[at]).start()


def wait(pairs, arrived, first=0):
    for at, (source, target) in enumerate(pairs):
        if at >= first:
            pltpu.make_async_copy(source, target, arrived.at[at]).wait()


def slot_masks(routes, blocks, width, me=0):
    tokens = routes.shape[1]
    pieces, _ = cut(width)
    experts = lax.broadcasted_iota(jnp.int32, (EXPERTS, tokens), 0)
    named = jnp.where(experts == routes, 1.0, 0.0)
    earlier = lax.broadcasted_iota(jnp.int32, (tokens, tokens), 0) < lax.broadcasted_iota(
        jnp.int32, (tokens, tokens), 1
    )
    before = dot(named.astype(jnp.bfloat16), ones(earlier))
    position = jnp.sum(before * named, axis=0, keepdims=True).astype(jnp.int32)
    slot = lax.broadcasted_iota(jnp.int32, (blocks * ROWS, tokens), 0)
    row = slot % ROWS
    mine = (slot // ROWS) ^ me == routes
    main = mine & (position == row)
    spill = mine & (position == ROWS + row // pieces)
    return main, spill, row % pieces


def pack(blocks, me, routes, gates, tokens, cotangent):
    count, width = tokens.shape
    pieces, step = cut(width)
    sources = (routes, gates, tokens, cotangent)
    block_shape = (2 * ROWS, width + step)

    def kernel(me_ref, *refs):
        outs, held = refs[4 : 4 + blocks], refs[4 + blocks : 8 + blocks]
        staged, arrived, gone = refs[8 + blocks :]
        pairs = list(zip(refs[:4], held))
        start(pairs, arrived)
        wait(pairs[:2], arrived)
        main, spill, piece = slot_masks(held[0][...], blocks, width, me_ref[0])
        mains = ones(main)
        picks = jnp.concatenate([ones(spill & (piece == at)) for at in range(pieces)], 1)
        main_scale = jnp.sum(jnp.where(main, held[1][...], 0.0), axis=1, keepdims=True)
        spill_scale = jnp.sum(jnp.where(spill, held[1][...], 0.0), axis=1, keepdims=True)
        leaving = []
        for half in range(2):
            wait(pairs[: 3 + half], arrived, 2 + half)
            values = held[2 + half]
            rows = dot(mains, values[...])
            cuts = [values[:, at * step : (at + 1) * step] for at in range(pieces)]
            extra = dot(picks, jnp.concatenate(cuts, 0))
            if half > 0:
                rows, extra = rows * main_scale, extra * spill_scale
            rows = rows.astype(jnp.bfloat16)
            extra = extra.astype(jnp.bfloat16)
            here = slice(half * ROWS, (half + 1) * ROWS)
            for block in range(blocks):
                part = slice(block * ROWS, (block + 1) * ROWS)
                staged[block, here, :width] = rows[part]
                staged[block, here, width:] = extra[part]
            sent = [(staged.at[at, here], outs[at].at[here, :]) for at in range(blocks)]
            leaving += sent
            start(leaving, gone, half * blocks)
        wait(leaving, gone)

    return pl.pallas_call(
        kernel,
        out_shape=[jax.ShapeDtypeStruct(block_shape, jnp.bfloat16)] * blocks,
        in_specs=[pl.BlockSpec(memory_space=pltpu.SMEM)] + anywhere(4),
        out_specs=anywhere(blocks),
        scratch_shapes=[pltpu.VMEM(source.shape, source.dtype) for source in sources]
        + [
            pltpu.VMEM((blocks,) + block_shape, jnp.bfloat16),
            pltpu.SemaphoreType.DMA((4,)),
            pltpu.SemaphoreType.DMA((2 * blocks,)),
        ],
        compiler_params=params(),
        cost_estimate=cost(8 * blocks * ROWS * count * width, 8 * count * width),
        name="pack",
    )(me, *sources)


def join(received, flops=0):
    count = len(received)
    shape = (count,) + received[0].shape

    def kernel(*refs):
        out, held, arrived, gone = refs[count:]
        pairs = [(refs[at], held.at[at]) for at in range(count)]
        leaving = [(held.at[at], out.at[at]) for at in range(count)]
        start(pairs, arrived)
        for at in range(count):
            wait(pairs[: at + 1], arrived, at)
            start(leaving[: at + 1], gone, at)
        wait(leaving, gone)

    return pl.pallas_call(
        kernel,
        out_shape=jax.ShapeDtypeStruct(shape, jnp.bfloat16),
        in_specs=anywhere(count),
        out_specs=pl.BlockSpec(memory_space=pl.ANY),
        scratch_shapes=[
            pltpu.VMEM(shape, jnp.bfloat16),
            pltpu.SemaphoreType.DMA((count,)),
            pltpu.SemaphoreType.DMA((count,)),
        ],
        compiler_params=params(),
        cost_estimate=cost(flops, 4 * received[0].size * count),
        name="join",
    )(*received)


def merge(routes, returned):
    blocks = returned.shape[0]
    tokens = routes.shape[1]
    width = width_of(returned)
    pieces, step = cut(width)

    def kernel(routes_ref, back_ref, out, named, held, arrived):
        pairs = [(routes_ref, named), (back_ref, held)]
        start(pairs, arrived)
        wait(pairs[:1], arrived)
        main, spill, piece = slot_masks(named[...], blocks, width)
        mains = ones(main)
        picks = [ones(spill & (piece == at)) for at in range(pieces)]
        wait(pairs, arrived, 1)
        rows = jnp.concatenate([held[at, :, :width] for at in range(blocks)], 0)
        extra = jnp.concatenate([held[at, :, width:] for at in range(blocks)], 0)
        picked = dot(mains, rows, BY_ROWS)
        for at in range(pieces):
            columns = slice(at * step, (at + 1) * step)
            out[:, columns] = (picked[:, columns] + dot(picks[at], extra, BY_ROWS)).astype(
                jnp.bfloat16
            )

    return pl.pallas_call(
        kernel,
        out_shape=jax.ShapeDtypeStruct((tokens, width), jnp.bfloat16),
        in_specs=anywhere(2),
        out_specs=pl.BlockSpec(memory_space=pltpu.VMEM),
        scratch_shapes=[
            pltpu.VMEM(routes.shape, routes.dtype),
            pltpu.VMEM(returned.shape, returned.dtype),
            pltpu.SemaphoreType.DMA((2,)),
        ],
        compiler_params=params(),
        cost_estimate=cost(4 * blocks * ROWS * tokens * width, 4 * tokens * width),
        name="merge",
    )(routes, returned)


def spill_picks(blocks, pieces):
    extras = blocks * (MOST - ROWS)
    shape = (pieces * extras, blocks * ROWS)
    index = lax.broadcasted_iota(jnp.int32, shape, 0)
    row = lax.broadcasted_iota(jnp.int32, shape, 1)
    return ones(row == (index % extras) * pieces + index // extras)


def unpack(packed, first, out):
    blocks, width = packed.shape[0], out.shape[1]
    pieces, step = cut(width)
    extras = blocks * (MOST - ROWS)
    for at in range(blocks):
        out[first + at * ROWS : first + (at + 1) * ROWS, :] = packed[at, :, :width]
    tails = jnp.concatenate([packed[at, :, width:] for at in range(blocks)], 0)
    placed = dot(spill_picks(blocks, pieces), tails).astype(jnp.bfloat16)
    spill = slice(first + blocks * ROWS, first + blocks * MOST)
    for at in range(pieces):
        out[spill, at * step : (at + 1) * step] = placed[at * extras : (at + 1) * extras]


def tile_of(index, tile):
    return pl.ds(pl.multiple_of(index * tile, tile), tile)


def weight_copy(source, target, arrived, index, axis, tile):
    here = tile_of(index, tile)
    view = source.at[:, here] if axis else source.at[here, :]
    return pltpu.make_async_copy(view, target.at[index], arrived.at[index])


def halves(group, half, out):
    here = slice(half * ROWS, (half + 1) * ROWS)
    pairs, at = [], 0
    for item in group:
        if len(item.shape) == 2:
            pairs.append((item.at[here, :], out.at[at]))
            at += 1
        else:
            pairs.append((item.at[:, here, :], out.at[at : at + item.shape[0]]))
            at += item.shape[0]
    return pairs


def hidden_grads(pre_gate, pre_up, d_hidden):
    sig = 0.5 * jnp.tanh(0.5 * pre_gate) + 0.5
    silu = pre_gate * sig
    hidden = (silu * pre_up).astype(jnp.bfloat16)
    d_gate = (d_hidden * pre_up * (sig + silu * (1.0 - sig))).astype(jnp.bfloat16)
    d_up = (d_hidden * silu).astype(jnp.bfloat16)
    return hidden, d_gate, d_up


def back(tile, share, me, part, order, group, gate_proj, up_proj, down_proj):
    blocks = len(group)
    width, hid = gate_proj.shape
    slots = blocks * MOST
    pieces, step = cut(width)
    tiles = hid // tile
    chunk = 2 * step
    chunks = width // chunk
    shape = (blocks, ROWS, width + step)
    given = 3 * hid + 2 * share

    def kernel(me_ref, part_ref, *refs):
        refs = list(refs)
        group_refs = [refs.pop(0) for _ in range(blocks)]
        gate_ref, up_ref, down_ref, out, kept, handed = [refs.pop(0) for _ in range(6)]
        x_held, dy_held, rows, scaled, factors, cuts = [refs.pop(0) for _ in range(6)]
        staged, gate, up, down = [refs.pop(0) for _ in range(4)]
        x_in, dy_in, gate_in, up_in, down_in, gone, cut_in = refs
        x_pairs, dy_pairs = halves(group_refs, 0, x_held), halves(group_refs, 1, dy_held)

        def column_copy(source, target, arrived, index):
            here = slice(index * tile, (index + 1) * tile)
            return pltpu.make_async_copy(
                source.at[:, here], target.at[:, here], arrived.at[index]
            )

        def fetch_x(index):
            column_copy(gate_ref, gate, gate_in, index).start()
            column_copy(up_ref, up, up_in, index).start()

        def fetch_dy(index):
            weight_copy(down_ref, down, down_in, index, 0, tile).start()

        def leave(index):
            columns = slice(index * chunk, (index + 1) * chunk)
            return pltpu.make_async_copy(
                staged.at[:, :, columns], out.at[:, :, columns], gone.at[index]
            )

        first, behind = slice(0, 3 * hid), slice(3 * hid, given)
        leaving = [(factors, kept.at[:, first]), (cuts.at[0], kept.at[:, behind])]
        leaving += [(factors, handed.at[:, first]), (cuts.at[1], handed.at[:, behind])]

        start(x_pairs, x_in)
        fetch_x(0)
        wait(x_pairs, x_in)
        start(dy_pairs, dy_in)
        fetch_dy(0)
        unpack(x_held, 0, rows)
        for now in range(tiles):
            columns = slice(now * tile, (now + 1) * tile)
            column_copy(gate_ref, gate, gate_in, now).wait()
            pre_gate = dot(rows[...], gate[:, columns])
            if now < tiles - 1:
                fetch_x(now + 1)
            column_copy(up_ref, up, up_in, now).wait()
            pre_up = dot(rows[...], up[:, columns])
            if now == 0:
                wait(dy_pairs, dy_in)
                unpack(dy_held, 0, scaled)
            if now < tiles - 1:
                fetch_dy(now + 1)
            weight_copy(down_ref, down, down_in, now, 0, tile).wait()
            d_hidden = dot(scaled[...], down[now], BY_WIDTH)
            made, d_gate, d_up = hidden_grads(pre_gate, pre_up, d_hidden)
            factors[:, columns] = made
            factors[:, hid + now * tile : hid + (now + 1) * tile] = d_gate
            factors[:, 2 * hid + now * tile : 2 * hid + (now + 1) * tile] = d_up

        for at in range(2):
            columns = tile_of(part_ref[0] ^ at, share)
            cuts[at, :, :share] = rows[:, columns]
            cuts[at, :, share:] = scaled[:, columns]
        start(leaving, cut_in)
        extras = []
        for at in range(chunks):
            here = slice(at * chunk, (at + 1) * chunk)
            done = dot(factors[:, hid : 2 * hid], gate[here, :], BY_WIDTH)
            done += dot(factors[:, 2 * hid :], up[here, :], BY_WIDTH)
            done = done.astype(jnp.bfloat16)
            for block in range(blocks):
                staged[me_ref[0] ^ order[block], :, here] = done[block * ROWS : (block + 1) * ROWS]
            leave(at).start()
            extras += [done[blocks * ROWS :, :step], done[blocks * ROWS :, step:]]
        tail = dot(spill_picks(blocks, pieces), jnp.concatenate(extras, 0), BY_ROWS)
        tail = tail.astype(jnp.bfloat16)
        for block in range(blocks):
            staged[me_ref[0] ^ order[block], :, width:] = tail[block * ROWS : (block + 1) * ROWS]
        last = pltpu.make_async_copy(
            staged.at[:, :, width:], out.at[:, :, width:], gone.at[chunks]
        )
        last.start()
        for at in range(chunks):
            leave(at).wait()
        wait(leaving, cut_in)
        last.wait()

    return pl.pallas_call(
        kernel,
        out_shape=[
            jax.ShapeDtypeStruct(shape, jnp.bfloat16),
            jax.ShapeDtypeStruct((slots, given), jnp.bfloat16),
            jax.ShapeDtypeStruct((slots, given), jnp.bfloat16),
        ],
        in_specs=[pl.BlockSpec(memory_space=pltpu.SMEM)] * 2 + anywhere(blocks + 3),
        out_specs=anywhere(3),
        scratch_shapes=[
            pltpu.VMEM(shape, jnp.bfloat16),
            pltpu.VMEM(shape, jnp.bfloat16),
            pltpu.VMEM((slots, width), jnp.bfloat16),
            pltpu.VMEM((slots, width), jnp.bfloat16),
            pltpu.VMEM((slots, 3 * hid), jnp.bfloat16),
            pltpu.VMEM((2, slots, 2 * share), jnp.bfloat16),
            pltpu.VMEM(shape, jnp.bfloat16),
            pltpu.VMEM((width, hid), jnp.bfloat16),
            pltpu.VMEM((width, hid), jnp.bfloat16),
            pltpu.VMEM((tiles, tile, width), jnp.bfloat16),
            pltpu.SemaphoreType.DMA((blocks,)),
            pltpu.SemaphoreType.DMA((blocks,)),
            pltpu.SemaphoreType.DMA((tiles,)),
            pltpu.SemaphoreType.DMA((tiles,)),
            pltpu.SemaphoreType.DMA((tiles,)),
            pltpu.SemaphoreType.DMA((chunks + 1,)),
            pltpu.SemaphoreType.DMA((4,)),
        ],
        compiler_params=params(),
        cost_estimate=cost(50 * slots * width * hid, 4 * slots * width),
        name="back",
    )(me, part, *group, gate_proj, up_proj, down_proj)


def weight_grads(tile, share, part, known, groups, gate_proj, up_proj, down_proj):
    count, items = len(groups), len(groups[0])
    blocks = sum(item.shape[0] if item.ndim == 3 else 1 for item in groups[0])
    given = len(known)
    hid, width = down_proj.shape
    pieces, step = cut(width)
    slots = blocks * MOST
    total = (given + count) * slots
    tiles = hid // tile

    def kernel(part_ref, *refs):
        refs = list(refs)
        known_refs = [refs.pop(0) for _ in range(given)]
        group_refs = [[refs.pop(0) for _ in range(items)] for _ in range(count)]
        gate_ref, up_ref, down_ref = [refs.pop(0) for _ in range(3)]
        d_gate_ref, d_up_ref, d_down_ref = [refs.pop(0) for _ in range(3)]
        x_held, dy_held, x_all, dy_all = [refs.pop(0) for _ in range(4)]
        x_mine, dy_mine, factors = [refs.pop(0) for _ in range(3)]
        gate, up, down, x_in, dy_in, known_in, gate_in, up_in, down_in = refs[:9]
        made_gate, made_up, made_down, gate_out, up_out, down_out = refs[9:]
        columns = tile_of(part_ref[0], share)
        x_pairs, dy_pairs, known_pairs = [], [], []
        for at in range(count):
            x_pairs += halves(group_refs[at], 0, x_held.at[at])
            dy_pairs += halves(group_refs[at], 1, dy_held.at[at])
        for at in range(given):
            here = slice(at * slots, (at + 1) * slots)
            behind = 3 * hid
            known_pairs += [
                (known_refs[at].at[:, :behind], factors.at[here, :]),
                (known_refs[at].at[:, behind : behind + share], x_mine.at[here, :]),
                (known_refs[at].at[:, behind + share :], dy_mine.at[here, :]),
            ]

        def arrange(held, rows_out, target):
            for at in range(count):
                unpack(held.at[at], at * slots, rows_out)
            target[given * slots :, :] = rows_out[:, columns]

        def leave(source, target, gone, index, axis):
            here = tile_of(index, tile)
            view = target.at[:, here] if axis else target.at[here, :]
            return pltpu.make_async_copy(source.at[index], view, gone.at[index])

        def fetch_x(index):
            weight_copy(gate_ref, gate, gate_in, index, 1, tile).start()
            weight_copy(up_ref, up, up_in, index, 1, tile).start()

        def fetch_dy(index):
            weight_copy(down_ref, down, down_in, index, 0, tile).start()

        start(x_pairs, x_in)
        fetch_x(0)
        wait(x_pairs, x_in)
        start(dy_pairs, dy_in)
        fetch_dy(0)
        arrange(x_held, x_all, x_mine)
        for now in range(tiles):
            here = slice(now * tile, (now + 1) * tile)
            weight_copy(gate_ref, gate, gate_in, now, 1, tile).wait()
            pre_gate = dot(x_all[...], gate[now])
            weight_copy(up_ref, up, up_in, now, 1, tile).wait()
            pre_up = dot(x_all[...], up[now])
            if now == 0:
                wait(dy_pairs, dy_in)
                start(known_pairs, known_in)
                arrange(dy_held, dy_all, dy_mine)
            if now < tiles - 1:
                fetch_x(now + 1)
                fetch_dy(now + 1)
            weight_copy(down_ref, down, down_in, now, 0, tile).wait()
            d_hidden = dot(dy_all[...], down[now], BY_WIDTH)
            made, d_gate, d_up = hidden_grads(pre_gate, pre_up, d_hidden)
            if now == 0:
                wait(known_pairs, known_in)
            made = jnp.concatenate([factors[:, here], made], 0)
            d_gate = jnp.concatenate([factors[:, hid + here.start : hid + here.stop], d_gate], 0)
            d_up = jnp.concatenate(
                [factors[:, 2 * hid + here.start : 2 * hid + here.stop], d_up], 0
            )
            sums = dot(x_mine[...], jnp.concatenate([d_gate, d_up], 1), BY_ROWS)
            made_gate[now] = sums[:, :tile]
            made_up[now] = sums[:, tile:]
            leave(made_gate, d_gate_ref, gate_out, now, 1).start()
            leave(made_up, d_up_ref, up_out, now, 1).start()
            made_down[now] = dot(made, dy_mine[...], BY_ROWS)
            leave(made_down, d_down_ref, down_out, now, 0).start()
        for at in range(tiles):
            leave(made_gate, d_gate_ref, gate_out, at, 1).wait()
            leave(made_up, d_up_ref, up_out, at, 1).wait()
            leave(made_down, d_down_ref, down_out, at, 0).wait()

    held = pltpu.VMEM((count, blocks, ROWS, width + step), jnp.bfloat16)
    arranged = pltpu.VMEM((count * slots, width), jnp.bfloat16)
    mine = pltpu.VMEM((total, share), jnp.bfloat16)
    return pl.pallas_call(
        kernel,
        out_shape=[
            jax.ShapeDtypeStruct((share, hid), jnp.float32),
            jax.ShapeDtypeStruct((share, hid), jnp.float32),
            jax.ShapeDtypeStruct((hid, share), jnp.float32),
        ],
        in_specs=[pl.BlockSpec(memory_space=pltpu.SMEM)] + anywhere(given + count * items + 3),
        out_specs=anywhere(3),
        scratch_shapes=[
            held,
            held,
            arranged,
            arranged,
            mine,
            mine,
            pltpu.VMEM((given * slots, 3 * hid), jnp.bfloat16),
            pltpu.VMEM((tiles, width, tile), jnp.bfloat16),
            pltpu.VMEM((tiles, width, tile), jnp.bfloat16),
            pltpu.VMEM((tiles, tile, width), jnp.bfloat16),
            pltpu.SemaphoreType.DMA((count * items,)),
            pltpu.SemaphoreType.DMA((count * items,)),
            pltpu.SemaphoreType.DMA((3 * given,)),
            pltpu.SemaphoreType.DMA((tiles,)),
            pltpu.SemaphoreType.DMA((tiles,)),
            pltpu.SemaphoreType.DMA((tiles,)),
            pltpu.VMEM((tiles, share, tile), jnp.float32),
            pltpu.VMEM((tiles, share, tile), jnp.float32),
            pltpu.VMEM((tiles, tile, share), jnp.float32),
            pltpu.SemaphoreType.DMA((tiles,)),
            pltpu.SemaphoreType.DMA((tiles,)),
            pltpu.SemaphoreType.DMA((tiles,)),
        ],
        compiler_params=params(),
        cost_estimate=cost(0, 4 * slots * width),
        name="weight_grads",
    )(part, *known, *[item for group in groups for item in group], gate_proj, up_proj, down_proj)


def swap(value, axis, distance):
    size = lax.axis_size(axis)
    return lax.ppermute(value, axis, [(at, at ^ distance) for at in range(size)])


def exchange(blocks):
    return lax.all_to_all(blocks, "expert", split_axis=0, concat_axis=0, tiled=True)


def after(value, *earlier):
    return lax.optimization_barrier((value, *earlier))[0]


def gather_body(tokens, cotangent, routes, expert_gates, gate_proj, up_proj, down_proj):
    blocks = lax.axis_size("expert")
    tile, share = 256, tokens.shape[1] // lax.axis_size("dp")
    me = lax.axis_index("expert").astype(jnp.int32).reshape(1)
    part = lax.axis_index("dp").astype(jnp.int32).reshape(1)
    routes = routes.reshape(1, -1)
    gates = expert_gates.reshape(1, -1)
    weights = (gate_proj, up_proj, down_proj)
    received = list(pack(blocks, me, routes, gates, tokens, cotangent))
    for distance in reversed(range(1, blocks)):
        received[distance] = swap(received[distance], "expert", distance)
    order = [0, 1, 2, 4, 6, 5, 7, 3]
    early = 3
    received = [received[index] for index in order]
    far = swap(join(received[:early]), "dp", 2)
    work = 50 * blocks * MOST * gate_proj.size
    far_rest = swap(join(received[early:], work), "dp", 2)
    sent, kept, handed = back(tile, share, me, part, order, received, *weights)
    last = swap(far, "dp", 1)
    sent, last = lax.optimization_barrier((sent, last))
    returned = exchange(sent)
    far = [far, after(far_rest, sent)]
    last = [last, swap(far[1], "dp", 1)]
    known = [kept, swap(handed, "dp", 1)]
    grads = weight_grads(tile, share, part, known, [far, last], *weights)
    return (merge(routes, after(returned, *grads)), *grads)


def body(tokens, cotangent, routes, expert_gates, gate_proj, up_proj, down_proj):
    groups, blocks = lax.axis_size("dp"), lax.axis_size("expert")
    width, hid = gate_proj.shape
    rows_sent = (groups - 1) * 2 * blocks * MOST * width
    grads_sent = 3 * width * hid * (groups - 1) // groups
    fits = blocks == EXPERTS and groups == 4 and hid % 256 == 0
    fits = fits and tokens.shape[0] == 128 and routes.shape[1] == 1 and width // groups % 128 == 0
    chosen = gather_body if fits and rows_sent < grads_sent else scatter_body
    return chosen(tokens, cotangent, routes, expert_gates, gate_proj, up_proj, down_proj)


def solution(mesh):
    in_specs = (
        P(("dp", "expert"), None),
        P(("dp", "expert"), None),
        P(("dp", "expert"), None),
        P(("dp", "expert"), None),
        P(None, "expert"),
        P(None, "expert"),
        P("expert", None),
    )
    out_specs = (P(("dp", "expert"), None), P("dp", "expert"), P("dp", "expert"), P("expert", "dp"))
    return jax.shard_map(body, mesh=mesh, in_specs=in_specs, out_specs=out_specs, check_vma=False)
```
